32 devices in a mesh: grp: 2 (over y), ep: 4 (over z), tp: 4 (over x, core).
Axes of the slice: x: 2, y: 2, z: 4, core: 2. Of those that a mesh axis runs over, the one named last changes fastest.
Arguments:
- question_q: bfloat16 [1024, 32, 128], P(('grp', 'ep'), 'tp'), parts along dimension 0, may hold values from -125 to 125
- question_kv: bfloat16 [1024, 4, 2, 128], P(('grp', 'ep')), parts along dimension 0, may hold values from -6 to 6
- doc_kv: bfloat16 [16, 128, 4, 2, 128], P(('grp', 'ep')), parts along dimension 0, may hold values from -6 to 6
- doc_lens: int32 [16], P('grp'), parts along dimension 0, may hold values from 1 to 128, as said below
- query_docs: int32 [8, 4], P('grp'), parts along dimension 0, may hold values from 0 to 7, as said below
- ctx_pos: int32 [8, 5], P('grp'), parts along dimension 0, may hold values from 0 to 827, as said below
- hidden: bfloat16 [1024, 4096], P(('grp', 'ep'), 'tp'), parts along dimension 0, may hold values from -1.5 to 1.5
- out_proj: bfloat16 [4096, 4096], P('ep', 'tp'), may hold values from -0.0234375 to 0.0234375
- norm_gain: bfloat16 [4096], P('tp'), may hold values from 0.5 to 1.5
- router_weight: bfloat16 [4096, 16], P('tp'), may hold values from -0.046875 to 0.046875
- w_gate_up: bfloat16 [16, 4096, 2, 1024], P('ep', 'tp'), may hold values from -0.09375 to 0.09375
- w_down: bfloat16 [16, 1024, 4096], P('ep', None, 'tp'), may hold values from -0.1875 to 0.1875
- expert_ids: int32 [1024, 8], P(('grp', 'ep')), parts along dimension 0, may hold values from 0 to 15, all different within a row; in each aligned block of 128 rows (0 to 127, 128 to 255, ...) at most 64 rows name the same one
Outputs:
- layer_out: bfloat16 [1024, 4096], P(('grp', 'ep'), 'tp'), parts along dimension 0
The draws below stay inside these ranges and needn't reach their ends.
There are 2 independent parts, one for each index of `grp`. The reference program is written for one: setup_inputs(seed, part) draws one part's arguments, and reference() takes and returns one part's arrays. A program takes and returns all parts, laid end to end along the dimension named above; an argument that names none is the same for every part. Nothing has to cross between parts.
Inputs may be any that keep to these rules, and one draw needn't show every extreme that they name: `doc_lens`: document d is held at row d of doc_kv; some document of some query's list has exactly 128 tokens. `query_docs`: the 4 documents of a query lie in 4 different blocks of 2 consecutive documents. `ctx_pos`: in each row, every entry is at least the one before it plus the length of the document before it. `expert_ids`: each query's 128 tokens name every expert exactly 64 times.
All inputs are finite; a program needn't handle non-finite values.
Results may differ from the reference program's by a relative error of at most 0.017.
Values may be sent and summed in bfloat16 or wider, within the bound.
No kernel may reach another device: no remote copies, remote signals or barrier semaphores. Data moves between devices by JAX's collectives and lax.ppermute only.
A program may use at most 128 MiB of HBM per device.

```python
import math
import jax
import jax.numpy as jnp
import numpy as np
from jax import lax

D = 4096
QH = 32
KVH = 4
HD = 128
HID = 1024
TOP = 8
QLEN = 128
DOC_MAX = 128
POOL_DEV = 2
EXPERTS = 16
CAP = 64
DPQ = 4
QUERIES = 4
TOKENS = 512
POOL_DOCS = 8
N_TP = 4


def pool_plan(key):
    base = jax.random.fold_in(key, 11)
    owner_key, local_key, length_key, gap_key = jax.random.split(base, 4)
    owners_all = POOL_DOCS // POOL_DEV
    scores = jax.random.randint(owner_key, (QUERIES, owners_all), 0, 1 << 20) * owners_all + jnp.arange(owners_all, dtype=jnp.int32)[None, :]
    owners = jnp.argsort(scores, axis=1)[:, :DPQ].astype(jnp.int32)
    local = jax.random.randint(local_key, (QUERIES, DPQ), 0, POOL_DEV)
    docs = owners * POOL_DEV + local
    lengths = jax.random.randint(length_key, (POOL_DOCS,), 1, DOC_MAX + 1)
    lengths = lengths.at[docs[0]].set(DOC_MAX)
    gaps = jax.random.randint(gap_key, (QUERIES, DPQ + 1), 0, 64)
    gaps = gaps.at[0].set(63)
    spans = jnp.concatenate([jnp.zeros((QUERIES, 1), jnp.int32), lengths[docs]], axis=1)
    positions = jnp.cumsum(gaps + spans, axis=1).astype(jnp.int32)
    return (docs.astype(jnp.int32), lengths.astype(jnp.int32), positions)


def draw_doc_lens(key, part):
    return pool_plan(key)[1]


def draw_query_docs(key, part):
    return pool_plan(key)[0]


def draw_ctx_pos(key, part):
    return pool_plan(key)[2]


def draw_question_q(key, part):
    shape = (TOKENS, QH, HD)
    base_key = jax.random.fold_in(jax.random.fold_in(key, 3), 0)
    values = jnp.clip(3.0 * jax.random.normal(base_key, shape, jnp.float32), -12.0, 12.0)
    return values.astype(jnp.bfloat16)


def level_of(stream_key, dims, pieces, least, largest):
    loudness = 1.0
    for dim, shards_of in pieces:
        heights = jax.random.uniform(jax.random.fold_in(jax.random.fold_in(stream_key, 6), dim), (shards_of,), jnp.float32, least / len(pieces), largest / len(pieces))
        loudness = loudness * jnp.repeat(jnp.exp(heights), dims[dim] // shards_of).reshape((-1,) + (1,) * (len(dims) - 1 - dim))
    return loudness


def shared_out(rng, own, number, rows, count, top, reach, lean):
    ranking = jax.random.permutation(rng, count)
    heavy_load, common = portions_of(count, rows * top, reach, lean, True), portions_of(count, rows * top, reach, lean, False)
    places = jnp.arange(count)

    def named(sizes, offset_by):
        used = int((sizes > 0).sum())
        fixed = max(1, used // 4)
        passed = fixed + (places - fixed + offset_by * (used - fixed)) % max(1, count - fixed)
        return jnp.zeros((count,), jnp.int32).at[ranking[jnp.where(places < fixed, places, passed)]].set(jnp.asarray(sizes, jnp.int32))

    sizes = jnp.where(number % 4 == 0, named(heavy_load, number // 4), named(common, number - number // 4 - 1))
    mixed = jax.random.permutation(jax.random.fold_in(own, 3), count)
    donor, receiver = mixed[0:count // 2 * 2:2], mixed[1:count // 2 * 2:2]
    slack = jnp.minimum(sizes[donor] - 1, reach - sizes[receiver]) // 2
    slack = jnp.where((donor == ranking[0]) | (receiver == ranking[0]) | (sizes[receiver] == 0), 0, jnp.maximum(slack, 0))
    passed = jax.random.randint(jax.random.fold_in(own, 4), (count // 2,), 0, 1 << 20) % (slack + 1)
    sizes = sizes.at[donor].add(-passed).at[receiver].add(passed)
    members = jnp.searchsorted(jnp.cumsum(sizes), jnp.arange(rows * top), side="right").astype(jnp.int32)
    grid = members.reshape(top, rows).T
    grid = grid[jax.random.permutation(jax.random.fold_in(own, 1), rows)]
    offset_by = jax.random.randint(jax.random.fold_in(own, 2), (rows, 1), 0, top)
    return jnp.take_along_axis(grid, (jnp.arange(top)[None, :] + offset_by) % top, axis=1)


def portions_of(number_of, total, limit, lean, full):
    weights = [(1 << 20) // math.isqrt(grade ** lean) + 1 for grade in range(1, number_of + 1)]
    largest = limit if full else min(limit, max(-(-total // number_of), total * weights[0] // sum(weights)))
    least = 1 if total - largest >= number_of - 1 else 0
    given, surplus = [largest] + [least] * (number_of - 1), total - largest - least * (number_of - 1)
    while surplus > 0:
        candidates = [i for i in range(1, number_of) if given[i] < largest] or [i for i in range(1, number_of) if given[i] < limit]
        pool, budget = sum([weights[i] for i in candidates]), surplus
        for i in candidates:
            extra = min(limit - given[i], max(1, budget * weights[i] // pool), surplus)
            given[i] = given[i] + extra
            surplus = surplus - extra
    return np.array(given)


def bell_draw(rng, shape, scale, limit, shards=(), kind=jnp.bfloat16):
    level = level_of(rng, shape, shards, -0.22, 0.18) if shards else 1.0
    values = jax.random.normal(rng, shape, jnp.float32) * scale * level
    return jnp.minimum(jnp.maximum(values, -limit), limit).astype(kind)


def setup_inputs(seed: int = 0, part: int = 0) -> dict:
    splits = jax.random.split(jax.random.key(seed), 14)
    part_keys = jax.random.split(jax.random.fold_in(splits[13], part), 14)
    question_q = draw_question_q(jax.random.fold_in(jax.random.fold_in(splits[13], part), 71), part)
    question_kv = bell_draw(part_keys[1], (TOKENS, KVH, 2, HD), 1.0, 6.0, ((0, 4),))
    doc_kv = bell_draw(part_keys[2], (POOL_DOCS, DOC_MAX, KVH, 2, HD), 1.0, 6.0, ((0, 4),))
    doc_lens = draw_doc_lens(jax.random.fold_in(jax.random.fold_in(splits[13], part), 71), part)
    query_docs = draw_query_docs(jax.random.fold_in(jax.random.fold_in(splits[13], part), 71), part)
    ctx_pos = draw_ctx_pos(jax.random.fold_in(jax.random.fold_in(splits[13], part), 71), part)
    hidden = bell_draw(part_keys[6], (TOKENS, D), 0.25, 1.5, ((0, 4), (1, 4)))
    out_proj = bell_draw(splits[7], (QH * HD, D), (16 * QH * HD) ** -0.5, 0.0234375, ((0, 4), (1, 4)))
    norm_gain = jnp.clip(1.0 + 0.1 * jax.random.normal(splits[8], (D,), jnp.float32), 0.5, 1.5).astype(jnp.bfloat16)
    router_weight = bell_draw(splits[9], (D, EXPERTS), (4 * D) ** -0.5, 0.046875, ((0, 4),))
    w_gate_up = bell_draw(splits[10], (EXPERTS, D, 2, HID), D ** -0.5, 0.09375, ((0, 4), (1, 4)))
    w_down = bell_draw(splits[11], (EXPERTS, HID, D), HID ** -0.5, 0.1875, ((0, 4), (2, 4)))
    expert_ids_keys = jax.random.split(jax.random.fold_in(part_keys[12], 1), TOKENS // QLEN)
    expert_ids_turns = jax.random.permutation(jax.random.fold_in(part_keys[12], 3), TOKENS // QLEN)
    expert_ids = jax.vmap(lambda own, number: shared_out(jax.random.fold_in(part_keys[12], 2), own, number, QLEN, EXPERTS, TOP, CAP, 0))(expert_ids_keys, expert_ids_turns).reshape((TOKENS, TOP))
    return {"question_q": question_q, "question_kv": question_kv, "doc_kv": doc_kv, "doc_lens": doc_lens, "query_docs": query_docs, "ctx_pos": ctx_pos, "hidden": hidden, "out_proj": out_proj, "norm_gain": norm_gain, "router_weight": router_weight, "w_gate_up": w_gate_up, "w_down": w_down, "expert_ids": expert_ids}


rope_theta = 1000000.0
norm_eps = 1e-06

def narrow(values):
    return lax.optimization_barrier(values.astype(jnp.bfloat16))

def rotate(values, positions):
    half = values.shape[-1] // 2
    freq = jnp.exp(jnp.arange(half, dtype=jnp.float32) * (-2.0 * math.log(rope_theta) / values.shape[-1]))
    angle = positions.astype(jnp.float32)[:, None] * freq[None, :]
    shape = (values.shape[0],) + (1,) * (values.ndim - 2) + (half,)
    cosine = jnp.cos(angle).reshape(shape)
    sine = jnp.sin(angle).reshape(shape)
    floats = values.astype(jnp.float32)
    first = floats[..., :half]
    second = floats[..., half:]
    return jnp.concatenate([first * cosine - second * sine, second * cosine + first * sine], axis=-1)

def attend(q_rows, kv_rows, context, lengths, starts):
    doc_pos = jnp.repeat(starts[:DPQ], DOC_MAX, total_repeat_length=DPQ * DOC_MAX)
    doc_keys = rotate(context[:, :, :, 0].reshape(DPQ * DOC_MAX, KVH, HD), doc_pos).astype(jnp.bfloat16)
    doc_values = context[:, :, :, 1].reshape(DPQ * DOC_MAX, KVH, HD)
    question_pos = starts[DPQ] + jnp.arange(QLEN, dtype=jnp.int32)
    queries = rotate(q_rows, question_pos).astype(jnp.bfloat16)
    own_keys = rotate(kv_rows[:, :, 0], question_pos).astype(jnp.bfloat16)
    keys = jnp.concatenate([doc_keys, own_keys], axis=0)
    values = jnp.concatenate([doc_values, kv_rows[:, :, 1]], axis=0)
    valid = (jnp.arange(DOC_MAX, dtype=jnp.int32)[None, :] < lengths[:, None]).reshape(DPQ * DOC_MAX)
    causal = jnp.arange(QLEN)[:, None] >= jnp.arange(QLEN)[None, :]
    allowed = jnp.concatenate([jnp.broadcast_to(valid[None, :], (QLEN, DPQ * DOC_MAX)), causal], axis=1)
    grouped = queries.reshape(QLEN, KVH, QH // KVH, HD)
    scores = jnp.einsum('ighd,jgd->ghij', grouped.astype(jnp.float32), keys.astype(jnp.float32)) * HD ** (-0.5)
    scores = jnp.where(allowed[None, None], scores, -jnp.inf)
    ceiling = lax.optimization_barrier(jnp.max(scores, axis=-1, keepdims=True))
    probs = jnp.exp(scores - ceiling)
    denominator = lax.optimization_barrier(jnp.sum(probs, axis=-1, keepdims=True))
    mixed = jnp.einsum('ghij,jgd->ghid', narrow(probs).astype(jnp.float32), values.astype(jnp.float32)) / denominator
    return jnp.transpose(mixed, (2, 0, 1, 3)).reshape(QLEN, QH * HD).astype(jnp.bfloat16)

def reference(question_q, question_kv, doc_kv, doc_lens, query_docs, ctx_pos, hidden, out_proj, norm_gain, router_weight, w_gate_up, w_down, expert_ids):

    def one_query(index):
        q_rows = lax.dynamic_slice_in_dim(question_q, index * QLEN, QLEN, 0)
        kv_rows = lax.dynamic_slice_in_dim(question_kv, index * QLEN, QLEN, 0)
        docs = query_docs[index]
        return attend(q_rows, kv_rows, doc_kv[docs], doc_lens[docs], ctx_pos[index])
    attended = lax.map(one_query, jnp.arange(QUERIES, dtype=jnp.int32)).reshape(TOKENS, QH * HD)
    projected = jnp.dot(attended, out_proj, preferred_element_type=jnp.float32)
    residual = narrow(hidden.astype(jnp.float32) + projected).astype(jnp.float32)
    gain = norm_gain.astype(jnp.float32)
    inv_rms = lax.rsqrt(lax.optimization_barrier(jnp.mean(residual * residual, axis=1)) + norm_eps)
    normed = narrow(residual * inv_rms[:, None] * gain[None, :])
    logits = jnp.dot(residual * gain[None, :], router_weight.astype(jnp.float32), precision=lax.Precision.HIGHEST) * inv_rms[:, None]
    mix = jax.nn.softmax(jnp.take_along_axis(logits, expert_ids, axis=1), axis=1)
    flat = expert_ids.reshape(TOKENS * TOP)
    per_expert = QUERIES * CAP

    def one_expert(expert):
        rows = jnp.nonzero(flat == expert, size=per_expert)[0].astype(jnp.int32)
        inputs = jnp.take(normed, rows // TOP, axis=0).astype(jnp.float32).reshape(per_expert, N_TP, D // N_TP)
        weights = w_gate_up[expert].astype(jnp.float32).reshape(N_TP, D // N_TP, 2 * HID)
        parts = narrow(jnp.einsum('rbd,bdh->brh', inputs, weights)).astype(jnp.float32)
        summed = lax.optimization_barrier(jnp.sum(parts, axis=0))
        activated = (jax.nn.silu(summed[:, :HID]) * summed[:, HID:]).astype(jnp.bfloat16)
        output = jnp.dot(activated, w_down[expert], preferred_element_type=jnp.float32).astype(jnp.bfloat16)
        return (rows, output)
    rows, outputs = lax.map(one_expert, jnp.arange(EXPERTS, dtype=jnp.int32))
    gathered = jnp.zeros((TOKENS * TOP, D), jnp.bfloat16).at[rows.reshape(-1)].set(outputs.reshape(-1, D))
    combined = jnp.einsum('tk,tkd->td', mix, gathered.reshape(TOKENS, TOP, D).astype(jnp.float32))
    return (residual + combined).astype(jnp.bfloat16)
```

```python
import math

import jax
import jax.numpy as jnp
from jax import lax
from jax.sharding import PartitionSpec as P

rope_theta = 1000000.0
norm_eps = 1e-06


def tables(positions, head_dim):
    half = head_dim // 2
    freq = jnp.exp(jnp.arange(half, dtype=jnp.float32) * (-2.0 * math.log(rope_theta) / head_dim))
    angle = positions.astype(jnp.float32)[:, None] * freq[None, :]
    return (jnp.cos(angle), jnp.sin(angle))


def rotate(values, positions):
    half = values.shape[-1] // 2
    cosine, sine = tables(positions, values.shape[-1])
    shape = (values.shape[0],) + (1,) * (values.ndim - 2) + (half,)
    cosine, sine = (cosine.reshape(shape), sine.reshape(shape))
    floats = values.astype(jnp.float32)
    first = floats[..., :half]
    second = floats[..., half:]
    return jnp.concatenate(
        [first * cosine - second * sine, second * cosine + first * sine], axis=-1
    )


def attend(q_rows, own_kv, context, starts, lengths, question_start):
    length, heads_here, head_dim = q_rows.shape
    docs_per, doc_max, _ = context.shape
    question_pos = question_start + jnp.arange(length, dtype=jnp.int32)
    queries = rotate(q_rows, question_pos).astype(jnp.bfloat16)
    own_keys = rotate(own_kv[:, :head_dim], question_pos).astype(jnp.bfloat16)
    positions = jnp.repeat(starts, doc_max, total_repeat_length=docs_per * doc_max)
    doc_keys = rotate(context[:, :, :head_dim].reshape(docs_per * doc_max, head_dim), positions)
    keys = jnp.concatenate([doc_keys.astype(jnp.bfloat16), own_keys], axis=0)
    values = jnp.concatenate(
        [context[:, :, head_dim:].reshape(docs_per * doc_max, head_dim), own_kv[:, head_dim:]],
        axis=0,
    )
    valid = (jnp.arange(doc_max, dtype=jnp.int32)[None, :] < lengths[:, None]).reshape(-1)
    causal = jnp.arange(length)[:, None] >= jnp.arange(length)[None, :]
    allowed = jnp.concatenate(
        [jnp.broadcast_to(valid[None, :], (length, valid.shape[0])), causal], axis=1
    )
    scores = jnp.einsum("ihd,jd->hij", queries, keys, preferred_element_type=jnp.float32)
    scores = jnp.where(allowed[None], scores * head_dim ** (-0.5), -jnp.inf)
    ceiling = jnp.max(scores, axis=-1, keepdims=True)
    probs = jnp.exp(scores - ceiling)
    denominator = jnp.sum(probs, axis=-1, keepdims=True)
    mixed = jnp.einsum(
        "hij,jd->hid", probs.astype(jnp.bfloat16), values, preferred_element_type=jnp.float32
    )
    return (
        jnp.transpose(mixed / denominator, (1, 0, 2))
        .reshape(length, heads_here * head_dim)
        .astype(jnp.bfloat16)
    )


def context_by_row(doc_kv, doc_lens, query_docs, ctx_pos, device, kv_pick):
    pool_dev, doc_max, _, pair, head_dim = doc_kv.shape
    docs_per = query_docs.shape[1]
    pool_head = lax.dynamic_index_in_dim(doc_kv, kv_pick, 2, keepdims=False).reshape(
        pool_dev, doc_max, pair * head_dim
    )
    held = device * pool_dev + jnp.arange(pool_dev, dtype=jnp.int32)
    wanted = jnp.sum((query_docs[:, :, None] == held[None, None, :]).astype(jnp.float32), axis=1)
    sending = jnp.einsum(
        "rl,lkc->rkc", wanted.astype(jnp.bfloat16), pool_head, preferred_element_type=jnp.float32
    ).astype(jnp.bfloat16)
    received = lax.all_to_all(sending, "ep", split_axis=0, concat_axis=0, tiled=True)
    my_docs = lax.dynamic_index_in_dim(query_docs, device, 0, keepdims=False)
    starts = lax.dynamic_index_in_dim(ctx_pos, device, 0, keepdims=False)
    return (jnp.take(received, my_docs // pool_dev, axis=0), starts[:docs_per], jnp.take(doc_lens, my_docs))


def context_by_column(doc_kv, doc_lens, query_docs, ctx_pos, device, query):
    pool_dev, doc_max, kv_heads, pair, head_dim = doc_kv.shape
    docs_per = query_docs.shape[1]
    my_docs = lax.dynamic_index_in_dim(query_docs, query, 0, keepdims=False)
    starts = lax.dynamic_index_in_dim(ctx_pos, query, 0, keepdims=False)
    held = device * pool_dev + jnp.arange(pool_dev, dtype=jnp.int32)
    local = jnp.sum(
        jnp.where(my_docs[:, None] == held[None, :], jnp.arange(pool_dev, dtype=jnp.int32)[None, :], 0)
    )
    block = lax.dynamic_index_in_dim(doc_kv, local, 0, keepdims=False)
    sending = jnp.transpose(block, (1, 0, 2, 3)).reshape(kv_heads, doc_max, pair * head_dim)
    received = lax.all_to_all(sending, "ep", split_axis=0, concat_axis=0, tiled=True)
    owner = my_docs // pool_dev
    here = owner[None, :] == jnp.arange(docs_per, dtype=jnp.int32)[:, None]
    lengths = jnp.sum(jnp.where(here, jnp.take(doc_lens, my_docs)[None, :], 0), axis=1)
    return (received, jnp.sum(jnp.where(here, starts[None, :docs_per], 0), axis=1), lengths)


def pairs(lanes, flip):
    return [(i, i ^ flip) for i in range(lanes)]


def gather_lanes(mine, lanes):
    across = jnp.stack([mine, lax.ppermute(mine, "tp", pairs(lanes, 2))])
    return jnp.concatenate([across, lax.ppermute(across, "tp", pairs(lanes, 1))])


def scatter_lanes(parts, lanes):
    chip = parts[:2].astype(jnp.float32) + lax.ppermute(parts[2:], "tp", pairs(lanes, 1)).astype(
        jnp.float32
    )
    away = lax.ppermute(chip[1].astype(jnp.bfloat16), "tp", pairs(lanes, 2))
    return chip[0] + away.astype(jnp.float32)


def per_device(
    question_q,
    question_kv,
    doc_kv,
    doc_lens,
    query_docs,
    ctx_pos,
    hidden,
    out_proj,
    norm_gain,
    router_weight,
    w_gate_up,
    w_down,
    expert_ids,
):
    lanes = lax.axis_size("tp")
    groups = lax.axis_size("ep")
    lane = lax.axis_index("tp")
    device = lax.axis_index("ep")
    length, heads_here, head_dim = question_q.shape
    kv_heads = question_kv.shape[1]
    docs_per = query_docs.shape[1]
    width_here = hidden.shape[1]
    square = lanes == 4 and groups == 4 and kv_heads == 4 and docs_per == groups
    ids = lax.all_gather(expert_ids, "ep", axis=0, tiled=False)
    order = lane ^ jnp.array([0, 2, 1, 3], jnp.int32) if square else None

    if square:
        kv_head = lax.dynamic_index_in_dim(question_kv, lane, 1, keepdims=False).reshape(
            length, 2 * head_dim
        )
        outgoing = jnp.concatenate(
            [question_q.reshape(length, heads_here * head_dim), kv_head], axis=1
        )
        turned = lax.ppermute(
            outgoing,
            ("ep", "tp"),
            [(e * lanes + t, t * lanes + e) for e in range(groups) for t in range(lanes)],
        )
        context, starts, lengths = context_by_column(
            doc_kv, doc_lens, query_docs, ctx_pos, device, lane
        )
        question_start = lax.dynamic_index_in_dim(ctx_pos, lane, 0, keepdims=False)[docs_per]
        q_rows = turned[:, : heads_here * head_dim].reshape(length, heads_here, head_dim)
        attended = attend(
            q_rows, turned[:, heads_here * head_dim :], context, starts, lengths, question_start
        )
        all_queries = gather_lanes(attended, lanes).reshape(lanes * length, -1)
        partial = jnp.dot(all_queries, out_proj, preferred_element_type=jnp.float32)
        partial = partial.astype(jnp.bfloat16).reshape(lanes, length, width_here)
        slot_of = jnp.array([0, 2, 1, 3], jnp.int32)[lane ^ jnp.arange(lanes, dtype=jnp.int32)]
        partial = jnp.take(partial, slot_of, axis=0)
        projected = lax.psum_scatter(partial, "ep", scatter_dimension=0, tiled=True)[0]
    else:
        kv_pick = lane * kv_heads // lanes
        kv_head = lax.dynamic_index_in_dim(question_kv, kv_pick, 1, keepdims=False).reshape(
            length, 2 * head_dim
        )
        context, starts, lengths = context_by_row(
            doc_kv, doc_lens, query_docs, ctx_pos, device, kv_pick
        )
        question_start = lax.dynamic_index_in_dim(ctx_pos, device, 0, keepdims=False)[docs_per]
        attended = attend(question_q, kv_head, context, starts, lengths, question_start)
        projected = jnp.dot(
            lax.all_gather(attended, "tp", axis=1, tiled=True),
            lax.all_gather(out_proj, "ep", axis=0, tiled=True),
            preferred_element_type=jnp.float32,
        )
    residual = (hidden.astype(jnp.float32) + projected.astype(jnp.float32)).astype(jnp.bfloat16)

    tokens = lax.all_gather(residual, "ep", axis=0, tiled=False)
    wide = tokens.astype(jnp.float32)
    gain = norm_gain.astype(jnp.float32)
    scaled = wide * gain
    logit_part = jnp.einsum(
        "snd,de->sne", scaled, router_weight.astype(jnp.float32), precision=lax.Precision.HIGHEST
    )
    square_part = jnp.sum(wide * wide, axis=2, keepdims=True)
    stats = jnp.sum(
        lax.all_gather(jnp.concatenate([logit_part, square_part], axis=2), "tp", axis=0), axis=0
    )
    experts = router_weight.shape[1]
    inv_rms = lax.rsqrt(stats[:, :, experts] / (width_here * lanes) + norm_eps)
    logits = stats[:, :, :experts] * inv_rms[:, :, None]

    local_experts = w_gate_up.shape[0]
    capacity = length * expert_ids.shape[1] // experts
    hid = w_gate_up.shape[3]
    chosen_all = jnp.any(
        ids[:, :, :, None] == jnp.arange(experts, dtype=jnp.int32), axis=2
    )
    top = jnp.max(jnp.where(chosen_all, logits, -jnp.inf), axis=2, keepdims=True)
    weight = jnp.where(chosen_all, jnp.exp(logits - top), 0.0)
    mix = weight / jnp.sum(weight, axis=2, keepdims=True)

    if square:
        shuffled = jnp.take(chosen_all, order, axis=0)
        scaled_rows = jnp.take(scaled.astype(jnp.bfloat16), order, axis=0)
        inv_rms = jnp.take(inv_rms, order, axis=0)
        mix = jnp.take(mix, order, axis=0)
    else:
        shuffled, scaled_rows = (chosen_all, scaled.astype(jnp.bfloat16))
    first = device * local_experts
    chosen = lax.dynamic_slice_in_dim(shuffled, first, local_experts, 2)
    mix_here = lax.dynamic_slice_in_dim(mix, first, local_experts, 2)
    before = (jnp.arange(length)[:, None] > jnp.arange(length)[None, :]).astype(jnp.bfloat16)
    rank = jnp.einsum(
        "mn,sne->sem", before, chosen.astype(jnp.bfloat16), preferred_element_type=jnp.float32
    ).astype(jnp.int32)
    pick = jnp.logical_and(
        jnp.transpose(chosen, (0, 2, 1))[:, :, None, :],
        rank[:, :, None, :] == jnp.arange(capacity, dtype=jnp.int32)[None, None, :, None],
    )
    onehot = pick.astype(jnp.bfloat16)
    inv_row = jnp.sum(jnp.where(pick, inv_rms[:, None, None, :], 0.0), axis=3)
    mix_row = jnp.sum(jnp.where(pick, jnp.transpose(mix_here, (0, 2, 1))[:, :, None, :], 0.0), axis=3)

    rows = jnp.einsum(
        "sern,snd->serd", onehot, scaled_rows, preferred_element_type=jnp.float32
    ).astype(jnp.bfloat16)
    term = jnp.einsum(
        "serd,edgh->sergh", rows, w_gate_up, preferred_element_type=jnp.float32
    ).astype(jnp.bfloat16)
    per_lane = groups * local_experts * capacity // lanes
    term = term.reshape(lanes, per_lane, 2 * hid)
    inv_row = inv_row.reshape(lanes, per_lane, 1)
    if square:
        summed = scatter_lanes(term, lanes)
        inv_mine = inv_row[0]
    else:
        summed = lax.psum_scatter(term, "tp", scatter_dimension=0, tiled=True)[0].astype(jnp.float32)
        inv_mine = lax.dynamic_index_in_dim(inv_row, lane, 0, keepdims=False)
    summed = summed * inv_mine
    act = (jax.nn.silu(summed[:, :hid]) * summed[:, hid:]).astype(jnp.bfloat16)
    if square:
        acts = gather_lanes(act, lanes)
    else:
        acts = lax.all_gather(act, "tp", axis=0, tiled=False)
    acts = acts.reshape(groups, local_experts, capacity, hid)
    expert_out = jnp.einsum("serh,ehd->serd", acts, w_down, preferred_element_type=jnp.float32)
    expert_out = (expert_out * mix_row[:, :, :, None]).astype(jnp.bfloat16)
    combined = jnp.einsum(
        "sern,serd->snd", onehot, expert_out, preferred_element_type=jnp.float32
    ).astype(jnp.bfloat16)
    if square:
        combined = jnp.take(combined, slot_of, axis=0)
    returned = lax.psum_scatter(combined, "ep", scatter_dimension=0, tiled=True)[0]
    return (residual.astype(jnp.float32) + returned.astype(jnp.float32)).astype(jnp.bfloat16)


def solution(mesh):
    placed = (
        P(("grp", "ep"), "tp", None),
        P(("grp", "ep"), None, None, None),
        P(("grp", "ep"), None, None, None, None),
        P("grp"),
        P("grp", None),
        P("grp", None),
        P(("grp", "ep"), "tp"),
        P("ep", "tp"),
        P("tp"),
        P("tp", None),
        P("ep", "tp", None, None),
        P("ep", None, "tp"),
        P(("grp", "ep"), None),
    )
    return jax.shard_map(
        per_device, mesh=mesh, in_specs=placed, out_specs=P(("grp", "ep"), "tp"), check_vma=False
    )
```

```python
import math

import jax
import jax.numpy as jnp
from jax import lax
from jax.experimental import pallas as pl
from jax.experimental.pallas import tpu as pltpu
from jax.sharding import PartitionSpec as P

rope_theta = 1000000.0
norm_eps = 1e-06


def tables(positions, head_dim):
    half = head_dim // 2
    freq = jnp.exp(jnp.arange(half, dtype=jnp.float32) * (-2.0 * math.log(rope_theta) / head_dim))
    angle = positions.astype(jnp.float32)[:, None] * freq[None, :]
    return (jnp.cos(angle), jnp.sin(angle))


def rotate(values, positions):
    half = values.shape[-1] // 2
    cosine, sine = tables(positions, values.shape[-1])
    shape = (values.shape[0],) + (1,) * (values.ndim - 2) + (half,)
    cosine, sine = (cosine.reshape(shape), sine.reshape(shape))
    floats = values.astype(jnp.float32)
    first = floats[..., :half]
    second = floats[..., half:]
    return jnp.concatenate(
        [first * cosine - second * sine, second * cosine + first * sine], axis=-1
    )


def attend(q_rows, own_kv, context, starts, lengths, question_start):
    length, heads_here, head_dim = q_rows.shape
    docs_per, doc_max, _ = context.shape
    question_pos = question_start + jnp.arange(length, dtype=jnp.int32)
    queries = rotate(q_rows, question_pos).astype(jnp.bfloat16)
    own_keys = rotate(own_kv[:, :head_dim], question_pos).astype(jnp.bfloat16)
    positions = jnp.repeat(starts, doc_max, total_repeat_length=docs_per * doc_max)
    doc_keys = rotate(context[:, :, :head_dim].reshape(docs_per * doc_max, head_dim), positions)
    keys = jnp.concatenate([doc_keys.astype(jnp.bfloat16), own_keys], axis=0)
    values = jnp.concatenate(
        [context[:, :, head_dim:].reshape(docs_per * doc_max, head_dim), own_kv[:, head_dim:]],
        axis=0,
    )
    valid = (jnp.arange(doc_max, dtype=jnp.int32)[None, :] < lengths[:, None]).reshape(-1)
    causal = jnp.arange(length)[:, None] >= jnp.arange(length)[None, :]
    allowed = jnp.concatenate(
        [jnp.broadcast_to(valid[None, :], (length, valid.shape[0])), causal], axis=1
    )
    scores = jnp.einsum("ihd,jd->hij", queries, keys, preferred_element_type=jnp.float32)
    scores = jnp.where(allowed[None], scores * head_dim ** (-0.5), -jnp.inf)
    ceiling = jnp.max(scores, axis=-1, keepdims=True)
    probs = jnp.exp(scores - ceiling)
    denominator = jnp.sum(probs, axis=-1, keepdims=True)
    mixed = jnp.einsum(
        "hij,jd->hid", probs.astype(jnp.bfloat16), values, preferred_element_type=jnp.float32
    )
    return (
        jnp.transpose(mixed / denominator, (1, 0, 2))
        .reshape(length, heads_here * head_dim)
        .astype(jnp.bfloat16)
    )


def context_by_row(doc_kv, doc_lens, query_docs, ctx_pos, device, kv_pick):
    pool_dev, doc_max, _, pair, head_dim = doc_kv.shape
    docs_per = query_docs.shape[1]
    pool_head = lax.dynamic_index_in_dim(doc_kv, kv_pick, 2, keepdims=False).reshape(
        pool_dev, doc_max, pair * head_dim
    )
    held = device * pool_dev + jnp.arange(pool_dev, dtype=jnp.int32)
    wanted = jnp.sum((query_docs[:, :, None] == held[None, None, :]).astype(jnp.float32), axis=1)
    sending = jnp.einsum(
        "rl,lkc->rkc", wanted.astype(jnp.bfloat16), pool_head, preferred_element_type=jnp.float32
    ).astype(jnp.bfloat16)
    received = lax.all_to_all(sending, "ep", split_axis=0, concat_axis=0, tiled=True)
    my_docs = lax.dynamic_index_in_dim(query_docs, device, 0, keepdims=False)
    starts = lax.dynamic_index_in_dim(ctx_pos, device, 0, keepdims=False)
    return (jnp.take(received, my_docs // pool_dev, axis=0), starts[:docs_per], jnp.take(doc_lens, my_docs))


def per_device_general(
    question_q,
    question_kv,
    doc_kv,
    doc_lens,
    query_docs,
    ctx_pos,
    hidden,
    out_proj,
    norm_gain,
    router_weight,
    w_gate_up,
    w_down,
    expert_ids,
):
    lanes = lax.axis_size("tp")
    groups = lax.axis_size("ep")
    lane = lax.axis_index("tp")
    device = lax.axis_index("ep")
    length, heads_here, head_dim = question_q.shape
    kv_heads = question_kv.shape[1]
    docs_per = query_docs.shape[1]
    width_here = hidden.shape[1]
    ids = lax.all_gather(expert_ids, "ep", axis=0, tiled=False)
    kv_pick = lane * kv_heads // lanes
    kv_head = lax.dynamic_index_in_dim(question_kv, kv_pick, 1, keepdims=False).reshape(
        length, 2 * head_dim
    )
    context, starts, lengths = context_by_row(
        doc_kv, doc_lens, query_docs, ctx_pos, device, kv_pick
    )
    question_start = lax.dynamic_index_in_dim(ctx_pos, device, 0, keepdims=False)[docs_per]
    attended = attend(question_q, kv_head, context, starts, lengths, question_start)
    projected = jnp.dot(
        lax.all_gather(attended, "tp", axis=1, tiled=True),
        lax.all_gather(out_proj, "ep", axis=0, tiled=True),
        preferred_element_type=jnp.float32,
    )
    residual = (hidden.astype(jnp.float32) + projected.astype(jnp.float32)).astype(jnp.bfloat16)

    tokens = lax.all_gather(residual, "ep", axis=0, tiled=False)
    wide = tokens.astype(jnp.float32)
    gain = norm_gain.astype(jnp.float32)
    scaled = wide * gain
    logit_part = jnp.einsum(
        "snd,de->sne", scaled, router_weight.astype(jnp.float32), precision=lax.Precision.HIGHEST
    )
    square_part = jnp.sum(wide * wide, axis=2, keepdims=True)
    stats = jnp.sum(
        lax.all_gather(jnp.concatenate([logit_part, square_part], axis=2), "tp", axis=0), axis=0
    )
    experts = router_weight.shape[1]
    inv_rms = lax.rsqrt(stats[:, :, experts] / (width_here * lanes) + norm_eps)
    logits = stats[:, :, :experts] * inv_rms[:, :, None]

    local_experts = w_gate_up.shape[0]
    capacity = length * expert_ids.shape[1] // experts
    hid = w_gate_up.shape[3]
    chosen_all = jnp.any(
        ids[:, :, :, None] == jnp.arange(experts, dtype=jnp.int32), axis=2
    )
    top = jnp.max(jnp.where(chosen_all, logits, -jnp.inf), axis=2, keepdims=True)
    weight = jnp.where(chosen_all, jnp.exp(logits - top), 0.0)
    mix = weight / jnp.sum(weight, axis=2, keepdims=True)

    shuffled, scaled_rows = (chosen_all, scaled.astype(jnp.bfloat16))
    first = device * local_experts
    chosen = lax.dynamic_slice_in_dim(shuffled, first, local_experts, 2)
    mix_here = lax.dynamic_slice_in_dim(mix, first, local_experts, 2)
    before = (jnp.arange(length)[:, None] > jnp.arange(length)[None, :]).astype(jnp.bfloat16)
    rank = jnp.einsum(
        "mn,sne->sem", before, chosen.astype(jnp.bfloat16), preferred_element_type=jnp.float32
    ).astype(jnp.int32)
    pick = jnp.logical_and(
        jnp.transpose(chosen, (0, 2, 1))[:, :, None, :],
        rank[:, :, None, :] == jnp.arange(capacity, dtype=jnp.int32)[None, None, :, None],
    )
    onehot = pick.astype(jnp.bfloat16)
    inv_row = jnp.sum(jnp.where(pick, inv_rms[:, None, None, :], 0.0), axis=3)
    mix_row = jnp.sum(jnp.where(pick, jnp.transpose(mix_here, (0, 2, 1))[:, :, None, :], 0.0), axis=3)

    rows = jnp.einsum(
        "sern,snd->serd", onehot, scaled_rows, preferred_element_type=jnp.float32
    ).astype(jnp.bfloat16)
    term = jnp.einsum(
        "serd,edgh->sergh", rows, w_gate_up, preferred_element_type=jnp.float32
    ).astype(jnp.bfloat16)
    per_lane = groups * local_experts * capacity // lanes
    term = term.reshape(lanes, per_lane, 2 * hid)
    inv_row = inv_row.reshape(lanes, per_lane, 1)
    summed = lax.psum_scatter(term, "tp", scatter_dimension=0, tiled=True)[0].astype(jnp.float32)
    inv_mine = lax.dynamic_index_in_dim(inv_row, lane, 0, keepdims=False)
    summed = summed * inv_mine
    act = (jax.nn.silu(summed[:, :hid]) * summed[:, hid:]).astype(jnp.bfloat16)
    acts = lax.all_gather(act, "tp", axis=0, tiled=False)
    acts = acts.reshape(groups, local_experts, capacity, hid)
    expert_out = jnp.einsum("serh,ehd->serd", acts, w_down, preferred_element_type=jnp.float32)
    expert_out = (expert_out * mix_row[:, :, :, None]).astype(jnp.bfloat16)
    combined = jnp.einsum(
        "sern,serd->snd", onehot, expert_out, preferred_element_type=jnp.float32
    ).astype(jnp.bfloat16)
    returned = lax.psum_scatter(combined, "ep", scatter_dimension=0, tiled=True)[0]
    return (residual.astype(jnp.float32) + returned.astype(jnp.float32)).astype(jnp.bfloat16)


def pairs(lanes, flip):
    return [(i, i ^ flip) for i in range(lanes)]


def chain_scatter(parts, axis):
    n = len(parts)
    right = left = None
    for k in range(n - 1):
        send_right, send_left = (parts[n - 1 - k], parts[k + 1])
        if k:
            send_right = send_right + right
            send_left = send_left + left
        right = lax.ppermute(send_right, axis, [(i, i + 1) for i in range(k + 1)])
        left = lax.ppermute(send_left, axis, [(i, i - 1) for i in range(n - 1 - k, n)])
    return (parts[0], right, left)


def chain_gather(mine, axis, n):
    right, left = ([], [])
    for k in range(n - 1):
        right.append(
            lax.ppermute(right[-1] if k else mine, axis, [(i, i + 1) for i in range(k, n - 1)])
        )
        left.append(
            lax.ppermute(left[-1] if k else mine, axis, [(i, i - 1) for i in range(1, n - k)])
        )
    return (right, left)


def query_of(device, lane):
    return 2 * (lane & 1) + ((lane >> 1) ^ (device & 1))


def turn(values, groups, lanes):
    moves = [
        (e * lanes + t, t * lanes + 2 * ((e ^ t) & 1) + (e >> 1))
        for e in range(groups)
        for t in range(lanes)
    ]
    return lax.ppermute(values, ("ep", "tp"), moves)


def call(body, outs, scratch, flops, moved, **kwargs):
    return pl.pallas_call(
        body,
        out_shape=outs,
        scratch_shapes=scratch,
        compiler_params=pltpu.CompilerParams(vmem_limit_bytes=40 * 1024 * 1024),
        cost_estimate=pl.CostEstimate(flops=flops, bytes_accessed=moved, transcendentals=0),
        **kwargs,
    )


VMEM = pl.BlockSpec(memory_space=pltpu.VMEM)
SMEM = pl.BlockSpec(memory_space=pltpu.SMEM)
NT = (((1,), (1,)), ((), ()))


def dot(a, b):
    return jnp.dot(a, b, preferred_element_type=jnp.float32)


def attention_body(lens, q, own, ctx, cos_q, sin_q, cos_d, sin_d, out, wide, keys, vals):
    length, head_dim = cos_q.shape
    heads = out.shape[1] // head_dim
    docs, doc_max, _ = ctx.shape
    half = head_dim // 2

    def turned(x, cosine, sine):
        return x * cosine + pltpu.roll(x, half, 1) * sine

    cosine, sine = (cos_q[...], sin_q[...])
    for j in range(docs):
        key = turned(
            ctx[j, :, :head_dim].astype(jnp.float32), cos_d[j : j + 1, :], sin_d[j : j + 1, :]
        )
        keys[j * doc_max : (j + 1) * doc_max, :] = key.astype(jnp.bfloat16)
        vals[j * doc_max : (j + 1) * doc_max, :] = ctx[j, :, head_dim:]
    base = docs * doc_max
    keys[base:, :] = turned(own[:, :head_dim].astype(jnp.float32), cosine, sine).astype(
        jnp.bfloat16
    )
    vals[base:, :] = own[:, head_dim:]
    wide[...] = q[...].astype(jnp.float32)
    column = lax.broadcasted_iota(jnp.int32, (1, doc_max), 1)
    allowed = [column < lens[j] for j in range(docs)]
    causal = lax.broadcasted_iota(jnp.int32, (length, length), 0) >= lax.broadcasted_iota(
        jnp.int32, (length, length), 1
    )
    for h in range(heads):
        query = turned(wide[pl.ds(h, length, stride=heads), :], cosine, sine).astype(jnp.bfloat16)
        scores = lax.dot_general(query, keys[...], NT, preferred_element_type=jnp.float32)
        scores = scores * head_dim ** (-0.5)
        parts = [
            jnp.where(allowed[j], scores[:, j * doc_max : (j + 1) * doc_max], -jnp.inf)
            for j in range(docs)
        ] + [jnp.where(causal, scores[:, base:], -jnp.inf)]
        scores = jnp.concatenate(parts, axis=1)
        ceiling = jnp.max(scores, axis=1, keepdims=True)
        probs = jnp.exp(scores - ceiling)
        denominator = jnp.sum(probs, axis=1, keepdims=True)
        mixed = dot(probs.astype(jnp.bfloat16), vals[...])
        out[:, h * head_dim : (h + 1) * head_dim] = (mixed / denominator).astype(jnp.bfloat16)


def attention(lens, q, own, ctx, tables_q, tables_d):
    length, head_dim = tables_q[0].shape
    heads = q.shape[0] // length
    rows = ctx.shape[0] * ctx.shape[1] + length
    return call(
        attention_body,
        jax.ShapeDtypeStruct((length, heads * head_dim), jnp.bfloat16),
        [
            pltpu.VMEM(q.shape, jnp.float32),
            pltpu.VMEM((rows, head_dim), jnp.bfloat16),
            pltpu.VMEM((rows, head_dim), jnp.bfloat16),
        ],
        4 * heads * length * rows * head_dim * 4,
        4 * 1024 * 1024,
        in_specs=[SMEM] + [VMEM] * 7,
        out_specs=VMEM,
        name="attention",
    )(lens, q, own, ctx, *tables_q, *tables_d)


def project_body(place, a, b, c, d, weight, *rest):
    outs, rows = (rest[:-1], rest[-1])
    for j, ref in enumerate((a, b, c, d)):
        rows[place[j]] = ref[...]
    for m, out in enumerate(outs):
        out[...] = dot(rows[m], weight[...]).astype(jnp.bfloat16)


def project(place, parts, weight):
    length, depth = parts[0].shape
    shape = jax.ShapeDtypeStruct((length, weight.shape[1]), jnp.bfloat16)
    return call(
        project_body,
        [shape] * 4,
        [pltpu.VMEM((4, length, depth), jnp.bfloat16)],
        2 * 4 * length * depth * weight.shape[1],
        4 * 1024 * 1024,
        in_specs=[SMEM] + [VMEM] * 5,
        out_specs=[VMEM] * 4,
        name="project",
    )(place, *parts, weight)


def assemble_body(mine, a0, a1, a2, b0, b1, b2, gain, router, scaled, stats):
    length = mine.shape[0]
    experts = router.shape[0]
    blocks = (mine[...], a2[...] + b0[...], a1[...] + b1[...], a0[...] + b2[...])
    ones = jnp.ones((8, mine.shape[1]), jnp.float32)
    for m, block in enumerate(blocks):
        wide = block.astype(jnp.float32)
        grown = wide * gain[...]
        scaled[m] = grown.astype(jnp.bfloat16)
        here = slice(m * length, (m + 1) * length)
        stats[:experts, here] = lax.dot_general(
            router[...], grown, NT, preferred_element_type=jnp.float32,
            precision=lax.Precision.HIGHEST,
        )
        stats[experts:, here] = lax.dot_general(
            ones, wide * wide, NT, preferred_element_type=jnp.float32,
            precision=lax.Precision.HIGHEST,
        )


def assemble(mine, right, left, gain, router):
    length, width = mine.shape
    return call(
        assemble_body,
        [
            jax.ShapeDtypeStruct((4, length, width), jnp.bfloat16),
            jax.ShapeDtypeStruct((router.shape[0] + 8, 4 * length), jnp.float32),
        ],
        [],
        2 * 4 * length * width * 256,
        3 * 1024 * 1024,
        in_specs=[VMEM] * 9,
        out_specs=[VMEM] * 2,
        name="assemble",
    )(mine, *right, *left, gain, router)


def gate_up_body(order, tokens, pick, weight, *rest):
    outs, rows = (rest[:-1], rest[-1])
    local = rows.shape[0]
    capacity = pick.shape[1] // local
    hid = weight.shape[3]

    @pl.when(pl.program_id(0) == 0)
    def _():
        for j in range(4):
            m = order[j]
            chosen = dot(pick[m], tokens[m]).astype(jnp.bfloat16)
            for e in range(local):
                rows[e, j * capacity : (j + 1) * capacity, :] = chosen[
                    e * capacity : (e + 1) * capacity, :
                ]

    mine = rows[pl.program_id(0)]
    for g in range(2):
        term = dot(mine, weight[0, g]).astype(jnp.bfloat16)
        for j, out in enumerate(outs):
            out[0, :, g * hid : (g + 1) * hid] = term[j * capacity : (j + 1) * capacity, :]


def gate_up(order, tokens, pick, weight):
    local, _, width, hid = weight.shape
    capacity = pick.shape[1] // local
    shape = jax.ShapeDtypeStruct((local, capacity, 2 * hid), jnp.bfloat16)
    return call(
        gate_up_body,
        [shape] * 4,
        [pltpu.VMEM((local, 4 * capacity, width), jnp.bfloat16)],
        2 * local * 4 * capacity * width * 2 * hid,
        22 * 1024 * 1024,
        grid=(local,),
        in_specs=[SMEM, VMEM, VMEM, pl.BlockSpec((1, 2, width, hid), lambda i: (i, 0, 0, 0))],
        out_specs=[pl.BlockSpec((1, capacity, 2 * hid), lambda i: (i, 0, 0))] * 4,
        name="gate_up",
    )(order, tokens, pick, weight)


def down_body(order, a, b, c, d, spread, weight, *rest):
    outs, results = (rest[:-1], rest[-1])
    e = pl.program_id(0)
    capacity = a.shape[1]
    acts = jnp.concatenate([a[0], b[0], c[0], d[0]], axis=0)
    result = dot(acts, weight[0]).astype(jnp.bfloat16)
    start = pl.multiple_of(e * capacity, capacity)
    for j in range(4):
        results[order[j], pl.ds(start, capacity), :] = result[j * capacity : (j + 1) * capacity, :]

    @pl.when(e == pl.num_programs(0) - 1)
    def _():
        for m, out in enumerate(outs):
            out[...] = dot(spread[m], results[m]).astype(jnp.bfloat16)


def down(order, acts, spread, weight):
    local, hid, width = weight.shape
    capacity = acts[0].shape[1]
    length = spread.shape[1]
    shape = jax.ShapeDtypeStruct((length, width), jnp.bfloat16)
    block = pl.BlockSpec((1, capacity, hid), lambda i: (i, 0, 0))
    return call(
        down_body,
        [shape] * 4,
        [pltpu.VMEM((4, local * capacity, width), jnp.bfloat16)],
        2 * local * 4 * capacity * width * hid,
        10 * 1024 * 1024,
        grid=(local,),
        in_specs=[SMEM] + [block] * 4 + [VMEM, pl.BlockSpec((1, hid, width), lambda i: (i, 0, 0))],
        out_specs=[VMEM] * 4,
        name="down",
    )(order, *acts, spread, weight)


def signed_tables(positions, head_dim):
    cosine, sine = tables(positions, head_dim)
    return (
        jnp.concatenate([cosine, cosine], axis=1),
        jnp.concatenate([-sine, sine], axis=1),
    )


def per_device_square(
    question_q,
    question_kv,
    doc_kv,
    doc_lens,
    query_docs,
    ctx_pos,
    hidden,
    out_proj,
    norm_gain,
    router_weight,
    w_gate_up,
    w_down,
    expert_ids,
):
    n = 4
    lane = lax.axis_index("tp")
    device = lax.axis_index("ep")
    length, heads_here, head_dim = question_q.shape
    pool_dev, doc_max, kv_heads, _, _ = doc_kv.shape
    docs_per = query_docs.shape[1]
    width_here = hidden.shape[1]
    experts = router_weight.shape[1]
    local = w_gate_up.shape[0]
    capacity = length * expert_ids.shape[1] // experts
    hid = w_gate_up.shape[3]
    seats = jnp.arange(n, dtype=jnp.int32)

    q_rows = turn(question_q.reshape(length * heads_here, head_dim), n, n)
    kv_head = lax.dynamic_index_in_dim(question_kv, lane, 1, keepdims=False)
    own = turn(kv_head.reshape(length, 2 * head_dim), n, n)

    for_query = query_of(seats, lane)
    docs_of = jnp.take(query_docs, for_query, axis=0)
    held = device * pool_dev + jnp.arange(pool_dev, dtype=jnp.int32)
    choice = jnp.any(docs_of[:, :, None] == held[None, None, :], axis=1)
    sending = doc_kv[0]
    for p in range(1, pool_dev):
        sending = jnp.where(choice[None, :, p, None, None], doc_kv[p], sending)
    sending = jnp.transpose(sending, (1, 0, 2, 3)).reshape(kv_heads, doc_max, 2 * head_dim)
    context = lax.all_to_all(sending, "ep", split_axis=0, concat_axis=0, tiled=True)
    ids = lax.all_gather(expert_ids, "ep", axis=0, tiled=False)

    query = query_of(device, lane)
    my_docs = lax.dynamic_index_in_dim(query_docs, query, 0, keepdims=False)
    starts = lax.dynamic_index_in_dim(ctx_pos, query, 0, keepdims=False)
    here = (my_docs // pool_dev)[None, :] == seats[:, None]
    lengths = jnp.sum(jnp.where(here, jnp.take(doc_lens, my_docs)[None, :], 0), axis=1)
    doc_starts = jnp.sum(jnp.where(here, starts[None, :docs_per], 0), axis=1)
    tables_q = signed_tables(starts[docs_per] + jnp.arange(length, dtype=jnp.int32), head_dim)
    tables_d = signed_tables(doc_starts, head_dim)

    ids = jnp.take(ids, (device + seats) % n, axis=0)
    named = device * local + jnp.arange(local, dtype=jnp.int32)
    chosen = jnp.any(ids[:, None, :, :] == named[None, :, None, None], axis=3)
    before = (jnp.arange(length)[:, None] < jnp.arange(length)[None, :]).astype(jnp.bfloat16)
    rank = jnp.einsum(
        "men,nk->mek", chosen.astype(jnp.bfloat16), before, preferred_element_type=jnp.float32
    ).astype(jnp.int32)
    picked = jnp.logical_and(
        chosen[:, :, None, :],
        rank[:, :, None, :] == jnp.arange(capacity, dtype=jnp.int32)[None, None, :, None],
    ).reshape(n, local * capacity, length)
    pick = picked.astype(jnp.bfloat16)
    spread = jnp.transpose(pick, (0, 2, 1))
    named_all = jnp.any(
        ids[:, None, :, :] == jnp.arange(experts, dtype=jnp.int32)[None, :, None, None], axis=3
    )
    weight = jnp.transpose(w_gate_up, (0, 2, 1, 3))

    attended = attention(lengths, q_rows, own, context, tables_q, tables_d)
    far = lax.ppermute(attended, "tp", pairs(n, 2))
    near = lax.ppermute(attended, "tp", pairs(n, 1))
    farther = lax.ppermute(far, "tp", pairs(n, 1))
    order = lane ^ jnp.array([0, 2, 1, 3], jnp.int32)
    place = (query_of(device, order) - device) % n
    parts = project(place, (attended, far, near, farther), out_proj)
    mine, right, left = chain_scatter(parts, "ep")
    residual = (
        hidden.astype(jnp.float32)
        + mine.astype(jnp.float32)
        + (right.astype(jnp.float32) + left.astype(jnp.float32))
    ).astype(jnp.bfloat16)

    right, left = chain_gather(residual, "ep", n)
    tokens, stats = assemble(
        residual,
        right,
        left,
        norm_gain.astype(jnp.float32)[None, :],
        router_weight.T.astype(jnp.float32),
    )
    stats = stats + lax.ppermute(stats, "tp", pairs(n, 2))
    stats = stats + lax.ppermute(stats, "tp", pairs(n, 1))

    terms = gate_up(order, tokens, pick, weight)
    for_far = lax.ppermute(terms[3], "tp", pairs(n, 1))
    for_me = lax.ppermute(terms[2], "tp", pairs(n, 1))
    chip_far = (terms[1].astype(jnp.float32) + for_far.astype(jnp.float32)).astype(jnp.bfloat16)
    across = lax.ppermute(chip_far, "tp", pairs(n, 2))

    stats = lax.dynamic_index_in_dim(stats.reshape(experts + 8, n, length), lane, 1, keepdims=False)
    inv_rms = lax.rsqrt(stats[experts] / (width_here * n) + norm_eps)
    logits = stats[:experts] * inv_rms[None, :]
    named_mine = lax.dynamic_index_in_dim(named_all, lane, 0, keepdims=False)
    top = jnp.max(jnp.where(named_mine, logits, -jnp.inf), axis=0, keepdims=True)
    grown = jnp.where(named_mine, jnp.exp(logits - top), 0.0)
    mix = grown / jnp.sum(grown, axis=0, keepdims=True)
    mix = lax.dynamic_slice_in_dim(mix, device * local, local, 0)
    picked_mine = lax.dynamic_index_in_dim(picked, lane, 0, keepdims=False).reshape(
        local, capacity, length
    )
    inv_row = jnp.sum(jnp.where(picked_mine, inv_rms[None, None, :], 0.0), axis=2)[:, :, None]
    mix_row = jnp.sum(jnp.where(picked_mine, mix[:, None, :], 0.0), axis=2)[:, :, None]

    summed = (
        terms[0].astype(jnp.float32) + for_me.astype(jnp.float32) + across.astype(jnp.float32)
    ) * inv_row
    act = jax.nn.silu(summed[:, :, :hid]) * summed[:, :, hid:] * mix_row
    act = act.astype(jnp.bfloat16)
    far = lax.ppermute(act, "tp", pairs(n, 2))
    near = lax.ppermute(act, "tp", pairs(n, 1))
    farther = lax.ppermute(far, "tp", pairs(n, 1))
    parts = down(order, (act, far, near, farther), spread, w_down)
    mine, right, left = chain_scatter(parts, "ep")
    return (
        residual.astype(jnp.float32)
        + mine.astype(jnp.float32)
        + (right.astype(jnp.float32) + left.astype(jnp.float32))
    ).astype(jnp.bfloat16)


def solution(mesh):
    placed = (
        P(("grp", "ep"), "tp", None),
        P(("grp", "ep"), None, None, None),
        P(("grp", "ep"), None, None, None, None),
        P("grp"),
        P("grp", None),
        P("grp", None),
        P(("grp", "ep"), "tp"),
        P("ep", "tp"),
        P("tp"),
        P("tp", None),
        P("ep", "tp", None, None),
        P("ep", None, "tp"),
        P(("grp", "ep"), None),
    )
    def per_device(*args):
        square = (
            lax.axis_size("tp") == 4
            and lax.axis_size("ep") == 4
            and args[1].shape[1] == 4
            and args[4].shape == (4, 4)
        )
        return (per_device_square if square else per_device_general)(*args)

    return jax.shard_map(
        per_device, mesh=mesh, in_specs=placed, out_specs=P(("grp", "ep"), "tp"), check_vma=False
    )
```

```python
import functools
import math

import jax
import jax.numpy as jnp
from jax import lax
from jax.experimental import pallas as pl
from jax.experimental.pallas import tpu as pltpu
from jax.sharding import PartitionSpec as P

rope_theta = 1000000.0
norm_eps = 1e-06


def tables(positions, head_dim):
    half = head_dim // 2
    freq = jnp.exp(jnp.arange(half, dtype=jnp.float32) * (-2.0 * math.log(rope_theta) / head_dim))
    angle = positions.astype(jnp.float32)[:, None] * freq[None, :]
    return (jnp.cos(angle), jnp.sin(angle))


def rotate(values, positions):
    half = values.shape[-1] // 2
    cosine, sine = tables(positions, values.shape[-1])
    shape = (values.shape[0],) + (1,) * (values.ndim - 2) + (half,)
    cosine, sine = (cosine.reshape(shape), sine.reshape(shape))
    floats = values.astype(jnp.float32)
    first = floats[..., :half]
    second = floats[..., half:]
    return jnp.concatenate(
        [first * cosine - second * sine, second * cosine + first * sine], axis=-1
    )


def attend(q_rows, own_kv, context, starts, lengths, question_start):
    length, heads_here, head_dim = q_rows.shape
    docs_per, doc_max, _ = context.shape
    question_pos = question_start + jnp.arange(length, dtype=jnp.int32)
    queries = rotate(q_rows, question_pos).astype(jnp.bfloat16)
    own_keys = rotate(own_kv[:, :head_dim], question_pos).astype(jnp.bfloat16)
    positions = jnp.repeat(starts, doc_max, total_repeat_length=docs_per * doc_max)
    doc_keys = rotate(context[:, :, :head_dim].reshape(docs_per * doc_max, head_dim), positions)
    keys = jnp.concatenate([doc_keys.astype(jnp.bfloat16), own_keys], axis=0)
    values = jnp.concatenate(
        [context[:, :, head_dim:].reshape(docs_per * doc_max, head_dim), own_kv[:, head_dim:]],
        axis=0,
    )
    valid = (jnp.arange(doc_max, dtype=jnp.int32)[None, :] < lengths[:, None]).reshape(-1)
    causal = jnp.arange(length)[:, None] >= jnp.arange(length)[None, :]
    allowed = jnp.concatenate(
        [jnp.broadcast_to(valid[None, :], (length, valid.shape[0])), causal], axis=1
    )
    scores = jnp.einsum("ihd,jd->hij", queries, keys, preferred_element_type=jnp.float32)
    scores = jnp.where(allowed[None], scores * head_dim ** (-0.5), -jnp.inf)
    ceiling = jnp.max(scores, axis=-1, keepdims=True)
    probs = jnp.exp(scores - ceiling)
    denominator = jnp.sum(probs, axis=-1, keepdims=True)
    mixed = jnp.einsum(
        "hij,jd->hid", probs.astype(jnp.bfloat16), values, preferred_element_type=jnp.float32
    )
    return (
        jnp.transpose(mixed / denominator, (1, 0, 2))
        .reshape(length, heads_here * head_dim)
        .astype(jnp.bfloat16)
    )


def context_by_row(doc_kv, doc_lens, query_docs, ctx_pos, device, kv_pick):
    pool_dev, doc_max, _, pair, head_dim = doc_kv.shape
    docs_per = query_docs.shape[1]
    pool_head = lax.dynamic_index_in_dim(doc_kv, kv_pick, 2, keepdims=False).reshape(
        pool_dev, doc_max, pair * head_dim
    )
    held = device * pool_dev + jnp.arange(pool_dev, dtype=jnp.int32)
    wanted = jnp.sum((query_docs[:, :, None] == held[None, None, :]).astype(jnp.float32), axis=1)
    sending = jnp.einsum(
        "rl,lkc->rkc", wanted.astype(jnp.bfloat16), pool_head, preferred_element_type=jnp.float32
    ).astype(jnp.bfloat16)
    received = lax.all_to_all(sending, "ep", split_axis=0, concat_axis=0, tiled=True)
    my_docs = lax.dynamic_index_in_dim(query_docs, device, 0, keepdims=False)
    starts = lax.dynamic_index_in_dim(ctx_pos, device, 0, keepdims=False)
    return (jnp.take(received, my_docs // pool_dev, axis=0), starts[:docs_per], jnp.take(doc_lens, my_docs))


def per_device_general(
    question_q,
    question_kv,
    doc_kv,
    doc_lens,
    query_docs,
    ctx_pos,
    hidden,
    out_proj,
    norm_gain,
    router_weight,
    w_gate_up,
    w_down,
    expert_ids,
):
    lanes = lax.axis_size("tp")
    groups = lax.axis_size("ep")
    lane = lax.axis_index("tp")
    device = lax.axis_index("ep")
    length, heads_here, head_dim = question_q.shape
    kv_heads = question_kv.shape[1]
    docs_per = query_docs.shape[1]
    width_here = hidden.shape[1]
    ids = lax.all_gather(expert_ids, "ep", axis=0, tiled=False)
    kv_pick = lane * kv_heads // lanes
    kv_head = lax.dynamic_index_in_dim(question_kv, kv_pick, 1, keepdims=False).reshape(
        length, 2 * head_dim
    )
    context, starts, lengths = context_by_row(
        doc_kv, doc_lens, query_docs, ctx_pos, device, kv_pick
    )
    question_start = lax.dynamic_index_in_dim(ctx_pos, device, 0, keepdims=False)[docs_per]
    attended = attend(question_q, kv_head, context, starts, lengths, question_start)
    projected = jnp.dot(
        lax.all_gather(attended, "tp", axis=1, tiled=True),
        lax.all_gather(out_proj, "ep", axis=0, tiled=True),
        preferred_element_type=jnp.float32,
    )
    residual = (hidden.astype(jnp.float32) + projected.astype(jnp.float32)).astype(jnp.bfloat16)

    tokens = lax.all_gather(residual, "ep", axis=0, tiled=False)
    wide = tokens.astype(jnp.float32)
    gain = norm_gain.astype(jnp.float32)
    scaled = wide * gain
    logit_part = jnp.einsum(
        "snd,de->sne", scaled, router_weight.astype(jnp.float32), precision=lax.Precision.HIGHEST
    )
    square_part = jnp.sum(wide * wide, axis=2, keepdims=True)
    stats = jnp.sum(
        lax.all_gather(jnp.concatenate([logit_part, square_part], axis=2), "tp", axis=0), axis=0
    )
    experts = router_weight.shape[1]
    inv_rms = lax.rsqrt(stats[:, :, experts] / (width_here * lanes) + norm_eps)
    logits = stats[:, :, :experts] * inv_rms[:, :, None]

    local_experts = w_gate_up.shape[0]
    capacity = length * expert_ids.shape[1] // experts
    hid = w_gate_up.shape[3]
    chosen_all = jnp.any(
        ids[:, :, :, None] == jnp.arange(experts, dtype=jnp.int32), axis=2
    )
    top = jnp.max(jnp.where(chosen_all, logits, -jnp.inf), axis=2, keepdims=True)
    weight = jnp.where(chosen_all, jnp.exp(logits - top), 0.0)
    mix = weight / jnp.sum(weight, axis=2, keepdims=True)

    shuffled, scaled_rows = (chosen_all, scaled.astype(jnp.bfloat16))
    first = device * local_experts
    chosen = lax.dynamic_slice_in_dim(shuffled, first, local_experts, 2)
    mix_here = lax.dynamic_slice_in_dim(mix, first, local_experts, 2)
    before = (jnp.arange(length)[:, None] > jnp.arange(length)[None, :]).astype(jnp.bfloat16)
    rank = jnp.einsum(
        "mn,sne->sem", before, chosen.astype(jnp.bfloat16), preferred_element_type=jnp.float32
    ).astype(jnp.int32)
    pick = jnp.logical_and(
        jnp.transpose(chosen, (0, 2, 1))[:, :, None, :],
        rank[:, :, None, :] == jnp.arange(capacity, dtype=jnp.int32)[None, None, :, None],
    )
    onehot = pick.astype(jnp.bfloat16)
    inv_row = jnp.sum(jnp.where(pick, inv_rms[:, None, None, :], 0.0), axis=3)
    mix_row = jnp.sum(jnp.where(pick, jnp.transpose(mix_here, (0, 2, 1))[:, :, None, :], 0.0), axis=3)

    rows = jnp.einsum(
        "sern,snd->serd", onehot, scaled_rows, preferred_element_type=jnp.float32
    ).astype(jnp.bfloat16)
    term = jnp.einsum(
        "serd,edgh->sergh", rows, w_gate_up, preferred_element_type=jnp.float32
    ).astype(jnp.bfloat16)
    per_lane = groups * local_experts * capacity // lanes
    term = term.reshape(lanes, per_lane, 2 * hid)
    inv_row = inv_row.reshape(lanes, per_lane, 1)
    summed = lax.psum_scatter(term, "tp", scatter_dimension=0, tiled=True)[0].astype(jnp.float32)
    inv_mine = lax.dynamic_index_in_dim(inv_row, lane, 0, keepdims=False)
    summed = summed * inv_mine
    act = (jax.nn.silu(summed[:, :hid]) * summed[:, hid:]).astype(jnp.bfloat16)
    acts = lax.all_gather(act, "tp", axis=0, tiled=False)
    acts = acts.reshape(groups, local_experts, capacity, hid)
    expert_out = jnp.einsum("serh,ehd->serd", acts, w_down, preferred_element_type=jnp.float32)
    expert_out = (expert_out * mix_row[:, :, :, None]).astype(jnp.bfloat16)
    combined = jnp.einsum(
        "sern,serd->snd", onehot, expert_out, preferred_element_type=jnp.float32
    ).astype(jnp.bfloat16)
    returned = lax.psum_scatter(combined, "ep", scatter_dimension=0, tiled=True)[0]
    return (residual.astype(jnp.float32) + returned.astype(jnp.float32)).astype(jnp.bfloat16)


def pairs(lanes, flip):
    return [(i, i ^ flip) for i in range(lanes)]


def query_of(device, lane):
    return 2 * (lane & 1) + ((lane >> 1) ^ (device & 1))


def turn(values, groups, lanes):
    moves = [
        (e * lanes + t, t * lanes + 2 * ((e ^ t) & 1) + (e >> 1))
        for e in range(groups)
        for t in range(lanes)
    ]
    return lax.ppermute(values, ("ep", "tp"), moves)


def call(body, outs, scratch, flops, moved, **kwargs):
    return pl.pallas_call(
        body,
        out_shape=outs,
        **({} if scratch is None else {"scratch_shapes": scratch}),
        compiler_params=pltpu.CompilerParams(vmem_limit_bytes=40 * 1024 * 1024),
        cost_estimate=pl.CostEstimate(flops=flops, bytes_accessed=moved, transcendentals=0),
        **kwargs,
    )


VMEM = pl.BlockSpec(memory_space=pltpu.VMEM)
SMEM = pl.BlockSpec(memory_space=pltpu.SMEM)
NT = (((1,), (1,)), ((), ()))


def dot(a, b):
    return jnp.dot(a, b, preferred_element_type=jnp.float32)


def prepare_body(here, query_docs, pool, ids, *outs):
    pool_dev = pool.shape[0]
    docs_per = query_docs.shape[1]
    rows = pool.shape[2] * pool.shape[3]
    device, lane = (here[0], here[1])
    for d, out in enumerate(outs):
        target = device ^ d
        query = query_of(target, lane)
        local = jnp.int32(0)
        for j in range(docs_per):
            offset = query_docs[query, j] - device * pool_dev
            inside = jnp.logical_and(offset >= 0, offset < pool_dev)
            local = jnp.where(inside, offset, local)
        out[:rows, :] = pool[local, target].reshape(rows, pool.shape[4])
        out[rows:, :] = ids[...]


def prepare(here, query_docs, pool, ids):
    _, _, pair, doc_max, head_dim = pool.shape
    shape = jax.ShapeDtypeStruct((pair * doc_max + ids.shape[0], head_dim), jnp.bfloat16)
    return call(
        prepare_body,
        [shape] * 4,
        [],
        1024,
        1024 * 1024,
        in_specs=[SMEM, SMEM, VMEM, VMEM],
        out_specs=[VMEM] * 4,
        name="prepare",
    )(here, query_docs, pool, ids)


def attention_body(lens, q, c0, c1, c2, c3, cos_q, sin_q, cos_d, sin_d, out, wide, keys, vals):
    length, head_dim = cos_q.shape
    heads = out.shape[1] // head_dim
    pieces = (c0, c1, c2, c3)
    docs = len(pieces)
    doc_max = (keys.shape[0] - length) // docs
    half = head_dim // 2

    def turned(x, cosine, sine):
        return x * cosine + pltpu.roll(x, half, 1) * sine

    cosine, sine = (cos_q[...], sin_q[...])
    for j, piece in enumerate(pieces):
        key = turned(piece[:doc_max, :].astype(jnp.float32), cos_d[j : j + 1, :], sin_d[j : j + 1, :])
        keys[j * doc_max : (j + 1) * doc_max, :] = key.astype(jnp.bfloat16)
        vals[j * doc_max : (j + 1) * doc_max, :] = piece[doc_max : 2 * doc_max, :]
    base = docs * doc_max
    first = heads * length
    keys[base:, :] = turned(q[first : first + length, :].astype(jnp.float32), cosine, sine).astype(
        jnp.bfloat16
    )
    vals[base:, :] = q[first + length : first + 2 * length, :]
    wide[...] = q[:first, :].astype(jnp.float32)
    column = lax.broadcasted_iota(jnp.int32, (1, doc_max), 1)
    allowed = [column < lens[j] for j in range(docs)]
    causal = lax.broadcasted_iota(jnp.int32, (length, length), 0) >= lax.broadcasted_iota(
        jnp.int32, (length, length), 1
    )
    for h in range(heads):
        query = turned(wide[pl.ds(h, length, stride=heads), :], cosine, sine).astype(jnp.bfloat16)
        scores = lax.dot_general(query, keys[...], NT, preferred_element_type=jnp.float32)
        scores = scores * head_dim ** (-0.5)
        parts = [
            jnp.where(allowed[j], scores[:, j * doc_max : (j + 1) * doc_max], -jnp.inf)
            for j in range(docs)
        ] + [jnp.where(causal, scores[:, base:], -jnp.inf)]
        scores = jnp.concatenate(parts, axis=1)
        ceiling = jnp.max(scores, axis=1, keepdims=True)
        probs = jnp.exp(scores - ceiling)
        denominator = jnp.sum(probs, axis=1, keepdims=True)
        mixed = dot(probs.astype(jnp.bfloat16), vals[...])
        out[:, h * head_dim : (h + 1) * head_dim] = (mixed / denominator).astype(jnp.bfloat16)


def attention(lens, q, pieces, heads, tables_q, tables_d):
    length, head_dim = tables_q[0].shape
    rows = 5 * length
    return call(
        attention_body,
        jax.ShapeDtypeStruct((length, heads * head_dim), jnp.bfloat16),
        [
            pltpu.VMEM((heads * length, head_dim), jnp.float32),
            pltpu.VMEM((rows, head_dim), jnp.bfloat16),
            pltpu.VMEM((rows, head_dim), jnp.bfloat16),
        ],
        4 * heads * length * rows * head_dim * 4,
        4 * 1024 * 1024,
        in_specs=[SMEM] + [VMEM] * 9,
        out_specs=VMEM,
        name="attention",
    )(lens, q, *pieces, *tables_q, *tables_d)


def project_body(here, a, b, c, d, weight, hidden, out, rows):
    device, lane = (here[0], here[1])
    for flip, ref in zip((0, 2, 1, 3), (a, b, c, d)):
        rows[query_of(device, lane ^ flip)] = ref[...]
    for s in range(4):
        base = jnp.where(device == s, hidden[...].astype(jnp.float32), 0.0)
        out[s] = (base + dot(rows[s], weight[...])).astype(jnp.bfloat16)


def project(here, parts, weight, hidden):
    length, depth = parts[0].shape
    return call(
        project_body,
        jax.ShapeDtypeStruct((4, length, weight.shape[1]), jnp.bfloat16),
        [pltpu.VMEM((4, length, depth), jnp.bfloat16)],
        2 * 4 * length * depth * weight.shape[1],
        4 * 1024 * 1024,
        in_specs=[SMEM] + [VMEM] * 6,
        out_specs=VMEM,
        name="project",
    )(here, *parts, weight, hidden)


def assemble_body(here, tokens, gain, router, scaled, stats, residual):
    length = tokens.shape[1]
    experts = router.shape[0]
    device = here[0]
    ones = jnp.ones((8, tokens.shape[2]), jnp.float32)
    residual[...] = tokens[device]
    for d in range(4):
        wide = tokens[device ^ d].astype(jnp.float32)
        grown = wide * gain[...]
        scaled[d] = grown.astype(jnp.bfloat16)
        block = slice(d * length, (d + 1) * length)
        stats[:experts, block] = lax.dot_general(
            router[...], grown, NT, preferred_element_type=jnp.float32,
            precision=lax.Precision.HIGHEST,
        )
        stats[experts:, block] = lax.dot_general(
            ones, wide * wide, NT, preferred_element_type=jnp.float32,
            precision=lax.Precision.HIGHEST,
        )


def assemble(here, tokens, gain, router):
    n, length, width = tokens.shape
    return call(
        assemble_body,
        [
            jax.ShapeDtypeStruct((n, length, width), jnp.bfloat16),
            jax.ShapeDtypeStruct((router.shape[0] + 8, n * length), jnp.float32),
            jax.ShapeDtypeStruct((length, width), jnp.bfloat16),
        ],
        [],
        2 * n * length * width * 256,
        3 * 1024 * 1024,
        in_specs=[SMEM] + [VMEM] * 3,
        out_specs=[VMEM] * 3,
        name="assemble",
    )(here, tokens, gain, router)


def gate_up_body(first, order, tokens, pick, weight, *outs):
    hid = weight.shape[3]
    capacity = pick.shape[2]
    expert = order[pl.program_id(0)]
    rows = jnp.concatenate(
        [dot(pick[d, expert], tokens[d]).astype(jnp.bfloat16) for d in (first, first + 1)], axis=0
    )
    for g in range(2):
        term = dot(rows, weight[0, g]).astype(jnp.bfloat16)
        for j, out in enumerate(outs):

            @pl.when(pl.program_id(0) == j)
            def _():
                out[:, g * hid : (g + 1) * hid] = term


def gate_up(first, order, tokens, pick, weight):
    local, _, width, hid = weight.shape
    capacity = pick.shape[2]
    shape = jax.ShapeDtypeStruct((2 * capacity, 2 * hid), jnp.bfloat16)
    whole = lambda rank: lambda i, order: (0,) * rank
    return call(
        functools.partial(gate_up_body, first),
        [shape] * 4,
        None,
        2 * local * 2 * capacity * width * 2 * hid,
        20 * 1024 * 1024,
        grid_spec=pltpu.PrefetchScalarGridSpec(
            num_scalar_prefetch=1,
            grid=(local,),
            in_specs=[
                pl.BlockSpec(tokens.shape, whole(3)),
                pl.BlockSpec(pick.shape, whole(4)),
                pl.BlockSpec((1, 2, width, hid), lambda i, order: (order[i], 0, 0, 0)),
            ],
            out_specs=[pl.BlockSpec(shape.shape, whole(2))] * 4,
        ),
        name="gate_up",
    )(order, tokens, pick, weight)


def down_body(order, a, b, c, d, spread, weight, *rest):
    outs, results = (rest[:-1], rest[-1])
    i = pl.program_id(0)
    capacity = results.shape[2]
    expert = order[i]
    for j, ref in enumerate((a, b, c, d)):

        @pl.when(i == j)
        def _():
            result = dot(ref[...], weight[0]).astype(jnp.bfloat16)
            for k in range(2):
                results[k, expert] = result[k * capacity : (k + 1) * capacity, :]

    @pl.when(i == pl.num_programs(0) - 1)
    def _():
        for k, out in enumerate(outs):
            out[...] = dot(spread[k], results[k].reshape(-1, results.shape[3])).astype(jnp.bfloat16)


def down(order, acts, spread, weight):
    local, hid, width = weight.shape
    capacity = acts[0].shape[0] // 2
    length = spread.shape[1]
    shape = jax.ShapeDtypeStruct((length, width), jnp.bfloat16)
    whole = lambda rank: lambda i, order: (0,) * rank
    return call(
        down_body,
        [shape] * 2,
        None,
        2 * local * 2 * capacity * width * hid,
        10 * 1024 * 1024,
        grid_spec=pltpu.PrefetchScalarGridSpec(
            num_scalar_prefetch=1,
            grid=(local,),
            in_specs=[pl.BlockSpec(acts[0].shape, whole(2))] * 4
            + [
                pl.BlockSpec(spread.shape, whole(3)),
                pl.BlockSpec((1, hid, width), lambda i, order: (order[i], 0, 0)),
            ],
            out_specs=[pl.BlockSpec(shape.shape, whole(2))] * 2,
            scratch_shapes=[pltpu.VMEM((2, local, capacity, width), jnp.bfloat16)],
        ),
        name="down",
    )(order, *acts, spread, weight)


def signed_tables(positions, head_dim):
    cosine, sine = tables(positions, head_dim)
    return (
        jnp.concatenate([cosine, cosine], axis=1),
        jnp.concatenate([-sine, sine], axis=1),
    )


def per_device_square(
    question_q,
    question_kv,
    doc_kv,
    doc_lens,
    query_docs,
    ctx_pos,
    hidden,
    out_proj,
    norm_gain,
    router_weight,
    w_gate_up,
    w_down,
    expert_ids,
):
    n = 4
    lane = lax.axis_index("tp")
    device = lax.axis_index("ep")
    length, heads_here, head_dim = question_q.shape
    pool_dev, doc_max, kv_heads, _, _ = doc_kv.shape
    docs_per = query_docs.shape[1]
    width_here = hidden.shape[1]
    experts = router_weight.shape[1]
    local = w_gate_up.shape[0]
    capacity = length * expert_ids.shape[1] // experts
    hid = w_gate_up.shape[3]
    seats = jnp.arange(n, dtype=jnp.int32)
    here = jnp.stack([device, lane]).astype(jnp.int32)
    order = (lane ^ jnp.array([0, 2, 1, 3], jnp.int32)).astype(jnp.int32)
    reach = device ^ seats

    kv_head = lax.dynamic_index_in_dim(question_kv, lane, 1, keepdims=False)
    kv_rows = jnp.transpose(kv_head, (1, 0, 2)).reshape(2 * length, head_dim)
    q_rows = turn(
        jnp.concatenate([question_q.reshape(length * heads_here, head_dim), kv_rows], axis=0), n, n
    )

    pool = jnp.transpose(doc_kv, (0, 2, 3, 1, 4))
    ids_rows = jnp.pad(expert_ids.T.astype(jnp.bfloat16), ((0, 8), (0, 0)))
    pieces = prepare(here, query_docs, pool, ids_rows)
    pieces = [pieces[0]] + [lax.ppermute(pieces[d], "ep", pairs(n, d)) for d in range(1, n)]

    query = query_of(device, lane)
    my_docs = lax.dynamic_index_in_dim(query_docs, query, 0, keepdims=False)
    starts = lax.dynamic_index_in_dim(ctx_pos, query, 0, keepdims=False)
    owned = (my_docs // pool_dev)[None, :] == reach[:, None]
    lengths = jnp.sum(jnp.where(owned, jnp.take(doc_lens, my_docs)[None, :], 0), axis=1)
    doc_starts = jnp.sum(jnp.where(owned, starts[None, :docs_per], 0), axis=1)
    tables_q = signed_tables(starts[docs_per] + jnp.arange(length, dtype=jnp.int32), head_dim)
    tables_d = signed_tables(doc_starts, head_dim)

    attended = attention(lengths, q_rows, pieces, heads_here, tables_q, tables_d)
    far = lax.ppermute(attended, "tp", pairs(n, 2))
    near = lax.ppermute(attended, "tp", pairs(n, 1))
    farther = lax.ppermute(far, "tp", pairs(n, 1))
    partial = project(here, (attended, far, near, farther), out_proj, hidden)
    tokens = lax.psum(partial, "ep")

    ids = jnp.stack([p[2 * doc_max : 2 * doc_max + expert_ids.shape[1]] for p in pieces])
    ids = ids.astype(jnp.int32)
    named = device * local + jnp.arange(local, dtype=jnp.int32)
    chosen = jnp.any(ids[:, None, :, :] == named[None, :, None, None], axis=2)
    before = (jnp.arange(length)[:, None] < jnp.arange(length)[None, :]).astype(jnp.bfloat16)
    rank = jnp.einsum(
        "men,nk->mek", chosen.astype(jnp.bfloat16), before, preferred_element_type=jnp.float32
    ).astype(jnp.int32)
    picked = jnp.logical_and(
        chosen[:, :, None, :],
        rank[:, :, None, :] == jnp.arange(capacity, dtype=jnp.int32)[None, None, :, None],
    )
    pick = picked.astype(jnp.bfloat16)
    spread = jnp.transpose(pick.reshape(n, local * capacity, length), (0, 2, 1))
    named_all = jnp.any(
        ids[:, None, :, :] == jnp.arange(experts, dtype=jnp.int32)[None, :, None, None], axis=2
    )
    weight = jnp.transpose(w_gate_up, (0, 2, 1, 3))

    scaled, stats, residual = assemble(
        here, tokens, norm_gain.astype(jnp.float32)[None, :], router_weight.T.astype(jnp.float32)
    )
    stats = stats + lax.ppermute(stats, "tp", pairs(n, 2))
    stats = stats + lax.ppermute(stats, "tp", pairs(n, 1))
    stats = stats.reshape(experts + 8, n, length)
    inv_rms = lax.rsqrt(stats[experts] / (width_here * n) + norm_eps)
    logits = jnp.transpose(stats[:experts], (1, 0, 2)) * inv_rms[:, None, :]
    top = jnp.max(jnp.where(named_all, logits, -jnp.inf), axis=1, keepdims=True)
    grown = jnp.where(named_all, jnp.exp(logits - top), 0.0)
    mine = device * local + lane
    mix = lax.dynamic_index_in_dim(grown, mine, 1, keepdims=False) / jnp.sum(grown, axis=1)
    picked_mine = lax.dynamic_index_in_dim(picked, lane, 1, keepdims=False)
    inv_row = jnp.sum(jnp.where(picked_mine, inv_rms[:, None, :], 0.0), axis=2)
    mix_row = jnp.sum(jnp.where(picked_mine, mix[:, None, :], 0.0), axis=2)

    total = None
    for first in (2, 0):
        rows = slice(first, first + 2)
        terms = gate_up(first, order, scaled, pick, weight)
        for_far = lax.ppermute(terms[3], "tp", pairs(n, 1))
        for_me = lax.ppermute(terms[2], "tp", pairs(n, 1))
        chip_far = (terms[1].astype(jnp.float32) + for_far.astype(jnp.float32)).astype(jnp.bfloat16)
        across = lax.ppermute(chip_far, "tp", pairs(n, 2))
        summed = (
            terms[0].astype(jnp.float32) + for_me.astype(jnp.float32) + across.astype(jnp.float32)
        ) * inv_row[rows].reshape(-1, 1)
        act = jax.nn.silu(summed[:, :hid]) * summed[:, hid:] * mix_row[rows].reshape(-1, 1)
        act = act.astype(jnp.bfloat16)
        far = lax.ppermute(act, "tp", pairs(n, 2))
        near = lax.ppermute(act, "tp", pairs(n, 1))
        farther = lax.ppermute(far, "tp", pairs(n, 1))
        parts = down(order, (act, far, near, farther), spread[rows], w_down)
        for d, part in zip((first, first + 1), parts):
            back = lax.ppermute(part, "ep", pairs(n, d)) if d else part
            back = back.astype(jnp.float32)
            total = back if total is None else total + back
    return (residual.astype(jnp.float32) + total).astype(jnp.bfloat16)


def solution(mesh):
    placed = (
        P(("grp", "ep"), "tp", None),
        P(("grp", "ep"), None, None, None),
        P(("grp", "ep"), None, None, None, None),
        P("grp"),
        P("grp", None),
        P("grp", None),
        P(("grp", "ep"), "tp"),
        P("ep", "tp"),
        P("tp"),
        P("tp", None),
        P("ep", "tp", None, None),
        P("ep", None, "tp"),
        P(("grp", "ep"), None),
    )
    def per_device(*args):
        square = (
            lax.axis_size("tp") == 4
            and lax.axis_size("ep") == 4
            and args[1].shape[1] == 4
            and args[4].shape == (4, 4)
        )
        return (per_device_square if square else per_device_general)(*args)

    return jax.shard_map(
        per_device, mesh=mesh, in_specs=placed, out_specs=P(("grp", "ep"), "tp"), check_vma=False
    )
```

```python
import functools
import math

import jax
import jax.numpy as jnp
from jax import lax
from jax.experimental import pallas as pl
from jax.experimental.pallas import tpu as pltpu
from jax.sharding import PartitionSpec as P

rope_theta = 1000000.0
norm_eps = 1e-06


def tables(positions, head_dim):
    half = head_dim // 2
    freq = jnp.exp(jnp.arange(half, dtype=jnp.float32) * (-2.0 * math.log(rope_theta) / head_dim))
    angle = positions.astype(jnp.float32)[:, None] * freq[None, :]
    return (jnp.cos(angle), jnp.sin(angle))


def rotate(values, positions):
    half = values.shape[-1] // 2
    cosine, sine = tables(positions, values.shape[-1])
    shape = (values.shape[0],) + (1,) * (values.ndim - 2) + (half,)
    cosine, sine = (cosine.reshape(shape), sine.reshape(shape))
    floats = values.astype(jnp.float32)
    first = floats[..., :half]
    second = floats[..., half:]
    return jnp.concatenate(
        [first * cosine - second * sine, second * cosine + first * sine], axis=-1
    )


def attend(q_rows, own_kv, context, starts, lengths, question_start):
    length, heads_here, head_dim = q_rows.shape
    docs_per, doc_max, _ = context.shape
    question_pos = question_start + jnp.arange(length, dtype=jnp.int32)
    queries = rotate(q_rows, question_pos).astype(jnp.bfloat16)
    own_keys = rotate(own_kv[:, :head_dim], question_pos).astype(jnp.bfloat16)
    positions = jnp.repeat(starts, doc_max, total_repeat_length=docs_per * doc_max)
    doc_keys = rotate(context[:, :, :head_dim].reshape(docs_per * doc_max, head_dim), positions)
    keys = jnp.concatenate([doc_keys.astype(jnp.bfloat16), own_keys], axis=0)
    values = jnp.concatenate(
        [context[:, :, head_dim:].reshape(docs_per * doc_max, head_dim), own_kv[:, head_dim:]],
        axis=0,
    )
    valid = (jnp.arange(doc_max, dtype=jnp.int32)[None, :] < lengths[:, None]).reshape(-1)
    causal = jnp.arange(length)[:, None] >= jnp.arange(length)[None, :]
    allowed = jnp.concatenate(
        [jnp.broadcast_to(valid[None, :], (length, valid.shape[0])), causal], axis=1
    )
    scores = jnp.einsum("ihd,jd->hij", queries, keys, preferred_element_type=jnp.float32)
    scores = jnp.where(allowed[None], scores * head_dim ** (-0.5), -jnp.inf)
    ceiling = jnp.max(scores, axis=-1, keepdims=True)
    probs = jnp.exp(scores - ceiling)
    denominator = jnp.sum(probs, axis=-1, keepdims=True)
    mixed = jnp.einsum(
        "hij,jd->hid", probs.astype(jnp.bfloat16), values, preferred_element_type=jnp.float32
    )
    return (
        jnp.transpose(mixed / denominator, (1, 0, 2))
        .reshape(length, heads_here * head_dim)
        .astype(jnp.bfloat16)
    )


def context_by_row(doc_kv, doc_lens, query_docs, ctx_pos, device, kv_pick):
    pool_dev, doc_max, _, pair, head_dim = doc_kv.shape
    docs_per = query_docs.shape[1]
    pool_head = lax.dynamic_index_in_dim(doc_kv, kv_pick, 2, keepdims=False).reshape(
        pool_dev, doc_max, pair * head_dim
    )
    held = device * pool_dev + jnp.arange(pool_dev, dtype=jnp.int32)
    wanted = jnp.sum((query_docs[:, :, None] == held[None, None, :]).astype(jnp.float32), axis=1)
    sending = jnp.einsum(
        "rl,lkc->rkc", wanted.astype(jnp.bfloat16), pool_head, preferred_element_type=jnp.float32
    ).astype(jnp.bfloat16)
    received = lax.all_to_all(sending, "ep", split_axis=0, concat_axis=0, tiled=True)
    my_docs = lax.dynamic_index_in_dim(query_docs, device, 0, keepdims=False)
    starts = lax.dynamic_index_in_dim(ctx_pos, device, 0, keepdims=False)
    return (jnp.take(received, my_docs // pool_dev, axis=0), starts[:docs_per], jnp.take(doc_lens, my_docs))


def per_device_general(
    question_q,
    question_kv,
    doc_kv,
    doc_lens,
    query_docs,
    ctx_pos,
    hidden,
    out_proj,
    norm_gain,
    router_weight,
    w_gate_up,
    w_down,
    expert_ids,
):
    lanes = lax.axis_size("tp")
    groups = lax.axis_size("ep")
    lane = lax.axis_index("tp")
    device = lax.axis_index("ep")
    length, heads_here, head_dim = question_q.shape
    kv_heads = question_kv.shape[1]
    docs_per = query_docs.shape[1]
    width_here = hidden.shape[1]
    ids = lax.all_gather(expert_ids, "ep", axis=0, tiled=False)
    kv_pick = lane * kv_heads // lanes
    kv_head = lax.dynamic_index_in_dim(question_kv, kv_pick, 1, keepdims=False).reshape(
        length, 2 * head_dim
    )
    context, starts, lengths = context_by_row(
        doc_kv, doc_lens, query_docs, ctx_pos, device, kv_pick
    )
    question_start = lax.dynamic_index_in_dim(ctx_pos, device, 0, keepdims=False)[docs_per]
    attended = attend(question_q, kv_head, context, starts, lengths, question_start)
    projected = jnp.dot(
        lax.all_gather(attended, "tp", axis=1, tiled=True),
        lax.all_gather(out_proj, "ep", axis=0, tiled=True),
        preferred_element_type=jnp.float32,
    )
    residual = (hidden.astype(jnp.float32) + projected.astype(jnp.float32)).astype(jnp.bfloat16)

    tokens = lax.all_gather(residual, "ep", axis=0, tiled=False)
    wide = tokens.astype(jnp.float32)
    gain = norm_gain.astype(jnp.float32)
    scaled = wide * gain
    logit_part = jnp.einsum(
        "snd,de->sne", scaled, router_weight.astype(jnp.float32), precision=lax.Precision.HIGHEST
    )
    square_part = jnp.sum(wide * wide, axis=2, keepdims=True)
    stats = jnp.sum(
        lax.all_gather(jnp.concatenate([logit_part, square_part], axis=2), "tp", axis=0), axis=0
    )
    experts = router_weight.shape[1]
    inv_rms = lax.rsqrt(stats[:, :, experts] / (width_here * lanes) + norm_eps)
    logits = stats[:, :, :experts] * inv_rms[:, :, None]

    local_experts = w_gate_up.shape[0]
    capacity = length * expert_ids.shape[1] // experts
    hid = w_gate_up.shape[3]
    chosen_all = jnp.any(
        ids[:, :, :, None] == jnp.arange(experts, dtype=jnp.int32), axis=2
    )
    top = jnp.max(jnp.where(chosen_all, logits, -jnp.inf), axis=2, keepdims=True)
    weight = jnp.where(chosen_all, jnp.exp(logits - top), 0.0)
    mix = weight / jnp.sum(weight, axis=2, keepdims=True)

    shuffled, scaled_rows = (chosen_all, scaled.astype(jnp.bfloat16))
    first = device * local_experts
    chosen = lax.dynamic_slice_in_dim(shuffled, first, local_experts, 2)
    mix_here = lax.dynamic_slice_in_dim(mix, first, local_experts, 2)
    before = (jnp.arange(length)[:, None] > jnp.arange(length)[None, :]).astype(jnp.bfloat16)
    rank = jnp.einsum(
        "mn,sne->sem", before, chosen.astype(jnp.bfloat16), preferred_element_type=jnp.float32
    ).astype(jnp.int32)
    pick = jnp.logical_and(
        jnp.transpose(chosen, (0, 2, 1))[:, :, None, :],
        rank[:, :, None, :] == jnp.arange(capacity, dtype=jnp.int32)[None, None, :, None],
    )
    onehot = pick.astype(jnp.bfloat16)
    inv_row = jnp.sum(jnp.where(pick, inv_rms[:, None, None, :], 0.0), axis=3)
    mix_row = jnp.sum(jnp.where(pick, jnp.transpose(mix_here, (0, 2, 1))[:, :, None, :], 0.0), axis=3)

    rows = jnp.einsum(
        "sern,snd->serd", onehot, scaled_rows, preferred_element_type=jnp.float32
    ).astype(jnp.bfloat16)
    term = jnp.einsum(
        "serd,edgh->sergh", rows, w_gate_up, preferred_element_type=jnp.float32
    ).astype(jnp.bfloat16)
    per_lane = groups * local_experts * capacity // lanes
    term = term.reshape(lanes, per_lane, 2 * hid)
    inv_row = inv_row.reshape(lanes, per_lane, 1)
    summed = lax.psum_scatter(term, "tp", scatter_dimension=0, tiled=True)[0].astype(jnp.float32)
    inv_mine = lax.dynamic_index_in_dim(inv_row, lane, 0, keepdims=False)
    summed = summed * inv_mine
    act = (jax.nn.silu(summed[:, :hid]) * summed[:, hid:]).astype(jnp.bfloat16)
    acts = lax.all_gather(act, "tp", axis=0, tiled=False)
    acts = acts.reshape(groups, local_experts, capacity, hid)
    expert_out = jnp.einsum("serh,ehd->serd", acts, w_down, preferred_element_type=jnp.float32)
    expert_out = (expert_out * mix_row[:, :, :, None]).astype(jnp.bfloat16)
    combined = jnp.einsum(
        "sern,serd->snd", onehot, expert_out, preferred_element_type=jnp.float32
    ).astype(jnp.bfloat16)
    returned = lax.psum_scatter(combined, "ep", scatter_dimension=0, tiled=True)[0]
    return (residual.astype(jnp.float32) + returned.astype(jnp.float32)).astype(jnp.bfloat16)


def pairs(lanes, flip):
    return [(i, i ^ flip) for i in range(lanes)]


def query_of(device, lane):
    return 2 * (lane & 1) + ((lane >> 1) ^ (device & 1))


def turn(question, keys_values, device, lane, n):
    crosses = lambda e, t: ((e ^ t) & 1) != (t >> 1)
    devices = [(e, t) for e in range(n) for t in range(n)]
    swap = [(e * n + t, e * n + (t ^ 3)) for e, t in devices if crosses(e, t)]
    crossed = lax.ppermute(question, ("ep", "tp"), swap)
    heads = jnp.where(crosses(device, lane), lane ^ 3, lane)
    picked = lax.dynamic_index_in_dim(keys_values, heads, 1, keepdims=False)
    picked = jnp.transpose(picked, (1, 0, 2)).reshape(-1, question.shape[1])
    held = jnp.where(crosses(device, lane), crossed, question)
    moves = []
    for e, t in devices:
        h = t ^ 3 if crosses(e, t) else t
        moves.append((e * n + t, h * n + 2 * ((e ^ h) & 1) + (e >> 1)))
    return lax.ppermute(jnp.concatenate([held, picked], axis=0), ("ep", "tp"), moves)


def call(body, outs, scratch, flops, moved, mib=40, **kwargs):
    return pl.pallas_call(
        body,
        out_shape=outs,
        **({} if scratch is None else {"scratch_shapes": scratch}),
        compiler_params=pltpu.CompilerParams(vmem_limit_bytes=mib * 1024 * 1024),
        cost_estimate=pl.CostEstimate(flops=flops, bytes_accessed=moved, transcendentals=0),
        **kwargs,
    )


VMEM = pl.BlockSpec(memory_space=pltpu.VMEM)
SMEM = pl.BlockSpec(memory_space=pltpu.SMEM)
NT = (((1,), (1,)), ((), ()))


def dot(a, b):
    return jnp.dot(a, b, preferred_element_type=jnp.float32)


def prepare_body(here, query_docs, pool, ids, *outs):
    pool_dev = pool.shape[0]
    docs_per = query_docs.shape[1]
    rows = pool.shape[2] * pool.shape[3]
    device, lane = (here[0], here[1])
    for d, out in enumerate(outs):
        target = device ^ d
        query = query_of(target, lane)
        local = jnp.int32(0)
        for j in range(docs_per):
            offset = query_docs[query, j] - device * pool_dev
            inside = jnp.logical_and(offset >= 0, offset < pool_dev)
            local = jnp.where(inside, offset, local)
        out[:rows, :] = pool[local, target].reshape(rows, pool.shape[4])
        out[rows:, :] = ids[...]


def prepare(here, query_docs, pool, ids):
    _, _, pair, doc_max, head_dim = pool.shape
    shape = jax.ShapeDtypeStruct((pair * doc_max + ids.shape[0], head_dim), jnp.bfloat16)
    return call(
        prepare_body,
        [shape] * 4,
        [],
        1024,
        1024 * 1024,
        in_specs=[SMEM, SMEM, VMEM, VMEM],
        out_specs=[VMEM] * 4,
        name="prepare",
    )(here, query_docs, pool, ids)


def attention_body(lens, q, c0, c1, c2, c3, cos_q, sin_q, cos_d, sin_d, out, wide, keys, vals):
    length, head_dim = cos_q.shape
    heads = out.shape[1] // head_dim
    pieces = (c0, c1, c2, c3)
    docs = len(pieces)
    doc_max = (keys.shape[0] - length) // docs
    half = head_dim // 2

    def turned(x, cosine, sine):
        return x * cosine + pltpu.roll(x, half, 1) * sine

    cosine, sine = (cos_q[...], sin_q[...])
    for j, piece in enumerate(pieces):
        key = turned(piece[:doc_max, :].astype(jnp.float32), cos_d[j : j + 1, :], sin_d[j : j + 1, :])
        keys[j * doc_max : (j + 1) * doc_max, :] = key.astype(jnp.bfloat16)
        vals[j * doc_max : (j + 1) * doc_max, :] = piece[doc_max : 2 * doc_max, :]
    base = docs * doc_max
    first = heads * length
    keys[base:, :] = turned(q[first : first + length, :].astype(jnp.float32), cosine, sine).astype(
        jnp.bfloat16
    )
    vals[base:, :] = q[first + length :, :]
    wide[...] = q[:first, :].astype(jnp.float32)
    column = lax.broadcasted_iota(jnp.int32, (1, doc_max), 1)
    allowed = [column < lens[j] for j in range(docs)]
    causal = lax.broadcasted_iota(jnp.int32, (length, length), 0) >= lax.broadcasted_iota(
        jnp.int32, (length, length), 1
    )
    for h in range(heads):
        query = turned(wide[pl.ds(h, length, stride=heads), :], cosine, sine).astype(jnp.bfloat16)
        scores = lax.dot_general(query, keys[...], NT, preferred_element_type=jnp.float32)
        scores = scores * head_dim ** (-0.5)
        parts = [
            jnp.where(allowed[j], scores[:, j * doc_max : (j + 1) * doc_max], -jnp.inf)
            for j in range(docs)
        ] + [jnp.where(causal, scores[:, base:], -jnp.inf)]
        scores = jnp.concatenate(parts, axis=1)
        ceiling = jnp.max(scores, axis=1, keepdims=True)
        probs = jnp.exp(scores - ceiling)
        denominator = jnp.sum(probs, axis=1, keepdims=True)
        mixed = dot(probs.astype(jnp.bfloat16), vals[...])
        out[:, h * head_dim : (h + 1) * head_dim] = (mixed / denominator).astype(jnp.bfloat16)


def attention(lens, q, pieces, tables_q, tables_d):
    length, head_dim = tables_q[0].shape
    heads = q.shape[0] // length - 2
    rows = 5 * length
    return call(
        attention_body,
        jax.ShapeDtypeStruct((length, heads * head_dim), jnp.bfloat16),
        [
            pltpu.VMEM((heads * length, head_dim), jnp.float32),
            pltpu.VMEM((rows, head_dim), jnp.bfloat16),
            pltpu.VMEM((rows, head_dim), jnp.bfloat16),
        ],
        4 * heads * length * rows * head_dim * 4,
        4 * 1024 * 1024,
        in_specs=[SMEM] + [VMEM] * 9,
        out_specs=VMEM,
        name="attention",
    )(lens, q, *pieces, *tables_q, *tables_d)


def project_body(here, a, b, c, d, weight, hidden, out, rows):
    device, lane = (here[0], here[1])

    @pl.when(pl.program_id(0) == 0)
    def _():
        for flip, ref in zip((0, 2, 1, 3), (a, b, c, d)):
            rows[query_of(device, lane ^ flip)] = ref[...]

    for s in range(4):
        base = jnp.where(device == s, hidden[...].astype(jnp.float32), 0.0)
        out[s] = (base + dot(rows[s], weight[...])).astype(jnp.bfloat16)


def project(here, parts, weight, hidden):
    length, depth = parts[0].shape
    width = weight.shape[1]
    step = width // 4
    whole = pl.BlockSpec((length, depth), lambda i: (0, 0))
    column = lambda rows: pl.BlockSpec((rows, step), lambda i: (0, i))
    return call(
        project_body,
        jax.ShapeDtypeStruct((4, length, width), jnp.bfloat16),
        [pltpu.VMEM((4, length, depth), jnp.bfloat16)],
        2 * 4 * length * depth * width,
        4 * 1024 * 1024,
        grid=(4,),
        in_specs=[SMEM] + [whole] * 4 + [column(depth), column(length)],
        out_specs=pl.BlockSpec((4, length, step), lambda i: (0, 0, i)),
        mib=58,
        name="project",
    )(here, *parts, weight, hidden)


def assemble_body(here, tokens, gain, router, after, scaled, stats, residual):
    length = tokens.shape[1]
    rows = stats.shape[0]
    device = here[0]
    residual[...] = tokens[device]
    column = lax.broadcasted_iota(jnp.int32, (length, router.shape[1]), 1)
    for d in range(4):
        wide = tokens[device ^ d].astype(jnp.float32)
        grown = wide * gain[...]
        high = grown.astype(jnp.bfloat16)
        rest = grown - high.astype(jnp.float32)
        middle = rest.astype(jnp.bfloat16)
        low = (rest - middle.astype(jnp.float32)).astype(jnp.bfloat16)
        scaled[d] = high
        logits = dot(high, router[...]) + (dot(middle, router[...]) + dot(low, router[...]))
        squares = jnp.sum(wide * wide, axis=1, keepdims=True)
        both = jnp.where(column == rows - 8, squares, logits)
        stats[:, d * length : (d + 1) * length] = jnp.transpose(both)[:rows, :]


def assemble(here, tokens, gain, router, experts, after):
    n, length, width = tokens.shape
    return call(
        assemble_body,
        [
            jax.ShapeDtypeStruct((n, length, width), jnp.bfloat16),
            jax.ShapeDtypeStruct((experts + 8, n * length), jnp.float32),
            jax.ShapeDtypeStruct((length, width), jnp.bfloat16),
        ],
        [],
        2 * n * length * width * 384,
        3 * 1024 * 1024,
        in_specs=[SMEM] + [VMEM] * 3 + [pl.BlockSpec(memory_space=pl.ANY)],
        out_specs=[VMEM] * 3,
        mib=58,
        name="assemble",
    )(here, tokens, gain, router, after)


def gate_up_body(first, order, tokens, pick, weight, *rest):
    outs, rows = (rest[:-1], rest[-1])
    hid = weight.shape[3]
    capacity = pick.shape[2]
    i, g = (pl.program_id(0), pl.program_id(1))
    expert = order[i]

    @pl.when(g == 0)
    def _():
        for k in range(2):
            chosen = dot(pick[first + k, expert], tokens[first + k])
            rows[k * capacity : (k + 1) * capacity, :] = chosen.astype(jnp.bfloat16)

    term = dot(rows[...], weight[0, 0]).astype(jnp.bfloat16)
    column = pl.multiple_of(g * hid, hid)
    for j, out in enumerate(outs):

        @pl.when(i == j)
        def _():
            out[:, pl.ds(column, hid)] = term


def gate_up(first, order, tokens, pick, weight):
    local, _, width, hid = weight.shape
    capacity = pick.shape[2]
    shape = jax.ShapeDtypeStruct((2 * capacity, 2 * hid), jnp.bfloat16)
    whole = lambda rank: lambda i, g, order: (0,) * rank
    return call(
        functools.partial(gate_up_body, first),
        [shape] * 4,
        None,
        2 * local * 2 * capacity * width * 2 * hid,
        20 * 1024 * 1024,
        grid_spec=pltpu.PrefetchScalarGridSpec(
            num_scalar_prefetch=1,
            grid=(local, 2),
            in_specs=[
                pl.BlockSpec(tokens.shape, whole(3)),
                pl.BlockSpec(pick.shape, whole(4)),
                pl.BlockSpec((1, 1, width, hid), lambda i, g, order: (order[i], g, 0, 0)),
            ],
            out_specs=[pl.BlockSpec(shape.shape, whole(2))] * 4,
            scratch_shapes=[pltpu.VMEM((2 * capacity, width), jnp.bfloat16)],
        ),
        mib=48,
        name="gate_up",
    )(order, tokens, pick, weight)


def down_body(order, a, b, c, d, spread, weight, *rest):
    outs, results = (rest[:-1], rest[-1])
    i = pl.program_id(0)
    capacity = results.shape[2]
    expert = order[i]
    for j, ref in enumerate((a, b, c, d)):

        @pl.when(i == j)
        def _():
            result = dot(ref[...], weight[0]).astype(jnp.bfloat16)
            for k in range(2):
                results[k, expert] = result[k * capacity : (k + 1) * capacity, :]

    @pl.when(i == pl.num_programs(0) - 1)
    def _():
        for k, out in enumerate(outs):
            out[...] = dot(spread[k], results[k].reshape(-1, results.shape[3])).astype(jnp.bfloat16)


def down(order, acts, spread, weight):
    local, hid, width = weight.shape
    capacity = acts[0].shape[0] // 2
    length = spread.shape[1]
    shape = jax.ShapeDtypeStruct((length, width), jnp.bfloat16)
    whole = lambda rank: lambda i, order: (0,) * rank
    return call(
        down_body,
        [shape] * 2,
        None,
        2 * local * 2 * capacity * width * hid,
        10 * 1024 * 1024,
        grid_spec=pltpu.PrefetchScalarGridSpec(
            num_scalar_prefetch=1,
            grid=(local,),
            in_specs=[pl.BlockSpec(acts[0].shape, whole(2))] * 4
            + [
                pl.BlockSpec(spread.shape, whole(3)),
                pl.BlockSpec((1, hid, width), lambda i, order: (order[i], 0, 0)),
            ],
            out_specs=[pl.BlockSpec(shape.shape, whole(2))] * 2,
            scratch_shapes=[pltpu.VMEM((2, local, capacity, width), jnp.bfloat16)],
        ),
        mib=54,
        name="down",
    )(order, *acts, spread, weight)


def signed_tables(positions, head_dim):
    cosine, sine = tables(positions, head_dim)
    return (
        jnp.concatenate([cosine, cosine], axis=1),
        jnp.concatenate([-sine, sine], axis=1),
    )


def per_device_square(
    question_q,
    question_kv,
    doc_kv,
    doc_lens,
    query_docs,
    ctx_pos,
    hidden,
    out_proj,
    norm_gain,
    router_weight,
    w_gate_up,
    w_down,
    expert_ids,
):
    n = 4
    lane = lax.axis_index("tp")
    device = lax.axis_index("ep")
    length, heads_here, head_dim = question_q.shape
    pool_dev, doc_max, kv_heads, _, _ = doc_kv.shape
    docs_per = query_docs.shape[1]
    width_here = hidden.shape[1]
    experts = router_weight.shape[1]
    local = w_gate_up.shape[0]
    capacity = length * expert_ids.shape[1] // experts
    hid = w_gate_up.shape[3]
    seats = jnp.arange(n, dtype=jnp.int32)
    here = jnp.stack([device, lane]).astype(jnp.int32)
    order = (lane ^ jnp.array([0, 2, 1, 3], jnp.int32)).astype(jnp.int32)
    reach = device ^ seats

    q_rows = turn(
        question_q.reshape(length * heads_here, head_dim), question_kv, device, lane, n
    )

    pool = jnp.transpose(doc_kv, (0, 2, 3, 1, 4))
    ids_rows = jnp.pad(expert_ids.T.astype(jnp.bfloat16), ((0, 8), (0, 0)))
    pieces = prepare(here, query_docs, pool, ids_rows)
    pieces = [pieces[0]] + [lax.ppermute(pieces[d], "ep", pairs(n, d)) for d in range(1, n)]

    query = query_of(device, lane)
    my_docs = lax.dynamic_index_in_dim(query_docs, query, 0, keepdims=False)
    starts = lax.dynamic_index_in_dim(ctx_pos, query, 0, keepdims=False)
    owned = (my_docs // pool_dev)[None, :] == reach[:, None]
    lengths = jnp.sum(jnp.where(owned, jnp.take(doc_lens, my_docs)[None, :], 0), axis=1)
    doc_starts = jnp.sum(jnp.where(owned, starts[None, :docs_per], 0), axis=1)
    tables_q = signed_tables(starts[docs_per] + jnp.arange(length, dtype=jnp.int32), head_dim)
    tables_d = signed_tables(doc_starts, head_dim)

    attended = attention(lengths, q_rows, pieces, tables_q, tables_d)
    far = lax.ppermute(attended, "tp", pairs(n, 2))
    near = lax.ppermute(attended, "tp", pairs(n, 1))
    farther = lax.ppermute(far, "tp", pairs(n, 1))
    gain = norm_gain.astype(jnp.float32)[None, :]
    router = jnp.pad(router_weight, ((0, 0), (0, 128 - experts)))
    partial = project(here, (attended, far, near, farther), out_proj, hidden)
    partial, w_gate_up = lax.optimization_barrier((partial, w_gate_up))
    tokens = lax.psum(partial, "ep")

    ids = jnp.stack([p[2 * doc_max : 2 * doc_max + expert_ids.shape[1]] for p in pieces])
    ids = ids.astype(jnp.int32)
    named = device * local + jnp.arange(local, dtype=jnp.int32)
    chosen = jnp.any(ids[:, None, :, :] == named[None, :, None, None], axis=2)
    before = (jnp.arange(length)[:, None] < jnp.arange(length)[None, :]).astype(jnp.bfloat16)
    rank = jnp.einsum(
        "men,nk->mek", chosen.astype(jnp.bfloat16), before, preferred_element_type=jnp.float32
    ).astype(jnp.int32)
    picked = jnp.logical_and(
        chosen[:, :, None, :],
        rank[:, :, None, :] == jnp.arange(capacity, dtype=jnp.int32)[None, None, :, None],
    )
    pick = picked.astype(jnp.bfloat16)
    spread = jnp.transpose(pick.reshape(n, local * capacity, length), (0, 2, 1))
    named_all = jnp.any(
        ids[:, None, :, :] == jnp.arange(experts, dtype=jnp.int32)[None, :, None, None], axis=2
    )
    weight = jnp.transpose(w_gate_up, (0, 2, 1, 3))

    scaled, stats, residual = assemble(here, tokens, gain, router, experts, weight)
    stats = stats + lax.ppermute(stats, "tp", pairs(n, 2))
    stats = stats + lax.ppermute(stats, "tp", pairs(n, 1))
    stats = stats.reshape(experts + 8, n, length)
    inv_rms = lax.rsqrt(stats[experts] / (width_here * n) + norm_eps)
    logits = jnp.transpose(stats[:experts], (1, 0, 2)) * inv_rms[:, None, :]
    top = jnp.max(jnp.where(named_all, logits, -jnp.inf), axis=1, keepdims=True)
    grown = jnp.where(named_all, jnp.exp(logits - top), 0.0)
    mine = device * local + lane
    mix = lax.dynamic_index_in_dim(grown, mine, 1, keepdims=False) / jnp.sum(grown, axis=1)
    picked_mine = lax.dynamic_index_in_dim(picked, lane, 1, keepdims=False)
    inv_row = jnp.sum(jnp.where(picked_mine, inv_rms[:, None, :], 0.0), axis=2)
    mix_row = jnp.sum(jnp.where(picked_mine, mix[:, None, :], 0.0), axis=2)

    def exchange(first, order):
        terms = gate_up(first, order, scaled, pick, weight)
        for_far = lax.ppermute(terms[3], "tp", pairs(n, 1))
        for_me = lax.ppermute(terms[2], "tp", pairs(n, 1))
        chip_far = (terms[1].astype(jnp.float32) + for_far.astype(jnp.float32)).astype(jnp.bfloat16)
        return (chip_far, terms[0], for_me, lax.ppermute(chip_far, "tp", pairs(n, 2)))

    def finish(first, order, mine, for_me, across):
        rows = slice(first, first + 2)
        summed = (
            mine.astype(jnp.float32) + for_me.astype(jnp.float32) + across.astype(jnp.float32)
        ) * inv_row[rows].reshape(-1, 1)
        act = jax.nn.silu(summed[:, :hid]) * summed[:, hid:] * mix_row[rows].reshape(-1, 1)
        act = act.astype(jnp.bfloat16)
        far = lax.ppermute(act, "tp", pairs(n, 2))
        near = lax.ppermute(act, "tp", pairs(n, 1))
        farther = lax.ppermute(far, "tp", pairs(n, 1))
        return down(order, (act, far, near, farther), spread[rows], w_down)

    chip_far, *ahead = exchange(2, order)
    order, _ = lax.optimization_barrier((order, chip_far))
    _, *behind = exchange(0, order)
    away_2, away_3 = finish(2, order, *ahead)
    behind[0], away_2, away_3 = lax.optimization_barrier((behind[0], away_2, away_3))
    away_2 = lax.ppermute(away_2, "ep", pairs(n, 2))
    away_3 = lax.ppermute(away_3, "ep", pairs(n, 3))
    mine, away_1 = finish(0, order, *behind)
    away_1 = lax.ppermute(away_1, "ep", pairs(n, 1))
    total = residual.astype(jnp.float32)
    for part in (mine, away_2, away_3, away_1):
        total = total + part.astype(jnp.float32)
    return total.astype(jnp.bfloat16)


def solution(mesh):
    placed = (
        P(("grp", "ep"), "tp", None),
        P(("grp", "ep"), None, None, None),
        P(("grp", "ep"), None, None, None, None),
        P("grp"),
        P("grp", None),
        P("grp", None),
        P(("grp", "ep"), "tp"),
        P("ep", "tp"),
        P("tp"),
        P("tp", None),
        P("ep", "tp", None, None),
        P("ep", None, "tp"),
        P(("grp", "ep"), None),
    )
    def per_device(*args):
        square = (
            lax.axis_size("tp") == 4
            and lax.axis_size("ep") == 4
            and args[1].shape[1] == 4
            and args[4].shape == (4, 4)
        )
        return (per_device_square if square else per_device_general)(*args)

    return jax.shard_map(
        per_device, mesh=mesh, in_specs=placed, out_specs=P(("grp", "ep"), "tp"), check_vma=False
    )
```

```python
import functools
import math

import jax
import jax.numpy as jnp
from jax import lax
from jax.experimental import pallas as pl
from jax.experimental.pallas import tpu as pltpu
from jax.sharding import PartitionSpec as P

rope_theta = 1000000.0
norm_eps = 1e-06


def tables(positions, head_dim):
    half = head_dim // 2
    freq = jnp.exp(jnp.arange(half, dtype=jnp.float32) * (-2.0 * math.log(rope_theta) / head_dim))
    angle = positions.astype(jnp.float32)[:, None] * freq[None, :]
    return (jnp.cos(angle), jnp.sin(angle))


def rotate(values, positions):
    half = values.shape[-1] // 2
    cosine, sine = tables(positions, values.shape[-1])
    shape = (values.shape[0],) + (1,) * (values.ndim - 2) + (half,)
    cosine, sine = (cosine.reshape(shape), sine.reshape(shape))
    floats = values.astype(jnp.float32)
    first = floats[..., :half]
    second = floats[..., half:]
    return jnp.concatenate(
        [first * cosine - second * sine, second * cosine + first * sine], axis=-1
    )


def attend(q_rows, own_kv, context, starts, lengths, question_start):
    length, heads_here, head_dim = q_rows.shape
    docs_per, doc_max, _ = context.shape
    question_pos = question_start + jnp.arange(length, dtype=jnp.int32)
    queries = rotate(q_rows, question_pos).astype(jnp.bfloat16)
    own_keys = rotate(own_kv[:, :head_dim], question_pos).astype(jnp.bfloat16)
    positions = jnp.repeat(starts, doc_max, total_repeat_length=docs_per * doc_max)
    doc_keys = rotate(context[:, :, :head_dim].reshape(docs_per * doc_max, head_dim), positions)
    keys = jnp.concatenate([doc_keys.astype(jnp.bfloat16), own_keys], axis=0)
    values = jnp.concatenate(
        [context[:, :, head_dim:].reshape(docs_per * doc_max, head_dim), own_kv[:, head_dim:]],
        axis=0,
    )
    valid = (jnp.arange(doc_max, dtype=jnp.int32)[None, :] < lengths[:, None]).reshape(-1)
    causal = jnp.arange(length)[:, None] >= jnp.arange(length)[None, :]
    allowed = jnp.concatenate(
        [jnp.broadcast_to(valid[None, :], (length, valid.shape[0])), causal], axis=1
    )
    scores = jnp.einsum("ihd,jd->hij", queries, keys, preferred_element_type=jnp.float32)
    scores = jnp.where(allowed[None], scores * head_dim ** (-0.5), -jnp.inf)
    ceiling = jnp.max(scores, axis=-1, keepdims=True)
    probs = jnp.exp(scores - ceiling)
    denominator = jnp.sum(probs, axis=-1, keepdims=True)
    mixed = jnp.einsum(
        "hij,jd->hid", probs.astype(jnp.bfloat16), values, preferred_element_type=jnp.float32
    )
    return (
        jnp.transpose(mixed / denominator, (1, 0, 2))
        .reshape(length, heads_here * head_dim)
        .astype(jnp.bfloat16)
    )


def context_by_row(doc_kv, doc_lens, query_docs, ctx_pos, device, kv_pick):
    pool_dev, doc_max, _, pair, head_dim = doc_kv.shape
    docs_per = query_docs.shape[1]
    pool_head = lax.dynamic_index_in_dim(doc_kv, kv_pick, 2, keepdims=False).reshape(
        pool_dev, doc_max, pair * head_dim
    )
    held = device * pool_dev + jnp.arange(pool_dev, dtype=jnp.int32)
    wanted = jnp.sum((query_docs[:, :, None] == held[None, None, :]).astype(jnp.float32), axis=1)
    sending = jnp.einsum(
        "rl,lkc->rkc", wanted.astype(jnp.bfloat16), pool_head, preferred_element_type=jnp.float32
    ).astype(jnp.bfloat16)
    received = lax.all_to_all(sending, "ep", split_axis=0, concat_axis=0, tiled=True)
    my_docs = lax.dynamic_index_in_dim(query_docs, device, 0, keepdims=False)
    starts = lax.dynamic_index_in_dim(ctx_pos, device, 0, keepdims=False)
    return (jnp.take(received, my_docs // pool_dev, axis=0), starts[:docs_per], jnp.take(doc_lens, my_docs))


def per_device_general(
    question_q,
    question_kv,
    doc_kv,
    doc_lens,
    query_docs,
    ctx_pos,
    hidden,
    out_proj,
    norm_gain,
    router_weight,
    w_gate_up,
    w_down,
    expert_ids,
):
    lanes = lax.axis_size("tp")
    groups = lax.axis_size("ep")
    lane = lax.axis_index("tp")
    device = lax.axis_index("ep")
    length, heads_here, head_dim = question_q.shape
    kv_heads = question_kv.shape[1]
    docs_per = query_docs.shape[1]
    width_here = hidden.shape[1]
    ids = lax.all_gather(expert_ids, "ep", axis=0, tiled=False)
    kv_pick = lane * kv_heads // lanes
    kv_head = lax.dynamic_index_in_dim(question_kv, kv_pick, 1, keepdims=False).reshape(
        length, 2 * head_dim
    )
    context, starts, lengths = context_by_row(
        doc_kv, doc_lens, query_docs, ctx_pos, device, kv_pick
    )
    question_start = lax.dynamic_index_in_dim(ctx_pos, device, 0, keepdims=False)[docs_per]
    attended = attend(question_q, kv_head, context, starts, lengths, question_start)
    projected = jnp.dot(
        lax.all_gather(attended, "tp", axis=1, tiled=True),
        lax.all_gather(out_proj, "ep", axis=0, tiled=True),
        preferred_element_type=jnp.float32,
    )
    residual = (hidden.astype(jnp.float32) + projected.astype(jnp.float32)).astype(jnp.bfloat16)

    tokens = lax.all_gather(residual, "ep", axis=0, tiled=False)
    wide = tokens.astype(jnp.float32)
    gain = norm_gain.astype(jnp.float32)
    scaled = wide * gain
    logit_part = jnp.einsum(
        "snd,de->sne", scaled, router_weight.astype(jnp.float32), precision=lax.Precision.HIGHEST
    )
    square_part = jnp.sum(wide * wide, axis=2, keepdims=True)
    stats = jnp.sum(
        lax.all_gather(jnp.concatenate([logit_part, square_part], axis=2), "tp", axis=0), axis=0
    )
    experts = router_weight.shape[1]
    inv_rms = lax.rsqrt(stats[:, :, experts] / (width_here * lanes) + norm_eps)
    logits = stats[:, :, :experts] * inv_rms[:, :, None]

    local_experts = w_gate_up.shape[0]
    capacity = length * expert_ids.shape[1] // experts
    hid = w_gate_up.shape[3]
    chosen_all = jnp.any(
        ids[:, :, :, None] == jnp.arange(experts, dtype=jnp.int32), axis=2
    )
    top = jnp.max(jnp.where(chosen_all, logits, -jnp.inf), axis=2, keepdims=True)
    weight = jnp.where(chosen_all, jnp.exp(logits - top), 0.0)
    mix = weight / jnp.sum(weight, axis=2, keepdims=True)

    shuffled, scaled_rows = (chosen_all, scaled.astype(jnp.bfloat16))
    first = device * local_experts
    chosen = lax.dynamic_slice_in_dim(shuffled, first, local_experts, 2)
    mix_here = lax.dynamic_slice_in_dim(mix, first, local_experts, 2)
    before = (jnp.arange(length)[:, None] > jnp.arange(length)[None, :]).astype(jnp.bfloat16)
    rank = jnp.einsum(
        "mn,sne->sem", before, chosen.astype(jnp.bfloat16), preferred_element_type=jnp.float32
    ).astype(jnp.int32)
    pick = jnp.logical_and(
        jnp.transpose(chosen, (0, 2, 1))[:, :, None, :],
        rank[:, :, None, :] == jnp.arange(capacity, dtype=jnp.int32)[None, None, :, None],
    )
    onehot = pick.astype(jnp.bfloat16)
    inv_row = jnp.sum(jnp.where(pick, inv_rms[:, None, None, :], 0.0), axis=3)
    mix_row = jnp.sum(jnp.where(pick, jnp.transpose(mix_here, (0, 2, 1))[:, :, None, :], 0.0), axis=3)

    rows = jnp.einsum(
        "sern,snd->serd", onehot, scaled_rows, preferred_element_type=jnp.float32
    ).astype(jnp.bfloat16)
    term = jnp.einsum(
        "serd,edgh->sergh", rows, w_gate_up, preferred_element_type=jnp.float32
    ).astype(jnp.bfloat16)
    per_lane = groups * local_experts * capacity // lanes
    term = term.reshape(lanes, per_lane, 2 * hid)
    inv_row = inv_row.reshape(lanes, per_lane, 1)
    summed = lax.psum_scatter(term, "tp", scatter_dimension=0, tiled=True)[0].astype(jnp.float32)
    inv_mine = lax.dynamic_index_in_dim(inv_row, lane, 0, keepdims=False)
    summed = summed * inv_mine
    act = (jax.nn.silu(summed[:, :hid]) * summed[:, hid:]).astype(jnp.bfloat16)
    acts = lax.all_gather(act, "tp", axis=0, tiled=False)
    acts = acts.reshape(groups, local_experts, capacity, hid)
    expert_out = jnp.einsum("serh,ehd->serd", acts, w_down, preferred_element_type=jnp.float32)
    expert_out = (expert_out * mix_row[:, :, :, None]).astype(jnp.bfloat16)
    combined = jnp.einsum(
        "sern,serd->snd", onehot, expert_out, preferred_element_type=jnp.float32
    ).astype(jnp.bfloat16)
    returned = lax.psum_scatter(combined, "ep", scatter_dimension=0, tiled=True)[0]
    return (residual.astype(jnp.float32) + returned.astype(jnp.float32)).astype(jnp.bfloat16)


def pairs(lanes, flip):
    return [(i, i ^ flip) for i in range(lanes)]


def query_of(device, lane):
    return 2 * (lane & 1) + ((lane >> 1) ^ (device & 1))


def turn(question, keys_values, device, lane, n, meanwhile):
    crosses = lambda e, t: ((e ^ t) & 1) != (t >> 1)
    devices = [(e, t) for e in range(n) for t in range(n)]
    swap = [(e * n + t, e * n + (t ^ 3)) for e, t in devices if crosses(e, t)]
    crossed = lax.ppermute(question, ("ep", "tp"), swap)
    crossed, *meanwhile = lax.optimization_barrier((crossed, *meanwhile))
    heads = jnp.where(crosses(device, lane), lane ^ 3, lane)
    picked = lax.dynamic_index_in_dim(keys_values, heads, 1, keepdims=False)
    picked = jnp.transpose(picked, (1, 0, 2)).reshape(-1, question.shape[1])
    held = jnp.where(crosses(device, lane), crossed, question)
    moves = []
    for e, t in devices:
        h = t ^ 3 if crosses(e, t) else t
        moves.append((e * n + t, h * n + 2 * ((e ^ h) & 1) + (e >> 1)))
    return (lax.ppermute(jnp.concatenate([held, picked], axis=0), ("ep", "tp"), moves), meanwhile)


def call(body, outs, scratch, **kwargs):
    return pl.pallas_call(
        body,
        out_shape=outs,
        **({} if scratch is None else {"scratch_shapes": scratch}),
        compiler_params=pltpu.CompilerParams(vmem_limit_bytes=20 * 1024 * 1024),
        cost_estimate=pl.CostEstimate(flops=1 << 20, bytes_accessed=1 << 18, transcendentals=0),
        **kwargs,
    )


VMEM = pl.BlockSpec(memory_space=pltpu.VMEM)
SMEM = pl.BlockSpec(memory_space=pltpu.SMEM)
NT = (((1,), (1,)), ((), ()))


def dot(a, b):
    return jnp.dot(a, b, preferred_element_type=jnp.float32)


def document_slots(here, query_docs, pool_dev):
    device, lane = (here[0], here[1])
    query = query_of(device, lane)
    slots = []
    for d in range(4):
        slot = jnp.int32(0)
        for j in range(query_docs.shape[1]):
            offset = query_docs[query, j] - (device ^ d) * pool_dev
            slot = jnp.where(jnp.logical_and(offset >= 0, offset < pool_dev), j, slot)
        slots.append(slot)
    return (query, slots)


def prepare_body(here, query_docs, pool, ids, *outs):
    pool_dev = pool.shape[0]
    docs_per = query_docs.shape[1]
    rows = pool.shape[2] * pool.shape[3]
    device, lane = (here[0], here[1])
    for d, out in enumerate(outs):
        target = device ^ d
        query = query_of(target, lane)
        local = jnp.int32(0)
        for j in range(docs_per):
            offset = query_docs[query, j] - device * pool_dev
            inside = jnp.logical_and(offset >= 0, offset < pool_dev)
            local = jnp.where(inside, offset, local)
        out[:rows, :] = pool[local, target].reshape(rows, pool.shape[4])
        out[rows:, :] = ids[...]


def prepare(here, query_docs, pool, ids):
    _, _, pair, doc_max, head_dim = pool.shape
    shape = jax.ShapeDtypeStruct((pair * doc_max + ids.shape[0], head_dim), jnp.bfloat16)
    return call(
        prepare_body,
        [shape] * 4,
        [],
        in_specs=[SMEM, SMEM, VMEM, VMEM],
        out_specs=[VMEM] * 4,
        name="prepare",
    )(here, query_docs, pool, ids)


def angles_body(pool_dev, here, query_docs, ctx_pos, cos_q, sin_q, cos_d, sin_d):
    query, slots = document_slots(here, query_docs, pool_dev)
    docs_per = query_docs.shape[1]
    head_dim = cos_q.shape[1]

    def fill(starts, cosine, sine):
        column = lax.broadcasted_iota(jnp.int32, cosine.shape, 1)
        half = jnp.where(column < head_dim // 2, column, column - head_dim // 2)
        freq = jnp.exp(half.astype(jnp.float32) * (-2.0 * math.log(rope_theta) / head_dim))
        angle = starts.astype(jnp.float32) * freq
        cosine[...] = jnp.cos(angle)
        wave = jnp.sin(angle)
        sine[...] = jnp.where(column < head_dim // 2, -wave, wave)

    row = lax.broadcasted_iota(jnp.int32, cos_q.shape, 0)
    fill(ctx_pos[query, docs_per] + row, cos_q, sin_q)
    row = lax.broadcasted_iota(jnp.int32, cos_d.shape, 0)
    starts = jnp.zeros(cos_d.shape, jnp.int32)
    for d, slot in enumerate(slots):
        starts = jnp.where(row == d, ctx_pos[query, slot], starts)
    fill(starts, cos_d, sin_d)


def angles(here, query_docs, ctx_pos, pool_dev, length, head_dim):
    shapes = [jax.ShapeDtypeStruct((rows, head_dim), jnp.float32) for rows in (length, length, 8, 8)]
    return call(
        functools.partial(angles_body, pool_dev),
        shapes,
        [],
        in_specs=[SMEM] * 3,
        out_specs=[VMEM] * 4,
        name="angles",
    )(here, query_docs, ctx_pos)


def attention_body(
    pool_dev, here, query_docs, doc_lens, q, c0, c1, c2, c3, cos_q, sin_q, cos_d, sin_d, out, wide, keys, vals
):
    length, head_dim = cos_q.shape
    heads = out.shape[1] // head_dim
    pieces = (c0, c1, c2, c3)
    docs = len(pieces)
    doc_max = (keys.shape[0] - length) // docs
    half = head_dim // 2
    query, slots = document_slots(here, query_docs, pool_dev)

    def turned(x, cosine, sine):
        return x * cosine + pltpu.roll(x, half, 1) * sine

    cosine, sine = (cos_q[...], sin_q[...])
    for j, piece in enumerate(pieces):
        key = turned(piece[:doc_max, :].astype(jnp.float32), cos_d[j : j + 1, :], sin_d[j : j + 1, :])
        keys[j * doc_max : (j + 1) * doc_max, :] = key.astype(jnp.bfloat16)
        vals[j * doc_max : (j + 1) * doc_max, :] = piece[doc_max : 2 * doc_max, :]
    base = docs * doc_max
    first = heads * length
    keys[base:, :] = turned(q[first : first + length, :].astype(jnp.float32), cosine, sine).astype(
        jnp.bfloat16
    )
    vals[base:, :] = q[first + length :, :]
    wide[...] = q[:first, :].astype(jnp.float32)
    column = lax.broadcasted_iota(jnp.int32, (1, doc_max), 1)
    allowed = [column < doc_lens[query_docs[query, slot]] for slot in slots]
    causal = lax.broadcasted_iota(jnp.int32, (length, length), 0) >= lax.broadcasted_iota(
        jnp.int32, (length, length), 1
    )
    for h in range(heads):
        rows = turned(wide[pl.ds(h, length, stride=heads), :], cosine, sine).astype(jnp.bfloat16)
        scores = lax.dot_general(rows, keys[...], NT, preferred_element_type=jnp.float32)
        scores = scores * head_dim ** (-0.5)
        parts = [
            jnp.where(allowed[j], scores[:, j * doc_max : (j + 1) * doc_max], -jnp.inf)
            for j in range(docs)
        ] + [jnp.where(causal, scores[:, base:], -jnp.inf)]
        scores = jnp.concatenate(parts, axis=1)
        ceiling = jnp.max(scores, axis=1, keepdims=True)
        probs = jnp.exp(scores - ceiling)
        denominator = jnp.sum(probs, axis=1, keepdims=True)
        mixed = dot(probs.astype(jnp.bfloat16), vals[...])
        out[:, h * head_dim : (h + 1) * head_dim] = (mixed / denominator).astype(jnp.bfloat16)


def attention(here, query_docs, doc_lens, q, pieces, tables, pool_dev):
    length, head_dim = tables[0].shape
    heads = q.shape[0] // length - 2
    rows = 5 * length
    return call(
        functools.partial(attention_body, pool_dev),
        jax.ShapeDtypeStruct((length, heads * head_dim), jnp.bfloat16),
        [
            pltpu.VMEM((heads * length, head_dim), jnp.float32),
            pltpu.VMEM((rows, head_dim), jnp.bfloat16),
            pltpu.VMEM((rows, head_dim), jnp.bfloat16),
        ],
        in_specs=[SMEM] * 3 + [VMEM] * 9,
        out_specs=VMEM,
        name="attention",
    )(here, query_docs, doc_lens, q, *pieces, *tables)


def project_body(here, a, b, c, d, weight, *rest):
    outs, rows = (rest[:-1], rest[-1])
    device, lane = (here[0], here[1])
    for flip, ref in zip((0, 2, 1, 3), (a, b, c, d)):
        rows[query_of(device, lane ^ flip)] = ref[...]
    for d in (2, 3, 1, 0):
        outs[d][...] = dot(rows[device ^ d], weight[...]).astype(jnp.bfloat16)


def project(here, parts, weight):
    length, depth = parts[0].shape
    return call(
        project_body,
        [jax.ShapeDtypeStruct((length, weight.shape[1]), jnp.bfloat16)] * 4,
        [pltpu.VMEM((4, length, depth), jnp.bfloat16)],
        in_specs=[SMEM] + [VMEM] * 5,
        out_specs=[VMEM] * 4,
        name="project",
    )(here, *parts, weight)


def routing_body(experts, here, c0, c1, c2, c3, pick, spread):
    _, local, capacity, length = pick.shape
    first = here[0] * local
    before = (
        lax.broadcasted_iota(jnp.int32, (length, length), 0)
        < lax.broadcasted_iota(jnp.int32, (length, length), 1)
    ).astype(jnp.bfloat16)
    place = lax.broadcasted_iota(jnp.int32, (capacity, length), 0).astype(jnp.float32)
    row = lax.broadcasted_iota(jnp.int32, (8, length), 0)
    for d, piece in enumerate((c0, c1, c2, c3)):
        ids = piece[piece.shape[0] - 16 :, :].astype(jnp.float32).astype(jnp.int32)
        chosen = jnp.zeros((8, length), jnp.float32)
        for k in range(8):
            named = jnp.logical_and(ids[k : k + 1, :] == first + row, row < local)
            chosen = jnp.where(named, 1.0, chosen)
        rank = dot(chosen.astype(jnp.bfloat16), before)
        wide = []
        for e in range(local):
            here_e = jnp.logical_and(rank[e : e + 1, :] == place, chosen[e : e + 1, :] > 0.0)
            wide.append(jnp.where(here_e, 1.0, 0.0))
            pick[d, e] = wide[-1].astype(jnp.bfloat16)
        spread[d] = jnp.transpose(jnp.concatenate(wide, axis=0)).astype(jnp.bfloat16)


def routing(here, pieces, experts, local, capacity):
    length = pieces[0].shape[1]
    rows = pieces[0].shape[0]
    return call(
        functools.partial(routing_body, experts),
        [
            jax.ShapeDtypeStruct((4, local, capacity, length), jnp.bfloat16),
            jax.ShapeDtypeStruct((4, length, local * capacity), jnp.bfloat16),
        ],
        [],
        in_specs=[SMEM] + [VMEM] * 4,
        out_specs=[VMEM] * 2,
        name="routing",
    )(here, *pieces)


def residual_body(hidden, p0, p1, p2, p3, gain, router, after, out, stats):
    rows = stats.shape[0]
    total = hidden[...].astype(jnp.float32) + p0[...].astype(jnp.float32)
    for part in (p1, p2, p3):
        total = total + part[...].astype(jnp.float32)
    narrow = total.astype(jnp.bfloat16)
    out[...] = narrow
    wide = narrow.astype(jnp.float32)
    grown = wide * gain[...]
    high = grown.astype(jnp.bfloat16)
    rest = grown - high.astype(jnp.float32)
    middle = rest.astype(jnp.bfloat16)
    low = (rest - middle.astype(jnp.float32)).astype(jnp.bfloat16)
    logits = dot(high, router[...]) + (dot(middle, router[...]) + dot(low, router[...]))
    squares = jnp.sum(wide * wide, axis=1, keepdims=True)
    column = lax.broadcasted_iota(jnp.int32, logits.shape, 1)
    stats[...] = jnp.transpose(jnp.where(column == rows - 8, squares, logits))[:rows, :]


def residual_and_stats(hidden, parts, gain, router, experts, after):
    length, width = hidden.shape
    return call(
        residual_body,
        [
            jax.ShapeDtypeStruct((length, width), jnp.bfloat16),
            jax.ShapeDtypeStruct((experts + 8, length), jnp.float32),
        ],
        [],
        in_specs=[VMEM] * 7 + [pl.BlockSpec(memory_space=pl.ANY)],
        out_specs=[VMEM] * 2,
        name="residual",
    )(hidden, *parts, gain, router, after)


def gate_up_body(ds, order, *refs):
    tokens = refs[: len(ds)]
    gain, pick, weight, kept, given, rows = refs[len(ds) :]
    hid = weight.shape[3]
    capacity = pick.shape[2]
    i = pl.program_id(0)
    expert = order[i]
    for k, d in enumerate(ds):
        chosen = dot(pick[d, expert], tokens[k][...]) * gain[...]
        rows[k * capacity : (k + 1) * capacity, :] = chosen.astype(jnp.bfloat16)
    for g in range(2):
        term = dot(rows[...], weight[0, g]).astype(jnp.bfloat16)
        for j in range(4):
            out = (kept, given)[j // 2]

            @pl.when(i == j)
            def _():
                out[j % 2, :, g * hid : (g + 1) * hid] = term


def gate_up(ds, order, tokens, gain, pick, weight):
    local, _, width, hid = weight.shape
    capacity = pick.shape[2]
    shape = jax.ShapeDtypeStruct((2, len(ds) * capacity, 2 * hid), jnp.bfloat16)
    whole = lambda rank: lambda i, order: (0,) * rank
    return call(
        functools.partial(gate_up_body, ds),
        [shape] * 2,
        None,
        grid_spec=pltpu.PrefetchScalarGridSpec(
            num_scalar_prefetch=1,
            grid=(local,),
            in_specs=[pl.BlockSpec(tokens[0].shape, whole(2))] * len(ds)
            + [
                pl.BlockSpec(gain.shape, whole(2)),
                pl.BlockSpec(pick.shape, whole(4)),
                pl.BlockSpec((1, 2, width, hid), lambda i, order: (order[i], 0, 0, 0)),
            ],
            out_specs=[pl.BlockSpec(shape.shape, whole(3))] * 2,
            scratch_shapes=[pltpu.VMEM((len(ds) * capacity, width), jnp.bfloat16)],
        ),
        name="gate_up",
    )(order, *tokens, gain, pick, weight)


def activate_body(ds, features, here, kept, taken, across, pick, *refs):
    stats = refs[: len(ds)]
    pieces = refs[len(ds) : 2 * len(ds)]
    out = refs[2 * len(ds)]
    _, local, capacity, length = pick.shape
    hid = out.shape[1]
    experts = stats[0].shape[0] - 8
    device, lane = (here[0], here[1])
    expert = lax.broadcasted_iota(jnp.int32, (experts, length), 0)
    for k, d in enumerate(ds):
        ids = pieces[k][pieces[k].shape[0] - 16 :, :].astype(jnp.float32).astype(jnp.int32)
        chosen = jnp.zeros((experts, length), jnp.float32)
        for c in range(8):
            chosen = jnp.where(ids[c : c + 1, :] == expert, 1.0, chosen)
        inv_rms = lax.rsqrt(stats[k][experts : experts + 1, :] / features + norm_eps)
        logits = jnp.where(chosen > 0.0, stats[k][:experts, :] * inv_rms, -jnp.inf)
        grown = jnp.exp(logits - jnp.max(logits, axis=0, keepdims=True))
        mix = grown / jnp.sum(grown, axis=0, keepdims=True)
        mix = jnp.sum(jnp.where(expert == device * local + lane, mix, 0.0), axis=0, keepdims=True)
        places = pick[d, lane].astype(jnp.float32)
        inv_row = jnp.sum(places * inv_rms, axis=1, keepdims=True)
        mix_row = jnp.sum(places * mix, axis=1, keepdims=True)
        rows = slice(k * capacity, (k + 1) * capacity)
        summed = kept[0, rows, :].astype(jnp.float32) + taken[0, rows, :].astype(jnp.float32)
        summed = (summed + across[rows, :].astype(jnp.float32)) * inv_row
        gate = summed[:, :hid]
        act = gate / (1.0 + jnp.exp(-gate)) * summed[:, hid:] * mix_row
        out[rows, :] = act.astype(jnp.bfloat16)


def activate(ds, features, here, kept, taken, across, pick, stats, pieces):
    rows, both = across.shape
    return call(
        functools.partial(activate_body, ds, features),
        jax.ShapeDtypeStruct((rows, both // 2), jnp.bfloat16),
        [],
        in_specs=[SMEM] + [VMEM] * (4 + 2 * len(ds)),
        out_specs=VMEM,
        name="activate",
    )(here, kept, taken, across, pick, *[stats[d] for d in ds], *[pieces[d] for d in ds])


def down_body(ds, order, a, b, c, d, spread, weight, *rest):
    outs, results = (rest[:-1], rest[-1])
    i = pl.program_id(0)
    capacity = results.shape[2]
    expert = order[i]
    for j, ref in enumerate((a, b, c, d)):

        @pl.when(i == j)
        def _():
            result = dot(ref[...], weight[0]).astype(jnp.bfloat16)
            for k in range(len(ds)):
                results[k, expert] = result[k * capacity : (k + 1) * capacity, :]

    @pl.when(i == pl.num_programs(0) - 1)
    def _():
        for k, out in enumerate(outs):
            rows = results[k].reshape(-1, results.shape[3])
            out[...] = dot(spread[ds[k]], rows).astype(jnp.bfloat16)


def down(ds, order, acts, spread, weight):
    local, hid, width = weight.shape
    capacity = acts[0].shape[0] // len(ds)
    length = spread.shape[1]
    shape = jax.ShapeDtypeStruct((length, width), jnp.bfloat16)
    whole = lambda rank: lambda i, order: (0,) * rank
    return call(
        functools.partial(down_body, ds),
        [shape] * len(ds),
        None,
        grid_spec=pltpu.PrefetchScalarGridSpec(
            num_scalar_prefetch=1,
            grid=(local,),
            in_specs=[pl.BlockSpec(acts[0].shape, whole(2))] * 4
            + [
                pl.BlockSpec(spread.shape, whole(3)),
                pl.BlockSpec((1, hid, width), lambda i, order: (order[i], 0, 0)),
            ],
            out_specs=[pl.BlockSpec(shape.shape, whole(2))] * len(ds),
            scratch_shapes=[pltpu.VMEM((len(ds), local, capacity, width), jnp.bfloat16)],
        ),
        name="down",
    )(order, *acts, spread, weight)


def per_device_square(
    question_q,
    question_kv,
    doc_kv,
    doc_lens,
    query_docs,
    ctx_pos,
    hidden,
    out_proj,
    norm_gain,
    router_weight,
    w_gate_up,
    w_down,
    expert_ids,
):
    n = 4
    lane = lax.axis_index("tp")
    device = lax.axis_index("ep")
    length, heads_here, head_dim = question_q.shape
    pool_dev = doc_kv.shape[0]
    width_here = hidden.shape[1]
    experts = router_weight.shape[1]
    local = w_gate_up.shape[0]
    capacity = length * expert_ids.shape[1] // experts
    here = jnp.stack([device, lane]).astype(jnp.int32)
    order = (lane ^ jnp.array([0, 2, 1, 3], jnp.int32)).astype(jnp.int32)

    pool = jnp.transpose(doc_kv, (0, 2, 3, 1, 4))
    ids_rows = jnp.pad(expert_ids.T.astype(jnp.bfloat16), ((0, 8), (0, 0)))
    pieces = prepare(here, query_docs, pool, ids_rows)
    q_rows, pieces = turn(
        question_q.reshape(length * heads_here, head_dim), question_kv, device, lane, n, pieces
    )
    pieces = [pieces[0]] + [lax.ppermute(pieces[d], "ep", pairs(n, d)) for d in range(1, n)]
    tables = list(angles(here, query_docs, ctx_pos, pool_dev, length, head_dim))

    one = lax.optimization_barrier(jnp.ones((), jnp.bfloat16))
    tables[0], out_proj = lax.optimization_barrier((tables[0], out_proj * one))
    attended = attention(here, query_docs, doc_lens, q_rows, pieces, tables, pool_dev)
    far = lax.ppermute(attended, "tp", pairs(n, 2))
    near = lax.ppermute(attended, "tp", pairs(n, 1))
    farther = lax.ppermute(far, "tp", pairs(n, 1))
    gain = norm_gain.astype(jnp.float32)[None, :]
    router = jnp.pad(router_weight, ((0, 0), (0, 128 - experts)))
    parts = project(here, (attended, far, near, farther), out_proj)
    kept, w_gate_up = lax.optimization_barrier((parts[0], w_gate_up))
    sent = [lax.ppermute(parts[d], "ep", pairs(n, d)) for d in (2, 3, 1)]
    pick, spread = routing(here, pieces, experts, local, capacity)
    weight = jnp.transpose(w_gate_up, (0, 2, 1, 3))
    residual, own_stats = residual_and_stats(
        hidden, [kept] + sent, gain, router, experts, weight
    )

    residual, w_down = lax.optimization_barrier((residual, w_down))
    w_down = w_down * one
    tokens = {0: residual}
    for d in (2, 3, 1):
        tokens[d] = lax.ppermute(residual, "ep", pairs(n, d))
    own_stats = own_stats + lax.ppermute(own_stats, "tp", pairs(n, 2))
    own_stats = own_stats + lax.ppermute(own_stats, "tp", pairs(n, 1))
    own_stats, w_down, tokens[1], tokens[2], tokens[3] = lax.optimization_barrier(
        (own_stats, w_down, tokens[1], tokens[2], tokens[3])
    )
    stats = {0: own_stats}
    for d in (2, 3, 1):
        stats[d] = lax.ppermute(own_stats, "ep", pairs(n, d))

    features = width_here * n

    def exchange(ds, order, before):
        kept, given = gate_up(ds, order, [tokens[d] for d in ds], gain, pick, weight)
        given, *before = lax.optimization_barrier((given, *before))
        taken = lax.ppermute(given, "tp", pairs(n, 1))
        chip_far = (kept[1].astype(jnp.float32) + taken[1].astype(jnp.float32)).astype(jnp.bfloat16)
        return (chip_far, before, kept, taken, lax.ppermute(chip_far, "tp", pairs(n, 2)))

    def spread_act(act):
        far = lax.ppermute(act, "tp", pairs(n, 2))
        near = lax.ppermute(act, "tp", pairs(n, 1))
        return [act, far, near, lax.ppermute(far, "tp", pairs(n, 1))]

    chip_far, _, *first = exchange((2, 3), order, [])
    order, *_ = lax.optimization_barrier((order, chip_far, stats[1], stats[2], stats[3]))
    _, first[2:], *second = exchange((0, 1), order, first[2:])
    act = activate((2, 3), features, here, *first, pick, stats, pieces)
    acts = spread_act(act)
    act = activate((0, 1), features, here, *second, pick, stats, pieces)
    acts[3], act = lax.optimization_barrier((acts[3], act))
    others = spread_act(act)
    parts = down((2, 3), order, acts, spread, w_down)
    returned = [lax.ppermute(part, "ep", pairs(n, d)) for part, d in zip(parts, (2, 3))]
    mine, near = down((0, 1), order, others, spread, w_down)
    returned += [mine, lax.ppermute(near, "ep", pairs(n, 1))]
    total = residual.astype(jnp.float32)
    for part in returned:
        total = total + part.astype(jnp.float32)
    return total.astype(jnp.bfloat16)


def solution(mesh):
    placed = (
        P(("grp", "ep"), "tp", None),
        P(("grp", "ep"), None, None, None),
        P(("grp", "ep"), None, None, None, None),
        P("grp"),
        P("grp", None),
        P("grp", None),
        P(("grp", "ep"), "tp"),
        P("ep", "tp"),
        P("tp"),
        P("tp", None),
        P("ep", "tp", None, None),
        P("ep", None, "tp"),
        P(("grp", "ep"), None),
    )
    def per_device(*args):
        square = (
            lax.axis_size("tp") == 4
            and lax.axis_size("ep") == 4
            and args[1].shape[1] == 4
            and args[4].shape == (4, 4)
        )
        return (per_device_square if square else per_device_general)(*args)

    return jax.shard_map(
        per_device, mesh=mesh, in_specs=placed, out_specs=P(("grp", "ep"), "tp"), check_vma=False
    )
```

```python
import functools
import math

import jax
import jax.numpy as jnp
from jax import lax
from jax.experimental import pallas as pl
from jax.experimental.pallas import tpu as pltpu
from jax.sharding import PartitionSpec as P

rope_theta = 1000000.0
norm_eps = 1e-06


def tables(positions, head_dim):
    half = head_dim // 2
    freq = jnp.exp(jnp.arange(half, dtype=jnp.float32) * (-2.0 * math.log(rope_theta) / head_dim))
    angle = positions.astype(jnp.float32)[:, None] * freq[None, :]
    return (jnp.cos(angle), jnp.sin(angle))


def rotate(values, positions):
    half = values.shape[-1] // 2
    cosine, sine = tables(positions, values.shape[-1])
    shape = (values.shape[0],) + (1,) * (values.ndim - 2) + (half,)
    cosine, sine = (cosine.reshape(shape), sine.reshape(shape))
    floats = values.astype(jnp.float32)
    first = floats[..., :half]
    second = floats[..., half:]
    return jnp.concatenate(
        [first * cosine - second * sine, second * cosine + first * sine], axis=-1
    )


def attend(q_rows, own_kv, context, starts, lengths, question_start):
    length, heads_here, head_dim = q_rows.shape
    docs_per, doc_max, _ = context.shape
    question_pos = question_start + jnp.arange(length, dtype=jnp.int32)
    queries = rotate(q_rows, question_pos).astype(jnp.bfloat16)
    own_keys = rotate(own_kv[:, :head_dim], question_pos).astype(jnp.bfloat16)
    positions = jnp.repeat(starts, doc_max, total_repeat_length=docs_per * doc_max)
    doc_keys = rotate(context[:, :, :head_dim].reshape(docs_per * doc_max, head_dim), positions)
    keys = jnp.concatenate([doc_keys.astype(jnp.bfloat16), own_keys], axis=0)
    values = jnp.concatenate(
        [context[:, :, head_dim:].reshape(docs_per * doc_max, head_dim), own_kv[:, head_dim:]],
        axis=0,
    )
    valid = (jnp.arange(doc_max, dtype=jnp.int32)[None, :] < lengths[:, None]).reshape(-1)
    causal = jnp.arange(length)[:, None] >= jnp.arange(length)[None, :]
    allowed = jnp.concatenate(
        [jnp.broadcast_to(valid[None, :], (length, valid.shape[0])), causal], axis=1
    )
    scores = jnp.einsum("ihd,jd->hij", queries, keys, preferred_element_type=jnp.float32)
    scores = jnp.where(allowed[None], scores * head_dim ** (-0.5), -jnp.inf)
    ceiling = jnp.max(scores, axis=-1, keepdims=True)
    probs = jnp.exp(scores - ceiling)
    denominator = jnp.sum(probs, axis=-1, keepdims=True)
    mixed = jnp.einsum(
        "hij,jd->hid", probs.astype(jnp.bfloat16), values, preferred_element_type=jnp.float32
    )
    return (
        jnp.transpose(mixed / denominator, (1, 0, 2))
        .reshape(length, heads_here * head_dim)
        .astype(jnp.bfloat16)
    )


def context_by_row(doc_kv, doc_lens, query_docs, ctx_pos, device, kv_pick):
    pool_dev, doc_max, _, pair, head_dim = doc_kv.shape
    docs_per = query_docs.shape[1]
    pool_head = lax.dynamic_index_in_dim(doc_kv, kv_pick, 2, keepdims=False).reshape(
        pool_dev, doc_max, pair * head_dim
    )
    held = device * pool_dev + jnp.arange(pool_dev, dtype=jnp.int32)
    wanted = jnp.sum((query_docs[:, :, None] == held[None, None, :]).astype(jnp.float32), axis=1)
    sending = jnp.einsum(
        "rl,lkc->rkc", wanted.astype(jnp.bfloat16), pool_head, preferred_element_type=jnp.float32
    ).astype(jnp.bfloat16)
    received = lax.all_to_all(sending, "ep", split_axis=0, concat_axis=0, tiled=True)
    my_docs = lax.dynamic_index_in_dim(query_docs, device, 0, keepdims=False)
    starts = lax.dynamic_index_in_dim(ctx_pos, device, 0, keepdims=False)
    return (jnp.take(received, my_docs // pool_dev, axis=0), starts[:docs_per], jnp.take(doc_lens, my_docs))


def per_device_general(
    question_q,
    question_kv,
    doc_kv,
    doc_lens,
    query_docs,
    ctx_pos,
    hidden,
    out_proj,
    norm_gain,
    router_weight,
    w_gate_up,
    w_down,
    expert_ids,
):
    lanes = lax.axis_size("tp")
    groups = lax.axis_size("ep")
    lane = lax.axis_index("tp")
    device = lax.axis_index("ep")
    length, heads_here, head_dim = question_q.shape
    kv_heads = question_kv.shape[1]
    docs_per = query_docs.shape[1]
    width_here = hidden.shape[1]
    ids = lax.all_gather(expert_ids, "ep", axis=0, tiled=False)
    kv_pick = lane * kv_heads // lanes
    kv_head = lax.dynamic_index_in_dim(question_kv, kv_pick, 1, keepdims=False).reshape(
        length, 2 * head_dim
    )
    context, starts, lengths = context_by_row(
        doc_kv, doc_lens, query_docs, ctx_pos, device, kv_pick
    )
    question_start = lax.dynamic_index_in_dim(ctx_pos, device, 0, keepdims=False)[docs_per]
    attended = attend(question_q, kv_head, context, starts, lengths, question_start)
    projected = jnp.dot(
        lax.all_gather(attended, "tp", axis=1, tiled=True),
        lax.all_gather(out_proj, "ep", axis=0, tiled=True),
        preferred_element_type=jnp.float32,
    )
    residual = (hidden.astype(jnp.float32) + projected.astype(jnp.float32)).astype(jnp.bfloat16)

    tokens = lax.all_gather(residual, "ep", axis=0, tiled=False)
    wide = tokens.astype(jnp.float32)
    gain = norm_gain.astype(jnp.float32)
    scaled = wide * gain
    logit_part = jnp.einsum(
        "snd,de->sne", scaled, router_weight.astype(jnp.float32), precision=lax.Precision.HIGHEST
    )
    square_part = jnp.sum(wide * wide, axis=2, keepdims=True)
    stats = jnp.sum(
        lax.all_gather(jnp.concatenate([logit_part, square_part], axis=2), "tp", axis=0), axis=0
    )
    experts = router_weight.shape[1]
    inv_rms = lax.rsqrt(stats[:, :, experts] / (width_here * lanes) + norm_eps)
    logits = stats[:, :, :experts] * inv_rms[:, :, None]

    local_experts = w_gate_up.shape[0]
    capacity = length * expert_ids.shape[1] // experts
    hid = w_gate_up.shape[3]
    chosen_all = jnp.any(
        ids[:, :, :, None] == jnp.arange(experts, dtype=jnp.int32), axis=2
    )
    top = jnp.max(jnp.where(chosen_all, logits, -jnp.inf), axis=2, keepdims=True)
    weight = jnp.where(chosen_all, jnp.exp(logits - top), 0.0)
    mix = weight / jnp.sum(weight, axis=2, keepdims=True)

    shuffled, scaled_rows = (chosen_all, scaled.astype(jnp.bfloat16))
    first = device * local_experts
    chosen = lax.dynamic_slice_in_dim(shuffled, first, local_experts, 2)
    mix_here = lax.dynamic_slice_in_dim(mix, first, local_experts, 2)
    before = (jnp.arange(length)[:, None] > jnp.arange(length)[None, :]).astype(jnp.bfloat16)
    rank = jnp.einsum(
        "mn,sne->sem", before, chosen.astype(jnp.bfloat16), preferred_element_type=jnp.float32
    ).astype(jnp.int32)
    pick = jnp.logical_and(
        jnp.transpose(chosen, (0, 2, 1))[:, :, None, :],
        rank[:, :, None, :] == jnp.arange(capacity, dtype=jnp.int32)[None, None, :, None],
    )
    onehot = pick.astype(jnp.bfloat16)
    inv_row = jnp.sum(jnp.where(pick, inv_rms[:, None, None, :], 0.0), axis=3)
    mix_row = jnp.sum(jnp.where(pick, jnp.transpose(mix_here, (0, 2, 1))[:, :, None, :], 0.0), axis=3)

    rows = jnp.einsum(
        "sern,snd->serd", onehot, scaled_rows, preferred_element_type=jnp.float32
    ).astype(jnp.bfloat16)
    term = jnp.einsum(
        "serd,edgh->sergh", rows, w_gate_up, preferred_element_type=jnp.float32
    ).astype(jnp.bfloat16)
    per_lane = groups * local_experts * capacity // lanes
    term = term.reshape(lanes, per_lane, 2 * hid)
    inv_row = inv_row.reshape(lanes, per_lane, 1)
    summed = lax.psum_scatter(term, "tp", scatter_dimension=0, tiled=True)[0].astype(jnp.float32)
    inv_mine = lax.dynamic_index_in_dim(inv_row, lane, 0, keepdims=False)
    summed = summed * inv_mine
    act = (jax.nn.silu(summed[:, :hid]) * summed[:, hid:]).astype(jnp.bfloat16)
    acts = lax.all_gather(act, "tp", axis=0, tiled=False)
    acts = acts.reshape(groups, local_experts, capacity, hid)
    expert_out = jnp.einsum("serh,ehd->serd", acts, w_down, preferred_element_type=jnp.float32)
    expert_out = (expert_out * mix_row[:, :, :, None]).astype(jnp.bfloat16)
    combined = jnp.einsum(
        "sern,serd->snd", onehot, expert_out, preferred_element_type=jnp.float32
    ).astype(jnp.bfloat16)
    returned = lax.psum_scatter(combined, "ep", scatter_dimension=0, tiled=True)[0]
    return (residual.astype(jnp.float32) + returned.astype(jnp.float32)).astype(jnp.bfloat16)


def pairs(lanes, flip):
    return [(i, i ^ flip) for i in range(lanes)]


def scatter_blocks(parts, n):
    near = lax.ppermute(parts[3], "ep", pairs(n, 1))
    far = (parts[2].astype(jnp.float32) + near.astype(jnp.float32)).astype(jnp.bfloat16)
    return [parts[0], lax.ppermute(far, "ep", pairs(n, 2)), lax.ppermute(parts[1], "ep", pairs(n, 1))]


def query_of(device, lane):
    return 2 * (lane & 1) + ((lane >> 1) ^ (device & 1))


def turn(question, keys_values, device, lane, n, meanwhile):
    crosses = lambda e, t: ((e ^ t) & 1) != (t >> 1)
    devices = [(e, t) for e in range(n) for t in range(n)]
    swap = [(e * n + t, e * n + (t ^ 3)) for e, t in devices if crosses(e, t)]
    crossed = lax.ppermute(question, ("ep", "tp"), swap)
    crossed, *meanwhile = lax.optimization_barrier((crossed, *meanwhile))
    heads = jnp.where(crosses(device, lane), lane ^ 3, lane)
    picked = lax.dynamic_index_in_dim(keys_values, heads, 1, keepdims=False)
    picked = jnp.transpose(picked, (1, 0, 2)).reshape(-1, question.shape[1])
    held = jnp.where(crosses(device, lane), crossed, question)
    moves = []
    for e, t in devices:
        h = t ^ 3 if crosses(e, t) else t
        moves.append((e * n + t, h * n + 2 * ((e ^ h) & 1) + (e >> 1)))
    return (lax.ppermute(jnp.concatenate([held, picked], axis=0), ("ep", "tp"), moves), meanwhile)


def call(body, outs, scratch, **kwargs):
    return pl.pallas_call(
        body,
        out_shape=outs,
        **({} if scratch is None else {"scratch_shapes": scratch}),
        compiler_params=pltpu.CompilerParams(vmem_limit_bytes=20 * 1024 * 1024),
        cost_estimate=pl.CostEstimate(flops=1 << 20, bytes_accessed=1 << 18, transcendentals=0),
        **kwargs,
    )


VMEM = pl.BlockSpec(memory_space=pltpu.VMEM)
SMEM = pl.BlockSpec(memory_space=pltpu.SMEM)
NT = (((1,), (1,)), ((), ()))


def dot(a, b):
    return jnp.dot(a, b, preferred_element_type=jnp.float32)


def document_slots(here, query_docs, pool_dev):
    device, lane = (here[0], here[1])
    query = query_of(device, lane)
    slots = []
    for d in range(4):
        slot = jnp.int32(0)
        for j in range(query_docs.shape[1]):
            offset = query_docs[query, j] - (device ^ d) * pool_dev
            slot = jnp.where(jnp.logical_and(offset >= 0, offset < pool_dev), j, slot)
        slots.append(slot)
    return (query, slots)


def prepare_body(here, query_docs, pool, ids, *outs):
    pool_dev = pool.shape[0]
    docs_per = query_docs.shape[1]
    rows = pool.shape[2] * pool.shape[3]
    device, lane = (here[0], here[1])
    for d, out in enumerate(outs):
        target = device ^ d
        query = query_of(target, lane)
        local = jnp.int32(0)
        for j in range(docs_per):
            offset = query_docs[query, j] - device * pool_dev
            inside = jnp.logical_and(offset >= 0, offset < pool_dev)
            local = jnp.where(inside, offset, local)
        out[:rows, :] = pool[local, target].reshape(rows, pool.shape[4])
        out[rows:, :] = ids[...]


def prepare(here, query_docs, pool, ids):
    _, _, pair, doc_max, head_dim = pool.shape
    shape = jax.ShapeDtypeStruct((pair * doc_max + ids.shape[0], head_dim), jnp.bfloat16)
    return call(
        prepare_body,
        [shape] * 4,
        [],
        in_specs=[SMEM, SMEM, VMEM, VMEM],
        out_specs=[VMEM] * 4,
        name="prepare",
    )(here, query_docs, pool, ids)


def angles_body(pool_dev, here, query_docs, ctx_pos, cos_q, sin_q, cos_d, sin_d):
    query, slots = document_slots(here, query_docs, pool_dev)
    docs_per = query_docs.shape[1]
    head_dim = cos_q.shape[1]

    def fill(starts, cosine, sine):
        column = lax.broadcasted_iota(jnp.int32, cosine.shape, 1)
        half = jnp.where(column < head_dim // 2, column, column - head_dim // 2)
        freq = jnp.exp(half.astype(jnp.float32) * (-2.0 * math.log(rope_theta) / head_dim))
        angle = starts.astype(jnp.float32) * freq
        cosine[...] = jnp.cos(angle)
        wave = jnp.sin(angle)
        sine[...] = jnp.where(column < head_dim // 2, -wave, wave)

    row = lax.broadcasted_iota(jnp.int32, cos_q.shape, 0)
    fill(ctx_pos[query, docs_per] + row, cos_q, sin_q)
    row = lax.broadcasted_iota(jnp.int32, cos_d.shape, 0)
    starts = jnp.zeros(cos_d.shape, jnp.int32)
    for d, slot in enumerate(slots):
        starts = jnp.where(row == d, ctx_pos[query, slot], starts)
    fill(starts, cos_d, sin_d)


def angles(here, query_docs, ctx_pos, pool_dev, length, head_dim):
    shapes = [jax.ShapeDtypeStruct((rows, head_dim), jnp.float32) for rows in (length, length, 8, 8)]
    return call(
        functools.partial(angles_body, pool_dev),
        shapes,
        [],
        in_specs=[SMEM] * 3,
        out_specs=[VMEM] * 4,
        name="angles",
    )(here, query_docs, ctx_pos)


def attention_body(
    pool_dev, here, query_docs, doc_lens, q, c0, c1, c2, c3, cos_q, sin_q, cos_d, sin_d, out, wide, keys, vals
):
    length, head_dim = cos_q.shape
    heads = out.shape[1] // head_dim
    pieces = (c0, c1, c2, c3)
    docs = len(pieces)
    doc_max = (keys.shape[0] - length) // docs
    half = head_dim // 2
    query, slots = document_slots(here, query_docs, pool_dev)

    def turned(x, cosine, sine):
        return x * cosine + pltpu.roll(x, half, 1) * sine

    cosine, sine = (cos_q[...], sin_q[...])
    for j, piece in enumerate(pieces):
        key = turned(piece[:doc_max, :].astype(jnp.float32), cos_d[j : j + 1, :], sin_d[j : j + 1, :])
        keys[j * doc_max : (j + 1) * doc_max, :] = key.astype(jnp.bfloat16)
        vals[j * doc_max : (j + 1) * doc_max, :] = piece[doc_max : 2 * doc_max, :]
    base = docs * doc_max
    first = heads * length
    keys[base:, :] = turned(q[first : first + length, :].astype(jnp.float32), cosine, sine).astype(
        jnp.bfloat16
    )
    vals[base:, :] = q[first + length :, :]
    wide[...] = q[:first, :].astype(jnp.float32)
    column = lax.broadcasted_iota(jnp.int32, (1, doc_max), 1)
    allowed = [column < doc_lens[query_docs[query, slot]] for slot in slots]
    causal = lax.broadcasted_iota(jnp.int32, (length, length), 0) >= lax.broadcasted_iota(
        jnp.int32, (length, length), 1
    )
    for h in range(heads):
        rows = turned(wide[pl.ds(h, length, stride=heads), :], cosine, sine).astype(jnp.bfloat16)
        scores = lax.dot_general(rows, keys[...], NT, preferred_element_type=jnp.float32)
        scores = scores * head_dim ** (-0.5)
        parts = [
            jnp.where(allowed[j], scores[:, j * doc_max : (j + 1) * doc_max], -jnp.inf)
            for j in range(docs)
        ] + [jnp.where(causal, scores[:, base:], -jnp.inf)]
        scores = jnp.concatenate(parts, axis=1)
        ceiling = jnp.max(scores, axis=1, keepdims=True)
        probs = jnp.exp(scores - ceiling)
        denominator = jnp.sum(probs, axis=1, keepdims=True)
        mixed = dot(probs.astype(jnp.bfloat16), vals[...])
        out[:, h * head_dim : (h + 1) * head_dim] = (mixed / denominator).astype(jnp.bfloat16)


def attention(here, query_docs, doc_lens, q, pieces, tables, pool_dev):
    length, head_dim = tables[0].shape
    heads = q.shape[0] // length - 2
    rows = 5 * length
    return call(
        functools.partial(attention_body, pool_dev),
        jax.ShapeDtypeStruct((length, heads * head_dim), jnp.bfloat16),
        [
            pltpu.VMEM((heads * length, head_dim), jnp.float32),
            pltpu.VMEM((rows, head_dim), jnp.bfloat16),
            pltpu.VMEM((rows, head_dim), jnp.bfloat16),
        ],
        in_specs=[SMEM] * 3 + [VMEM] * 9,
        out_specs=VMEM,
        name="attention",
    )(here, query_docs, doc_lens, q, *pieces, *tables)


def project_body(here, a, b, c, d, weight, *rest):
    outs, rows = (rest[:-1], rest[-1])
    device, lane = (here[0], here[1])
    for flip, ref in zip((0, 2, 1, 3), (a, b, c, d)):
        rows[query_of(device, lane ^ flip)] = ref[...]
    for d in (2, 3, 1, 0):
        outs[d][...] = dot(rows[device ^ d], weight[...]).astype(jnp.bfloat16)


def project(here, parts, weight):
    length, depth = parts[0].shape
    return call(
        project_body,
        [jax.ShapeDtypeStruct((length, weight.shape[1]), jnp.bfloat16)] * 4,
        [pltpu.VMEM((4, length, depth), jnp.bfloat16)],
        in_specs=[SMEM] + [VMEM] * 5,
        out_specs=[VMEM] * 4,
        name="project",
    )(here, *parts, weight)


def routing_body(experts, here, c0, c1, c2, c3, pick, spread):
    _, local, capacity, length = pick.shape
    first = here[0] * local
    before = (
        lax.broadcasted_iota(jnp.int32, (length, length), 0)
        < lax.broadcasted_iota(jnp.int32, (length, length), 1)
    ).astype(jnp.bfloat16)
    place = lax.broadcasted_iota(jnp.int32, (capacity, length), 0).astype(jnp.float32)
    row = lax.broadcasted_iota(jnp.int32, (8, length), 0)
    for d, piece in enumerate((c0, c1, c2, c3)):
        ids = piece[piece.shape[0] - 16 :, :].astype(jnp.float32).astype(jnp.int32)
        chosen = jnp.zeros((8, length), jnp.float32)
        for k in range(8):
            named = jnp.logical_and(ids[k : k + 1, :] == first + row, row < local)
            chosen = jnp.where(named, 1.0, chosen)
        rank = dot(chosen.astype(jnp.bfloat16), before)
        wide = []
        for e in range(local):
            here_e = jnp.logical_and(rank[e : e + 1, :] == place, chosen[e : e + 1, :] > 0.0)
            wide.append(jnp.where(here_e, 1.0, 0.0))
            pick[d, e] = wide[-1].astype(jnp.bfloat16)
        spread[d] = jnp.transpose(jnp.concatenate(wide, axis=0)).astype(jnp.bfloat16)


def routing(here, pieces, experts, local, capacity):
    length = pieces[0].shape[1]
    rows = pieces[0].shape[0]
    return call(
        functools.partial(routing_body, experts),
        [
            jax.ShapeDtypeStruct((4, local, capacity, length), jnp.bfloat16),
            jax.ShapeDtypeStruct((4, length, local * capacity), jnp.bfloat16),
        ],
        [],
        in_specs=[SMEM] + [VMEM] * 4,
        out_specs=[VMEM] * 2,
        name="routing",
    )(here, *pieces)


def residual_body(hidden, p0, p1, p2, gain, router, after, out, stats):
    rows = stats.shape[0]
    total = hidden[...].astype(jnp.float32) + p0[...].astype(jnp.float32)
    for part in (p1, p2):
        total = total + part[...].astype(jnp.float32)
    narrow = total.astype(jnp.bfloat16)
    out[...] = narrow
    wide = narrow.astype(jnp.float32)
    grown = wide * gain[...]
    high = grown.astype(jnp.bfloat16)
    rest = grown - high.astype(jnp.float32)
    middle = rest.astype(jnp.bfloat16)
    low = (rest - middle.astype(jnp.float32)).astype(jnp.bfloat16)
    logits = dot(high, router[...]) + (dot(middle, router[...]) + dot(low, router[...]))
    squares = jnp.sum(wide * wide, axis=1, keepdims=True)
    column = lax.broadcasted_iota(jnp.int32, logits.shape, 1)
    stats[...] = jnp.transpose(jnp.where(column == rows - 8, squares, logits))[:rows, :]


def residual_and_stats(hidden, parts, gain, router, experts, after):
    length, width = hidden.shape
    return call(
        residual_body,
        [
            jax.ShapeDtypeStruct((length, width), jnp.bfloat16),
            jax.ShapeDtypeStruct((experts + 8, length), jnp.float32),
        ],
        [],
        in_specs=[VMEM] * 6 + [pl.BlockSpec(memory_space=pl.ANY)],
        out_specs=[VMEM] * 2,
        name="residual",
    )(hidden, *parts, gain, router, after)


def join_body(a, b, c, d, out):
    length = a.shape[1]
    for j, ref in enumerate((a, b, c, d)):
        out[:, j * length : (j + 1) * length] = ref[...]


def join(parts):
    rows, length = parts[0].shape
    return call(
        join_body,
        jax.ShapeDtypeStruct((rows, 4 * length), parts[0].dtype),
        [],
        in_specs=[VMEM] * 4,
        out_specs=VMEM,
        name="join",
    )(*parts)


def gate_up_body(ds, order, *refs):
    tokens = refs[: len(ds)]
    gain, pick, weight, kept, given, rows = refs[len(ds) :]
    hid = weight.shape[3]
    capacity = pick.shape[2]
    i = pl.program_id(0)
    expert = order[i]
    for k, d in enumerate(ds):
        chosen = dot(pick[d, expert], tokens[k][...]) * gain[...]
        rows[k * capacity : (k + 1) * capacity, :] = chosen.astype(jnp.bfloat16)
    for g in range(2):
        term = dot(rows[...], weight[0, g]).astype(jnp.bfloat16)
        for j in range(4):
            out = (kept, given)[j // 2]

            @pl.when(i == j)
            def _():
                out[j % 2, :, g * hid : (g + 1) * hid] = term


def gate_up(ds, order, tokens, gain, pick, weight):
    local, _, width, hid = weight.shape
    capacity = pick.shape[2]
    shape = jax.ShapeDtypeStruct((2, len(ds) * capacity, 2 * hid), jnp.bfloat16)
    whole = lambda rank: lambda i, order: (0,) * rank
    return call(
        functools.partial(gate_up_body, ds),
        [shape] * 2,
        None,
        grid_spec=pltpu.PrefetchScalarGridSpec(
            num_scalar_prefetch=1,
            grid=(local,),
            in_specs=[pl.BlockSpec(tokens[0].shape, whole(2))] * len(ds)
            + [
                pl.BlockSpec(gain.shape, whole(2)),
                pl.BlockSpec(pick.shape, whole(4)),
                pl.BlockSpec((1, 2, width, hid), lambda i, order: (order[i], 0, 0, 0)),
            ],
            out_specs=[pl.BlockSpec(shape.shape, whole(3))] * 2,
            scratch_shapes=[pltpu.VMEM((len(ds) * capacity, width), jnp.bfloat16)],
        ),
        name="gate_up",
    )(order, *tokens, gain, pick, weight)


def activate_body(ds, features, here, kept, taken, across, pick, *refs):
    stats = refs[0]
    pieces = refs[1 : 1 + len(ds)]
    out = refs[1 + len(ds)]
    _, local, capacity, length = pick.shape
    hid = out.shape[1]
    experts = stats.shape[0] - 8
    device, lane = (here[0], here[1])
    expert = lax.broadcasted_iota(jnp.int32, (experts, length), 0)
    for k, d in enumerate(ds):
        ids = pieces[k][pieces[k].shape[0] - 16 :, :].astype(jnp.float32).astype(jnp.int32)
        chosen = jnp.zeros((experts, length), jnp.float32)
        for c in range(8):
            chosen = jnp.where(ids[c : c + 1, :] == expert, 1.0, chosen)
        block = slice(d * length, (d + 1) * length)
        inv_rms = lax.rsqrt(stats[experts : experts + 1, block] / features + norm_eps)
        logits = jnp.where(chosen > 0.0, stats[:experts, block] * inv_rms, -jnp.inf)
        grown = jnp.exp(logits - jnp.max(logits, axis=0, keepdims=True))
        mix = grown / jnp.sum(grown, axis=0, keepdims=True)
        mix = jnp.sum(jnp.where(expert == device * local + lane, mix, 0.0), axis=0, keepdims=True)
        places = pick[d, lane].astype(jnp.float32)
        inv_row = jnp.sum(places * inv_rms, axis=1, keepdims=True)
        mix_row = jnp.sum(places * mix, axis=1, keepdims=True)
        rows = slice(k * capacity, (k + 1) * capacity)
        summed = kept[0, rows, :].astype(jnp.float32) + taken[0, rows, :].astype(jnp.float32)
        summed = (summed + across[rows, :].astype(jnp.float32)) * inv_row
        gate = summed[:, :hid]
        act = gate / (1.0 + jnp.exp(-gate)) * summed[:, hid:] * mix_row
        out[rows, :] = act.astype(jnp.bfloat16)


def activate(ds, features, here, kept, taken, across, pick, stats, pieces):
    rows, both = across.shape
    return call(
        functools.partial(activate_body, ds, features),
        jax.ShapeDtypeStruct((rows, both // 2), jnp.bfloat16),
        [],
        in_specs=[SMEM] + [VMEM] * (5 + len(ds)),
        out_specs=VMEM,
        name="activate",
    )(here, kept, taken, across, pick, stats, *[pieces[d] for d in ds])


def down_body(ds, order, a, b, c, d, spread, weight, *rest):
    outs, results = (rest[:-1], rest[-1])
    i = pl.program_id(0)
    capacity = results.shape[2]
    expert = order[i]
    for j, ref in enumerate((a, b, c, d)):

        @pl.when(i == j)
        def _():
            result = dot(ref[...], weight[0]).astype(jnp.bfloat16)
            for k in range(len(ds)):
                results[k, expert] = result[k * capacity : (k + 1) * capacity, :]

    @pl.when(i == pl.num_programs(0) - 1)
    def _():
        for k, out in enumerate(outs):
            rows = results[k].reshape(-1, results.shape[3])
            out[...] = dot(spread[ds[k]], rows).astype(jnp.bfloat16)


def down(ds, order, acts, spread, weight):
    local, hid, width = weight.shape
    capacity = acts[0].shape[0] // len(ds)
    length = spread.shape[1]
    shape = jax.ShapeDtypeStruct((length, width), jnp.bfloat16)
    whole = lambda rank: lambda i, order: (0,) * rank
    return call(
        functools.partial(down_body, ds),
        [shape] * len(ds),
        None,
        grid_spec=pltpu.PrefetchScalarGridSpec(
            num_scalar_prefetch=1,
            grid=(local,),
            in_specs=[pl.BlockSpec(acts[0].shape, whole(2))] * 4
            + [
                pl.BlockSpec(spread.shape, whole(3)),
                pl.BlockSpec((1, hid, width), lambda i, order: (order[i], 0, 0)),
            ],
            out_specs=[pl.BlockSpec(shape.shape, whole(2))] * len(ds),
            scratch_shapes=[pltpu.VMEM((len(ds), local, capacity, width), jnp.bfloat16)],
        ),
        name="down",
    )(order, *acts, spread, weight)


def per_device_square(
    question_q,
    question_kv,
    doc_kv,
    doc_lens,
    query_docs,
    ctx_pos,
    hidden,
    out_proj,
    norm_gain,
    router_weight,
    w_gate_up,
    w_down,
    expert_ids,
):
    n = 4
    lane = lax.axis_index("tp")
    device = lax.axis_index("ep")
    length, heads_here, head_dim = question_q.shape
    pool_dev = doc_kv.shape[0]
    width_here = hidden.shape[1]
    experts = router_weight.shape[1]
    local = w_gate_up.shape[0]
    capacity = length * expert_ids.shape[1] // experts
    here = jnp.stack([device, lane]).astype(jnp.int32)
    order = (lane ^ jnp.array([0, 2, 1, 3], jnp.int32)).astype(jnp.int32)

    pool = jnp.transpose(doc_kv, (0, 2, 3, 1, 4))
    ids_rows = jnp.pad(expert_ids.T.astype(jnp.bfloat16), ((0, 8), (0, 0)))
    pieces = prepare(here, query_docs, pool, ids_rows)
    q_rows, pieces = turn(
        question_q.reshape(length * heads_here, head_dim), question_kv, device, lane, n, pieces
    )
    pieces = [pieces[0]] + [lax.ppermute(pieces[d], "ep", pairs(n, d)) for d in range(1, n)]
    tables = list(angles(here, query_docs, ctx_pos, pool_dev, length, head_dim))

    one = lax.optimization_barrier(jnp.ones((), jnp.bfloat16))
    tables[0], out_proj = lax.optimization_barrier((tables[0], out_proj * one))
    attended = attention(here, query_docs, doc_lens, q_rows, pieces, tables, pool_dev)
    far = lax.ppermute(attended, "tp", pairs(n, 2))
    near = lax.ppermute(attended, "tp", pairs(n, 1))
    farther = lax.ppermute(far, "tp", pairs(n, 1))
    gain = norm_gain.astype(jnp.float32)[None, :]
    router = jnp.pad(router_weight, ((0, 0), (0, 128 - experts)))
    parts = project(here, (attended, far, near, farther), out_proj)
    kept, w_gate_up = lax.optimization_barrier((parts[0], w_gate_up))
    sent = scatter_blocks([kept] + list(parts[1:]), n)
    pick, spread = routing(here, pieces, experts, local, capacity)
    weight = jnp.transpose(w_gate_up, (0, 2, 1, 3))
    sent[0], pick = lax.optimization_barrier((sent[0], pick))
    residual, own_stats = residual_and_stats(hidden, sent, gain, router, experts, weight)

    tokens, stats = ({0: residual}, {0: own_stats})
    for d in (2, 3, 1):
        tokens[d] = lax.ppermute(residual, "ep", pairs(n, d))
    for d in (2, 3, 1):
        stats[d] = lax.ppermute(own_stats, "ep", pairs(n, d))
    tokens, stats = lax.optimization_barrier((tokens, stats))
    stats = join([stats[d] for d in range(n)])
    stats_far = lax.ppermute(stats, "tp", pairs(n, 2))

    features = width_here * n

    def spread_act(act):
        far = lax.ppermute(act, "tp", pairs(n, 2))
        near = lax.ppermute(act, "tp", pairs(n, 1))
        return [act, far, near, lax.ppermute(far, "tp", pairs(n, 1))]

    def chip_sum(kept, taken):
        return (kept[1].astype(jnp.float32) + taken[1].astype(jnp.float32)).astype(jnp.bfloat16)

    one_chunk, two_chunk = ((2, 3), (0, 1))
    kept, given = gate_up(one_chunk, order, [tokens[d] for d in one_chunk], gain, pick, weight)
    given, stats_far = lax.optimization_barrier((given, stats_far))
    taken = lax.ppermute(given, "tp", pairs(n, 1))
    stats = stats + stats_far
    stats_near = lax.ppermute(stats, "tp", pairs(n, 1))
    far_sum = chip_sum(kept, taken)
    across = lax.ppermute(far_sum, "tp", pairs(n, 2))

    order, _, stats_near = lax.optimization_barrier((order, far_sum, stats_near))
    stats = stats + stats_near
    kept_2, given = gate_up(two_chunk, order, [tokens[d] for d in two_chunk], gain, pick, weight)
    given, across = lax.optimization_barrier((given, across))
    taken_2 = lax.ppermute(given, "tp", pairs(n, 1))
    acts = spread_act(activate(one_chunk, features, here, kept, taken, across, pick, stats, pieces))
    far_sum = chip_sum(kept_2, taken_2)
    far_sum, acts[1] = lax.optimization_barrier((far_sum, acts[1]))
    acts[3] = lax.ppermute(acts[1], "tp", pairs(n, 1))
    across = lax.ppermute(far_sum, "tp", pairs(n, 2))
    parts = down(one_chunk, order, acts, spread, w_down)
    near = lax.ppermute(parts[1], "ep", pairs(n, 1))
    far = (parts[0].astype(jnp.float32) + near.astype(jnp.float32)).astype(jnp.bfloat16)
    across, far = lax.optimization_barrier((across, far))
    far = lax.ppermute(far, "ep", pairs(n, 2))
    acts = spread_act(
        activate(two_chunk, features, here, kept_2, taken_2, across, pick, stats, pieces)
    )
    mine, near = down(two_chunk, order, acts, spread, w_down)
    returned = [mine, far, lax.ppermute(near, "ep", pairs(n, 1))]
    total = residual.astype(jnp.float32)
    for part in returned:
        total = total + part.astype(jnp.float32)
    return total.astype(jnp.bfloat16)


def solution(mesh):
    placed = (
        P(("grp", "ep"), "tp", None),
        P(("grp", "ep"), None, None, None),
        P(("grp", "ep"), None, None, None, None),
        P("grp"),
        P("grp", None),
        P("grp", None),
        P(("grp", "ep"), "tp"),
        P("ep", "tp"),
        P("tp"),
        P("tp", None),
        P("ep", "tp", None, None),
        P("ep", None, "tp"),
        P(("grp", "ep"), None),
    )
    def per_device(*args):
        square = (
            lax.axis_size("tp") == 4
            and lax.axis_size("ep") == 4
            and args[1].shape[1] == 4
            and args[4].shape == (4, 4)
        )
        return (per_device_square if square else per_device_general)(*args)

    return jax.shard_map(
        per_device, mesh=mesh, in_specs=placed, out_specs=P(("grp", "ep"), "tp"), check_vma=False
    )
```

```python
import functools
import math

import jax
import jax.numpy as jnp
from jax import lax
from jax.experimental import pallas as pl
from jax.experimental.pallas import tpu as pltpu
from jax.sharding import PartitionSpec as P

rope_theta = 1000000.0
norm_eps = 1e-06


def tables(positions, head_dim):
    half = head_dim // 2
    freq = jnp.exp(jnp.arange(half, dtype=jnp.float32) * (-2.0 * math.log(rope_theta) / head_dim))
    angle = positions.astype(jnp.float32)[:, None] * freq[None, :]
    return (jnp.cos(angle), jnp.sin(angle))


def rotate(values, positions):
    half = values.shape[-1] // 2
    cosine, sine = tables(positions, values.shape[-1])
    shape = (values.shape[0],) + (1,) * (values.ndim - 2) + (half,)
    cosine, sine = (cosine.reshape(shape), sine.reshape(shape))
    floats = values.astype(jnp.float32)
    first = floats[..., :half]
    second = floats[..., half:]
    return jnp.concatenate(
        [first * cosine - second * sine, second * cosine + first * sine], axis=-1
    )


def attend(q_rows, own_kv, context, starts, lengths, question_start):
    length, heads_here, head_dim = q_rows.shape
    docs_per, doc_max, _ = context.shape
    question_pos = question_start + jnp.arange(length, dtype=jnp.int32)
    queries = rotate(q_rows, question_pos).astype(jnp.bfloat16)
    own_keys = rotate(own_kv[:, :head_dim], question_pos).astype(jnp.bfloat16)
    positions = jnp.repeat(starts, doc_max, total_repeat_length=docs_per * doc_max)
    doc_keys = rotate(context[:, :, :head_dim].reshape(docs_per * doc_max, head_dim), positions)
    keys = jnp.concatenate([doc_keys.astype(jnp.bfloat16), own_keys], axis=0)
    values = jnp.concatenate(
        [context[:, :, head_dim:].reshape(docs_per * doc_max, head_dim), own_kv[:, head_dim:]],
        axis=0,
    )
    valid = (jnp.arange(doc_max, dtype=jnp.int32)[None, :] < lengths[:, None]).reshape(-1)
    causal = jnp.arange(length)[:, None] >= jnp.arange(length)[None, :]
    allowed = jnp.concatenate(
        [jnp.broadcast_to(valid[None, :], (length, valid.shape[0])), causal], axis=1
    )
    scores = jnp.einsum("ihd,jd->hij", queries, keys, preferred_element_type=jnp.float32)
    scores = jnp.where(allowed[None], scores * head_dim ** (-0.5), -jnp.inf)
    ceiling = jnp.max(scores, axis=-1, keepdims=True)
    probs = jnp.exp(scores - ceiling)
    denominator = jnp.sum(probs, axis=-1, keepdims=True)
    mixed = jnp.einsum(
        "hij,jd->hid", probs.astype(jnp.bfloat16), values, preferred_element_type=jnp.float32
    )
    return (
        jnp.transpose(mixed / denominator, (1, 0, 2))
        .reshape(length, heads_here * head_dim)
        .astype(jnp.bfloat16)
    )


def context_by_row(doc_kv, doc_lens, query_docs, ctx_pos, device, kv_pick):
    pool_dev, doc_max, _, pair, head_dim = doc_kv.shape
    docs_per = query_docs.shape[1]
    pool_head = lax.dynamic_index_in_dim(doc_kv, kv_pick, 2, keepdims=False).reshape(
        pool_dev, doc_max, pair * head_dim
    )
    held = device * pool_dev + jnp.arange(pool_dev, dtype=jnp.int32)
    wanted = jnp.sum((query_docs[:, :, None] == held[None, None, :]).astype(jnp.float32), axis=1)
    sending = jnp.einsum(
        "rl,lkc->rkc", wanted.astype(jnp.bfloat16), pool_head, preferred_element_type=jnp.float32
    ).astype(jnp.bfloat16)
    received = lax.all_to_all(sending, "ep", split_axis=0, concat_axis=0, tiled=True)
    my_docs = lax.dynamic_index_in_dim(query_docs, device, 0, keepdims=False)
    starts = lax.dynamic_index_in_dim(ctx_pos, device, 0, keepdims=False)
    return (jnp.take(received, my_docs // pool_dev, axis=0), starts[:docs_per], jnp.take(doc_lens, my_docs))


def per_device_general(
    question_q,
    question_kv,
    doc_kv,
    doc_lens,
    query_docs,
    ctx_pos,
    hidden,
    out_proj,
    norm_gain,
    router_weight,
    w_gate_up,
    w_down,
    expert_ids,
):
    lanes = lax.axis_size("tp")
    groups = lax.axis_size("ep")
    lane = lax.axis_index("tp")
    device = lax.axis_index("ep")
    length, heads_here, head_dim = question_q.shape
    kv_heads = question_kv.shape[1]
    docs_per = query_docs.shape[1]
    width_here = hidden.shape[1]
    ids = lax.all_gather(expert_ids, "ep", axis=0, tiled=False)
    kv_pick = lane * kv_heads // lanes
    kv_head = lax.dynamic_index_in_dim(question_kv, kv_pick, 1, keepdims=False).reshape(
        length, 2 * head_dim
    )
    context, starts, lengths = context_by_row(
        doc_kv, doc_lens, query_docs, ctx_pos, device, kv_pick
    )
    question_start = lax.dynamic_index_in_dim(ctx_pos, device, 0, keepdims=False)[docs_per]
    attended = attend(question_q, kv_head, context, starts, lengths, question_start)
    projected = jnp.dot(
        lax.all_gather(attended, "tp", axis=1, tiled=True),
        lax.all_gather(out_proj, "ep", axis=0, tiled=True),
        preferred_element_type=jnp.float32,
    )
    residual = (hidden.astype(jnp.float32) + projected.astype(jnp.float32)).astype(jnp.bfloat16)

    tokens = lax.all_gather(residual, "ep", axis=0, tiled=False)
    wide = tokens.astype(jnp.float32)
    gain = norm_gain.astype(jnp.float32)
    scaled = wide * gain
    logit_part = jnp.einsum(
        "snd,de->sne", scaled, router_weight.astype(jnp.float32), precision=lax.Precision.HIGHEST
    )
    square_part = jnp.sum(wide * wide, axis=2, keepdims=True)
    stats = jnp.sum(
        lax.all_gather(jnp.concatenate([logit_part, square_part], axis=2), "tp", axis=0), axis=0
    )
    experts = router_weight.shape[1]
    inv_rms = lax.rsqrt(stats[:, :, experts] / (width_here * lanes) + norm_eps)
    logits = stats[:, :, :experts] * inv_rms[:, :, None]

    local_experts = w_gate_up.shape[0]
    capacity = length * expert_ids.shape[1] // experts
    hid = w_gate_up.shape[3]
    chosen_all = jnp.any(
        ids[:, :, :, None] == jnp.arange(experts, dtype=jnp.int32), axis=2
    )
    top = jnp.max(jnp.where(chosen_all, logits, -jnp.inf), axis=2, keepdims=True)
    weight = jnp.where(chosen_all, jnp.exp(logits - top), 0.0)
    mix = weight / jnp.sum(weight, axis=2, keepdims=True)

    shuffled, scaled_rows = (chosen_all, scaled.astype(jnp.bfloat16))
    first = device * local_experts
    chosen = lax.dynamic_slice_in_dim(shuffled, first, local_experts, 2)
    mix_here = lax.dynamic_slice_in_dim(mix, first, local_experts, 2)
    before = (jnp.arange(length)[:, None] > jnp.arange(length)[None, :]).astype(jnp.bfloat16)
    rank = jnp.einsum(
        "mn,sne->sem", before, chosen.astype(jnp.bfloat16), preferred_element_type=jnp.float32
    ).astype(jnp.int32)
    pick = jnp.logical_and(
        jnp.transpose(chosen, (0, 2, 1))[:, :, None, :],
        rank[:, :, None, :] == jnp.arange(capacity, dtype=jnp.int32)[None, None, :, None],
    )
    onehot = pick.astype(jnp.bfloat16)
    inv_row = jnp.sum(jnp.where(pick, inv_rms[:, None, None, :], 0.0), axis=3)
    mix_row = jnp.sum(jnp.where(pick, jnp.transpose(mix_here, (0, 2, 1))[:, :, None, :], 0.0), axis=3)

    rows = jnp.einsum(
        "sern,snd->serd", onehot, scaled_rows, preferred_element_type=jnp.float32
    ).astype(jnp.bfloat16)
    term = jnp.einsum(
        "serd,edgh->sergh", rows, w_gate_up, preferred_element_type=jnp.float32
    ).astype(jnp.bfloat16)
    per_lane = groups * local_experts * capacity // lanes
    term = term.reshape(lanes, per_lane, 2 * hid)
    inv_row = inv_row.reshape(lanes, per_lane, 1)
    summed = lax.psum_scatter(term, "tp", scatter_dimension=0, tiled=True)[0].astype(jnp.float32)
    inv_mine = lax.dynamic_index_in_dim(inv_row, lane, 0, keepdims=False)
    summed = summed * inv_mine
    act = (jax.nn.silu(summed[:, :hid]) * summed[:, hid:]).astype(jnp.bfloat16)
    acts = lax.all_gather(act, "tp", axis=0, tiled=False)
    acts = acts.reshape(groups, local_experts, capacity, hid)
    expert_out = jnp.einsum("serh,ehd->serd", acts, w_down, preferred_element_type=jnp.float32)
    expert_out = (expert_out * mix_row[:, :, :, None]).astype(jnp.bfloat16)
    combined = jnp.einsum(
        "sern,serd->snd", onehot, expert_out, preferred_element_type=jnp.float32
    ).astype(jnp.bfloat16)
    returned = lax.psum_scatter(combined, "ep", scatter_dimension=0, tiled=True)[0]
    return (residual.astype(jnp.float32) + returned.astype(jnp.float32)).astype(jnp.bfloat16)


def pairs(lanes, flip):
    return [(i, i ^ flip) for i in range(lanes)]


def scatter_blocks(parts, n):
    near = lax.ppermute(parts[3], "ep", pairs(n, 1))
    far = (parts[2].astype(jnp.float32) + near.astype(jnp.float32)).astype(jnp.bfloat16)
    return [parts[0], lax.ppermute(far, "ep", pairs(n, 2)), lax.ppermute(parts[1], "ep", pairs(n, 1))]


def query_of(device, lane):
    return 2 * (lane & 1) + ((lane >> 1) ^ (device & 1))


def turn(question, keys_values, device, lane, n, meanwhile):
    crosses = lambda e, t: ((e ^ t) & 1) != (t >> 1)
    devices = [(e, t) for e in range(n) for t in range(n)]
    swap = [(e * n + t, e * n + (t ^ 3)) for e, t in devices if crosses(e, t)]
    crossed = lax.ppermute(question, ("ep", "tp"), swap)
    crossed, *meanwhile = lax.optimization_barrier((crossed, *meanwhile))
    heads = jnp.where(crosses(device, lane), lane ^ 3, lane)
    picked = lax.dynamic_index_in_dim(keys_values, heads, 1, keepdims=False)
    picked = jnp.transpose(picked, (1, 0, 2)).reshape(-1, question.shape[1])
    held = jnp.where(crosses(device, lane), crossed, question)
    moves = []
    for e, t in devices:
        h = t ^ 3 if crosses(e, t) else t
        moves.append((e * n + t, h * n + 2 * ((e ^ h) & 1) + (e >> 1)))
    return (lax.ppermute(jnp.concatenate([held, picked], axis=0), ("ep", "tp"), moves), meanwhile)


def call(body, outs, scratch, **kwargs):
    return pl.pallas_call(
        body,
        out_shape=outs,
        **({} if scratch is None else {"scratch_shapes": scratch}),
        compiler_params=pltpu.CompilerParams(vmem_limit_bytes=20 * 1024 * 1024),
        cost_estimate=pl.CostEstimate(flops=1 << 20, bytes_accessed=1 << 18, transcendentals=0),
        **kwargs,
    )


VMEM = pl.BlockSpec(memory_space=pltpu.VMEM)
SMEM = pl.BlockSpec(memory_space=pltpu.SMEM)
NT = (((1,), (1,)), ((), ()))


def dot(a, b):
    return jnp.dot(a, b, preferred_element_type=jnp.float32)


def document_slots(here, query_docs, pool_dev):
    device, lane = (here[0], here[1])
    query = query_of(device, lane)
    slots = []
    for d in range(4):
        slot = jnp.int32(0)
        for j in range(query_docs.shape[1]):
            offset = query_docs[query, j] - (device ^ d) * pool_dev
            slot = jnp.where(jnp.logical_and(offset >= 0, offset < pool_dev), j, slot)
        slots.append(slot)
    return (query, slots)


def prepare_body(here, query_docs, pool, ids, *outs):
    pool_dev = pool.shape[0]
    docs_per = query_docs.shape[1]
    rows = pool.shape[2] * pool.shape[3]
    device, lane = (here[0], here[1])
    for d, out in enumerate(outs):
        target = device ^ d
        query = query_of(target, lane)
        local = jnp.int32(0)
        for j in range(docs_per):
            offset = query_docs[query, j] - device * pool_dev
            inside = jnp.logical_and(offset >= 0, offset < pool_dev)
            local = jnp.where(inside, offset, local)
        out[:rows, :] = pool[local, target].reshape(rows, pool.shape[4])
        out[rows:, :] = ids[...]


def prepare(here, query_docs, pool, ids):
    _, _, pair, doc_max, head_dim = pool.shape
    shape = jax.ShapeDtypeStruct((pair * doc_max + ids.shape[0], head_dim), jnp.bfloat16)
    return call(
        prepare_body,
        [shape] * 4,
        [],
        in_specs=[SMEM, SMEM, VMEM, VMEM],
        out_specs=[VMEM] * 4,
        name="prepare",
    )(here, query_docs, pool, ids)


def angles_body(pool_dev, here, query_docs, ctx_pos, cos_q, sin_q, cos_d, sin_d):
    query, slots = document_slots(here, query_docs, pool_dev)
    docs_per = query_docs.shape[1]
    head_dim = cos_q.shape[1]

    def fill(starts, cosine, sine):
        column = lax.broadcasted_iota(jnp.int32, cosine.shape, 1)
        half = jnp.where(column < head_dim // 2, column, column - head_dim // 2)
        freq = jnp.exp(half.astype(jnp.float32) * (-2.0 * math.log(rope_theta) / head_dim))
        angle = starts.astype(jnp.float32) * freq
        cosine[...] = jnp.cos(angle)
        wave = jnp.sin(angle)
        sine[...] = jnp.where(column < head_dim // 2, -wave, wave)

    row = lax.broadcasted_iota(jnp.int32, cos_q.shape, 0)
    fill(ctx_pos[query, docs_per] + row, cos_q, sin_q)
    row = lax.broadcasted_iota(jnp.int32, cos_d.shape, 0)
    starts = jnp.zeros(cos_d.shape, jnp.int32)
    for d, slot in enumerate(slots):
        starts = jnp.where(row == d, ctx_pos[query, slot], starts)
    fill(starts, cos_d, sin_d)


def angles(here, query_docs, ctx_pos, pool_dev, length, head_dim):
    shapes = [jax.ShapeDtypeStruct((rows, head_dim), jnp.float32) for rows in (length, length, 8, 8)]
    return call(
        functools.partial(angles_body, pool_dev),
        shapes,
        [],
        in_specs=[SMEM] * 3,
        out_specs=[VMEM] * 4,
        name="angles",
    )(here, query_docs, ctx_pos)


def attention_body(
    pool_dev, here, query_docs, doc_lens, q, c0, c1, c2, c3, cos_q, sin_q, cos_d, sin_d, out, wide, keys, vals
):
    length, head_dim = cos_q.shape
    heads = out.shape[1] // head_dim
    pieces = (c0, c1, c2, c3)
    docs = len(pieces)
    doc_max = (keys.shape[0] - length) // docs
    half = head_dim // 2
    query, slots = document_slots(here, query_docs, pool_dev)

    def turned(x, cosine, sine):
        return x * cosine + pltpu.roll(x, half, 1) * sine

    cosine, sine = (cos_q[...], sin_q[...])
    for j, piece in enumerate(pieces):
        key = turned(piece[:doc_max, :].astype(jnp.float32), cos_d[j : j + 1, :], sin_d[j : j + 1, :])
        keys[j * doc_max : (j + 1) * doc_max, :] = key.astype(jnp.bfloat16)
        vals[j * doc_max : (j + 1) * doc_max, :] = piece[doc_max : 2 * doc_max, :]
    base = docs * doc_max
    first = heads * length
    keys[base:, :] = turned(q[first : first + length, :].astype(jnp.float32), cosine, sine).astype(
        jnp.bfloat16
    )
    vals[base:, :] = q[first + length :, :]
    wide[...] = q[:first, :].astype(jnp.float32)
    column = lax.broadcasted_iota(jnp.int32, (1, doc_max), 1)
    allowed = [column < doc_lens[query_docs[query, slot]] for slot in slots]
    causal = lax.broadcasted_iota(jnp.int32, (length, length), 0) >= lax.broadcasted_iota(
        jnp.int32, (length, length), 1
    )
    for h in range(heads):
        rows = turned(wide[pl.ds(h, length, stride=heads), :], cosine, sine).astype(jnp.bfloat16)
        scores = lax.dot_general(rows, keys[...], NT, preferred_element_type=jnp.float32)
        scores = scores * head_dim ** (-0.5)
        parts = [
            jnp.where(allowed[j], scores[:, j * doc_max : (j + 1) * doc_max], -jnp.inf)
            for j in range(docs)
        ] + [jnp.where(causal, scores[:, base:], -jnp.inf)]
        scores = jnp.concatenate(parts, axis=1)
        ceiling = jnp.max(scores, axis=1, keepdims=True)
        probs = jnp.exp(scores - ceiling)
        denominator = jnp.sum(probs, axis=1, keepdims=True)
        mixed = dot(probs.astype(jnp.bfloat16), vals[...])
        out[:, h * head_dim : (h + 1) * head_dim] = (mixed / denominator).astype(jnp.bfloat16)


def attention(here, query_docs, doc_lens, q, pieces, tables, pool_dev):
    length, head_dim = tables[0].shape
    heads = q.shape[0] // length - 2
    rows = 5 * length
    return call(
        functools.partial(attention_body, pool_dev),
        jax.ShapeDtypeStruct((length, heads * head_dim), jnp.bfloat16),
        [
            pltpu.VMEM((heads * length, head_dim), jnp.float32),
            pltpu.VMEM((rows, head_dim), jnp.bfloat16),
            pltpu.VMEM((rows, head_dim), jnp.bfloat16),
        ],
        in_specs=[SMEM] * 3 + [VMEM] * 9,
        out_specs=VMEM,
        name="attention",
    )(here, query_docs, doc_lens, q, *pieces, *tables)


def project_body(here, a, b, c, d, weight, *rest):
    outs, rows = (rest[:-1], rest[-1])
    device, lane = (here[0], here[1])
    for flip, ref in zip((0, 2, 1, 3), (a, b, c, d)):
        rows[query_of(device, lane ^ flip)] = ref[...]
    for d in (2, 3, 1, 0):
        outs[d][...] = dot(rows[device ^ d], weight[...]).astype(jnp.bfloat16)


def project(here, parts, weight):
    length, depth = parts[0].shape
    return call(
        project_body,
        [jax.ShapeDtypeStruct((length, weight.shape[1]), jnp.bfloat16)] * 4,
        [pltpu.VMEM((4, length, depth), jnp.bfloat16)],
        in_specs=[SMEM] + [VMEM] * 5,
        out_specs=[VMEM] * 4,
        name="project",
    )(here, *parts, weight)


def routing_body(experts, here, c0, c1, c2, c3, pick, spread):
    _, local, capacity, length = pick.shape
    first = here[0] * local
    before = (
        lax.broadcasted_iota(jnp.int32, (length, length), 0)
        < lax.broadcasted_iota(jnp.int32, (length, length), 1)
    ).astype(jnp.bfloat16)
    place = lax.broadcasted_iota(jnp.int32, (capacity, length), 0).astype(jnp.float32)
    row = lax.broadcasted_iota(jnp.int32, (8, length), 0)
    for d, piece in enumerate((c0, c1, c2, c3)):
        ids = piece[piece.shape[0] - 16 :, :].astype(jnp.float32).astype(jnp.int32)
        chosen = jnp.zeros((8, length), jnp.float32)
        for k in range(8):
            named = jnp.logical_and(ids[k : k + 1, :] == first + row, row < local)
            chosen = jnp.where(named, 1.0, chosen)
        rank = dot(chosen.astype(jnp.bfloat16), before)
        wide = []
        for e in range(local):
            here_e = jnp.logical_and(rank[e : e + 1, :] == place, chosen[e : e + 1, :] > 0.0)
            wide.append(jnp.where(here_e, 1.0, 0.0))
            pick[d, e] = wide[-1].astype(jnp.bfloat16)
        spread[d] = jnp.transpose(jnp.concatenate(wide, axis=0)).astype(jnp.bfloat16)


def routing(here, pieces, experts, local, capacity):
    length = pieces[0].shape[1]
    rows = pieces[0].shape[0]
    return call(
        functools.partial(routing_body, experts),
        [
            jax.ShapeDtypeStruct((4, local, capacity, length), jnp.bfloat16),
            jax.ShapeDtypeStruct((4, length, local * capacity), jnp.bfloat16),
        ],
        [],
        in_specs=[SMEM] + [VMEM] * 4,
        out_specs=[VMEM] * 2,
        name="routing",
    )(here, *pieces)


def residual_body(hidden, p0, p1, p2, after, out):
    total = hidden[...].astype(jnp.float32) + p0[...].astype(jnp.float32)
    for part in (p1, p2):
        total = total + part[...].astype(jnp.float32)
    out[...] = total.astype(jnp.bfloat16)


def add_parts(hidden, parts, after):
    return call(
        residual_body,
        jax.ShapeDtypeStruct(hidden.shape, jnp.bfloat16),
        [],
        in_specs=[VMEM] * 4 + [pl.BlockSpec(memory_space=pl.ANY)],
        out_specs=VMEM,
        name="residual",
    )(hidden, *parts, after)


def measure_body(t0, t1, t2, t3, gain, router, stats):
    rows = stats.shape[0]
    length = t0.shape[0]
    for d, ref in enumerate((t0, t1, t2, t3)):
        wide = ref[...].astype(jnp.float32)
        grown = wide * gain[...]
        high = grown.astype(jnp.bfloat16)
        rest = grown - high.astype(jnp.float32)
        middle = rest.astype(jnp.bfloat16)
        low = (rest - middle.astype(jnp.float32)).astype(jnp.bfloat16)
        logits = dot(high, router[...]) + (dot(middle, router[...]) + dot(low, router[...]))
        squares = jnp.sum(wide * wide, axis=1, keepdims=True)
        column = lax.broadcasted_iota(jnp.int32, logits.shape, 1)
        both = jnp.where(column == rows - 8, squares, logits)
        stats[:, d * length : (d + 1) * length] = jnp.transpose(both)[:rows, :]


def squares_and_logits(tokens, gain, router, experts):
    n, length = (len(tokens), tokens[0].shape[0])
    return call(
        measure_body,
        jax.ShapeDtypeStruct((experts + 8, n * length), jnp.float32),
        [],
        in_specs=[VMEM] * (n + 2),
        out_specs=VMEM,
        name="stats",
    )(*tokens, gain, router)


def gate_up_body(ds, order, *refs):
    tokens = refs[: len(ds)]
    gain, pick, weight, kept, given, rows = refs[len(ds) :]
    hid = weight.shape[3]
    capacity = pick.shape[2]
    i = pl.program_id(0)
    expert = order[i]
    for k, d in enumerate(ds):
        chosen = dot(pick[d, expert], tokens[k][...]) * gain[...]
        rows[k * capacity : (k + 1) * capacity, :] = chosen.astype(jnp.bfloat16)
    for g in range(2):
        term = dot(rows[...], weight[0, g]).astype(jnp.bfloat16)
        for j in range(4):
            out = (kept, given)[j // 2]

            @pl.when(i == j)
            def _():
                out[j % 2, :, g * hid : (g + 1) * hid] = term


def gate_up(ds, order, tokens, gain, pick, weight):
    local, _, width, hid = weight.shape
    capacity = pick.shape[2]
    shape = jax.ShapeDtypeStruct((2, len(ds) * capacity, 2 * hid), jnp.bfloat16)
    whole = lambda rank: lambda i, order: (0,) * rank
    return call(
        functools.partial(gate_up_body, ds),
        [shape] * 2,
        None,
        grid_spec=pltpu.PrefetchScalarGridSpec(
            num_scalar_prefetch=1,
            grid=(local,),
            in_specs=[pl.BlockSpec(tokens[0].shape, whole(2))] * len(ds)
            + [
                pl.BlockSpec(gain.shape, whole(2)),
                pl.BlockSpec(pick.shape, whole(4)),
                pl.BlockSpec((1, 2, width, hid), lambda i, order: (order[i], 0, 0, 0)),
            ],
            out_specs=[pl.BlockSpec(shape.shape, whole(3))] * 2,
            scratch_shapes=[pltpu.VMEM((len(ds) * capacity, width), jnp.bfloat16)],
        ),
        name="gate_up",
    )(order, *tokens, gain, pick, weight)


def activate_body(groups, features, here, pick, stats, *refs):
    out = refs[-1]
    _, local, capacity, length = pick.shape
    hid = out.shape[1]
    experts = stats.shape[0] - 8
    device, lane = (here[0], here[1])
    expert = lax.broadcasted_iota(jnp.int32, (experts, length), 0)
    base, refs = (0, list(refs))
    for ds in groups:
        kept, taken, across = refs[:3]
        pieces = refs[3 : 3 + len(ds)]
        refs = refs[3 + len(ds) :]
        for k, d in enumerate(ds):
            ids = pieces[k][pieces[k].shape[0] - 16 :, :].astype(jnp.float32).astype(jnp.int32)
            chosen = jnp.zeros((experts, length), jnp.float32)
            for c in range(8):
                chosen = jnp.where(ids[c : c + 1, :] == expert, 1.0, chosen)
            block = slice(d * length, (d + 1) * length)
            inv_rms = lax.rsqrt(stats[experts : experts + 1, block] / features + norm_eps)
            logits = jnp.where(chosen > 0.0, stats[:experts, block] * inv_rms, -jnp.inf)
            grown = jnp.exp(logits - jnp.max(logits, axis=0, keepdims=True))
            mix = grown / jnp.sum(grown, axis=0, keepdims=True)
            mine = jnp.where(expert == device * local + lane, mix, 0.0)
            mix = jnp.sum(mine, axis=0, keepdims=True)
            places = pick[d, lane].astype(jnp.float32)
            inv_row = jnp.sum(places * inv_rms, axis=1, keepdims=True)
            mix_row = jnp.sum(places * mix, axis=1, keepdims=True)
            rows = slice(k * capacity, (k + 1) * capacity)
            summed = kept[0, rows, :].astype(jnp.float32) + taken[0, rows, :].astype(jnp.float32)
            summed = (summed + across[rows, :].astype(jnp.float32)) * inv_row
            gate = summed[:, :hid]
            act = gate / (1.0 + jnp.exp(-gate)) * summed[:, hid:] * mix_row
            out[base + k * capacity : base + (k + 1) * capacity, :] = act.astype(jnp.bfloat16)
        base += len(ds) * capacity


def activate(groups, features, here, sums, pick, stats, pieces):
    operands = []
    for ds, terms in zip(groups, sums):
        operands += list(terms) + [pieces[d] for d in ds]
    rows = sum(terms[2].shape[0] for terms in sums)
    return call(
        functools.partial(activate_body, groups, features),
        jax.ShapeDtypeStruct((rows, sums[0][2].shape[1] // 2), jnp.bfloat16),
        [],
        in_specs=[SMEM] + [VMEM] * (2 + len(operands)),
        out_specs=VMEM,
        name="activate",
    )(here, pick, stats, *operands)


def down_body(ds, order, a, b, c, d, spread, weight, *rest):
    outs, results = (rest[:-1], rest[-1])
    i = pl.program_id(0)
    capacity = results.shape[2]
    expert = order[i]
    for j, ref in enumerate((a, b, c, d)):

        @pl.when(i == j)
        def _():
            result = dot(ref[...], weight[0]).astype(jnp.bfloat16)
            for k in range(len(ds)):
                results[k, expert] = result[k * capacity : (k + 1) * capacity, :]

    @pl.when(i == pl.num_programs(0) - 1)
    def _():
        for k, out in enumerate(outs):
            rows = results[k].reshape(-1, results.shape[3])
            out[...] = dot(spread[ds[k]], rows).astype(jnp.bfloat16)


def down(ds, order, acts, spread, weight):
    local, hid, width = weight.shape
    capacity = acts[0].shape[0] // len(ds)
    length = spread.shape[1]
    shape = jax.ShapeDtypeStruct((length, width), jnp.bfloat16)
    whole = lambda rank: lambda i, order: (0,) * rank
    return call(
        functools.partial(down_body, ds),
        [shape] * len(ds),
        None,
        grid_spec=pltpu.PrefetchScalarGridSpec(
            num_scalar_prefetch=1,
            grid=(local,),
            in_specs=[pl.BlockSpec(acts[0].shape, whole(2))] * 4
            + [
                pl.BlockSpec(spread.shape, whole(3)),
                pl.BlockSpec((1, hid, width), lambda i, order: (order[i], 0, 0)),
            ],
            out_specs=[pl.BlockSpec(shape.shape, whole(2))] * len(ds),
            scratch_shapes=[pltpu.VMEM((len(ds), local, capacity, width), jnp.bfloat16)],
        ),
        name="down",
    )(order, *acts, spread, weight)


def per_device_square(
    question_q,
    question_kv,
    doc_kv,
    doc_lens,
    query_docs,
    ctx_pos,
    hidden,
    out_proj,
    norm_gain,
    router_weight,
    w_gate_up,
    w_down,
    expert_ids,
):
    n = 4
    lane = lax.axis_index("tp")
    device = lax.axis_index("ep")
    length, heads_here, head_dim = question_q.shape
    pool_dev = doc_kv.shape[0]
    width_here = hidden.shape[1]
    experts = router_weight.shape[1]
    local = w_gate_up.shape[0]
    capacity = length * expert_ids.shape[1] // experts
    here = jnp.stack([device, lane]).astype(jnp.int32)
    order = (lane ^ jnp.array([0, 2, 1, 3], jnp.int32)).astype(jnp.int32)

    pool = jnp.transpose(doc_kv, (0, 2, 3, 1, 4))
    ids_rows = jnp.pad(expert_ids.T.astype(jnp.bfloat16), ((0, 8), (0, 0)))
    pieces = prepare(here, query_docs, pool, ids_rows)
    q_rows, pieces = turn(
        question_q.reshape(length * heads_here, head_dim), question_kv, device, lane, n, pieces
    )
    pieces = [pieces[0]] + [lax.ppermute(pieces[d], "ep", pairs(n, d)) for d in range(1, n)]
    tables = list(angles(here, query_docs, ctx_pos, pool_dev, length, head_dim))

    one = lax.optimization_barrier(jnp.ones((), jnp.bfloat16))
    tables[0], out_proj = lax.optimization_barrier((tables[0], out_proj * one))
    attended = attention(here, query_docs, doc_lens, q_rows, pieces, tables, pool_dev)
    far = lax.ppermute(attended, "tp", pairs(n, 2))
    near = lax.ppermute(attended, "tp", pairs(n, 1))
    farther = lax.ppermute(far, "tp", pairs(n, 1))
    gain = norm_gain.astype(jnp.float32)[None, :]
    router = jnp.pad(router_weight, ((0, 0), (0, 128 - experts)))
    parts = project(here, (attended, far, near, farther), out_proj)
    kept, w_gate_up = lax.optimization_barrier((parts[0], w_gate_up))
    sent = scatter_blocks([kept] + list(parts[1:]), n)
    pick, spread = routing(here, pieces, experts, local, capacity)
    weight = jnp.transpose(w_gate_up, (0, 2, 1, 3))
    sent[0], pick, router, gain = lax.optimization_barrier((sent[0], pick, router, gain))
    residual = add_parts(hidden, sent, weight)

    tokens = [residual] + [None] * (n - 1)
    for d in (2, 3, 1):
        tokens[d] = lax.ppermute(residual, "ep", pairs(n, d))

    features = width_here * n

    def spread_act(act):
        far = lax.ppermute(act, "tp", pairs(n, 2))
        near = lax.ppermute(act, "tp", pairs(n, 1))
        return [act, far, near, lax.ppermute(far, "tp", pairs(n, 1))]

    def chip_sum(kept, taken):
        return (kept[1].astype(jnp.float32) + taken[1].astype(jnp.float32)).astype(jnp.bfloat16)

    def terms_of(ds, order):
        return gate_up(ds, order, [tokens[d] for d in ds], gain, pick, weight)

    kept_0, given = terms_of((0,), order)
    given, tokens = lax.optimization_barrier((given, tokens))
    taken_0 = lax.ppermute(given, "tp", pairs(n, 1))
    stats = squares_and_logits(tokens, gain, router, experts)
    far_sum = chip_sum(kept_0, taken_0)
    far_sum, stats = lax.optimization_barrier((far_sum, stats))
    stats_far = lax.ppermute(stats, "tp", pairs(n, 2))
    across_0 = lax.ppermute(far_sum, "tp", pairs(n, 2))

    order, _ = lax.optimization_barrier((order, far_sum))
    kept_2, given = terms_of((2, 3), order)
    given, across_0, stats_far = lax.optimization_barrier((given, across_0, stats_far))
    taken_2 = lax.ppermute(given, "tp", pairs(n, 1))
    stats = stats + stats_far
    stats_near = lax.ppermute(stats, "tp", pairs(n, 1))
    far_sum = chip_sum(kept_2, taken_2)
    across_2 = lax.ppermute(far_sum, "tp", pairs(n, 2))

    order, _, stats_near = lax.optimization_barrier((order, far_sum, stats_near))
    stats = stats + stats_near
    kept_1, given = terms_of((1,), order)
    given, across_2 = lax.optimization_barrier((given, across_2))
    taken_1 = lax.ppermute(given, "tp", pairs(n, 1))

    groups = ((2, 3),)
    sums = [(kept_2, taken_2, across_2)]
    acts = spread_act(activate(groups, features, here, sums, pick, stats, pieces))
    far_sum = chip_sum(kept_1, taken_1)
    far_sum, acts[1] = lax.optimization_barrier((far_sum, acts[1]))
    acts[3] = lax.ppermute(acts[1], "tp", pairs(n, 1))
    across_1 = lax.ppermute(far_sum, "tp", pairs(n, 2))
    parts = down((2, 3), order, acts, spread, w_down)
    across_1, *parts = lax.optimization_barrier((across_1, *parts))
    near = lax.ppermute(parts[1], "ep", pairs(n, 1))
    far = (parts[0].astype(jnp.float32) + near.astype(jnp.float32)).astype(jnp.bfloat16)
    across_1, far = lax.optimization_barrier((across_1, far))
    far = lax.ppermute(far, "ep", pairs(n, 2))

    groups = ((0,), (1,))
    sums = [(kept_0, taken_0, across_0), (kept_1, taken_1, across_1)]
    acts = spread_act(activate(groups, features, here, sums, pick, stats, pieces))
    mine, near = down((0, 1), order, acts, spread, w_down)
    returned = [mine, far, lax.ppermute(near, "ep", pairs(n, 1))]
    total = residual.astype(jnp.float32)
    for part in returned:
        total = total + part.astype(jnp.float32)
    return total.astype(jnp.bfloat16)


def solution(mesh):
    placed = (
        P(("grp", "ep"), "tp", None),
        P(("grp", "ep"), None, None, None),
        P(("grp", "ep"), None, None, None, None),
        P("grp"),
        P("grp", None),
        P("grp", None),
        P(("grp", "ep"), "tp"),
        P("ep", "tp"),
        P("tp"),
        P("tp", None),
        P("ep", "tp", None, None),
        P("ep", None, "tp"),
        P(("grp", "ep"), None),
    )
    def per_device(*args):
        square = (
            lax.axis_size("tp") == 4
            and lax.axis_size("ep") == 4
            and args[1].shape[1] == 4
            and args[4].shape == (4, 4)
        )
        return (per_device_square if square else per_device_general)(*args)

    return jax.shard_map(
        per_device, mesh=mesh, in_specs=placed, out_specs=P(("grp", "ep"), "tp"), check_vma=False
    )
```

```python
import functools
import math

import jax
import jax.numpy as jnp
from jax import lax
from jax.experimental import pallas as pl
from jax.experimental.pallas import tpu as pltpu
from jax.sharding import PartitionSpec as P

rope_theta = 1000000.0
norm_eps = 1e-06


def tables(positions, head_dim):
    half = head_dim // 2
    freq = jnp.exp(jnp.arange(half, dtype=jnp.float32) * (-2.0 * math.log(rope_theta) / head_dim))
    angle = positions.astype(jnp.float32)[:, None] * freq[None, :]
    return (jnp.cos(angle), jnp.sin(angle))


def rotate(values, positions):
    half = values.shape[-1] // 2
    cosine, sine = tables(positions, values.shape[-1])
    shape = (values.shape[0],) + (1,) * (values.ndim - 2) + (half,)
    cosine, sine = (cosine.reshape(shape), sine.reshape(shape))
    floats = values.astype(jnp.float32)
    first = floats[..., :half]
    second = floats[..., half:]
    return jnp.concatenate(
        [first * cosine - second * sine, second * cosine + first * sine], axis=-1
    )


def attend(q_rows, own_kv, context, starts, lengths, question_start):
    length, heads_here, head_dim = q_rows.shape
    docs_per, doc_max, _ = context.shape
    question_pos = question_start + jnp.arange(length, dtype=jnp.int32)
    queries = rotate(q_rows, question_pos).astype(jnp.bfloat16)
    own_keys = rotate(own_kv[:, :head_dim], question_pos).astype(jnp.bfloat16)
    positions = jnp.repeat(starts, doc_max, total_repeat_length=docs_per * doc_max)
    doc_keys = rotate(context[:, :, :head_dim].reshape(docs_per * doc_max, head_dim), positions)
    keys = jnp.concatenate([doc_keys.astype(jnp.bfloat16), own_keys], axis=0)
    values = jnp.concatenate(
        [context[:, :, head_dim:].reshape(docs_per * doc_max, head_dim), own_kv[:, head_dim:]],
        axis=0,
    )
    valid = (jnp.arange(doc_max, dtype=jnp.int32)[None, :] < lengths[:, None]).reshape(-1)
    causal = jnp.arange(length)[:, None] >= jnp.arange(length)[None, :]
    allowed = jnp.concatenate(
        [jnp.broadcast_to(valid[None, :], (length, valid.shape[0])), causal], axis=1
    )
    scores = jnp.einsum("ihd,jd->hij", queries, keys, preferred_element_type=jnp.float32)
    scores = jnp.where(allowed[None], scores * head_dim ** (-0.5), -jnp.inf)
    ceiling = jnp.max(scores, axis=-1, keepdims=True)
    probs = jnp.exp(scores - ceiling)
    denominator = jnp.sum(probs, axis=-1, keepdims=True)
    mixed = jnp.einsum(
        "hij,jd->hid", probs.astype(jnp.bfloat16), values, preferred_element_type=jnp.float32
    )
    return (
        jnp.transpose(mixed / denominator, (1, 0, 2))
        .reshape(length, heads_here * head_dim)
        .astype(jnp.bfloat16)
    )


def context_by_row(doc_kv, doc_lens, query_docs, ctx_pos, device, kv_pick):
    pool_dev, doc_max, _, pair, head_dim = doc_kv.shape
    docs_per = query_docs.shape[1]
    pool_head = lax.dynamic_index_in_dim(doc_kv, kv_pick, 2, keepdims=False).reshape(
        pool_dev, doc_max, pair * head_dim
    )
    held = device * pool_dev + jnp.arange(pool_dev, dtype=jnp.int32)
    wanted = jnp.sum((query_docs[:, :, None] == held[None, None, :]).astype(jnp.float32), axis=1)
    sending = jnp.einsum(
        "rl,lkc->rkc", wanted.astype(jnp.bfloat16), pool_head, preferred_element_type=jnp.float32
    ).astype(jnp.bfloat16)
    received = lax.all_to_all(sending, "ep", split_axis=0, concat_axis=0, tiled=True)
    my_docs = lax.dynamic_index_in_dim(query_docs, device, 0, keepdims=False)
    starts = lax.dynamic_index_in_dim(ctx_pos, device, 0, keepdims=False)
    return (jnp.take(received, my_docs // pool_dev, axis=0), starts[:docs_per], jnp.take(doc_lens, my_docs))


def per_device_general(
    question_q,
    question_kv,
    doc_kv,
    doc_lens,
    query_docs,
    ctx_pos,
    hidden,
    out_proj,
    norm_gain,
    router_weight,
    w_gate_up,
    w_down,
    expert_ids,
):
    lanes = lax.axis_size("tp")
    groups = lax.axis_size("ep")
    lane = lax.axis_index("tp")
    device = lax.axis_index("ep")
    length, heads_here, head_dim = question_q.shape
    kv_heads = question_kv.shape[1]
    docs_per = query_docs.shape[1]
    width_here = hidden.shape[1]
    ids = lax.all_gather(expert_ids, "ep", axis=0, tiled=False)
    kv_pick = lane * kv_heads // lanes
    kv_head = lax.dynamic_index_in_dim(question_kv, kv_pick, 1, keepdims=False).reshape(
        length, 2 * head_dim
    )
    context, starts, lengths = context_by_row(
        doc_kv, doc_lens, query_docs, ctx_pos, device, kv_pick
    )
    question_start = lax.dynamic_index_in_dim(ctx_pos, device, 0, keepdims=False)[docs_per]
    attended = attend(question_q, kv_head, context, starts, lengths, question_start)
    projected = jnp.dot(
        lax.all_gather(attended, "tp", axis=1, tiled=True),
        lax.all_gather(out_proj, "ep", axis=0, tiled=True),
        preferred_element_type=jnp.float32,
    )
    residual = (hidden.astype(jnp.float32) + projected.astype(jnp.float32)).astype(jnp.bfloat16)

    tokens = lax.all_gather(residual, "ep", axis=0, tiled=False)
    wide = tokens.astype(jnp.float32)
    gain = norm_gain.astype(jnp.float32)
    scaled = wide * gain
    logit_part = jnp.einsum(
        "snd,de->sne", scaled, router_weight.astype(jnp.float32), precision=lax.Precision.HIGHEST
    )
    square_part = jnp.sum(wide * wide, axis=2, keepdims=True)
    stats = jnp.sum(
        lax.all_gather(jnp.concatenate([logit_part, square_part], axis=2), "tp", axis=0), axis=0
    )
    experts = router_weight.shape[1]
    inv_rms = lax.rsqrt(stats[:, :, experts] / (width_here * lanes) + norm_eps)
    logits = stats[:, :, :experts] * inv_rms[:, :, None]

    local_experts = w_gate_up.shape[0]
    capacity = length * expert_ids.shape[1] // experts
    hid = w_gate_up.shape[3]
    chosen_all = jnp.any(
        ids[:, :, :, None] == jnp.arange(experts, dtype=jnp.int32), axis=2
    )
    top = jnp.max(jnp.where(chosen_all, logits, -jnp.inf), axis=2, keepdims=True)
    weight = jnp.where(chosen_all, jnp.exp(logits - top), 0.0)
    mix = weight / jnp.sum(weight, axis=2, keepdims=True)

    shuffled, scaled_rows = (chosen_all, scaled.astype(jnp.bfloat16))
    first = device * local_experts
    chosen = lax.dynamic_slice_in_dim(shuffled, first, local_experts, 2)
    mix_here = lax.dynamic_slice_in_dim(mix, first, local_experts, 2)
    before = (jnp.arange(length)[:, None] > jnp.arange(length)[None, :]).astype(jnp.bfloat16)
    rank = jnp.einsum(
        "mn,sne->sem", before, chosen.astype(jnp.bfloat16), preferred_element_type=jnp.float32
    ).astype(jnp.int32)
    pick = jnp.logical_and(
        jnp.transpose(chosen, (0, 2, 1))[:, :, None, :],
        rank[:, :, None, :] == jnp.arange(capacity, dtype=jnp.int32)[None, None, :, None],
    )
    onehot = pick.astype(jnp.bfloat16)
    inv_row = jnp.sum(jnp.where(pick, inv_rms[:, None, None, :], 0.0), axis=3)
    mix_row = jnp.sum(jnp.where(pick, jnp.transpose(mix_here, (0, 2, 1))[:, :, None, :], 0.0), axis=3)

    rows = jnp.einsum(
        "sern,snd->serd", onehot, scaled_rows, preferred_element_type=jnp.float32
    ).astype(jnp.bfloat16)
    term = jnp.einsum(
        "serd,edgh->sergh", rows, w_gate_up, preferred_element_type=jnp.float32
    ).astype(jnp.bfloat16)
    per_lane = groups * local_experts * capacity // lanes
    term = term.reshape(lanes, per_lane, 2 * hid)
    inv_row = inv_row.reshape(lanes, per_lane, 1)
    summed = lax.psum_scatter(term, "tp", scatter_dimension=0, tiled=True)[0].astype(jnp.float32)
    inv_mine = lax.dynamic_index_in_dim(inv_row, lane, 0, keepdims=False)
    summed = summed * inv_mine
    act = (jax.nn.silu(summed[:, :hid]) * summed[:, hid:]).astype(jnp.bfloat16)
    acts = lax.all_gather(act, "tp", axis=0, tiled=False)
    acts = acts.reshape(groups, local_experts, capacity, hid)
    expert_out = jnp.einsum("serh,ehd->serd", acts, w_down, preferred_element_type=jnp.float32)
    expert_out = (expert_out * mix_row[:, :, :, None]).astype(jnp.bfloat16)
    combined = jnp.einsum(
        "sern,serd->snd", onehot, expert_out, preferred_element_type=jnp.float32
    ).astype(jnp.bfloat16)
    returned = lax.psum_scatter(combined, "ep", scatter_dimension=0, tiled=True)[0]
    return (residual.astype(jnp.float32) + returned.astype(jnp.float32)).astype(jnp.bfloat16)


def pairs(lanes, flip):
    return [(i, i ^ flip) for i in range(lanes)]


def scatter_blocks(parts, n):
    near = lax.ppermute(parts[3], "ep", pairs(n, 1))
    far = (parts[2].astype(jnp.float32) + near.astype(jnp.float32)).astype(jnp.bfloat16)
    return [parts[0], lax.ppermute(far, "ep", pairs(n, 2)), lax.ppermute(parts[1], "ep", pairs(n, 1))]


def query_of(device, lane):
    return 2 * (lane & 1) + ((lane >> 1) ^ (device & 1))


def turn(question, keys_values, device, lane, n, meanwhile):
    crosses = lambda e, t: ((e ^ t) & 1) != (t >> 1)
    devices = [(e, t) for e in range(n) for t in range(n)]
    swap = [(e * n + t, e * n + (t ^ 3)) for e, t in devices if crosses(e, t)]
    crossed = lax.ppermute(question, ("ep", "tp"), swap)
    crossed, *meanwhile = lax.optimization_barrier((crossed, *meanwhile))
    heads = jnp.where(crosses(device, lane), lane ^ 3, lane)
    picked = lax.dynamic_index_in_dim(keys_values, heads, 1, keepdims=False)
    picked = jnp.transpose(picked, (1, 0, 2)).reshape(-1, question.shape[1])
    held = jnp.where(crosses(device, lane), crossed, question)
    moves = []
    for e, t in devices:
        h = t ^ 3 if crosses(e, t) else t
        moves.append((e * n + t, h * n + 2 * ((e ^ h) & 1) + (e >> 1)))
    return (lax.ppermute(jnp.concatenate([held, picked], axis=0), ("ep", "tp"), moves), meanwhile)


def call(body, outs, scratch, **kwargs):
    return pl.pallas_call(
        body,
        out_shape=outs,
        **({} if scratch is None else {"scratch_shapes": scratch}),
        compiler_params=pltpu.CompilerParams(vmem_limit_bytes=20 * 1024 * 1024),
        cost_estimate=pl.CostEstimate(flops=1 << 20, bytes_accessed=1 << 18, transcendentals=0),
        **kwargs,
    )


VMEM = pl.BlockSpec(memory_space=pltpu.VMEM)
SMEM = pl.BlockSpec(memory_space=pltpu.SMEM)
NT = (((1,), (1,)), ((), ()))


def dot(a, b):
    return jnp.dot(a, b, preferred_element_type=jnp.float32)


def document_slots(here, query_docs, pool_dev):
    device, lane = (here[0], here[1])
    query = query_of(device, lane)
    slots = []
    for d in range(4):
        slot = jnp.int32(0)
        for j in range(query_docs.shape[1]):
            offset = query_docs[query, j] - (device ^ d) * pool_dev
            slot = jnp.where(jnp.logical_and(offset >= 0, offset < pool_dev), j, slot)
        slots.append(slot)
    return (query, slots)


def prepare_body(here, query_docs, pool, ids, *outs):
    pool_dev = pool.shape[0]
    docs_per = query_docs.shape[1]
    rows = pool.shape[2] * pool.shape[3]
    device, lane = (here[0], here[1])
    for d, out in enumerate(outs):
        target = device ^ d
        query = query_of(target, lane)
        local = jnp.int32(0)
        for j in range(docs_per):
            offset = query_docs[query, j] - device * pool_dev
            inside = jnp.logical_and(offset >= 0, offset < pool_dev)
            local = jnp.where(inside, offset, local)
        out[:rows, :] = pool[local, target].reshape(rows, pool.shape[4])
        out[rows:, :] = ids[...]


def prepare(here, query_docs, pool, ids):
    _, _, pair, doc_max, head_dim = pool.shape
    shape = jax.ShapeDtypeStruct((pair * doc_max + ids.shape[0], head_dim), jnp.bfloat16)
    return call(
        prepare_body,
        [shape] * 4,
        [],
        in_specs=[SMEM, SMEM, VMEM, VMEM],
        out_specs=[VMEM] * 4,
        name="prepare",
    )(here, query_docs, pool, ids)


def angles_body(pool_dev, here, query_docs, ctx_pos, cos_q, sin_q, cos_d, sin_d):
    query, slots = document_slots(here, query_docs, pool_dev)
    docs_per = query_docs.shape[1]
    head_dim = cos_q.shape[1]

    def fill(starts, cosine, sine):
        column = lax.broadcasted_iota(jnp.int32, cosine.shape, 1)
        half = jnp.where(column < head_dim // 2, column, column - head_dim // 2)
        freq = jnp.exp(half.astype(jnp.float32) * (-2.0 * math.log(rope_theta) / head_dim))
        angle = starts.astype(jnp.float32) * freq
        cosine[...] = jnp.cos(angle)
        wave = jnp.sin(angle)
        sine[...] = jnp.where(column < head_dim // 2, -wave, wave)

    row = lax.broadcasted_iota(jnp.int32, cos_q.shape, 0)
    fill(ctx_pos[query, docs_per] + row, cos_q, sin_q)
    row = lax.broadcasted_iota(jnp.int32, cos_d.shape, 0)
    starts = jnp.zeros(cos_d.shape, jnp.int32)
    for d, slot in enumerate(slots):
        starts = jnp.where(row == d, ctx_pos[query, slot], starts)
    fill(starts, cos_d, sin_d)


def angles(here, query_docs, ctx_pos, pool_dev, length, head_dim):
    shapes = [jax.ShapeDtypeStruct((rows, head_dim), jnp.float32) for rows in (length, length, 8, 8)]
    return call(
        functools.partial(angles_body, pool_dev),
        shapes,
        [],
        in_specs=[SMEM] * 3,
        out_specs=[VMEM] * 4,
        name="angles",
    )(here, query_docs, ctx_pos)


def attention_body(
    pool_dev, here, query_docs, doc_lens, q, c0, c1, c2, c3, cos_q, sin_q, cos_d, sin_d, out, wide, keys, vals
):
    length, head_dim = cos_q.shape
    heads = out.shape[1] // head_dim
    pieces = (c0, c1, c2, c3)
    docs = len(pieces)
    doc_max = (keys.shape[0] - length) // docs
    half = head_dim // 2
    query, slots = document_slots(here, query_docs, pool_dev)

    def turned(x, cosine, sine):
        return x * cosine + pltpu.roll(x, half, 1) * sine

    cosine, sine = (cos_q[...], sin_q[...])
    for j, piece in enumerate(pieces):
        key = turned(piece[:doc_max, :].astype(jnp.float32), cos_d[j : j + 1, :], sin_d[j : j + 1, :])
        keys[j * doc_max : (j + 1) * doc_max, :] = key.astype(jnp.bfloat16)
        vals[j * doc_max : (j + 1) * doc_max, :] = piece[doc_max : 2 * doc_max, :]
    base = docs * doc_max
    first = heads * length
    keys[base:, :] = turned(q[first : first + length, :].astype(jnp.float32), cosine, sine).astype(
        jnp.bfloat16
    )
    vals[base:, :] = q[first + length :, :]
    wide[...] = q[:first, :].astype(jnp.float32)
    column = lax.broadcasted_iota(jnp.int32, (1, doc_max), 1)
    allowed = [column < doc_lens[query_docs[query, slot]] for slot in slots]
    causal = lax.broadcasted_iota(jnp.int32, (length, length), 0) >= lax.broadcasted_iota(
        jnp.int32, (length, length), 1
    )
    for h in range(heads):
        rows = turned(wide[pl.ds(h, length, stride=heads), :], cosine, sine).astype(jnp.bfloat16)
        scores = lax.dot_general(rows, keys[...], NT, preferred_element_type=jnp.float32)
        scores = scores * head_dim ** (-0.5)
        parts = [
            jnp.where(allowed[j], scores[:, j * doc_max : (j + 1) * doc_max], -jnp.inf)
            for j in range(docs)
        ] + [jnp.where(causal, scores[:, base:], -jnp.inf)]
        scores = jnp.concatenate(parts, axis=1)
        ceiling = jnp.max(scores, axis=1, keepdims=True)
        probs = jnp.exp(scores - ceiling)
        denominator = jnp.sum(probs, axis=1, keepdims=True)
        mixed = dot(probs.astype(jnp.bfloat16), vals[...])
        out[:, h * head_dim : (h + 1) * head_dim] = (mixed / denominator).astype(jnp.bfloat16)


def attention(here, query_docs, doc_lens, q, pieces, tables, pool_dev):
    length, head_dim = tables[0].shape
    heads = q.shape[0] // length - 2
    rows = 5 * length
    return call(
        functools.partial(attention_body, pool_dev),
        jax.ShapeDtypeStruct((length, heads * head_dim), jnp.bfloat16),
        [
            pltpu.VMEM((heads * length, head_dim), jnp.float32),
            pltpu.VMEM((rows, head_dim), jnp.bfloat16),
            pltpu.VMEM((rows, head_dim), jnp.bfloat16),
        ],
        in_specs=[SMEM] * 3 + [VMEM] * 9,
        out_specs=VMEM,
        name="attention",
    )(here, query_docs, doc_lens, q, *pieces, *tables)


def project_body(here, a, b, c, d, weight, *rest):
    outs, rows = (rest[:-1], rest[-1])
    device, lane = (here[0], here[1])
    for flip, ref in zip((0, 2, 1, 3), (a, b, c, d)):
        rows[query_of(device, lane ^ flip)] = ref[...]
    for d in (2, 3, 1, 0):
        outs[d][...] = dot(rows[device ^ d], weight[...]).astype(jnp.bfloat16)


def project(here, parts, weight):
    length, depth = parts[0].shape
    return call(
        project_body,
        [jax.ShapeDtypeStruct((length, weight.shape[1]), jnp.bfloat16)] * 4,
        [pltpu.VMEM((4, length, depth), jnp.bfloat16)],
        in_specs=[SMEM] + [VMEM] * 5,
        out_specs=[VMEM] * 4,
        name="project",
    )(here, *parts, weight)


def routing_body(experts, here, c0, c1, c2, c3, pick, spread):
    _, local, capacity, length = pick.shape
    first = here[0] * local
    before = (
        lax.broadcasted_iota(jnp.int32, (length, length), 0)
        < lax.broadcasted_iota(jnp.int32, (length, length), 1)
    ).astype(jnp.bfloat16)
    place = lax.broadcasted_iota(jnp.int32, (capacity, length), 0).astype(jnp.float32)
    row = lax.broadcasted_iota(jnp.int32, (8, length), 0)
    for d, piece in enumerate((c0, c1, c2, c3)):
        ids = piece[piece.shape[0] - 16 :, :].astype(jnp.float32).astype(jnp.int32)
        chosen = jnp.zeros((8, length), jnp.float32)
        for k in range(8):
            named = jnp.logical_and(ids[k : k + 1, :] == first + row, row < local)
            chosen = jnp.where(named, 1.0, chosen)
        rank = dot(chosen.astype(jnp.bfloat16), before)
        wide = []
        for e in range(local):
            here_e = jnp.logical_and(rank[e : e + 1, :] == place, chosen[e : e + 1, :] > 0.0)
            wide.append(jnp.where(here_e, 1.0, 0.0))
            pick[d, e] = wide[-1].astype(jnp.bfloat16)
        spread[d] = jnp.transpose(jnp.concatenate(wide, axis=0)).astype(jnp.bfloat16)


def routing(here, pieces, experts, local, capacity):
    length = pieces[0].shape[1]
    rows = pieces[0].shape[0]
    return call(
        functools.partial(routing_body, experts),
        [
            jax.ShapeDtypeStruct((4, local, capacity, length), jnp.bfloat16),
            jax.ShapeDtypeStruct((4, length, local * capacity), jnp.bfloat16),
        ],
        [],
        in_specs=[SMEM] + [VMEM] * 4,
        out_specs=[VMEM] * 2,
        name="routing",
    )(here, *pieces)


def residual_body(hidden, p0, p1, p2, after, out):
    total = hidden[...].astype(jnp.float32) + p0[...].astype(jnp.float32)
    for part in (p1, p2):
        total = total + part[...].astype(jnp.float32)
    out[...] = total.astype(jnp.bfloat16)


def add_parts(hidden, parts, after):
    return call(
        residual_body,
        jax.ShapeDtypeStruct(hidden.shape, jnp.bfloat16),
        [],
        in_specs=[VMEM] * 4 + [pl.BlockSpec(memory_space=pl.ANY)],
        out_specs=VMEM,
        name="residual",
    )(hidden, *parts, after)


def measure_body(t0, t1, t2, t3, gain, router, stats):
    rows = stats.shape[0]
    length = t0.shape[0]
    for d, ref in enumerate((t0, t1, t2, t3)):
        wide = ref[...].astype(jnp.float32)
        grown = wide * gain[...]
        high = grown.astype(jnp.bfloat16)
        rest = grown - high.astype(jnp.float32)
        middle = rest.astype(jnp.bfloat16)
        low = (rest - middle.astype(jnp.float32)).astype(jnp.bfloat16)
        logits = dot(high, router[...]) + (dot(middle, router[...]) + dot(low, router[...]))
        squares = jnp.sum(wide * wide, axis=1, keepdims=True)
        column = lax.broadcasted_iota(jnp.int32, logits.shape, 1)
        both = jnp.where(column == rows - 8, squares, logits)
        stats[:, d * length : (d + 1) * length] = jnp.transpose(both)[:rows, :]


def squares_and_logits(tokens, gain, router, experts):
    n, length = (len(tokens), tokens[0].shape[0])
    return call(
        measure_body,
        jax.ShapeDtypeStruct((experts + 8, n * length), jnp.float32),
        [],
        in_specs=[VMEM] * (n + 2),
        out_specs=VMEM,
        name="stats",
    )(*tokens, gain, router)


def gate_up_body(ds, order, *refs):
    tokens = refs[: len(ds)]
    gain, pick, weight, kept, given, rows = refs[len(ds) :]
    hid = weight.shape[3]
    capacity = pick.shape[2]
    i = pl.program_id(0)
    expert = order[i]
    for k, d in enumerate(ds):
        chosen = dot(pick[d, expert], tokens[k][...]) * gain[...]
        rows[k * capacity : (k + 1) * capacity, :] = chosen.astype(jnp.bfloat16)
    for g in range(2):
        term = dot(rows[...], weight[0, g]).astype(jnp.bfloat16)
        for j in range(4):
            out = (kept, given)[j // 2]

            @pl.when(i == j)
            def _():
                out[j % 2, :, g * hid : (g + 1) * hid] = term


def gate_up(ds, order, tokens, gain, pick, weight):
    local, _, width, hid = weight.shape
    capacity = pick.shape[2]
    shape = jax.ShapeDtypeStruct((2, len(ds) * capacity, 2 * hid), jnp.bfloat16)
    whole = lambda rank: lambda i, order: (0,) * rank
    return call(
        functools.partial(gate_up_body, ds),
        [shape] * 2,
        None,
        grid_spec=pltpu.PrefetchScalarGridSpec(
            num_scalar_prefetch=1,
            grid=(local,),
            in_specs=[pl.BlockSpec(tokens[0].shape, whole(2))] * len(ds)
            + [
                pl.BlockSpec(gain.shape, whole(2)),
                pl.BlockSpec(pick.shape, whole(4)),
                pl.BlockSpec((1, 2, width, hid), lambda i, order: (order[i], 0, 0, 0)),
            ],
            out_specs=[pl.BlockSpec(shape.shape, whole(3))] * 2,
            scratch_shapes=[pltpu.VMEM((len(ds) * capacity, width), jnp.bfloat16)],
        ),
        name="gate_up",
    )(order, *tokens, gain, pick, weight)


def activate_body(groups, features, here, pick, stats, *refs):
    out = refs[-1]
    _, local, capacity, length = pick.shape
    hid = out.shape[1]
    experts = stats.shape[0] - 8
    device, lane = (here[0], here[1])
    expert = lax.broadcasted_iota(jnp.int32, (experts, length), 0)
    base, refs = (0, list(refs))
    for ds in groups:
        kept, taken, across = refs[:3]
        pieces = refs[3 : 3 + len(ds)]
        refs = refs[3 + len(ds) :]
        for k, d in enumerate(ds):
            ids = pieces[k][pieces[k].shape[0] - 16 :, :].astype(jnp.float32).astype(jnp.int32)
            chosen = jnp.zeros((experts, length), jnp.float32)
            for c in range(8):
                chosen = jnp.where(ids[c : c + 1, :] == expert, 1.0, chosen)
            block = slice(d * length, (d + 1) * length)
            inv_rms = lax.rsqrt(stats[experts : experts + 1, block] / features + norm_eps)
            logits = jnp.where(chosen > 0.0, stats[:experts, block] * inv_rms, -jnp.inf)
            grown = jnp.exp(logits - jnp.max(logits, axis=0, keepdims=True))
            mix = grown / jnp.sum(grown, axis=0, keepdims=True)
            mine = jnp.where(expert == device * local + lane, mix, 0.0)
            mix = jnp.sum(mine, axis=0, keepdims=True)
            places = pick[d, lane].astype(jnp.float32)
            inv_row = jnp.sum(places * inv_rms, axis=1, keepdims=True)
            mix_row = jnp.sum(places * mix, axis=1, keepdims=True)
            rows = slice(k * capacity, (k + 1) * capacity)
            summed = kept[0, rows, :].astype(jnp.float32) + taken[0, rows, :].astype(jnp.float32)
            summed = (summed + across[rows, :].astype(jnp.float32)) * inv_row
            gate = summed[:, :hid]
            act = gate / (1.0 + jnp.exp(-gate)) * summed[:, hid:] * mix_row
            out[base + k * capacity : base + (k + 1) * capacity, :] = act.astype(jnp.bfloat16)
        base += len(ds) * capacity


def activate(groups, features, here, sums, pick, stats, pieces):
    operands = []
    for ds, terms in zip(groups, sums):
        operands += list(terms) + [pieces[d] for d in ds]
    rows = sum(terms[2].shape[0] for terms in sums)
    return call(
        functools.partial(activate_body, groups, features),
        jax.ShapeDtypeStruct((rows, sums[0][2].shape[1] // 2), jnp.bfloat16),
        [],
        in_specs=[SMEM] + [VMEM] * (2 + len(operands)),
        out_specs=VMEM,
        name="activate",
    )(here, pick, stats, *operands)


def down_body(ds, order, a, b, c, d, spread, weight, *rest):
    outs, results = (rest[:-1], rest[-1])
    i = pl.program_id(0)
    capacity = results.shape[2]
    expert = order[i]
    for j, ref in enumerate((a, b, c, d)):

        @pl.when(i == j)
        def _():
            result = dot(ref[...], weight[0]).astype(jnp.bfloat16)
            for k in range(len(ds)):
                results[k, expert] = result[k * capacity : (k + 1) * capacity, :]

    @pl.when(i == pl.num_programs(0) - 1)
    def _():
        for k, out in enumerate(outs):
            rows = results[k].reshape(-1, results.shape[3])
            out[...] = dot(spread[ds[k]], rows).astype(jnp.bfloat16)


def down(ds, order, acts, spread, weight):
    local, hid, width = weight.shape
    capacity = acts[0].shape[0] // len(ds)
    length = spread.shape[1]
    shape = jax.ShapeDtypeStruct((length, width), jnp.bfloat16)
    whole = lambda rank: lambda i, order: (0,) * rank
    return call(
        functools.partial(down_body, ds),
        [shape] * len(ds),
        None,
        grid_spec=pltpu.PrefetchScalarGridSpec(
            num_scalar_prefetch=1,
            grid=(local,),
            in_specs=[pl.BlockSpec(acts[0].shape, whole(2))] * 4
            + [
                pl.BlockSpec(spread.shape, whole(3)),
                pl.BlockSpec((1, hid, width), lambda i, order: (order[i], 0, 0)),
            ],
            out_specs=[pl.BlockSpec(shape.shape, whole(2))] * len(ds),
            scratch_shapes=[pltpu.VMEM((len(ds), local, capacity, width), jnp.bfloat16)],
        ),
        name="down",
    )(order, *acts, spread, weight)


def per_device_square(
    question_q,
    question_kv,
    doc_kv,
    doc_lens,
    query_docs,
    ctx_pos,
    hidden,
    out_proj,
    norm_gain,
    router_weight,
    w_gate_up,
    w_down,
    expert_ids,
):
    n = 4
    lane = lax.axis_index("tp")
    device = lax.axis_index("ep")
    length, heads_here, head_dim = question_q.shape
    pool_dev = doc_kv.shape[0]
    width_here = hidden.shape[1]
    experts = router_weight.shape[1]
    local = w_gate_up.shape[0]
    capacity = length * expert_ids.shape[1] // experts
    here = jnp.stack([device, lane]).astype(jnp.int32)
    order = (lane ^ jnp.array([0, 2, 1, 3], jnp.int32)).astype(jnp.int32)

    pool = jnp.transpose(doc_kv, (0, 2, 3, 1, 4))
    ids_rows = jnp.pad(expert_ids.T.astype(jnp.bfloat16), ((0, 8), (0, 0)))
    pieces = prepare(here, query_docs, pool, ids_rows)
    q_rows, pieces = turn(
        question_q.reshape(length * heads_here, head_dim), question_kv, device, lane, n, pieces
    )
    pieces = [pieces[0]] + [lax.ppermute(pieces[d], "ep", pairs(n, d)) for d in range(1, n)]
    tables = list(angles(here, query_docs, ctx_pos, pool_dev, length, head_dim))

    one = lax.optimization_barrier(jnp.ones((), jnp.bfloat16))
    tables[0], out_proj = lax.optimization_barrier((tables[0], out_proj * one))
    attended = attention(here, query_docs, doc_lens, q_rows, pieces, tables, pool_dev)
    far = lax.ppermute(attended, "tp", pairs(n, 2))
    near = lax.ppermute(attended, "tp", pairs(n, 1))
    farther = lax.ppermute(far, "tp", pairs(n, 1))
    gain = norm_gain.astype(jnp.float32)[None, :]
    router = jnp.pad(router_weight, ((0, 0), (0, 128 - experts)))
    parts = project(here, (attended, far, near, farther), out_proj)
    kept, w_gate_up = lax.optimization_barrier((parts[0], w_gate_up))
    sent = scatter_blocks([kept] + list(parts[1:]), n)
    pick, spread = routing(here, pieces, experts, local, capacity)
    weight = jnp.transpose(w_gate_up, (0, 2, 1, 3))
    sent[0], pick, router, gain = lax.optimization_barrier((sent[0], pick, router, gain))
    residual = add_parts(hidden, sent, weight)

    tokens = [residual] + [None] * (n - 1)
    for d in (2, 3, 1):
        tokens[d] = lax.ppermute(residual, "ep", pairs(n, d))

    features = width_here * n

    def spread_act(act):
        far = lax.ppermute(act, "tp", pairs(n, 2))
        near = lax.ppermute(act, "tp", pairs(n, 1))
        return [act, far, near, lax.ppermute(far, "tp", pairs(n, 1))]

    def chip_sum(kept, taken):
        return (kept[1].astype(jnp.float32) + taken[1].astype(jnp.float32)).astype(jnp.bfloat16)

    def terms_of(ds, order):
        return gate_up(ds, order, [tokens[d] for d in ds], gain, pick, weight)

    tokens = list(lax.optimization_barrier(tuple(tokens)))
    kept, given = terms_of((2, 3), order)
    taken = lax.ppermute(given, "tp", pairs(n, 1))
    given, stats = lax.optimization_barrier((given, squares_and_logits(tokens, gain, router, experts)))
    stats_far = lax.ppermute(stats, "tp", pairs(n, 2))
    taken, stats_far = lax.optimization_barrier((taken, stats_far))
    stats = stats + stats_far
    stats_near = lax.ppermute(stats, "tp", pairs(n, 1))
    far_sum = chip_sum(kept, taken)
    across = lax.ppermute(far_sum, "tp", pairs(n, 2))

    order, _, stats_near = lax.optimization_barrier((order, far_sum, stats_near))
    stats = stats + stats_near
    kept_2, given = terms_of((0, 1), order)
    given, across = lax.optimization_barrier((given, across))
    taken_2 = lax.ppermute(given, "tp", pairs(n, 1))
    sums = [(kept, taken, across)]
    acts = spread_act(activate(((2, 3),), features, here, sums, pick, stats, pieces))
    far_sum = chip_sum(kept_2, taken_2)
    far_sum, acts[1] = lax.optimization_barrier((far_sum, acts[1]))
    acts[3] = lax.ppermute(acts[1], "tp", pairs(n, 1))
    across = lax.ppermute(far_sum, "tp", pairs(n, 2))
    parts = down((2, 3), order, acts, spread, w_down)
    near = lax.ppermute(parts[1], "ep", pairs(n, 1))
    far = (parts[0].astype(jnp.float32) + near.astype(jnp.float32)).astype(jnp.bfloat16)
    across, far = lax.optimization_barrier((across, far))
    far = lax.ppermute(far, "ep", pairs(n, 2))
    sums = [(kept_2, taken_2, across)]
    acts = spread_act(activate(((0, 1),), features, here, sums, pick, stats, pieces))
    mine, near = down((0, 1), order, acts, spread, w_down)
    returned = [mine, far, lax.ppermute(near, "ep", pairs(n, 1))]
    total = residual.astype(jnp.float32)
    for part in returned:
        total = total + part.astype(jnp.float32)
    return total.astype(jnp.bfloat16)


def solution(mesh):
    placed = (
        P(("grp", "ep"), "tp", None),
        P(("grp", "ep"), None, None, None),
        P(("grp", "ep"), None, None, None, None),
        P("grp"),
        P("grp", None),
        P("grp", None),
        P(("grp", "ep"), "tp"),
        P("ep", "tp"),
        P("tp"),
        P("tp", None),
        P("ep", "tp", None, None),
        P("ep", None, "tp"),
        P(("grp", "ep"), None),
    )
    def per_device(*args):
        square = (
            lax.axis_size("tp") == 4
            and lax.axis_size("ep") == 4
            and args[1].shape[1] == 4
            and args[4].shape == (4, 4)
        )
        return (per_device_square if square else per_device_general)(*args)

    return jax.shard_map(
        per_device, mesh=mesh, in_specs=placed, out_specs=P(("grp", "ep"), "tp"), check_vma=False
    )
```

```python
import functools
import math

import jax
import jax.numpy as jnp
from jax import lax
from jax.experimental import pallas as pl
from jax.experimental.pallas import tpu as pltpu
from jax.sharding import PartitionSpec as P

rope_theta = 1000000.0
norm_eps = 1e-06


def tables(positions, head_dim):
    half = head_dim // 2
    freq = jnp.exp(jnp.arange(half, dtype=jnp.float32) * (-2.0 * math.log(rope_theta) / head_dim))
    angle = positions.astype(jnp.float32)[:, None] * freq[None, :]
    return (jnp.cos(angle), jnp.sin(angle))


def rotate(values, positions):
    half = values.shape[-1] // 2
    cosine, sine = tables(positions, values.shape[-1])
    shape = (values.shape[0],) + (1,) * (values.ndim - 2) + (half,)
    cosine, sine = (cosine.reshape(shape), sine.reshape(shape))
    floats = values.astype(jnp.float32)
    first = floats[..., :half]
    second = floats[..., half:]
    return jnp.concatenate(
        [first * cosine - second * sine, second * cosine + first * sine], axis=-1
    )


def attend(q_rows, own_kv, context, starts, lengths, question_start):
    length, heads_here, head_dim = q_rows.shape
    docs_per, doc_max, _ = context.shape
    question_pos = question_start + jnp.arange(length, dtype=jnp.int32)
    queries = rotate(q_rows, question_pos).astype(jnp.bfloat16)
    own_keys = rotate(own_kv[:, :head_dim], question_pos).astype(jnp.bfloat16)
    positions = jnp.repeat(starts, doc_max, total_repeat_length=docs_per * doc_max)
    doc_keys = rotate(context[:, :, :head_dim].reshape(docs_per * doc_max, head_dim), positions)
    keys = jnp.concatenate([doc_keys.astype(jnp.bfloat16), own_keys], axis=0)
    values = jnp.concatenate(
        [context[:, :, head_dim:].reshape(docs_per * doc_max, head_dim), own_kv[:, head_dim:]],
        axis=0,
    )
    valid = (jnp.arange(doc_max, dtype=jnp.int32)[None, :] < lengths[:, None]).reshape(-1)
    causal = jnp.arange(length)[:, None] >= jnp.arange(length)[None, :]
    allowed = jnp.concatenate(
        [jnp.broadcast_to(valid[None, :], (length, valid.shape[0])), causal], axis=1
    )
    scores = jnp.einsum("ihd,jd->hij", queries, keys, preferred_element_type=jnp.float32)
    scores = jnp.where(allowed[None], scores * head_dim ** (-0.5), -jnp.inf)
    ceiling = jnp.max(scores, axis=-1, keepdims=True)
    probs = jnp.exp(scores - ceiling)
    denominator = jnp.sum(probs, axis=-1, keepdims=True)
    mixed = jnp.einsum(
        "hij,jd->hid", probs.astype(jnp.bfloat16), values, preferred_element_type=jnp.float32
    )
    return (
        jnp.transpose(mixed / denominator, (1, 0, 2))
        .reshape(length, heads_here * head_dim)
        .astype(jnp.bfloat16)
    )


def context_by_row(doc_kv, doc_lens, query_docs, ctx_pos, device, kv_pick):
    pool_dev, doc_max, _, pair, head_dim = doc_kv.shape
    docs_per = query_docs.shape[1]
    pool_head = lax.dynamic_index_in_dim(doc_kv, kv_pick, 2, keepdims=False).reshape(
        pool_dev, doc_max, pair * head_dim
    )
    held = device * pool_dev + jnp.arange(pool_dev, dtype=jnp.int32)
    wanted = jnp.sum((query_docs[:, :, None] == held[None, None, :]).astype(jnp.float32), axis=1)
    sending = jnp.einsum(
        "rl,lkc->rkc", wanted.astype(jnp.bfloat16), pool_head, preferred_element_type=jnp.float32
    ).astype(jnp.bfloat16)
    received = lax.all_to_all(sending, "ep", split_axis=0, concat_axis=0, tiled=True)
    my_docs = lax.dynamic_index_in_dim(query_docs, device, 0, keepdims=False)
    starts = lax.dynamic_index_in_dim(ctx_pos, device, 0, keepdims=False)
    return (jnp.take(received, my_docs // pool_dev, axis=0), starts[:docs_per], jnp.take(doc_lens, my_docs))


def per_device_general(
    question_q,
    question_kv,
    doc_kv,
    doc_lens,
    query_docs,
    ctx_pos,
    hidden,
    out_proj,
    norm_gain,
    router_weight,
    w_gate_up,
    w_down,
    expert_ids,
):
    lanes = lax.axis_size("tp")
    groups = lax.axis_size("ep")
    lane = lax.axis_index("tp")
    device = lax.axis_index("ep")
    length, heads_here, head_dim = question_q.shape
    kv_heads = question_kv.shape[1]
    docs_per = query_docs.shape[1]
    width_here = hidden.shape[1]
    ids = lax.all_gather(expert_ids, "ep", axis=0, tiled=False)
    kv_pick = lane * kv_heads // lanes
    kv_head = lax.dynamic_index_in_dim(question_kv, kv_pick, 1, keepdims=False).reshape(
        length, 2 * head_dim
    )
    context, starts, lengths = context_by_row(
        doc_kv, doc_lens, query_docs, ctx_pos, device, kv_pick
    )
    question_start = lax.dynamic_index_in_dim(ctx_pos, device, 0, keepdims=False)[docs_per]
    attended = attend(question_q, kv_head, context, starts, lengths, question_start)
    projected = jnp.dot(
        lax.all_gather(attended, "tp", axis=1, tiled=True),
        lax.all_gather(out_proj, "ep", axis=0, tiled=True),
        preferred_element_type=jnp.float32,
    )
    residual = (hidden.astype(jnp.float32) + projected.astype(jnp.float32)).astype(jnp.bfloat16)

    tokens = lax.all_gather(residual, "ep", axis=0, tiled=False)
    wide = tokens.astype(jnp.float32)
    gain = norm_gain.astype(jnp.float32)
    scaled = wide * gain
    logit_part = jnp.einsum(
        "snd,de->sne", scaled, router_weight.astype(jnp.float32), precision=lax.Precision.HIGHEST
    )
    square_part = jnp.sum(wide * wide, axis=2, keepdims=True)
    stats = jnp.sum(
        lax.all_gather(jnp.concatenate([logit_part, square_part], axis=2), "tp", axis=0), axis=0
    )
    experts = router_weight.shape[1]
    inv_rms = lax.rsqrt(stats[:, :, experts] / (width_here * lanes) + norm_eps)
    logits = stats[:, :, :experts] * inv_rms[:, :, None]

    local_experts = w_gate_up.shape[0]
    capacity = length * expert_ids.shape[1] // experts
    hid = w_gate_up.shape[3]
    chosen_all = jnp.any(
        ids[:, :, :, None] == jnp.arange(experts, dtype=jnp.int32), axis=2
    )
    top = jnp.max(jnp.where(chosen_all, logits, -jnp.inf), axis=2, keepdims=True)
    weight = jnp.where(chosen_all, jnp.exp(logits - top), 0.0)
    mix = weight / jnp.sum(weight, axis=2, keepdims=True)

    shuffled, scaled_rows = (chosen_all, scaled.astype(jnp.bfloat16))
    first = device * local_experts
    chosen = lax.dynamic_slice_in_dim(shuffled, first, local_experts, 2)
    mix_here = lax.dynamic_slice_in_dim(mix, first, local_experts, 2)
    before = (jnp.arange(length)[:, None] > jnp.arange(length)[None, :]).astype(jnp.bfloat16)
    rank = jnp.einsum(
        "mn,sne->sem", before, chosen.astype(jnp.bfloat16), preferred_element_type=jnp.float32
    ).astype(jnp.int32)
    pick = jnp.logical_and(
        jnp.transpose(chosen, (0, 2, 1))[:, :, None, :],
        rank[:, :, None, :] == jnp.arange(capacity, dtype=jnp.int32)[None, None, :, None],
    )
    onehot = pick.astype(jnp.bfloat16)
    inv_row = jnp.sum(jnp.where(pick, inv_rms[:, None, None, :], 0.0), axis=3)
    mix_row = jnp.sum(jnp.where(pick, jnp.transpose(mix_here, (0, 2, 1))[:, :, None, :], 0.0), axis=3)

    rows = jnp.einsum(
        "sern,snd->serd", onehot, scaled_rows, preferred_element_type=jnp.float32
    ).astype(jnp.bfloat16)
    term = jnp.einsum(
        "serd,edgh->sergh", rows, w_gate_up, preferred_element_type=jnp.float32
    ).astype(jnp.bfloat16)
    per_lane = groups * local_experts * capacity // lanes
    term = term.reshape(lanes, per_lane, 2 * hid)
    inv_row = inv_row.reshape(lanes, per_lane, 1)
    summed = lax.psum_scatter(term, "tp", scatter_dimension=0, tiled=True)[0].astype(jnp.float32)
    inv_mine = lax.dynamic_index_in_dim(inv_row, lane, 0, keepdims=False)
    summed = summed * inv_mine
    act = (jax.nn.silu(summed[:, :hid]) * summed[:, hid:]).astype(jnp.bfloat16)
    acts = lax.all_gather(act, "tp", axis=0, tiled=False)
    acts = acts.reshape(groups, local_experts, capacity, hid)
    expert_out = jnp.einsum("serh,ehd->serd", acts, w_down, preferred_element_type=jnp.float32)
    expert_out = (expert_out * mix_row[:, :, :, None]).astype(jnp.bfloat16)
    combined = jnp.einsum(
        "sern,serd->snd", onehot, expert_out, preferred_element_type=jnp.float32
    ).astype(jnp.bfloat16)
    returned = lax.psum_scatter(combined, "ep", scatter_dimension=0, tiled=True)[0]
    return (residual.astype(jnp.float32) + returned.astype(jnp.float32)).astype(jnp.bfloat16)


def pairs(lanes, flip):
    return [(i, i ^ flip) for i in range(lanes)]


def scatter_blocks(parts, n):
    near = lax.ppermute(parts[3], "ep", pairs(n, 1))
    far = (parts[2].astype(jnp.float32) + near.astype(jnp.float32)).astype(jnp.bfloat16)
    return [parts[0], lax.ppermute(far, "ep", pairs(n, 2)), lax.ppermute(parts[1], "ep", pairs(n, 1))]


def query_of(device, lane):
    return 2 * (lane & 1) + ((lane >> 1) ^ (device & 1))


def turn(question, keys_values, device, lane, n, meanwhile):
    crosses = lambda e, t: ((e ^ t) & 1) != (t >> 1)
    devices = [(e, t) for e in range(n) for t in range(n)]
    swap = [(e * n + t, e * n + (t ^ 3)) for e, t in devices if crosses(e, t)]
    crossed = lax.ppermute(question, ("ep", "tp"), swap)
    crossed, *meanwhile = lax.optimization_barrier((crossed, *meanwhile))
    heads = jnp.where(crosses(device, lane), lane ^ 3, lane)
    picked = lax.dynamic_index_in_dim(keys_values, heads, 1, keepdims=False)
    picked = jnp.transpose(picked, (1, 0, 2)).reshape(-1, question.shape[1])
    held = jnp.where(crosses(device, lane), crossed, question)
    moves = []
    for e, t in devices:
        h = t ^ 3 if crosses(e, t) else t
        moves.append((e * n + t, h * n + 2 * ((e ^ h) & 1) + (e >> 1)))
    return (lax.ppermute(jnp.concatenate([held, picked], axis=0), ("ep", "tp"), moves), meanwhile)


def call(body, outs, scratch, **kwargs):
    return pl.pallas_call(
        body,
        out_shape=outs,
        **({} if scratch is None else {"scratch_shapes": scratch}),
        compiler_params=pltpu.CompilerParams(vmem_limit_bytes=20 * 1024 * 1024),
        cost_estimate=pl.CostEstimate(flops=1 << 20, bytes_accessed=1 << 18, transcendentals=0),
        **kwargs,
    )


VMEM = pl.BlockSpec(memory_space=pltpu.VMEM)
SMEM = pl.BlockSpec(memory_space=pltpu.SMEM)
NT = (((1,), (1,)), ((), ()))


def dot(a, b):
    return jnp.dot(a, b, preferred_element_type=jnp.float32)


def document_slots(here, query_docs, pool_dev):
    device, lane = (here[0], here[1])
    query = query_of(device, lane)
    slots = []
    for d in range(4):
        slot = jnp.int32(0)
        for j in range(query_docs.shape[1]):
            offset = query_docs[query, j] - (device ^ d) * pool_dev
            slot = jnp.where(jnp.logical_and(offset >= 0, offset < pool_dev), j, slot)
        slots.append(slot)
    return (query, slots)


def prepare_body(here, query_docs, pool, ids, *outs):
    pool_dev = pool.shape[0]
    docs_per = query_docs.shape[1]
    rows = pool.shape[2] * pool.shape[3]
    device, lane = (here[0], here[1])
    for d, out in enumerate(outs):
        target = device ^ d
        query = query_of(target, lane)
        local = jnp.int32(0)
        for j in range(docs_per):
            offset = query_docs[query, j] - device * pool_dev
            inside = jnp.logical_and(offset >= 0, offset < pool_dev)
            local = jnp.where(inside, offset, local)
        out[:rows, :] = pool[local, target].reshape(rows, pool.shape[4])
        out[rows:, :] = ids[...]


def prepare(here, query_docs, pool, ids):
    _, _, pair, doc_max, head_dim = pool.shape
    shape = jax.ShapeDtypeStruct((pair * doc_max + ids.shape[0], head_dim), jnp.bfloat16)
    return call(
        prepare_body,
        [shape] * 4,
        [],
        in_specs=[SMEM, SMEM, VMEM, VMEM],
        out_specs=[VMEM] * 4,
        name="prepare",
    )(here, query_docs, pool, ids)


def angles_body(pool_dev, here, query_docs, ctx_pos, cos_q, sin_q, cos_d, sin_d):
    query, slots = document_slots(here, query_docs, pool_dev)
    docs_per = query_docs.shape[1]
    head_dim = cos_q.shape[1]

    def fill(starts, cosine, sine):
        column = lax.broadcasted_iota(jnp.int32, cosine.shape, 1)
        half = jnp.where(column < head_dim // 2, column, column - head_dim // 2)
        freq = jnp.exp(half.astype(jnp.float32) * (-2.0 * math.log(rope_theta) / head_dim))
        angle = starts.astype(jnp.float32) * freq
        cosine[...] = jnp.cos(angle)
        wave = jnp.sin(angle)
        sine[...] = jnp.where(column < head_dim // 2, -wave, wave)

    row = lax.broadcasted_iota(jnp.int32, cos_q.shape, 0)
    fill(ctx_pos[query, docs_per] + row, cos_q, sin_q)
    row = lax.broadcasted_iota(jnp.int32, cos_d.shape, 0)
    starts = jnp.zeros(cos_d.shape, jnp.int32)
    for d, slot in enumerate(slots):
        starts = jnp.where(row == d, ctx_pos[query, slot], starts)
    fill(starts, cos_d, sin_d)


def angles(here, query_docs, ctx_pos, pool_dev, length, head_dim):
    shapes = [jax.ShapeDtypeStruct((rows, head_dim), jnp.float32) for rows in (length, length, 8, 8)]
    return call(
        functools.partial(angles_body, pool_dev),
        shapes,
        [],
        in_specs=[SMEM] * 3,
        out_specs=[VMEM] * 4,
        name="angles",
    )(here, query_docs, ctx_pos)


def attention_body(
    pool_dev, here, query_docs, doc_lens, q, c0, c1, c2, c3, cos_q, sin_q, cos_d, sin_d, out, wide, keys, vals
):
    length, head_dim = cos_q.shape
    heads = out.shape[1] // head_dim
    pieces = (c0, c1, c2, c3)
    docs = len(pieces)
    doc_max = (keys.shape[0] - length) // docs
    half = head_dim // 2
    query, slots = document_slots(here, query_docs, pool_dev)

    def turned(x, cosine, sine):
        return x * cosine + pltpu.roll(x, half, 1) * sine

    cosine, sine = (cos_q[...], sin_q[...])
    for j, piece in enumerate(pieces):
        key = turned(piece[:doc_max, :].astype(jnp.float32), cos_d[j : j + 1, :], sin_d[j : j + 1, :])
        keys[j * doc_max : (j + 1) * doc_max, :] = key.astype(jnp.bfloat16)
        vals[j * doc_max : (j + 1) * doc_max, :] = piece[doc_max : 2 * doc_max, :]
    base = docs * doc_max
    first = heads * length
    keys[base:, :] = turned(q[first : first + length, :].astype(jnp.float32), cosine, sine).astype(
        jnp.bfloat16
    )
    vals[base:, :] = q[first + length :, :]
    wide[...] = q[:first, :].astype(jnp.float32)
    column = lax.broadcasted_iota(jnp.int32, (1, doc_max), 1)
    allowed = [column < doc_lens[query_docs[query, slot]] for slot in slots]
    causal = lax.broadcasted_iota(jnp.int32, (length, length), 0) >= lax.broadcasted_iota(
        jnp.int32, (length, length), 1
    )
    for h in range(heads):
        rows = turned(wide[pl.ds(h, length, stride=heads), :], cosine, sine).astype(jnp.bfloat16)
        scores = lax.dot_general(rows, keys[...], NT, preferred_element_type=jnp.float32)
        scores = scores * head_dim ** (-0.5)
        parts = [
            jnp.where(allowed[j], scores[:, j * doc_max : (j + 1) * doc_max], -jnp.inf)
            for j in range(docs)
        ] + [jnp.where(causal, scores[:, base:], -jnp.inf)]
        scores = jnp.concatenate(parts, axis=1)
        ceiling = jnp.max(scores, axis=1, keepdims=True)
        probs = jnp.exp(scores - ceiling)
        denominator = jnp.sum(probs, axis=1, keepdims=True)
        mixed = dot(probs.astype(jnp.bfloat16), vals[...])
        out[:, h * head_dim : (h + 1) * head_dim] = (mixed / denominator).astype(jnp.bfloat16)


def attention(here, query_docs, doc_lens, q, pieces, tables, pool_dev):
    length, head_dim = tables[0].shape
    heads = q.shape[0] // length - 2
    rows = 5 * length
    return call(
        functools.partial(attention_body, pool_dev),
        jax.ShapeDtypeStruct((length, heads * head_dim), jnp.bfloat16),
        [
            pltpu.VMEM((heads * length, head_dim), jnp.float32),
            pltpu.VMEM((rows, head_dim), jnp.bfloat16),
            pltpu.VMEM((rows, head_dim), jnp.bfloat16),
        ],
        in_specs=[SMEM] * 3 + [VMEM] * 9,
        out_specs=VMEM,
        name="attention",
    )(here, query_docs, doc_lens, q, *pieces, *tables)


def project_body(here, a, b, c, d, weight, *rest):
    outs, rows = (rest[:-1], rest[-1])
    device, lane = (here[0], here[1])
    for flip, ref in zip((0, 2, 1, 3), (a, b, c, d)):
        rows[query_of(device, lane ^ flip)] = ref[...]
    for d in (2, 3, 1, 0):
        outs[d][...] = dot(rows[device ^ d], weight[...]).astype(jnp.bfloat16)


def project(here, parts, weight):
    length, depth = parts[0].shape
    return call(
        project_body,
        [jax.ShapeDtypeStruct((length, weight.shape[1]), jnp.bfloat16)] * 4,
        [pltpu.VMEM((4, length, depth), jnp.bfloat16)],
        in_specs=[SMEM] + [VMEM] * 5,
        out_specs=[VMEM] * 4,
        name="project",
    )(here, *parts, weight)


def routing_body(experts, here, c0, c1, c2, c3, pick, spread):
    _, local, capacity, length = pick.shape
    first = here[0] * local
    before = (
        lax.broadcasted_iota(jnp.int32, (length, length), 0)
        < lax.broadcasted_iota(jnp.int32, (length, length), 1)
    ).astype(jnp.bfloat16)
    place = lax.broadcasted_iota(jnp.int32, (capacity, length), 0).astype(jnp.float32)
    row = lax.broadcasted_iota(jnp.int32, (8, length), 0)
    for d, piece in enumerate((c0, c1, c2, c3)):
        ids = piece[piece.shape[0] - 16 :, :].astype(jnp.float32).astype(jnp.int32)
        chosen = jnp.zeros((8, length), jnp.float32)
        for k in range(8):
            named = jnp.logical_and(ids[k : k + 1, :] == first + row, row < local)
            chosen = jnp.where(named, 1.0, chosen)
        rank = dot(chosen.astype(jnp.bfloat16), before)
        wide = []
        for e in range(local):
            here_e = jnp.logical_and(rank[e : e + 1, :] == place, chosen[e : e + 1, :] > 0.0)
            wide.append(jnp.where(here_e, 1.0, 0.0))
            pick[d, e] = wide[-1].astype(jnp.bfloat16)
        spread[d] = jnp.transpose(jnp.concatenate(wide, axis=0)).astype(jnp.bfloat16)


def routing(here, pieces, experts, local, capacity):
    length = pieces[0].shape[1]
    rows = pieces[0].shape[0]
    return call(
        functools.partial(routing_body, experts),
        [
            jax.ShapeDtypeStruct((4, local, capacity, length), jnp.bfloat16),
            jax.ShapeDtypeStruct((4, length, local * capacity), jnp.bfloat16),
        ],
        [],
        in_specs=[SMEM] + [VMEM] * 4,
        out_specs=[VMEM] * 2,
        name="routing",
    )(here, *pieces)


def residual_body(hidden, p0, p1, p2, after, out):
    total = hidden[...].astype(jnp.float32) + p0[...].astype(jnp.float32)
    for part in (p1, p2):
        total = total + part[...].astype(jnp.float32)
    out[...] = total.astype(jnp.bfloat16)


def add_parts(hidden, parts, after):
    return call(
        residual_body,
        jax.ShapeDtypeStruct(hidden.shape, jnp.bfloat16),
        [],
        in_specs=[VMEM] * 4 + [pl.BlockSpec(memory_space=pl.ANY)],
        out_specs=VMEM,
        name="residual",
    )(hidden, *parts, after)


def measure_body(*refs):
    *tokens, gain, router, stats = refs
    rows = stats.shape[0]
    length = tokens[0].shape[0]
    for d, ref in enumerate(tokens):
        wide = ref[...].astype(jnp.float32)
        grown = wide * gain[...]
        high = grown.astype(jnp.bfloat16)
        rest = grown - high.astype(jnp.float32)
        middle = rest.astype(jnp.bfloat16)
        low = (rest - middle.astype(jnp.float32)).astype(jnp.bfloat16)
        logits = dot(high, router[...]) + (dot(middle, router[...]) + dot(low, router[...]))
        squares = jnp.sum(wide * wide, axis=1, keepdims=True)
        column = lax.broadcasted_iota(jnp.int32, logits.shape, 1)
        both = jnp.where(column == rows - 8, squares, logits)
        stats[:, d * length : (d + 1) * length] = jnp.transpose(both)[:rows, :]


def squares_and_logits(tokens, gain, router, experts):
    n, length = (len(tokens), tokens[0].shape[0])
    return call(
        measure_body,
        jax.ShapeDtypeStruct((experts + 8, n * length), jnp.float32),
        [],
        in_specs=[VMEM] * (n + 2),
        out_specs=VMEM,
        name="stats",
    )(*tokens, gain, router)


def gate_up_body(ds, order, *refs):
    tokens = refs[: len(ds)]
    gain, pick, weight, kept, given, rows = refs[len(ds) :]
    hid = weight.shape[3]
    capacity = pick.shape[2]
    i = pl.program_id(0)
    expert = order[i]
    for k, d in enumerate(ds):
        chosen = dot(pick[d, expert], tokens[k][...]) * gain[...]
        rows[k * capacity : (k + 1) * capacity, :] = chosen.astype(jnp.bfloat16)
    for g in range(2):
        term = dot(rows[...], weight[0, g]).astype(jnp.bfloat16)
        for j in range(4):
            out = (kept, given)[j // 2]

            @pl.when(i == j)
            def _():
                out[j % 2, :, g * hid : (g + 1) * hid] = term


def gate_up(ds, order, tokens, gain, pick, weight):
    local, _, width, hid = weight.shape
    capacity = pick.shape[2]
    shape = jax.ShapeDtypeStruct((2, len(ds) * capacity, 2 * hid), jnp.bfloat16)
    whole = lambda rank: lambda i, order: (0,) * rank
    return call(
        functools.partial(gate_up_body, ds),
        [shape] * 2,
        None,
        grid_spec=pltpu.PrefetchScalarGridSpec(
            num_scalar_prefetch=1,
            grid=(local,),
            in_specs=[pl.BlockSpec(tokens[0].shape, whole(2))] * len(ds)
            + [
                pl.BlockSpec(gain.shape, whole(2)),
                pl.BlockSpec(pick.shape, whole(4)),
                pl.BlockSpec((1, 2, width, hid), lambda i, order: (order[i], 0, 0, 0)),
            ],
            out_specs=[pl.BlockSpec(shape.shape, whole(3))] * 2,
            scratch_shapes=[pltpu.VMEM((len(ds) * capacity, width), jnp.bfloat16)],
        ),
        name="gate_up",
    )(order, *tokens, gain, pick, weight)


def activate_body(groups, features, here, pick, stats, *refs):
    out = refs[-1]
    _, local, capacity, length = pick.shape
    hid = out.shape[1]
    experts = stats.shape[0] - 8
    device, lane = (here[0], here[1])
    expert = lax.broadcasted_iota(jnp.int32, (experts, length), 0)
    base, refs = (0, list(refs))
    for ds in groups:
        kept, taken, across = refs[:3]
        pieces = refs[3 : 3 + len(ds)]
        refs = refs[3 + len(ds) :]
        for k, d in enumerate(ds):
            ids = pieces[k][pieces[k].shape[0] - 16 :, :].astype(jnp.float32).astype(jnp.int32)
            chosen = jnp.zeros((experts, length), jnp.float32)
            for c in range(8):
                chosen = jnp.where(ids[c : c + 1, :] == expert, 1.0, chosen)
            block = slice((base // capacity + k) * length, (base // capacity + k + 1) * length)
            inv_rms = lax.rsqrt(stats[experts : experts + 1, block] / features + norm_eps)
            logits = jnp.where(chosen > 0.0, stats[:experts, block] * inv_rms, -jnp.inf)
            grown = jnp.exp(logits - jnp.max(logits, axis=0, keepdims=True))
            mix = grown / jnp.sum(grown, axis=0, keepdims=True)
            mine = jnp.where(expert == device * local + lane, mix, 0.0)
            mix = jnp.sum(mine, axis=0, keepdims=True)
            places = pick[d, lane].astype(jnp.float32)
            inv_row = jnp.sum(places * inv_rms, axis=1, keepdims=True)
            mix_row = jnp.sum(places * mix, axis=1, keepdims=True)
            rows = slice(k * capacity, (k + 1) * capacity)
            summed = kept[0, rows, :].astype(jnp.float32) + taken[0, rows, :].astype(jnp.float32)
            summed = (summed + across[rows, :].astype(jnp.float32)) * inv_row
            gate = summed[:, :hid]
            act = gate / (1.0 + jnp.exp(-gate)) * summed[:, hid:] * mix_row
            out[base + k * capacity : base + (k + 1) * capacity, :] = act.astype(jnp.bfloat16)
        base += len(ds) * capacity


def activate(groups, features, here, sums, pick, stats, pieces):
    operands = []
    for ds, terms in zip(groups, sums):
        operands += list(terms) + [pieces[d] for d in ds]
    rows = sum(terms[2].shape[0] for terms in sums)
    return call(
        functools.partial(activate_body, groups, features),
        jax.ShapeDtypeStruct((rows, sums[0][2].shape[1] // 2), jnp.bfloat16),
        [],
        in_specs=[SMEM] + [VMEM] * (2 + len(operands)),
        out_specs=VMEM,
        name="activate",
    )(here, pick, stats, *operands)


def down_body(ds, order, a, b, c, d, spread, weight, *rest):
    outs, results = (rest[:-1], rest[-1])
    i = pl.program_id(0)
    capacity = results.shape[2]
    expert = order[i]
    for j, ref in enumerate((a, b, c, d)):

        @pl.when(i == j)
        def _():
            result = dot(ref[...], weight[0]).astype(jnp.bfloat16)
            for k in range(len(ds)):
                results[k, expert] = result[k * capacity : (k + 1) * capacity, :]

    @pl.when(i == pl.num_programs(0) - 1)
    def _():
        half = spread.shape[1] // 2
        for k, d in enumerate(ds):
            rows = results[k].reshape(-1, results.shape[3])
            block = dot(spread[d], rows).astype(jnp.bfloat16)
            if k < len(ds) - 1:
                outs[k][...] = block
            elif len(outs) == len(ds):
                outs[k][...] = block
            else:
                outs[k][...] = block[:half]
                outs[k + 1][...] = block[half:]


def down(ds, order, acts, spread, weight, halved=False):
    local, hid, width = weight.shape
    capacity = acts[0].shape[0] // len(ds)
    length = spread.shape[1]
    shape = jax.ShapeDtypeStruct((length, width), jnp.bfloat16)
    half = jax.ShapeDtypeStruct((length // 2, width), jnp.bfloat16)
    shapes = [shape] * (len(ds) - 1) + [half] * 2 if halved else [shape] * len(ds)
    whole = lambda rank: lambda i, order: (0,) * rank
    return call(
        functools.partial(down_body, ds),
        shapes,
        None,
        grid_spec=pltpu.PrefetchScalarGridSpec(
            num_scalar_prefetch=1,
            grid=(local,),
            in_specs=[pl.BlockSpec(acts[0].shape, whole(2))] * 4
            + [
                pl.BlockSpec(spread.shape, whole(3)),
                pl.BlockSpec((1, hid, width), lambda i, order: (order[i], 0, 0)),
            ],
            out_specs=[pl.BlockSpec(s.shape, whole(2)) for s in shapes],
            scratch_shapes=[pltpu.VMEM((len(ds), local, capacity, width), jnp.bfloat16)],
        ),
        name="down",
    )(order, *acts, spread, weight)


def per_device_square(
    question_q,
    question_kv,
    doc_kv,
    doc_lens,
    query_docs,
    ctx_pos,
    hidden,
    out_proj,
    norm_gain,
    router_weight,
    w_gate_up,
    w_down,
    expert_ids,
):
    n = 4
    lane = lax.axis_index("tp")
    device = lax.axis_index("ep")
    length, heads_here, head_dim = question_q.shape
    pool_dev = doc_kv.shape[0]
    width_here = hidden.shape[1]
    experts = router_weight.shape[1]
    local = w_gate_up.shape[0]
    capacity = length * expert_ids.shape[1] // experts
    here = jnp.stack([device, lane]).astype(jnp.int32)
    order = (lane ^ jnp.array([0, 2, 1, 3], jnp.int32)).astype(jnp.int32)

    pool = jnp.transpose(doc_kv, (0, 2, 3, 1, 4))
    ids_rows = jnp.pad(expert_ids.T.astype(jnp.bfloat16), ((0, 8), (0, 0)))
    pieces = prepare(here, query_docs, pool, ids_rows)
    q_rows, pieces = turn(
        question_q.reshape(length * heads_here, head_dim), question_kv, device, lane, n, pieces
    )
    pieces = [pieces[0]] + [lax.ppermute(pieces[d], "ep", pairs(n, d)) for d in range(1, n)]
    tables = list(angles(here, query_docs, ctx_pos, pool_dev, length, head_dim))

    one = lax.optimization_barrier(jnp.ones((), jnp.bfloat16))
    tables[0], out_proj = lax.optimization_barrier((tables[0], out_proj * one))
    attended = attention(here, query_docs, doc_lens, q_rows, pieces, tables, pool_dev)
    far = lax.ppermute(attended, "tp", pairs(n, 2))
    near = lax.ppermute(attended, "tp", pairs(n, 1))
    farther = lax.ppermute(far, "tp", pairs(n, 1))
    gain = norm_gain.astype(jnp.float32)[None, :]
    router = jnp.pad(router_weight, ((0, 0), (0, 128 - experts)))
    parts = project(here, (attended, far, near, farther), out_proj)
    kept, w_gate_up = lax.optimization_barrier((parts[0], w_gate_up))
    sent = scatter_blocks([kept] + list(parts[1:]), n)
    pick, spread = routing(here, pieces, experts, local, capacity)
    weight = jnp.transpose(w_gate_up, (0, 2, 1, 3))
    sent[0], pick, router, gain = lax.optimization_barrier((sent[0], pick, router, gain))
    residual = add_parts(hidden, sent, weight)

    tokens = [residual] + [None] * (n - 1)
    for d in (2, 1):
        tokens[d] = lax.ppermute(residual, "ep", pairs(n, d))
    tokens[3] = lax.ppermute(tokens[2], "ep", pairs(n, 1))

    features = width_here * n

    def spread_act(act):
        far = lax.ppermute(act, "tp", pairs(n, 2))
        near = lax.ppermute(act, "tp", pairs(n, 1))
        return [act, far, near, lax.ppermute(far, "tp", pairs(n, 1))]

    def chip_sum(kept, taken):
        return (kept[1].astype(jnp.float32) + taken[1].astype(jnp.float32)).astype(jnp.bfloat16)

    def terms_of(ds, order):
        return gate_up(ds, order, [tokens[d] for d in ds], gain, pick, weight)

    def stats_of(ds):
        return squares_and_logits([tokens[d] for d in ds], gain, router, experts)

    one_chunk, two_chunk = ((1, 2), (0, 3))
    kept, given = terms_of(one_chunk, order)
    taken = lax.ppermute(given, "tp", pairs(n, 1))
    _, stats = lax.optimization_barrier((given, stats_of(one_chunk)))
    stats_far = lax.ppermute(stats, "tp", pairs(n, 2))
    taken, stats_far = lax.optimization_barrier((taken, stats_far))
    stats = stats + stats_far
    stats_near = lax.ppermute(stats, "tp", pairs(n, 1))
    far_sum = chip_sum(kept, taken)
    across = lax.ppermute(far_sum, "tp", pairs(n, 2))

    order, _, stats_near = lax.optimization_barrier((order, far_sum, stats_near))
    stats = stats + stats_near
    kept_2, given = terms_of(two_chunk, order)
    stats_2 = stats_of(two_chunk)
    given, across, stats_2 = lax.optimization_barrier((given, across, stats_2))
    stats_far = lax.ppermute(stats_2, "tp", pairs(n, 2))
    taken_2 = lax.ppermute(given, "tp", pairs(n, 1))
    sums = [(kept, taken, across)]
    acts = spread_act(activate((one_chunk,), features, here, sums, pick, stats, pieces))
    far_sum = chip_sum(kept_2, taken_2)
    far_sum, stats_far, acts[1] = lax.optimization_barrier((far_sum, stats_far, acts[1]))
    stats_2 = stats_2 + stats_far
    stats_near = lax.ppermute(stats_2, "tp", pairs(n, 1))
    acts[3] = lax.ppermute(acts[1], "tp", pairs(n, 1))
    across = lax.ppermute(far_sum, "tp", pairs(n, 2))
    near, *far = down(one_chunk, order, acts, spread, w_down, halved=True)
    far = [lax.ppermute(part, "ep", pairs(n, 2)) for part in far]
    across, far[0] = lax.optimization_barrier((across, far[0]))
    near = lax.ppermute(near, "ep", pairs(n, 1))
    sums = [(kept_2, taken_2, across)]
    stats_2 = stats_2 + stats_near
    acts = spread_act(activate((two_chunk,), features, here, sums, pick, stats_2, pieces))
    acts[3], far[1] = lax.optimization_barrier((acts[3], far[1]))
    mine, last = down(two_chunk, order, acts, spread, w_down)
    last = lax.ppermute(last, "ep", pairs(n, 3))
    returned = [mine, near, jnp.concatenate(far, axis=0), last]
    total = residual.astype(jnp.float32)
    for part in returned:
        total = total + part.astype(jnp.float32)
    return total.astype(jnp.bfloat16)


def solution(mesh):
    placed = (
        P(("grp", "ep"), "tp", None),
        P(("grp", "ep"), None, None, None),
        P(("grp", "ep"), None, None, None, None),
        P("grp"),
        P("grp", None),
        P("grp", None),
        P(("grp", "ep"), "tp"),
        P("ep", "tp"),
        P("tp"),
        P("tp", None),
        P("ep", "tp", None, None),
        P("ep", None, "tp"),
        P(("grp", "ep"), None),
    )
    def per_device(*args):
        square = (
            lax.axis_size("tp") == 4
            and lax.axis_size("ep") == 4
            and args[1].shape[1] == 4
            and args[4].shape == (4, 4)
        )
        return (per_device_square if square else per_device_general)(*args)

    return jax.shard_map(
        per_device, mesh=mesh, in_specs=placed, out_specs=P(("grp", "ep"), "tp"), check_vma=False
    )
```

```python
import functools
import math

import jax
import jax.numpy as jnp
from jax import lax
from jax.experimental import pallas as pl
from jax.experimental.pallas import tpu as pltpu
from jax.sharding import PartitionSpec as P

rope_theta = 1000000.0
norm_eps = 1e-06


def tables(positions, head_dim):
    half = head_dim // 2
    freq = jnp.exp(jnp.arange(half, dtype=jnp.float32) * (-2.0 * math.log(rope_theta) / head_dim))
    angle = positions.astype(jnp.float32)[:, None] * freq[None, :]
    return (jnp.cos(angle), jnp.sin(angle))


def rotate(values, positions):
    half = values.shape[-1] // 2
    cosine, sine = tables(positions, values.shape[-1])
    shape = (values.shape[0],) + (1,) * (values.ndim - 2) + (half,)
    cosine, sine = (cosine.reshape(shape), sine.reshape(shape))
    floats = values.astype(jnp.float32)
    first = floats[..., :half]
    second = floats[..., half:]
    return jnp.concatenate(
        [first * cosine - second * sine, second * cosine + first * sine], axis=-1
    )


def attend(q_rows, own_kv, context, starts, lengths, question_start):
    length, heads_here, head_dim = q_rows.shape
    docs_per, doc_max, _ = context.shape
    question_pos = question_start + jnp.arange(length, dtype=jnp.int32)
    queries = rotate(q_rows, question_pos).astype(jnp.bfloat16)
    own_keys = rotate(own_kv[:, :head_dim], question_pos).astype(jnp.bfloat16)
    positions = jnp.repeat(starts, doc_max, total_repeat_length=docs_per * doc_max)
    doc_keys = rotate(context[:, :, :head_dim].reshape(docs_per * doc_max, head_dim), positions)
    keys = jnp.concatenate([doc_keys.astype(jnp.bfloat16), own_keys], axis=0)
    values = jnp.concatenate(
        [context[:, :, head_dim:].reshape(docs_per * doc_max, head_dim), own_kv[:, head_dim:]],
        axis=0,
    )
    valid = (jnp.arange(doc_max, dtype=jnp.int32)[None, :] < lengths[:, None]).reshape(-1)
    causal = jnp.arange(length)[:, None] >= jnp.arange(length)[None, :]
    allowed = jnp.concatenate(
        [jnp.broadcast_to(valid[None, :], (length, valid.shape[0])), causal], axis=1
    )
    scores = jnp.einsum("ihd,jd->hij", queries, keys, preferred_element_type=jnp.float32)
    scores = jnp.where(allowed[None], scores * head_dim ** (-0.5), -jnp.inf)
    ceiling = jnp.max(scores, axis=-1, keepdims=True)
    probs = jnp.exp(scores - ceiling)
    denominator = jnp.sum(probs, axis=-1, keepdims=True)
    mixed = jnp.einsum(
        "hij,jd->hid", probs.astype(jnp.bfloat16), values, preferred_element_type=jnp.float32
    )
    return (
        jnp.transpose(mixed / denominator, (1, 0, 2))
        .reshape(length, heads_here * head_dim)
        .astype(jnp.bfloat16)
    )


def context_by_row(doc_kv, doc_lens, query_docs, ctx_pos, device, kv_pick):
    pool_dev, doc_max, _, pair, head_dim = doc_kv.shape
    docs_per = query_docs.shape[1]
    pool_head = lax.dynamic_index_in_dim(doc_kv, kv_pick, 2, keepdims=False).reshape(
        pool_dev, doc_max, pair * head_dim
    )
    held = device * pool_dev + jnp.arange(pool_dev, dtype=jnp.int32)
    wanted = jnp.sum((query_docs[:, :, None] == held[None, None, :]).astype(jnp.float32), axis=1)
    sending = jnp.einsum(
        "rl,lkc->rkc", wanted.astype(jnp.bfloat16), pool_head, preferred_element_type=jnp.float32
    ).astype(jnp.bfloat16)
    received = lax.all_to_all(sending, "ep", split_axis=0, concat_axis=0, tiled=True)
    my_docs = lax.dynamic_index_in_dim(query_docs, device, 0, keepdims=False)
    starts = lax.dynamic_index_in_dim(ctx_pos, device, 0, keepdims=False)
    return (jnp.take(received, my_docs // pool_dev, axis=0), starts[:docs_per], jnp.take(doc_lens, my_docs))


def per_device_general(
    question_q,
    question_kv,
    doc_kv,
    doc_lens,
    query_docs,
    ctx_pos,
    hidden,
    out_proj,
    norm_gain,
    router_weight,
    w_gate_up,
    w_down,
    expert_ids,
):
    lanes = lax.axis_size("tp")
    groups = lax.axis_size("ep")
    lane = lax.axis_index("tp")
    device = lax.axis_index("ep")
    length, heads_here, head_dim = question_q.shape
    kv_heads = question_kv.shape[1]
    docs_per = query_docs.shape[1]
    width_here = hidden.shape[1]
    ids = lax.all_gather(expert_ids, "ep", axis=0, tiled=False)
    kv_pick = lane * kv_heads // lanes
    kv_head = lax.dynamic_index_in_dim(question_kv, kv_pick, 1, keepdims=False).reshape(
        length, 2 * head_dim
    )
    context, starts, lengths = context_by_row(
        doc_kv, doc_lens, query_docs, ctx_pos, device, kv_pick
    )
    question_start = lax.dynamic_index_in_dim(ctx_pos, device, 0, keepdims=False)[docs_per]
    attended = attend(question_q, kv_head, context, starts, lengths, question_start)
    projected = jnp.dot(
        lax.all_gather(attended, "tp", axis=1, tiled=True),
        lax.all_gather(out_proj, "ep", axis=0, tiled=True),
        preferred_element_type=jnp.float32,
    )
    residual = (hidden.astype(jnp.float32) + projected.astype(jnp.float32)).astype(jnp.bfloat16)

    tokens = lax.all_gather(residual, "ep", axis=0, tiled=False)
    wide = tokens.astype(jnp.float32)
    gain = norm_gain.astype(jnp.float32)
    scaled = wide * gain
    logit_part = jnp.einsum(
        "snd,de->sne", scaled, router_weight.astype(jnp.float32), precision=lax.Precision.HIGHEST
    )
    square_part = jnp.sum(wide * wide, axis=2, keepdims=True)
    stats = jnp.sum(
        lax.all_gather(jnp.concatenate([logit_part, square_part], axis=2), "tp", axis=0), axis=0
    )
    experts = router_weight.shape[1]
    inv_rms = lax.rsqrt(stats[:, :, experts] / (width_here * lanes) + norm_eps)
    logits = stats[:, :, :experts] * inv_rms[:, :, None]

    local_experts = w_gate_up.shape[0]
    capacity = length * expert_ids.shape[1] // experts
    hid = w_gate_up.shape[3]
    chosen_all = jnp.any(
        ids[:, :, :, None] == jnp.arange(experts, dtype=jnp.int32), axis=2
    )
    top = jnp.max(jnp.where(chosen_all, logits, -jnp.inf), axis=2, keepdims=True)
    weight = jnp.where(chosen_all, jnp.exp(logits - top), 0.0)
    mix = weight / jnp.sum(weight, axis=2, keepdims=True)

    shuffled, scaled_rows = (chosen_all, scaled.astype(jnp.bfloat16))
    first = device * local_experts
    chosen = lax.dynamic_slice_in_dim(shuffled, first, local_experts, 2)
    mix_here = lax.dynamic_slice_in_dim(mix, first, local_experts, 2)
    before = (jnp.arange(length)[:, None] > jnp.arange(length)[None, :]).astype(jnp.bfloat16)
    rank = jnp.einsum(
        "mn,sne->sem", before, chosen.astype(jnp.bfloat16), preferred_element_type=jnp.float32
    ).astype(jnp.int32)
    pick = jnp.logical_and(
        jnp.transpose(chosen, (0, 2, 1))[:, :, None, :],
        rank[:, :, None, :] == jnp.arange(capacity, dtype=jnp.int32)[None, None, :, None],
    )
    onehot = pick.astype(jnp.bfloat16)
    inv_row = jnp.sum(jnp.where(pick, inv_rms[:, None, None, :], 0.0), axis=3)
    mix_row = jnp.sum(jnp.where(pick, jnp.transpose(mix_here, (0, 2, 1))[:, :, None, :], 0.0), axis=3)

    rows = jnp.einsum(
        "sern,snd->serd", onehot, scaled_rows, preferred_element_type=jnp.float32
    ).astype(jnp.bfloat16)
    term = jnp.einsum(
        "serd,edgh->sergh", rows, w_gate_up, preferred_element_type=jnp.float32
    ).astype(jnp.bfloat16)
    per_lane = groups * local_experts * capacity // lanes
    term = term.reshape(lanes, per_lane, 2 * hid)
    inv_row = inv_row.reshape(lanes, per_lane, 1)
    summed = lax.psum_scatter(term, "tp", scatter_dimension=0, tiled=True)[0].astype(jnp.float32)
    inv_mine = lax.dynamic_index_in_dim(inv_row, lane, 0, keepdims=False)
    summed = summed * inv_mine
    act = (jax.nn.silu(summed[:, :hid]) * summed[:, hid:]).astype(jnp.bfloat16)
    acts = lax.all_gather(act, "tp", axis=0, tiled=False)
    acts = acts.reshape(groups, local_experts, capacity, hid)
    expert_out = jnp.einsum("serh,ehd->serd", acts, w_down, preferred_element_type=jnp.float32)
    expert_out = (expert_out * mix_row[:, :, :, None]).astype(jnp.bfloat16)
    combined = jnp.einsum(
        "sern,serd->snd", onehot, expert_out, preferred_element_type=jnp.float32
    ).astype(jnp.bfloat16)
    returned = lax.psum_scatter(combined, "ep", scatter_dimension=0, tiled=True)[0]
    return (residual.astype(jnp.float32) + returned.astype(jnp.float32)).astype(jnp.bfloat16)


def pairs(lanes, flip):
    return [(i, i ^ flip) for i in range(lanes)]


def query_of(device, lane):
    return 2 * (lane & 1) + ((lane >> 1) ^ (device & 1))


def turn(question, keys_values, device, lane, n, meanwhile):
    crosses = lambda e, t: ((e ^ t) & 1) != (t >> 1)
    devices = [(e, t) for e in range(n) for t in range(n)]
    swap = [(e * n + t, e * n + (t ^ 3)) for e, t in devices if crosses(e, t)]
    crossed = lax.ppermute(question, ("ep", "tp"), swap)
    crossed, *meanwhile = lax.optimization_barrier((crossed, *meanwhile))
    heads = jnp.where(crosses(device, lane), lane ^ 3, lane)
    picked = lax.dynamic_index_in_dim(keys_values, heads, 1, keepdims=False)
    picked = jnp.transpose(picked, (1, 0, 2)).reshape(-1, question.shape[1])
    held = jnp.where(crosses(device, lane), crossed, question)
    moves = []
    for e, t in devices:
        h = t ^ 3 if crosses(e, t) else t
        moves.append((e * n + t, h * n + 2 * ((e ^ h) & 1) + (e >> 1)))
    return (lax.ppermute(jnp.concatenate([held, picked], axis=0), ("ep", "tp"), moves), meanwhile)


def call(body, outs, scratch, **kwargs):
    return pl.pallas_call(
        body,
        out_shape=outs,
        **({} if scratch is None else {"scratch_shapes": scratch}),
        compiler_params=pltpu.CompilerParams(vmem_limit_bytes=20 * 1024 * 1024),
        cost_estimate=pl.CostEstimate(flops=1 << 20, bytes_accessed=1 << 18, transcendentals=0),
        **kwargs,
    )


VMEM = pl.BlockSpec(memory_space=pltpu.VMEM)
SMEM = pl.BlockSpec(memory_space=pltpu.SMEM)
NT = (((1,), (1,)), ((), ()))


def dot(a, b):
    return jnp.dot(a, b, preferred_element_type=jnp.float32)


def document_slots(here, query_docs, pool_dev):
    device, lane = (here[0], here[1])
    query = query_of(device, lane)
    slots = []
    for d in range(4):
        slot = jnp.int32(0)
        for j in range(query_docs.shape[1]):
            offset = query_docs[query, j] - (device ^ d) * pool_dev
            slot = jnp.where(jnp.logical_and(offset >= 0, offset < pool_dev), j, slot)
        slots.append(slot)
    return (query, slots)


def prepare_body(here, query_docs, pool, ids, *outs):
    pool_dev = pool.shape[0]
    docs_per = query_docs.shape[1]
    rows = pool.shape[2] * pool.shape[3]
    device, lane = (here[0], here[1])
    for d, out in enumerate(outs):
        target = device ^ d
        query = query_of(target, lane)
        local = jnp.int32(0)
        for j in range(docs_per):
            offset = query_docs[query, j] - device * pool_dev
            inside = jnp.logical_and(offset >= 0, offset < pool_dev)
            local = jnp.where(inside, offset, local)
        out[:rows, :] = pool[local, target].reshape(rows, pool.shape[4])
        out[rows:, :] = ids[...]


def prepare(here, query_docs, pool, ids):
    _, _, pair, doc_max, head_dim = pool.shape
    shape = jax.ShapeDtypeStruct((pair * doc_max + ids.shape[0], head_dim), jnp.bfloat16)
    return call(
        prepare_body,
        [shape] * 4,
        [],
        in_specs=[SMEM, SMEM, VMEM, VMEM],
        out_specs=[VMEM] * 4,
        name="prepare",
    )(here, query_docs, pool, ids)


def angles_body(pool_dev, here, query_docs, ctx_pos, cos_q, sin_q, cos_d, sin_d):
    query, slots = document_slots(here, query_docs, pool_dev)
    docs_per = query_docs.shape[1]
    head_dim = cos_q.shape[1]

    def fill(starts, cosine, sine):
        column = lax.broadcasted_iota(jnp.int32, cosine.shape, 1)
        half = jnp.where(column < head_dim // 2, column, column - head_dim // 2)
        freq = jnp.exp(half.astype(jnp.float32) * (-2.0 * math.log(rope_theta) / head_dim))
        angle = starts.astype(jnp.float32) * freq
        cosine[...] = jnp.cos(angle)
        wave = jnp.sin(angle)
        sine[...] = jnp.where(column < head_dim // 2, -wave, wave)

    row = lax.broadcasted_iota(jnp.int32, cos_q.shape, 0)
    fill(ctx_pos[query, docs_per] + row, cos_q, sin_q)
    row = lax.broadcasted_iota(jnp.int32, cos_d.shape, 0)
    starts = jnp.zeros(cos_d.shape, jnp.int32)
    for d, slot in enumerate(slots):
        starts = jnp.where(row == d, ctx_pos[query, slot], starts)
    fill(starts, cos_d, sin_d)


def angles(here, query_docs, ctx_pos, pool_dev, length, head_dim):
    shapes = [jax.ShapeDtypeStruct((rows, head_dim), jnp.float32) for rows in (length, length, 8, 8)]
    return call(
        functools.partial(angles_body, pool_dev),
        shapes,
        [],
        in_specs=[SMEM] * 3,
        out_specs=[VMEM] * 4,
        name="angles",
    )(here, query_docs, ctx_pos)


def attention_body(
    pool_dev, here, query_docs, doc_lens, q, c0, c1, c2, c3, cos_q, sin_q, cos_d, sin_d, out, wide, keys, vals
):
    length, head_dim = cos_q.shape
    heads = out.shape[1] // head_dim
    pieces = (c0, c1, c2, c3)
    docs = len(pieces)
    doc_max = (keys.shape[0] - length) // docs
    half = head_dim // 2
    query, slots = document_slots(here, query_docs, pool_dev)

    def turned(x, cosine, sine):
        return x * cosine + pltpu.roll(x, half, 1) * sine

    cosine, sine = (cos_q[...], sin_q[...])
    for j, piece in enumerate(pieces):
        key = turned(piece[:doc_max, :].astype(jnp.float32), cos_d[j : j + 1, :], sin_d[j : j + 1, :])
        keys[j * doc_max : (j + 1) * doc_max, :] = key.astype(jnp.bfloat16)
        vals[j * doc_max : (j + 1) * doc_max, :] = piece[doc_max : 2 * doc_max, :]
    base = docs * doc_max
    first = heads * length
    keys[base:, :] = turned(q[first : first + length, :].astype(jnp.float32), cosine, sine).astype(
        jnp.bfloat16
    )
    vals[base:, :] = q[first + length :, :]
    wide[...] = q[:first, :].astype(jnp.float32)
    column = lax.broadcasted_iota(jnp.int32, (1, doc_max), 1)
    allowed = [column < doc_lens[query_docs[query, slot]] for slot in slots]
    causal = lax.broadcasted_iota(jnp.int32, (length, length), 0) >= lax.broadcasted_iota(
        jnp.int32, (length, length), 1
    )
    for h in range(heads):
        rows = turned(wide[pl.ds(h, length, stride=heads), :], cosine, sine).astype(jnp.bfloat16)
        scores = lax.dot_general(rows, keys[...], NT, preferred_element_type=jnp.float32)
        scores = scores * head_dim ** (-0.5)
        parts = [
            jnp.where(allowed[j], scores[:, j * doc_max : (j + 1) * doc_max], -jnp.inf)
            for j in range(docs)
        ] + [jnp.where(causal, scores[:, base:], -jnp.inf)]
        scores = jnp.concatenate(parts, axis=1)
        ceiling = jnp.max(scores, axis=1, keepdims=True)
        probs = jnp.exp(scores - ceiling)
        denominator = jnp.sum(probs, axis=1, keepdims=True)
        mixed = dot(probs.astype(jnp.bfloat16), vals[...])
        out[:, h * head_dim : (h + 1) * head_dim] = (mixed / denominator).astype(jnp.bfloat16)


def attention(here, query_docs, doc_lens, q, pieces, tables, pool_dev):
    length, head_dim = tables[0].shape
    heads = q.shape[0] // length - 2
    rows = 5 * length
    return call(
        functools.partial(attention_body, pool_dev),
        jax.ShapeDtypeStruct((length, heads * head_dim), jnp.bfloat16),
        [
            pltpu.VMEM((heads * length, head_dim), jnp.float32),
            pltpu.VMEM((rows, head_dim), jnp.bfloat16),
            pltpu.VMEM((rows, head_dim), jnp.bfloat16),
        ],
        in_specs=[SMEM] * 3 + [VMEM] * 9,
        out_specs=VMEM,
        name="attention",
    )(here, query_docs, doc_lens, q, *pieces, *tables)


def project_rows(here, flip, a, b, rows):
    device, lane = (here[0], here[1])
    high = (device ^ query_of(device, lane ^ flip)) >> 1
    rows[high] = a[...]
    rows[1 - high] = b[...]


def project_early_body(here, a, b, weight, close, far, rows):
    project_rows(here, 0, a, b, rows)
    far[...] = dot(rows[1], weight[...]).astype(jnp.bfloat16)
    close[...] = dot(rows[0], weight[...]).astype(jnp.bfloat16)


def project_late_body(here, a, b, weight, early, own, near, far, rows):
    project_rows(here, 2, a, b, rows)
    far[...] = dot(rows[1], weight[...]).astype(jnp.bfloat16)
    late = dot(rows[0], weight[...]).astype(jnp.bfloat16)
    first = here[1] < 2
    own[...] = jnp.where(first, early[...], late)
    near[...] = jnp.where(first, late, early[...])


def project(body, here, parts, weight, outs, *early):
    length, depth = parts[0].shape
    return call(
        body,
        [jax.ShapeDtypeStruct((length, weight.shape[1]), jnp.bfloat16)] * outs,
        [pltpu.VMEM((2, length, depth), jnp.bfloat16)],
        in_specs=[SMEM] + [VMEM] * (3 + len(early)),
        out_specs=[VMEM] * outs,
        name="project",
    )(here, *parts, weight, *early)


def routing_body(experts, here, c0, c1, c2, c3, pick, spread):
    _, local, capacity, length = pick.shape
    first = here[0] * local
    before = (
        lax.broadcasted_iota(jnp.int32, (length, length), 0)
        < lax.broadcasted_iota(jnp.int32, (length, length), 1)
    ).astype(jnp.bfloat16)
    place = lax.broadcasted_iota(jnp.int32, (capacity, length), 0).astype(jnp.float32)
    row = lax.broadcasted_iota(jnp.int32, (8, length), 0)
    for d, piece in enumerate((c0, c1, c2, c3)):
        ids = piece[piece.shape[0] - 16 :, :].astype(jnp.float32).astype(jnp.int32)
        chosen = jnp.zeros((8, length), jnp.float32)
        for k in range(8):
            named = jnp.logical_and(ids[k : k + 1, :] == first + row, row < local)
            chosen = jnp.where(named, 1.0, chosen)
        rank = dot(chosen.astype(jnp.bfloat16), before)
        wide = []
        for e in range(local):
            here_e = jnp.logical_and(rank[e : e + 1, :] == place, chosen[e : e + 1, :] > 0.0)
            wide.append(jnp.where(here_e, 1.0, 0.0))
            pick[d, e] = wide[-1].astype(jnp.bfloat16)
        spread[d] = jnp.transpose(jnp.concatenate(wide, axis=0)).astype(jnp.bfloat16)


def routing(here, pieces, experts, local, capacity):
    length = pieces[0].shape[1]
    rows = pieces[0].shape[0]
    return call(
        functools.partial(routing_body, experts),
        [
            jax.ShapeDtypeStruct((4, local, capacity, length), jnp.bfloat16),
            jax.ShapeDtypeStruct((4, length, local * capacity), jnp.bfloat16),
        ],
        [],
        in_specs=[SMEM] + [VMEM] * 4,
        out_specs=[VMEM] * 2,
        name="routing",
    )(here, *pieces)


def residual_body(hidden, p0, p1, p2, after, out):
    total = hidden[...].astype(jnp.float32) + p0[...].astype(jnp.float32)
    for part in (p1, p2):
        total = total + part[...].astype(jnp.float32)
    out[...] = total.astype(jnp.bfloat16)


def add_parts(hidden, parts, after):
    return call(
        residual_body,
        jax.ShapeDtypeStruct(hidden.shape, jnp.bfloat16),
        [],
        in_specs=[VMEM] * 4 + [pl.BlockSpec(memory_space=pl.ANY)],
        out_specs=VMEM,
        name="residual",
    )(hidden, *parts, after)


def measure_body(*refs):
    *tokens, gain, router, stats = refs
    rows = stats.shape[0]
    length = tokens[0].shape[0]
    for d, ref in enumerate(tokens):
        wide = ref[...].astype(jnp.float32)
        grown = wide * gain[...]
        high = grown.astype(jnp.bfloat16)
        rest = grown - high.astype(jnp.float32)
        middle = rest.astype(jnp.bfloat16)
        low = (rest - middle.astype(jnp.float32)).astype(jnp.bfloat16)
        logits = dot(high, router[...]) + (dot(middle, router[...]) + dot(low, router[...]))
        squares = jnp.sum(wide * wide, axis=1, keepdims=True)
        column = lax.broadcasted_iota(jnp.int32, logits.shape, 1)
        both = jnp.where(column == rows - 8, squares, logits)
        stats[:, d * length : (d + 1) * length] = jnp.transpose(both)[:rows, :]


def squares_and_logits(tokens, gain, router, experts):
    n, length = (len(tokens), tokens[0].shape[0])
    return call(
        measure_body,
        jax.ShapeDtypeStruct((experts + 8, n * length), jnp.float32),
        [],
        in_specs=[VMEM] * (n + 2),
        out_specs=VMEM,
        name="stats",
    )(*tokens, gain, router)


def gate_up_body(ds, order, *refs):
    tokens = refs[: len(ds)]
    gain, pick, weight, out, rows = refs[len(ds) :]
    hid = weight.shape[3]
    capacity = pick.shape[2]
    expert = order[pl.program_id(0)]
    for k, d in enumerate(ds):
        chosen = dot(pick[d, expert], tokens[k][...]) * gain[...]
        rows[k * capacity : (k + 1) * capacity, :] = chosen.astype(jnp.bfloat16)
    for g in range(2):
        out[0, :, g * hid : (g + 1) * hid] = dot(rows[...], weight[0, g]).astype(jnp.bfloat16)


def gate_up(ds, order, tokens, gain, pick, weight):
    _, _, width, hid = weight.shape
    count = order.shape[0]
    capacity = pick.shape[2]
    rows = len(ds) * capacity
    whole = lambda rank: lambda i, order: (0,) * rank
    return call(
        functools.partial(gate_up_body, ds),
        jax.ShapeDtypeStruct((count, rows, 2 * hid), jnp.bfloat16),
        None,
        grid_spec=pltpu.PrefetchScalarGridSpec(
            num_scalar_prefetch=1,
            grid=(count,),
            in_specs=[pl.BlockSpec(tokens[0].shape, whole(2))] * len(ds)
            + [
                pl.BlockSpec(gain.shape, whole(2)),
                pl.BlockSpec(pick.shape, whole(4)),
                pl.BlockSpec((1, 2, width, hid), lambda i, order: (order[i], 0, 0, 0)),
            ],
            out_specs=pl.BlockSpec((1, rows, 2 * hid), lambda i, order: (i, 0, 0)),
            scratch_shapes=[pltpu.VMEM((rows, width), jnp.bfloat16)],
        ),
        name="gate_up",
    )(order, *tokens, gain, pick, weight)


def activate_body(groups, features, here, pick, stats, *refs):
    out = refs[-1]
    _, local, capacity, length = pick.shape
    hid = out.shape[1]
    experts = stats.shape[0] - 8
    device, lane = (here[0], here[1])
    expert = lax.broadcasted_iota(jnp.int32, (experts, length), 0)
    base, refs = (0, list(refs))
    for ds in groups:
        kept, taken, across = refs[:3]
        pieces = refs[3 : 3 + len(ds)]
        refs = refs[3 + len(ds) :]
        for k, d in enumerate(ds):
            ids = pieces[k][pieces[k].shape[0] - 16 :, :].astype(jnp.float32).astype(jnp.int32)
            chosen = jnp.zeros((experts, length), jnp.float32)
            for c in range(8):
                chosen = jnp.where(ids[c : c + 1, :] == expert, 1.0, chosen)
            block = slice((base // capacity + k) * length, (base // capacity + k + 1) * length)
            inv_rms = lax.rsqrt(stats[experts : experts + 1, block] / features + norm_eps)
            logits = jnp.where(chosen > 0.0, stats[:experts, block] * inv_rms, -jnp.inf)
            grown = jnp.exp(logits - jnp.max(logits, axis=0, keepdims=True))
            mix = grown / jnp.sum(grown, axis=0, keepdims=True)
            mine = jnp.where(expert == device * local + lane, mix, 0.0)
            mix = jnp.sum(mine, axis=0, keepdims=True)
            places = pick[d, lane].astype(jnp.float32)
            inv_row = jnp.sum(places * inv_rms, axis=1, keepdims=True)
            mix_row = jnp.sum(places * mix, axis=1, keepdims=True)
            rows = slice(k * capacity, (k + 1) * capacity)
            summed = kept[0, rows, :].astype(jnp.float32) + taken[0, rows, :].astype(jnp.float32)
            summed = (summed + across[rows, :].astype(jnp.float32)) * inv_row
            gate = summed[:, :hid]
            act = gate / (1.0 + jnp.exp(-gate)) * summed[:, hid:] * mix_row
            out[base + k * capacity : base + (k + 1) * capacity, :] = act.astype(jnp.bfloat16)
        base += len(ds) * capacity


def activate(groups, features, here, sums, pick, stats, pieces):
    operands = []
    for ds, terms in zip(groups, sums):
        operands += list(terms) + [pieces[d] for d in ds]
    rows = sum(terms[2].shape[0] for terms in sums)
    return call(
        functools.partial(activate_body, groups, features),
        jax.ShapeDtypeStruct((rows, sums[0][2].shape[1] // 2), jnp.bfloat16),
        [],
        in_specs=[SMEM] + [VMEM] * (2 + len(operands)),
        out_specs=VMEM,
        name="activate",
    )(here, pick, stats, *operands)


def down_body(ds, order, a, b, c, d, spread, weight, *rest):
    outs, results = (rest[:-1], rest[-1])
    i = pl.program_id(0)
    capacity = results.shape[2]
    expert = order[i]
    for j, ref in enumerate((a, b, c, d)):

        @pl.when(i == j)
        def _():
            result = dot(ref[...], weight[0]).astype(jnp.bfloat16)
            for k in range(len(ds)):
                results[k, expert] = result[k * capacity : (k + 1) * capacity, :]

    @pl.when(i == pl.num_programs(0) - 1)
    def _():
        half = spread.shape[1] // 2
        for k, d in enumerate(ds):
            rows = results[k].reshape(-1, results.shape[3])
            block = dot(spread[d], rows).astype(jnp.bfloat16)
            if k < len(ds) - 1:
                outs[k][...] = block
            elif len(outs) == len(ds):
                outs[k][...] = block
            else:
                outs[k][...] = block[:half]
                outs[k + 1][...] = block[half:]


def down(ds, order, acts, spread, weight, halved=False):
    local, hid, width = weight.shape
    capacity = acts[0].shape[0] // len(ds)
    length = spread.shape[1]
    shape = jax.ShapeDtypeStruct((length, width), jnp.bfloat16)
    half = jax.ShapeDtypeStruct((length // 2, width), jnp.bfloat16)
    shapes = [shape] * (len(ds) - 1) + [half] * 2 if halved else [shape] * len(ds)
    whole = lambda rank: lambda i, order: (0,) * rank
    return call(
        functools.partial(down_body, ds),
        shapes,
        None,
        grid_spec=pltpu.PrefetchScalarGridSpec(
            num_scalar_prefetch=1,
            grid=(local,),
            in_specs=[pl.BlockSpec(acts[0].shape, whole(2))] * 4
            + [
                pl.BlockSpec(spread.shape, whole(3)),
                pl.BlockSpec((1, hid, width), lambda i, order: (order[i], 0, 0)),
            ],
            out_specs=[pl.BlockSpec(s.shape, whole(2)) for s in shapes],
            scratch_shapes=[pltpu.VMEM((len(ds), local, capacity, width), jnp.bfloat16)],
        ),
        name="down",
    )(order, *acts, spread, weight)


def per_device_square(
    question_q,
    question_kv,
    doc_kv,
    doc_lens,
    query_docs,
    ctx_pos,
    hidden,
    out_proj,
    norm_gain,
    router_weight,
    w_gate_up,
    w_down,
    expert_ids,
):
    n = 4
    lane = lax.axis_index("tp")
    device = lax.axis_index("ep")
    length, heads_here, head_dim = question_q.shape
    pool_dev = doc_kv.shape[0]
    width_here = hidden.shape[1]
    experts = router_weight.shape[1]
    local = w_gate_up.shape[0]
    capacity = length * expert_ids.shape[1] // experts
    here = jnp.stack([device, lane]).astype(jnp.int32)
    order = (lane ^ jnp.array([0, 2, 1, 3], jnp.int32)).astype(jnp.int32)

    pool = jnp.transpose(doc_kv, (0, 2, 3, 1, 4))
    ids_rows = jnp.pad(expert_ids.T.astype(jnp.bfloat16), ((0, 8), (0, 0)))
    pieces = prepare(here, query_docs, pool, ids_rows)
    q_rows, pieces = turn(
        question_q.reshape(length * heads_here, head_dim), question_kv, device, lane, n, pieces
    )
    pieces = [pieces[0]] + [lax.ppermute(pieces[d], "ep", pairs(n, d)) for d in range(1, n)]
    tables = list(angles(here, query_docs, ctx_pos, pool_dev, length, head_dim))

    one = lax.optimization_barrier(jnp.ones((), jnp.bfloat16))
    tables[0], out_proj = lax.optimization_barrier((tables[0], out_proj * one))
    attended = attention(here, query_docs, doc_lens, q_rows, pieces, tables, pool_dev)
    far = lax.ppermute(attended, "tp", pairs(n, 2))
    near = lax.ppermute(attended, "tp", pairs(n, 1))
    farther = lax.ppermute(far, "tp", pairs(n, 1))
    gain = norm_gain.astype(jnp.float32)[None, :]
    router = jnp.pad(router_weight, ((0, 0), (0, 128 - experts)))
    close, early = project(project_early_body, here, (attended, near), out_proj, 2)
    given = lax.ppermute(early, "ep", pairs(n, 1))
    kept, near, late = project(project_late_body, here, (far, farther), out_proj, 3, close)
    kept, w_gate_up = lax.optimization_barrier((kept, w_gate_up))
    late = (late.astype(jnp.float32) + given.astype(jnp.float32)).astype(jnp.bfloat16)
    moves = [
        (e * n + t, (e ^ (3 if t < 2 else 2)) * n + t) for e in range(n) for t in range(n)
    ]
    sent = [kept, lax.ppermute(late, ("ep", "tp"), moves), lax.ppermute(near, "ep", pairs(n, 1))]
    pick, spread = routing(here, pieces, experts, local, capacity)
    weight = jnp.transpose(w_gate_up, (0, 2, 1, 3))
    sent[0], pick, router, gain = lax.optimization_barrier((sent[0], pick, router, gain))
    residual = add_parts(hidden, sent, weight)

    tokens = [residual] + [None] * (n - 1)
    for d in (2, 1):
        tokens[d] = lax.ppermute(residual, "ep", pairs(n, d))
    tokens[3] = lax.ppermute(tokens[2], "ep", pairs(n, 1))

    features = width_here * n

    def spread_act(act, before=()):
        far = lax.ppermute(act, "tp", pairs(n, 2))
        far, *before = lax.optimization_barrier((far, *before))
        near = lax.ppermute(act, "tp", pairs(n, 1))
        return [act, far, near, lax.ppermute(far, "tp", pairs(n, 1))]

    def chip_sum(kept, taken):
        return (kept[1].astype(jnp.float32) + taken[1].astype(jnp.float32)).astype(jnp.bfloat16)

    def terms_of(ds, order):
        blocks = [tokens[d] for d in ds]
        given = gate_up(ds, order[2:], blocks, gain, pick, weight)
        return (gate_up(ds, order[:2], blocks, gain, pick, weight), given)

    def stats_of(ds):
        return squares_and_logits([tokens[d] for d in ds], gain, router, experts)

    one_chunk, two_chunk = ((1, 2), (0, 3))
    kept, given = terms_of(one_chunk, order)
    taken = lax.ppermute(given, "tp", pairs(n, 1))
    _, stats = lax.optimization_barrier((given, stats_of(one_chunk)))
    stats_far = lax.ppermute(stats, "tp", pairs(n, 2))
    taken, stats_far = lax.optimization_barrier((taken, stats_far))
    stats = stats + stats_far
    stats_near = lax.ppermute(stats, "tp", pairs(n, 1))
    far_sum = chip_sum(kept, taken)
    across = lax.ppermute(far_sum, "tp", pairs(n, 2))

    order, _, stats_near = lax.optimization_barrier((order, far_sum, stats_near))
    stats = stats + stats_near
    kept_2, given = terms_of(two_chunk, order)
    stats_2 = stats_of(two_chunk)
    given, across, stats_2 = lax.optimization_barrier((given, across, stats_2))
    stats_far = lax.ppermute(stats_2, "tp", pairs(n, 2))
    taken_2 = lax.ppermute(given, "tp", pairs(n, 1))
    sums = [(kept, taken, across)]
    acts = spread_act(activate((one_chunk,), features, here, sums, pick, stats, pieces))
    far_sum = chip_sum(kept_2, taken_2)
    far_sum, stats_far, acts[1] = lax.optimization_barrier((far_sum, stats_far, acts[1]))
    stats_2 = stats_2 + stats_far
    stats_near = lax.ppermute(stats_2, "tp", pairs(n, 1))
    acts[3] = lax.ppermute(acts[1], "tp", pairs(n, 1))
    across = lax.ppermute(far_sum, "tp", pairs(n, 2))
    near, *far = down(one_chunk, order, acts, spread, w_down, halved=True)
    far = [lax.ppermute(part, "ep", pairs(n, 2)) for part in far]
    across, far[0] = lax.optimization_barrier((across, far[0]))
    near = lax.ppermute(near, "ep", pairs(n, 1))
    sums = [(kept_2, taken_2, across)]
    stats_2 = stats_2 + stats_near
    acts = spread_act(
        activate((two_chunk,), features, here, sums, pick, stats_2, pieces), far[1:]
    )
    mine, last = down(two_chunk, order, acts, spread, w_down)
    last = lax.ppermute(last, "ep", pairs(n, 3))
    returned = [mine, near, jnp.concatenate(far, axis=0), last]
    total = residual.astype(jnp.float32)
    for part in returned:
        total = total + part.astype(jnp.float32)
    return total.astype(jnp.bfloat16)


def solution(mesh):
    placed = (
        P(("grp", "ep"), "tp", None),
        P(("grp", "ep"), None, None, None),
        P(("grp", "ep"), None, None, None, None),
        P("grp"),
        P("grp", None),
        P("grp", None),
        P(("grp", "ep"), "tp"),
        P("ep", "tp"),
        P("tp"),
        P("tp", None),
        P("ep", "tp", None, None),
        P("ep", None, "tp"),
        P(("grp", "ep"), None),
    )
    def per_device(*args):
        square = (
            lax.axis_size("tp") == 4
            and lax.axis_size("ep") == 4
            and args[1].shape[1] == 4
            and args[4].shape == (4, 4)
        )
        return (per_device_square if square else per_device_general)(*args)

    return jax.shard_map(
        per_device, mesh=mesh, in_specs=placed, out_specs=P(("grp", "ep"), "tp"), check_vma=False
    )
```

```python
import functools
import math

import jax
import jax.numpy as jnp
from jax import lax
from jax.experimental import pallas as pl
from jax.experimental.pallas import tpu as pltpu
from jax.sharding import PartitionSpec as P

rope_theta = 1000000.0
norm_eps = 1e-06


def tables(positions, head_dim):
    half = head_dim // 2
    freq = jnp.exp(jnp.arange(half, dtype=jnp.float32) * (-2.0 * math.log(rope_theta) / head_dim))
    angle = positions.astype(jnp.float32)[:, None] * freq[None, :]
    return (jnp.cos(angle), jnp.sin(angle))


def rotate(values, positions):
    half = values.shape[-1] // 2
    cosine, sine = tables(positions, values.shape[-1])
    shape = (values.shape[0],) + (1,) * (values.ndim - 2) + (half,)
    cosine, sine = (cosine.reshape(shape), sine.reshape(shape))
    floats = values.astype(jnp.float32)
    first = floats[..., :half]
    second = floats[..., half:]
    return jnp.concatenate(
        [first * cosine - second * sine, second * cosine + first * sine], axis=-1
    )


def attend(q_rows, own_kv, context, starts, lengths, question_start):
    length, heads_here, head_dim = q_rows.shape
    docs_per, doc_max, _ = context.shape
    question_pos = question_start + jnp.arange(length, dtype=jnp.int32)
    queries = rotate(q_rows, question_pos).astype(jnp.bfloat16)
    own_keys = rotate(own_kv[:, :head_dim], question_pos).astype(jnp.bfloat16)
    positions = jnp.repeat(starts, doc_max, total_repeat_length=docs_per * doc_max)
    doc_keys = rotate(context[:, :, :head_dim].reshape(docs_per * doc_max, head_dim), positions)
    keys = jnp.concatenate([doc_keys.astype(jnp.bfloat16), own_keys], axis=0)
    values = jnp.concatenate(
        [context[:, :, head_dim:].reshape(docs_per * doc_max, head_dim), own_kv[:, head_dim:]],
        axis=0,
    )
    valid = (jnp.arange(doc_max, dtype=jnp.int32)[None, :] < lengths[:, None]).reshape(-1)
    causal = jnp.arange(length)[:, None] >= jnp.arange(length)[None, :]
    allowed = jnp.concatenate(
        [jnp.broadcast_to(valid[None, :], (length, valid.shape[0])), causal], axis=1
    )
    scores = jnp.einsum("ihd,jd->hij", queries, keys, preferred_element_type=jnp.float32)
    scores = jnp.where(allowed[None], scores * head_dim ** (-0.5), -jnp.inf)
    ceiling = jnp.max(scores, axis=-1, keepdims=True)
    probs = jnp.exp(scores - ceiling)
    denominator = jnp.sum(probs, axis=-1, keepdims=True)
    mixed = jnp.einsum(
        "hij,jd->hid", probs.astype(jnp.bfloat16), values, preferred_element_type=jnp.float32
    )
    return (
        jnp.transpose(mixed / denominator, (1, 0, 2))
        .reshape(length, heads_here * head_dim)
        .astype(jnp.bfloat16)
    )


def context_by_row(doc_kv, doc_lens, query_docs, ctx_pos, device, kv_pick):
    pool_dev, doc_max, _, pair, head_dim = doc_kv.shape
    docs_per = query_docs.shape[1]
    pool_head = lax.dynamic_index_in_dim(doc_kv, kv_pick, 2, keepdims=False).reshape(
        pool_dev, doc_max, pair * head_dim
    )
    held = device * pool_dev + jnp.arange(pool_dev, dtype=jnp.int32)
    wanted = jnp.sum((query_docs[:, :, None] == held[None, None, :]).astype(jnp.float32), axis=1)
    sending = jnp.einsum(
        "rl,lkc->rkc", wanted.astype(jnp.bfloat16), pool_head, preferred_element_type=jnp.float32
    ).astype(jnp.bfloat16)
    received = lax.all_to_all(sending, "ep", split_axis=0, concat_axis=0, tiled=True)
    my_docs = lax.dynamic_index_in_dim(query_docs, device, 0, keepdims=False)
    starts = lax.dynamic_index_in_dim(ctx_pos, device, 0, keepdims=False)
    return (jnp.take(received, my_docs // pool_dev, axis=0), starts[:docs_per], jnp.take(doc_lens, my_docs))


def per_device_general(
    question_q,
    question_kv,
    doc_kv,
    doc_lens,
    query_docs,
    ctx_pos,
    hidden,
    out_proj,
    norm_gain,
    router_weight,
    w_gate_up,
    w_down,
    expert_ids,
):
    lanes = lax.axis_size("tp")
    groups = lax.axis_size("ep")
    lane = lax.axis_index("tp")
    device = lax.axis_index("ep")
    length, heads_here, head_dim = question_q.shape
    kv_heads = question_kv.shape[1]
    docs_per = query_docs.shape[1]
    width_here = hidden.shape[1]
    ids = lax.all_gather(expert_ids, "ep", axis=0, tiled=False)
    kv_pick = lane * kv_heads // lanes
    kv_head = lax.dynamic_index_in_dim(question_kv, kv_pick, 1, keepdims=False).reshape(
        length, 2 * head_dim
    )
    context, starts, lengths = context_by_row(
        doc_kv, doc_lens, query_docs, ctx_pos, device, kv_pick
    )
    question_start = lax.dynamic_index_in_dim(ctx_pos, device, 0, keepdims=False)[docs_per]
    attended = attend(question_q, kv_head, context, starts, lengths, question_start)
    projected = jnp.dot(
        lax.all_gather(attended, "tp", axis=1, tiled=True),
        lax.all_gather(out_proj, "ep", axis=0, tiled=True),
        preferred_element_type=jnp.float32,
    )
    residual = (hidden.astype(jnp.float32) + projected.astype(jnp.float32)).astype(jnp.bfloat16)

    tokens = lax.all_gather(residual, "ep", axis=0, tiled=False)
    wide = tokens.astype(jnp.float32)
    gain = norm_gain.astype(jnp.float32)
    scaled = wide * gain
    logit_part = jnp.einsum(
        "snd,de->sne", scaled, router_weight.astype(jnp.float32), precision=lax.Precision.HIGHEST
    )
    square_part = jnp.sum(wide * wide, axis=2, keepdims=True)
    stats = jnp.sum(
        lax.all_gather(jnp.concatenate([logit_part, square_part], axis=2), "tp", axis=0), axis=0
    )
    experts = router_weight.shape[1]
    inv_rms = lax.rsqrt(stats[:, :, experts] / (width_here * lanes) + norm_eps)
    logits = stats[:, :, :experts] * inv_rms[:, :, None]

    local_experts = w_gate_up.shape[0]
    capacity = length * expert_ids.shape[1] // experts
    hid = w_gate_up.shape[3]
    chosen_all = jnp.any(
        ids[:, :, :, None] == jnp.arange(experts, dtype=jnp.int32), axis=2
    )
    top = jnp.max(jnp.where(chosen_all, logits, -jnp.inf), axis=2, keepdims=True)
    weight = jnp.where(chosen_all, jnp.exp(logits - top), 0.0)
    mix = weight / jnp.sum(weight, axis=2, keepdims=True)

    shuffled, scaled_rows = (chosen_all, scaled.astype(jnp.bfloat16))
    first = device * local_experts
    chosen = lax.dynamic_slice_in_dim(shuffled, first, local_experts, 2)
    mix_here = lax.dynamic_slice_in_dim(mix, first, local_experts, 2)
    before = (jnp.arange(length)[:, None] > jnp.arange(length)[None, :]).astype(jnp.bfloat16)
    rank = jnp.einsum(
        "mn,sne->sem", before, chosen.astype(jnp.bfloat16), preferred_element_type=jnp.float32
    ).astype(jnp.int32)
    pick = jnp.logical_and(
        jnp.transpose(chosen, (0, 2, 1))[:, :, None, :],
        rank[:, :, None, :] == jnp.arange(capacity, dtype=jnp.int32)[None, None, :, None],
    )
    onehot = pick.astype(jnp.bfloat16)
    inv_row = jnp.sum(jnp.where(pick, inv_rms[:, None, None, :], 0.0), axis=3)
    mix_row = jnp.sum(jnp.where(pick, jnp.transpose(mix_here, (0, 2, 1))[:, :, None, :], 0.0), axis=3)

    rows = jnp.einsum(
        "sern,snd->serd", onehot, scaled_rows, preferred_element_type=jnp.float32
    ).astype(jnp.bfloat16)
    term = jnp.einsum(
        "serd,edgh->sergh", rows, w_gate_up, preferred_element_type=jnp.float32
    ).astype(jnp.bfloat16)
    per_lane = groups * local_experts * capacity // lanes
    term = term.reshape(lanes, per_lane, 2 * hid)
    inv_row = inv_row.reshape(lanes, per_lane, 1)
    summed = lax.psum_scatter(term, "tp", scatter_dimension=0, tiled=True)[0].astype(jnp.float32)
    inv_mine = lax.dynamic_index_in_dim(inv_row, lane, 0, keepdims=False)
    summed = summed * inv_mine
    act = (jax.nn.silu(summed[:, :hid]) * summed[:, hid:]).astype(jnp.bfloat16)
    acts = lax.all_gather(act, "tp", axis=0, tiled=False)
    acts = acts.reshape(groups, local_experts, capacity, hid)
    expert_out = jnp.einsum("serh,ehd->serd", acts, w_down, preferred_element_type=jnp.float32)
    expert_out = (expert_out * mix_row[:, :, :, None]).astype(jnp.bfloat16)
    combined = jnp.einsum(
        "sern,serd->snd", onehot, expert_out, preferred_element_type=jnp.float32
    ).astype(jnp.bfloat16)
    returned = lax.psum_scatter(combined, "ep", scatter_dimension=0, tiled=True)[0]
    return (residual.astype(jnp.float32) + returned.astype(jnp.float32)).astype(jnp.bfloat16)


def pairs(lanes, flip):
    return [(i, i ^ flip) for i in range(lanes)]


def query_of(device, lane):
    return 2 * (lane & 1) + ((lane >> 1) ^ (device & 1))


def turn(question, keys_values, device, lane, n, meanwhile):
    crosses = lambda e, t: ((e ^ t) & 1) != (t >> 1)
    devices = [(e, t) for e in range(n) for t in range(n)]
    swap = [(e * n + t, e * n + (t ^ 3)) for e, t in devices if crosses(e, t)]
    crossed = lax.ppermute(question, ("ep", "tp"), swap)
    crossed, *meanwhile = lax.optimization_barrier((crossed, *meanwhile))
    heads = jnp.where(crosses(device, lane), lane ^ 3, lane)
    picked = lax.dynamic_index_in_dim(keys_values, heads, 1, keepdims=False)
    picked = jnp.transpose(picked, (1, 0, 2)).reshape(-1, question.shape[1])
    held = jnp.where(crosses(device, lane), crossed, question)
    moves = []
    for e, t in devices:
        h = t ^ 3 if crosses(e, t) else t
        moves.append((e * n + t, h * n + 2 * ((e ^ h) & 1) + (e >> 1)))
    return (lax.ppermute(jnp.concatenate([held, picked], axis=0), ("ep", "tp"), moves), meanwhile)


def call(body, outs, scratch, flops=1 << 20, **kwargs):
    return pl.pallas_call(
        body,
        out_shape=outs,
        **({} if scratch is None else {"scratch_shapes": scratch}),
        compiler_params=pltpu.CompilerParams(vmem_limit_bytes=20 * 1024 * 1024),
        cost_estimate=pl.CostEstimate(flops=flops, bytes_accessed=1 << 18, transcendentals=0),
        **kwargs,
    )


VMEM = pl.BlockSpec(memory_space=pltpu.VMEM)
SMEM = pl.BlockSpec(memory_space=pltpu.SMEM)
NT = (((1,), (1,)), ((), ()))


def dot(a, b):
    return jnp.dot(a, b, preferred_element_type=jnp.float32)


def document_slots(here, query_docs, pool_dev):
    device, lane = (here[0], here[1])
    query = query_of(device, lane)
    slots = []
    for d in range(4):
        slot = jnp.int32(0)
        for j in range(query_docs.shape[1]):
            offset = query_docs[query, j] - (device ^ d) * pool_dev
            slot = jnp.where(jnp.logical_and(offset >= 0, offset < pool_dev), j, slot)
        slots.append(slot)
    return (query, slots)


def prepare_body(here, query_docs, pool, ids, *outs):
    pool_dev = pool.shape[0]
    docs_per = query_docs.shape[1]
    rows = pool.shape[2] * pool.shape[3]
    device, lane = (here[0], here[1])
    for d, out in enumerate(outs):
        target = device ^ d
        query = query_of(target, lane)
        local = jnp.int32(0)
        for j in range(docs_per):
            offset = query_docs[query, j] - device * pool_dev
            inside = jnp.logical_and(offset >= 0, offset < pool_dev)
            local = jnp.where(inside, offset, local)
        out[:rows, :] = pool[local, target].reshape(rows, pool.shape[4])
        out[rows:, :] = ids[...]


def prepare(here, query_docs, pool, ids):
    _, _, pair, doc_max, head_dim = pool.shape
    shape = jax.ShapeDtypeStruct((pair * doc_max + ids.shape[0], head_dim), jnp.bfloat16)
    return call(
        prepare_body,
        [shape] * 4,
        [],
        in_specs=[SMEM, SMEM, VMEM, VMEM],
        out_specs=[VMEM] * 4,
        name="prepare",
    )(here, query_docs, pool, ids)


def angles_body(pool_dev, here, query_docs, ctx_pos, cos_q, sin_q, cos_d, sin_d):
    query, slots = document_slots(here, query_docs, pool_dev)
    docs_per = query_docs.shape[1]
    head_dim = cos_q.shape[1]

    def fill(starts, cosine, sine):
        column = lax.broadcasted_iota(jnp.int32, cosine.shape, 1)
        half = jnp.where(column < head_dim // 2, column, column - head_dim // 2)
        freq = jnp.exp(half.astype(jnp.float32) * (-2.0 * math.log(rope_theta) / head_dim))
        angle = starts.astype(jnp.float32) * freq
        cosine[...] = jnp.cos(angle)
        wave = jnp.sin(angle)
        sine[...] = jnp.where(column < head_dim // 2, -wave, wave)

    row = lax.broadcasted_iota(jnp.int32, cos_q.shape, 0)
    fill(ctx_pos[query, docs_per] + row, cos_q, sin_q)
    row = lax.broadcasted_iota(jnp.int32, cos_d.shape, 0)
    starts = jnp.zeros(cos_d.shape, jnp.int32)
    for d, slot in enumerate(slots):
        starts = jnp.where(row == d, ctx_pos[query, slot], starts)
    fill(starts, cos_d, sin_d)


def angles(here, query_docs, ctx_pos, pool_dev, length, head_dim):
    shapes = [jax.ShapeDtypeStruct((rows, head_dim), jnp.float32) for rows in (length, length, 8, 8)]
    return call(
        functools.partial(angles_body, pool_dev),
        shapes,
        [],
        in_specs=[SMEM] * 3,
        out_specs=[VMEM] * 4,
        name="angles",
    )(here, query_docs, ctx_pos)


def attention_body(
    pool_dev, here, query_docs, doc_lens, q, c0, c1, c2, c3, cos_q, sin_q, cos_d, sin_d, out, wide, keys, vals
):
    length, head_dim = cos_q.shape
    heads = out.shape[1] // head_dim
    pieces = (c0, c1, c2, c3)
    docs = len(pieces)
    doc_max = (keys.shape[0] - length) // docs
    half = head_dim // 2
    query, slots = document_slots(here, query_docs, pool_dev)

    def turned(x, cosine, sine):
        return x * cosine + pltpu.roll(x, half, 1) * sine

    cosine, sine = (cos_q[...], sin_q[...])
    for j, piece in enumerate(pieces):
        key = turned(piece[:doc_max, :].astype(jnp.float32), cos_d[j : j + 1, :], sin_d[j : j + 1, :])
        keys[j * doc_max : (j + 1) * doc_max, :] = key.astype(jnp.bfloat16)
        vals[j * doc_max : (j + 1) * doc_max, :] = piece[doc_max : 2 * doc_max, :]
    base = docs * doc_max
    first = heads * length
    keys[base:, :] = turned(q[first : first + length, :].astype(jnp.float32), cosine, sine).astype(
        jnp.bfloat16
    )
    vals[base:, :] = q[first + length :, :]
    wide[...] = q[:first, :].astype(jnp.float32)
    column = lax.broadcasted_iota(jnp.int32, (1, doc_max), 1)
    allowed = [column < doc_lens[query_docs[query, slot]] for slot in slots]
    causal = lax.broadcasted_iota(jnp.int32, (length, length), 0) >= lax.broadcasted_iota(
        jnp.int32, (length, length), 1
    )
    for h in range(heads):
        rows = turned(wide[pl.ds(h, length, stride=heads), :], cosine, sine).astype(jnp.bfloat16)
        scores = lax.dot_general(rows, keys[...], NT, preferred_element_type=jnp.float32)
        scores = scores * head_dim ** (-0.5)
        parts = [
            jnp.where(allowed[j], scores[:, j * doc_max : (j + 1) * doc_max], -jnp.inf)
            for j in range(docs)
        ] + [jnp.where(causal, scores[:, base:], -jnp.inf)]
        scores = jnp.concatenate(parts, axis=1)
        ceiling = jnp.max(scores, axis=1, keepdims=True)
        probs = jnp.exp(scores - ceiling)
        denominator = jnp.sum(probs, axis=1, keepdims=True)
        mixed = dot(probs.astype(jnp.bfloat16), vals[...])
        out[:, h * head_dim : (h + 1) * head_dim] = (mixed / denominator).astype(jnp.bfloat16)


def attention(here, query_docs, doc_lens, q, pieces, tables, pool_dev):
    length, head_dim = tables[0].shape
    heads = q.shape[0] // length - 2
    rows = 5 * length
    return call(
        functools.partial(attention_body, pool_dev),
        jax.ShapeDtypeStruct((length, heads * head_dim), jnp.bfloat16),
        [
            pltpu.VMEM((heads * length, head_dim), jnp.float32),
            pltpu.VMEM((rows, head_dim), jnp.bfloat16),
            pltpu.VMEM((rows, head_dim), jnp.bfloat16),
        ],
        in_specs=[SMEM] * 3 + [VMEM] * 9,
        out_specs=VMEM,
        name="attention",
    )(here, query_docs, doc_lens, q, *pieces, *tables)


def project_rows(here, flip, a, b, rows):
    device, lane = (here[0], here[1])
    high = (device ^ query_of(device, lane ^ flip)) >> 1
    rows[high] = a[...]
    rows[1 - high] = b[...]


def project_early_body(here, a, b, weight, close, far, rows):
    project_rows(here, 0, a, b, rows)
    far[...] = dot(rows[1], weight[...]).astype(jnp.bfloat16)
    close[...] = dot(rows[0], weight[...]).astype(jnp.bfloat16)


def project_late_body(here, a, b, weight, early, own, near, far, rows):
    project_rows(here, 2, a, b, rows)
    far[...] = dot(rows[1], weight[...]).astype(jnp.bfloat16)
    late = dot(rows[0], weight[...]).astype(jnp.bfloat16)
    first = here[1] < 2
    own[...] = jnp.where(first, early[...], late)
    near[...] = jnp.where(first, late, early[...])


def project(body, here, parts, weight, outs, *early):
    length, depth = parts[0].shape
    return call(
        body,
        [jax.ShapeDtypeStruct((length, weight.shape[1]), jnp.bfloat16)] * outs,
        [pltpu.VMEM((2, length, depth), jnp.bfloat16)],
        in_specs=[SMEM] + [VMEM] * (3 + len(early)),
        out_specs=[VMEM] * outs,
        name="project",
    )(here, *parts, weight, *early)


def routing_body(experts, here, c0, c1, c2, c3, pick, spread):
    _, local, capacity, length = pick.shape
    first = here[0] * local
    before = (
        lax.broadcasted_iota(jnp.int32, (length, length), 0)
        < lax.broadcasted_iota(jnp.int32, (length, length), 1)
    ).astype(jnp.bfloat16)
    place = lax.broadcasted_iota(jnp.int32, (capacity, length), 0).astype(jnp.float32)
    row = lax.broadcasted_iota(jnp.int32, (8, length), 0)
    for d, piece in enumerate((c0, c1, c2, c3)):
        ids = piece[piece.shape[0] - 16 :, :].astype(jnp.float32).astype(jnp.int32)
        chosen = jnp.zeros((8, length), jnp.float32)
        for k in range(8):
            named = jnp.logical_and(ids[k : k + 1, :] == first + row, row < local)
            chosen = jnp.where(named, 1.0, chosen)
        rank = dot(chosen.astype(jnp.bfloat16), before)
        wide = []
        for e in range(local):
            here_e = jnp.logical_and(rank[e : e + 1, :] == place, chosen[e : e + 1, :] > 0.0)
            wide.append(jnp.where(here_e, 1.0, 0.0))
            pick[d, e] = wide[-1].astype(jnp.bfloat16)
        spread[d] = jnp.transpose(jnp.concatenate(wide, axis=0)).astype(jnp.bfloat16)


def routing(here, pieces, experts, local, capacity):
    length = pieces[0].shape[1]
    rows = pieces[0].shape[0]
    return call(
        functools.partial(routing_body, experts),
        [
            jax.ShapeDtypeStruct((4, local, capacity, length), jnp.bfloat16),
            jax.ShapeDtypeStruct((4, length, local * capacity), jnp.bfloat16),
        ],
        [],
        in_specs=[SMEM] + [VMEM] * 4,
        out_specs=[VMEM] * 2,
        name="routing",
    )(here, *pieces)


def residual_body(hidden, p0, p1, p2, after, out):
    total = hidden[...].astype(jnp.float32) + p0[...].astype(jnp.float32)
    for part in (p1, p2):
        total = total + part[...].astype(jnp.float32)
    out[...] = total.astype(jnp.bfloat16)


def add_parts(hidden, parts, after):
    return call(
        residual_body,
        jax.ShapeDtypeStruct(hidden.shape, jnp.bfloat16),
        [],
        in_specs=[VMEM] * 4 + [pl.BlockSpec(memory_space=pl.ANY)],
        out_specs=VMEM,
        name="residual",
    )(hidden, *parts, after)


def measure_body(*refs):
    *tokens, gain, router, stats = refs
    rows = stats.shape[0]
    length = tokens[0].shape[0]
    for d, ref in enumerate(tokens):
        wide = ref[...].astype(jnp.float32)
        grown = wide * gain[...]
        high = grown.astype(jnp.bfloat16)
        rest = grown - high.astype(jnp.float32)
        middle = rest.astype(jnp.bfloat16)
        low = (rest - middle.astype(jnp.float32)).astype(jnp.bfloat16)
        logits = dot(high, router[...]) + (dot(middle, router[...]) + dot(low, router[...]))
        squares = jnp.sum(wide * wide, axis=1, keepdims=True)
        column = lax.broadcasted_iota(jnp.int32, logits.shape, 1)
        both = jnp.where(column == rows - 8, squares, logits)
        stats[:, d * length : (d + 1) * length] = jnp.transpose(both)[:rows, :]


def squares_and_logits(tokens, gain, router, experts):
    n, length = (len(tokens), tokens[0].shape[0])
    return call(
        measure_body,
        jax.ShapeDtypeStruct((experts + 8, n * length), jnp.float32),
        [],
        in_specs=[VMEM] * (n + 2),
        out_specs=VMEM,
        name="stats",
    )(*tokens, gain, router)


def gate_up_body(ds, order, *refs):
    tokens = refs[: len(ds)]
    gain, pick, weight, out, rows = refs[len(ds) :]
    hid = weight.shape[3]
    capacity = pick.shape[2]
    expert = order[pl.program_id(0)]
    for k, d in enumerate(ds):
        chosen = dot(pick[d, expert], tokens[k][...]) * gain[...]
        rows[k * capacity : (k + 1) * capacity, :] = chosen.astype(jnp.bfloat16)
    for g in range(2):
        out[0, :, g * hid : (g + 1) * hid] = dot(rows[...], weight[0, g]).astype(jnp.bfloat16)


def gate_up(ds, order, tokens, gain, pick, weight):
    _, _, width, hid = weight.shape
    count = order.shape[0]
    capacity = pick.shape[2]
    rows = len(ds) * capacity
    whole = lambda rank: lambda i, order: (0,) * rank
    return call(
        functools.partial(gate_up_body, ds),
        jax.ShapeDtypeStruct((count, rows, 2 * hid), jnp.bfloat16),
        None,
        grid_spec=pltpu.PrefetchScalarGridSpec(
            num_scalar_prefetch=1,
            grid=(count,),
            in_specs=[pl.BlockSpec(tokens[0].shape, whole(2))] * len(ds)
            + [
                pl.BlockSpec(gain.shape, whole(2)),
                pl.BlockSpec(pick.shape, whole(4)),
                pl.BlockSpec((1, 2, width, hid), lambda i, order: (order[i], 0, 0, 0)),
            ],
            out_specs=pl.BlockSpec((1, rows, 2 * hid), lambda i, order: (i, 0, 0)),
            scratch_shapes=[pltpu.VMEM((rows, width), jnp.bfloat16)],
        ),
        name="gate_up",
    )(order, *tokens, gain, pick, weight)


def activate_body(groups, features, here, pick, stats, *refs):
    out = refs[-1]
    _, local, capacity, length = pick.shape
    hid = out.shape[1]
    experts = stats.shape[0] - 8
    device, lane = (here[0], here[1])
    expert = lax.broadcasted_iota(jnp.int32, (experts, length), 0)
    base, refs = (0, list(refs))
    for ds in groups:
        kept, taken, across = refs[:3]
        pieces = refs[3 : 3 + len(ds)]
        refs = refs[3 + len(ds) :]
        for k, d in enumerate(ds):
            ids = pieces[k][pieces[k].shape[0] - 16 :, :].astype(jnp.float32).astype(jnp.int32)
            chosen = jnp.zeros((experts, length), jnp.float32)
            for c in range(8):
                chosen = jnp.where(ids[c : c + 1, :] == expert, 1.0, chosen)
            block = slice((base // capacity + k) * length, (base // capacity + k + 1) * length)
            inv_rms = lax.rsqrt(stats[experts : experts + 1, block] / features + norm_eps)
            logits = jnp.where(chosen > 0.0, stats[:experts, block] * inv_rms, -jnp.inf)
            grown = jnp.exp(logits - jnp.max(logits, axis=0, keepdims=True))
            mix = grown / jnp.sum(grown, axis=0, keepdims=True)
            mine = jnp.where(expert == device * local + lane, mix, 0.0)
            mix = jnp.sum(mine, axis=0, keepdims=True)
            places = pick[d, lane].astype(jnp.float32)
            inv_row = jnp.sum(places * inv_rms, axis=1, keepdims=True)
            mix_row = jnp.sum(places * mix, axis=1, keepdims=True)
            rows = slice(k * capacity, (k + 1) * capacity)
            summed = kept[0, rows, :].astype(jnp.float32) + taken[0, rows, :].astype(jnp.float32)
            summed = (summed + across[rows, :].astype(jnp.float32)) * inv_row
            gate = summed[:, :hid]
            act = gate / (1.0 + jnp.exp(-gate)) * summed[:, hid:] * mix_row
            out[base + k * capacity : base + (k + 1) * capacity, :] = act.astype(jnp.bfloat16)
        base += len(ds) * capacity


def activate(groups, features, here, sums, pick, stats, pieces):
    operands = []
    for ds, terms in zip(groups, sums):
        operands += list(terms) + [pieces[d] for d in ds]
    rows = sum(terms[2].shape[0] for terms in sums)
    return call(
        functools.partial(activate_body, groups, features),
        jax.ShapeDtypeStruct((rows, sums[0][2].shape[1] // 2), jnp.bfloat16),
        [],
        in_specs=[SMEM] + [VMEM] * (2 + len(operands)),
        out_specs=VMEM,
        flops=1 << 32,
        name="activate",
    )(here, pick, stats, *operands)


def down_body(ds, order, a, b, c, d, spread, weight, *rest):
    outs, results = (rest[:-1], rest[-1])
    i = pl.program_id(0)
    capacity = results.shape[2]
    expert = order[i]
    for j, ref in enumerate((a, b, c, d)):

        @pl.when(i == j)
        def _():
            result = dot(ref[...], weight[0]).astype(jnp.bfloat16)
            for k in range(len(ds)):
                results[k, expert] = result[k * capacity : (k + 1) * capacity, :]

    @pl.when(i == pl.num_programs(0) - 1)
    def _():
        half = spread.shape[1] // 2
        for k, d in enumerate(ds):
            rows = results[k].reshape(-1, results.shape[3])
            block = dot(spread[d], rows).astype(jnp.bfloat16)
            if k < len(ds) - 1:
                outs[k][...] = block
            elif len(outs) == len(ds):
                outs[k][...] = block
            else:
                outs[k][...] = block[:half]
                outs[k + 1][...] = block[half:]


def down(ds, order, acts, spread, weight, halved=False):
    local, hid, width = weight.shape
    capacity = acts[0].shape[0] // len(ds)
    length = spread.shape[1]
    shape = jax.ShapeDtypeStruct((length, width), jnp.bfloat16)
    half = jax.ShapeDtypeStruct((length // 2, width), jnp.bfloat16)
    shapes = [shape] * (len(ds) - 1) + [half] * 2 if halved else [shape] * len(ds)
    whole = lambda rank: lambda i, order: (0,) * rank
    return call(
        functools.partial(down_body, ds),
        shapes,
        None,
        grid_spec=pltpu.PrefetchScalarGridSpec(
            num_scalar_prefetch=1,
            grid=(local,),
            in_specs=[pl.BlockSpec(acts[0].shape, whole(2))] * 4
            + [
                pl.BlockSpec(spread.shape, whole(3)),
                pl.BlockSpec((1, hid, width), lambda i, order: (order[i], 0, 0)),
            ],
            out_specs=[pl.BlockSpec(s.shape, whole(2)) for s in shapes],
            scratch_shapes=[pltpu.VMEM((len(ds), local, capacity, width), jnp.bfloat16)],
        ),
        name="down",
    )(order, *acts, spread, weight)


def per_device_square(
    question_q,
    question_kv,
    doc_kv,
    doc_lens,
    query_docs,
    ctx_pos,
    hidden,
    out_proj,
    norm_gain,
    router_weight,
    w_gate_up,
    w_down,
    expert_ids,
):
    n = 4
    lane = lax.axis_index("tp")
    device = lax.axis_index("ep")
    length, heads_here, head_dim = question_q.shape
    pool_dev = doc_kv.shape[0]
    width_here = hidden.shape[1]
    experts = router_weight.shape[1]
    local = w_gate_up.shape[0]
    capacity = length * expert_ids.shape[1] // experts
    here = jnp.stack([device, lane]).astype(jnp.int32)
    order = (lane ^ jnp.array([0, 2, 1, 3], jnp.int32)).astype(jnp.int32)

    pool = jnp.transpose(doc_kv, (0, 2, 3, 1, 4))
    ids_rows = jnp.pad(expert_ids.T.astype(jnp.bfloat16), ((0, 8), (0, 0)))
    pieces = prepare(here, query_docs, pool, ids_rows)
    q_rows, pieces = turn(
        question_q.reshape(length * heads_here, head_dim), question_kv, device, lane, n, pieces
    )
    pieces = [pieces[0]] + [lax.ppermute(pieces[d], "ep", pairs(n, d)) for d in range(1, n)]
    tables = list(angles(here, query_docs, ctx_pos, pool_dev, length, head_dim))

    one = lax.optimization_barrier(jnp.ones((), jnp.bfloat16))
    tables[0], out_proj = lax.optimization_barrier((tables[0], out_proj * one))
    attended = attention(here, query_docs, doc_lens, q_rows, pieces, tables, pool_dev)
    far = lax.ppermute(attended, "tp", pairs(n, 2))
    near = lax.ppermute(attended, "tp", pairs(n, 1))
    gain = norm_gain.astype(jnp.float32)[None, :]
    router = jnp.pad(router_weight, ((0, 0), (0, 128 - experts)))
    close, early = project(project_early_body, here, (attended, near), out_proj, 2)
    early, far = lax.optimization_barrier((early, far))
    given = lax.ppermute(early, "ep", pairs(n, 1))
    farther = lax.ppermute(far, "tp", pairs(n, 1))
    kept, near, late = project(project_late_body, here, (far, farther), out_proj, 3, close)
    kept, w_gate_up = lax.optimization_barrier((kept, w_gate_up))
    late = (late.astype(jnp.float32) + given.astype(jnp.float32)).astype(jnp.bfloat16)
    moves = [
        (e * n + t, (e ^ (3 if t < 2 else 2)) * n + t) for e in range(n) for t in range(n)
    ]
    sent = [kept, lax.ppermute(late, ("ep", "tp"), moves), lax.ppermute(near, "ep", pairs(n, 1))]
    pick, spread = routing(here, pieces, experts, local, capacity)
    weight = jnp.transpose(w_gate_up, (0, 2, 1, 3))
    sent[0], pick, router, gain = lax.optimization_barrier((sent[0], pick, router, gain))
    residual = add_parts(hidden, sent, weight)

    tokens = [residual] + [None] * (n - 1)
    for d in (2, 1):
        tokens[d] = lax.ppermute(residual, "ep", pairs(n, d))
    tokens[3] = lax.ppermute(tokens[2], "ep", pairs(n, 1))

    features = width_here * n

    def spread_act(act, before=()):
        far = lax.ppermute(act, "tp", pairs(n, 2))
        far, *before = lax.optimization_barrier((far, *before))
        near = lax.ppermute(act, "tp", pairs(n, 1))
        return [act, far, near, lax.ppermute(far, "tp", pairs(n, 1))]

    def chip_sum(kept, taken):
        return (kept[1].astype(jnp.float32) + taken[1].astype(jnp.float32)).astype(jnp.bfloat16)

    def terms_of(ds, order):
        blocks = [tokens[d] for d in ds]
        given = gate_up(ds, order[2:], blocks, gain, pick, weight)
        return (gate_up(ds, order[:2], blocks, gain, pick, weight), given)

    def stats_of(ds):
        return squares_and_logits([tokens[d] for d in ds], gain, router, experts)

    one_chunk, two_chunk = ((1, 2), (0, 3))
    kept_0, given_0 = terms_of((0,), order)
    order, kept_0, given_0 = lax.optimization_barrier((order, kept_0, given_0))
    kept, given = terms_of(one_chunk, order)
    given, given_0 = lax.optimization_barrier((given, given_0))
    taken_0 = lax.ppermute(given_0, "tp", pairs(n, 1))
    taken = lax.ppermute(given, "tp", pairs(n, 1))
    across_0 = lax.ppermute(chip_sum(kept_0, taken_0), "tp", pairs(n, 2))
    _, stats = lax.optimization_barrier((given, stats_of(one_chunk)))
    stats_far = lax.ppermute(stats, "tp", pairs(n, 2))
    taken, stats_far = lax.optimization_barrier((taken, stats_far))
    stats = stats + stats_far
    stats_near = lax.ppermute(stats, "tp", pairs(n, 1))
    far_sum = chip_sum(kept, taken)
    far_sum, across_0 = lax.optimization_barrier((far_sum, across_0))
    across = lax.ppermute(far_sum, "tp", pairs(n, 2))

    order, _, stats_near = lax.optimization_barrier((order, far_sum, stats_near))
    stats = stats + stats_near
    kept_2, given = terms_of((3,), order)
    stats_2 = stats_of(two_chunk)
    given, across, stats_2 = lax.optimization_barrier((given, across, stats_2))
    stats_far = lax.ppermute(stats_2, "tp", pairs(n, 2))
    taken_2 = lax.ppermute(given, "tp", pairs(n, 1))
    sums = [(kept, taken, across)]
    acts = spread_act(activate((one_chunk,), features, here, sums, pick, stats, pieces))
    far_sum = chip_sum(kept_2, taken_2)
    far_sum, stats_far, acts[1] = lax.optimization_barrier((far_sum, stats_far, acts[1]))
    stats_2 = stats_2 + stats_far
    stats_near = lax.ppermute(stats_2, "tp", pairs(n, 1))
    acts[3] = lax.ppermute(acts[1], "tp", pairs(n, 1))
    across = lax.ppermute(far_sum, "tp", pairs(n, 2))
    near, *far = down(one_chunk, order, acts, spread, w_down, halved=True)
    far = [lax.ppermute(part, "ep", pairs(n, 2)) for part in far]
    near = lax.ppermute(near, "ep", pairs(n, 1))
    sums = [(kept_0, taken_0, across_0), (kept_2, taken_2, across)]
    stats_2 = stats_2 + stats_near
    acts = spread_act(
        activate(((0,), (3,)), features, here, sums, pick, stats_2, pieces), far[:1]
    )
    mine, last = down(two_chunk, order, acts, spread, w_down)
    last = lax.ppermute(last, "ep", pairs(n, 3))
    returned = [mine, near, jnp.concatenate(far, axis=0), last]
    total = residual.astype(jnp.float32)
    for part in returned:
        total = total + part.astype(jnp.float32)
    return total.astype(jnp.bfloat16)


def solution(mesh):
    placed = (
        P(("grp", "ep"), "tp", None),
        P(("grp", "ep"), None, None, None),
        P(("grp", "ep"), None, None, None, None),
        P("grp"),
        P("grp", None),
        P("grp", None),
        P(("grp", "ep"), "tp"),
        P("ep", "tp"),
        P("tp"),
        P("tp", None),
        P("ep", "tp", None, None),
        P("ep", None, "tp"),
        P(("grp", "ep"), None),
    )
    def per_device(*args):
        square = (
            lax.axis_size("tp") == 4
            and lax.axis_size("ep") == 4
            and args[1].shape[1] == 4
            and args[4].shape == (4, 4)
        )
        return (per_device_square if square else per_device_general)(*args)

    return jax.shard_map(
        per_device, mesh=mesh, in_specs=placed, out_specs=P(("grp", "ep"), "tp"), check_vma=False
    )
```

```python
import functools
import math

import jax
import jax.numpy as jnp
from jax import lax
from jax.experimental import pallas as pl
from jax.experimental.pallas import tpu as pltpu
from jax.sharding import PartitionSpec as P

rope_theta = 1000000.0
norm_eps = 1e-06


def tables(positions, head_dim):
    half = head_dim // 2
    freq = jnp.exp(jnp.arange(half, dtype=jnp.float32) * (-2.0 * math.log(rope_theta) / head_dim))
    angle = positions.astype(jnp.float32)[:, None] * freq[None, :]
    return (jnp.cos(angle), jnp.sin(angle))


def rotate(values, positions):
    half = values.shape[-1] // 2
    cosine, sine = tables(positions, values.shape[-1])
    shape = (values.shape[0],) + (1,) * (values.ndim - 2) + (half,)
    cosine, sine = (cosine.reshape(shape), sine.reshape(shape))
    floats = values.astype(jnp.float32)
    first = floats[..., :half]
    second = floats[..., half:]
    return jnp.concatenate(
        [first * cosine - second * sine, second * cosine + first * sine], axis=-1
    )


def attend(q_rows, own_kv, context, starts, lengths, question_start):
    length, heads_here, head_dim = q_rows.shape
    docs_per, doc_max, _ = context.shape
    question_pos = question_start + jnp.arange(length, dtype=jnp.int32)
    queries = rotate(q_rows, question_pos).astype(jnp.bfloat16)
    own_keys = rotate(own_kv[:, :head_dim], question_pos).astype(jnp.bfloat16)
    positions = jnp.repeat(starts, doc_max, total_repeat_length=docs_per * doc_max)
    doc_keys = rotate(context[:, :, :head_dim].reshape(docs_per * doc_max, head_dim), positions)
    keys = jnp.concatenate([doc_keys.astype(jnp.bfloat16), own_keys], axis=0)
    values = jnp.concatenate(
        [context[:, :, head_dim:].reshape(docs_per * doc_max, head_dim), own_kv[:, head_dim:]],
        axis=0,
    )
    valid = (jnp.arange(doc_max, dtype=jnp.int32)[None, :] < lengths[:, None]).reshape(-1)
    causal = jnp.arange(length)[:, None] >= jnp.arange(length)[None, :]
    allowed = jnp.concatenate(
        [jnp.broadcast_to(valid[None, :], (length, valid.shape[0])), causal], axis=1
    )
    scores = jnp.einsum("ihd,jd->hij", queries, keys, preferred_element_type=jnp.float32)
    scores = jnp.where(allowed[None], scores * head_dim ** (-0.5), -jnp.inf)
    ceiling = jnp.max(scores, axis=-1, keepdims=True)
    probs = jnp.exp(scores - ceiling)
    denominator = jnp.sum(probs, axis=-1, keepdims=True)
    mixed = jnp.einsum(
        "hij,jd->hid", probs.astype(jnp.bfloat16), values, preferred_element_type=jnp.float32
    )
    return (
        jnp.transpose(mixed / denominator, (1, 0, 2))
        .reshape(length, heads_here * head_dim)
        .astype(jnp.bfloat16)
    )


def context_by_row(doc_kv, doc_lens, query_docs, ctx_pos, device, kv_pick):
    pool_dev, doc_max, _, pair, head_dim = doc_kv.shape
    docs_per = query_docs.shape[1]
    pool_head = lax.dynamic_index_in_dim(doc_kv, kv_pick, 2, keepdims=False).reshape(
        pool_dev, doc_max, pair * head_dim
    )
    held = device * pool_dev + jnp.arange(pool_dev, dtype=jnp.int32)
    wanted = jnp.sum((query_docs[:, :, None] == held[None, None, :]).astype(jnp.float32), axis=1)
    sending = jnp.einsum(
        "rl,lkc->rkc", wanted.astype(jnp.bfloat16), pool_head, preferred_element_type=jnp.float32
    ).astype(jnp.bfloat16)
    received = lax.all_to_all(sending, "ep", split_axis=0, concat_axis=0, tiled=True)
    my_docs = lax.dynamic_index_in_dim(query_docs, device, 0, keepdims=False)
    starts = lax.dynamic_index_in_dim(ctx_pos, device, 0, keepdims=False)
    return (jnp.take(received, my_docs // pool_dev, axis=0), starts[:docs_per], jnp.take(doc_lens, my_docs))


def per_device_general(
    question_q,
    question_kv,
    doc_kv,
    doc_lens,
    query_docs,
    ctx_pos,
    hidden,
    out_proj,
    norm_gain,
    router_weight,
    w_gate_up,
    w_down,
    expert_ids,
):
    lanes = lax.axis_size("tp")
    groups = lax.axis_size("ep")
    lane = lax.axis_index("tp")
    device = lax.axis_index("ep")
    length, heads_here, head_dim = question_q.shape
    kv_heads = question_kv.shape[1]
    docs_per = query_docs.shape[1]
    width_here = hidden.shape[1]
    ids = lax.all_gather(expert_ids, "ep", axis=0, tiled=False)
    kv_pick = lane * kv_heads // lanes
    kv_head = lax.dynamic_index_in_dim(question_kv, kv_pick, 1, keepdims=False).reshape(
        length, 2 * head_dim
    )
    context, starts, lengths = context_by_row(
        doc_kv, doc_lens, query_docs, ctx_pos, device, kv_pick
    )
    question_start = lax.dynamic_index_in_dim(ctx_pos, device, 0, keepdims=False)[docs_per]
    attended = attend(question_q, kv_head, context, starts, lengths, question_start)
    projected = jnp.dot(
        lax.all_gather(attended, "tp", axis=1, tiled=True),
        lax.all_gather(out_proj, "ep", axis=0, tiled=True),
        preferred_element_type=jnp.float32,
    )
    residual = (hidden.astype(jnp.float32) + projected.astype(jnp.float32)).astype(jnp.bfloat16)

    tokens = lax.all_gather(residual, "ep", axis=0, tiled=False)
    wide = tokens.astype(jnp.float32)
    gain = norm_gain.astype(jnp.float32)
    scaled = wide * gain
    logit_part = jnp.einsum(
        "snd,de->sne", scaled, router_weight.astype(jnp.float32), precision=lax.Precision.HIGHEST
    )
    square_part = jnp.sum(wide * wide, axis=2, keepdims=True)
    stats = jnp.sum(
        lax.all_gather(jnp.concatenate([logit_part, square_part], axis=2), "tp", axis=0), axis=0
    )
    experts = router_weight.shape[1]
    inv_rms = lax.rsqrt(stats[:, :, experts] / (width_here * lanes) + norm_eps)
    logits = stats[:, :, :experts] * inv_rms[:, :, None]

    local_experts = w_gate_up.shape[0]
    capacity = length * expert_ids.shape[1] // experts
    hid = w_gate_up.shape[3]
    chosen_all = jnp.any(
        ids[:, :, :, None] == jnp.arange(experts, dtype=jnp.int32), axis=2
    )
    top = jnp.max(jnp.where(chosen_all, logits, -jnp.inf), axis=2, keepdims=True)
    weight = jnp.where(chosen_all, jnp.exp(logits - top), 0.0)
    mix = weight / jnp.sum(weight, axis=2, keepdims=True)

    shuffled, scaled_rows = (chosen_all, scaled.astype(jnp.bfloat16))
    first = device * local_experts
    chosen = lax.dynamic_slice_in_dim(shuffled, first, local_experts, 2)
    mix_here = lax.dynamic_slice_in_dim(mix, first, local_experts, 2)
    before = (jnp.arange(length)[:, None] > jnp.arange(length)[None, :]).astype(jnp.bfloat16)
    rank = jnp.einsum(
        "mn,sne->sem", before, chosen.astype(jnp.bfloat16), preferred_element_type=jnp.float32
    ).astype(jnp.int32)
    pick = jnp.logical_and(
        jnp.transpose(chosen, (0, 2, 1))[:, :, None, :],
        rank[:, :, None, :] == jnp.arange(capacity, dtype=jnp.int32)[None, None, :, None],
    )
    onehot = pick.astype(jnp.bfloat16)
    inv_row = jnp.sum(jnp.where(pick, inv_rms[:, None, None, :], 0.0), axis=3)
    mix_row = jnp.sum(jnp.where(pick, jnp.transpose(mix_here, (0, 2, 1))[:, :, None, :], 0.0), axis=3)

    rows = jnp.einsum(
        "sern,snd->serd", onehot, scaled_rows, preferred_element_type=jnp.float32
    ).astype(jnp.bfloat16)
    term = jnp.einsum(
        "serd,edgh->sergh", rows, w_gate_up, preferred_element_type=jnp.float32
    ).astype(jnp.bfloat16)
    per_lane = groups * local_experts * capacity // lanes
    term = term.reshape(lanes, per_lane, 2 * hid)
    inv_row = inv_row.reshape(lanes, per_lane, 1)
    summed = lax.psum_scatter(term, "tp", scatter_dimension=0, tiled=True)[0].astype(jnp.float32)
    inv_mine = lax.dynamic_index_in_dim(inv_row, lane, 0, keepdims=False)
    summed = summed * inv_mine
    act = (jax.nn.silu(summed[:, :hid]) * summed[:, hid:]).astype(jnp.bfloat16)
    acts = lax.all_gather(act, "tp", axis=0, tiled=False)
    acts = acts.reshape(groups, local_experts, capacity, hid)
    expert_out = jnp.einsum("serh,ehd->serd", acts, w_down, preferred_element_type=jnp.float32)
    expert_out = (expert_out * mix_row[:, :, :, None]).astype(jnp.bfloat16)
    combined = jnp.einsum(
        "sern,serd->snd", onehot, expert_out, preferred_element_type=jnp.float32
    ).astype(jnp.bfloat16)
    returned = lax.psum_scatter(combined, "ep", scatter_dimension=0, tiled=True)[0]
    return (residual.astype(jnp.float32) + returned.astype(jnp.float32)).astype(jnp.bfloat16)


def pairs(lanes, flip):
    return [(i, i ^ flip) for i in range(lanes)]


def query_of(device, lane):
    return 2 * (lane & 1) + ((lane >> 1) ^ (device & 1))


def turn(question, keys_values, device, lane, n, meanwhile):
    crosses = lambda e, t: ((e ^ t) & 1) != (t >> 1)
    devices = [(e, t) for e in range(n) for t in range(n)]
    swap = [(e * n + t, e * n + (t ^ 3)) for e, t in devices if crosses(e, t)]
    crossed = lax.ppermute(question, ("ep", "tp"), swap)
    crossed, *meanwhile = lax.optimization_barrier((crossed, *meanwhile))
    heads = jnp.where(crosses(device, lane), lane ^ 3, lane)
    picked = lax.dynamic_index_in_dim(keys_values, heads, 1, keepdims=False)
    picked = jnp.transpose(picked, (1, 0, 2)).reshape(-1, question.shape[1])
    held = jnp.where(crosses(device, lane), crossed, question)
    moves = []
    for e, t in devices:
        h = t ^ 3 if crosses(e, t) else t
        moves.append((e * n + t, h * n + 2 * ((e ^ h) & 1) + (e >> 1)))
    return (lax.ppermute(jnp.concatenate([held, picked], axis=0), ("ep", "tp"), moves), meanwhile)


def call(body, outs, scratch, flops=1 << 20, **kwargs):
    return pl.pallas_call(
        body,
        out_shape=outs,
        **({} if scratch is None else {"scratch_shapes": scratch}),
        compiler_params=pltpu.CompilerParams(vmem_limit_bytes=20 * 1024 * 1024),
        cost_estimate=pl.CostEstimate(flops=flops, bytes_accessed=1 << 18, transcendentals=0),
        **kwargs,
    )


VMEM = pl.BlockSpec(memory_space=pltpu.VMEM)
SMEM = pl.BlockSpec(memory_space=pltpu.SMEM)
NT = (((1,), (1,)), ((), ()))


def dot(a, b):
    return jnp.dot(a, b, preferred_element_type=jnp.float32)


def document_slots(here, query_docs, pool_dev):
    device, lane = (here[0], here[1])
    query = query_of(device, lane)
    slots = []
    for d in range(4):
        slot = jnp.int32(0)
        for j in range(query_docs.shape[1]):
            offset = query_docs[query, j] - (device ^ d) * pool_dev
            slot = jnp.where(jnp.logical_and(offset >= 0, offset < pool_dev), j, slot)
        slots.append(slot)
    return (query, slots)


def prepare_body(here, query_docs, pool, ids, *outs):
    pool_dev = pool.shape[0]
    docs_per = query_docs.shape[1]
    rows = pool.shape[2] * pool.shape[3]
    device, lane = (here[0], here[1])
    for d, out in enumerate(outs):
        target = device ^ d
        query = query_of(target, lane)
        local = jnp.int32(0)
        for j in range(docs_per):
            offset = query_docs[query, j] - device * pool_dev
            inside = jnp.logical_and(offset >= 0, offset < pool_dev)
            local = jnp.where(inside, offset, local)
        out[:rows, :] = pool[local, target].reshape(rows, pool.shape[4])
        out[rows:, :] = ids[...]


def prepare(here, query_docs, pool, ids):
    _, _, pair, doc_max, head_dim = pool.shape
    shape = jax.ShapeDtypeStruct((pair * doc_max + ids.shape[0], head_dim), jnp.bfloat16)
    return call(
        prepare_body,
        [shape] * 4,
        [],
        in_specs=[SMEM, SMEM, VMEM, VMEM],
        out_specs=[VMEM] * 4,
        name="prepare",
    )(here, query_docs, pool, ids)


def angles_body(pool_dev, here, query_docs, ctx_pos, cos_q, sin_q, cos_d, sin_d):
    query, slots = document_slots(here, query_docs, pool_dev)
    docs_per = query_docs.shape[1]
    head_dim = cos_q.shape[1]

    def fill(starts, cosine, sine):
        column = lax.broadcasted_iota(jnp.int32, cosine.shape, 1)
        half = jnp.where(column < head_dim // 2, column, column - head_dim // 2)
        freq = jnp.exp(half.astype(jnp.float32) * (-2.0 * math.log(rope_theta) / head_dim))
        angle = starts.astype(jnp.float32) * freq
        cosine[...] = jnp.cos(angle)
        wave = jnp.sin(angle)
        sine[...] = jnp.where(column < head_dim // 2, -wave, wave)

    row = lax.broadcasted_iota(jnp.int32, cos_q.shape, 0)
    fill(ctx_pos[query, docs_per] + row, cos_q, sin_q)
    row = lax.broadcasted_iota(jnp.int32, cos_d.shape, 0)
    starts = jnp.zeros(cos_d.shape, jnp.int32)
    for d, slot in enumerate(slots):
        starts = jnp.where(row == d, ctx_pos[query, slot], starts)
    fill(starts, cos_d, sin_d)


def angles(here, query_docs, ctx_pos, pool_dev, length, head_dim):
    shapes = [jax.ShapeDtypeStruct((rows, head_dim), jnp.float32) for rows in (length, length, 8, 8)]
    return call(
        functools.partial(angles_body, pool_dev),
        shapes,
        [],
        in_specs=[SMEM] * 3,
        out_specs=[VMEM] * 4,
        name="angles",
    )(here, query_docs, ctx_pos)


def attention_body(
    pool_dev, here, query_docs, doc_lens, q, c0, c1, c2, c3, cos_q, sin_q, cos_d, sin_d, out, wide, keys, vals
):
    length, head_dim = cos_q.shape
    heads = out.shape[1] // head_dim
    pieces = (c0, c1, c2, c3)
    docs = len(pieces)
    doc_max = (keys.shape[0] - length) // docs
    half = head_dim // 2
    query, slots = document_slots(here, query_docs, pool_dev)

    def turned(x, cosine, sine):
        return x * cosine + pltpu.roll(x, half, 1) * sine

    cosine, sine = (cos_q[...], sin_q[...])
    for j, piece in enumerate(pieces):
        key = turned(piece[:doc_max, :].astype(jnp.float32), cos_d[j : j + 1, :], sin_d[j : j + 1, :])
        keys[j * doc_max : (j + 1) * doc_max, :] = key.astype(jnp.bfloat16)
        vals[j * doc_max : (j + 1) * doc_max, :] = piece[doc_max : 2 * doc_max, :]
    base = docs * doc_max
    first = heads * length
    keys[base:, :] = turned(q[first : first + length, :].astype(jnp.float32), cosine, sine).astype(
        jnp.bfloat16
    )
    vals[base:, :] = q[first + length :, :]
    wide[...] = q[:first, :].astype(jnp.float32)
    column = lax.broadcasted_iota(jnp.int32, (1, doc_max), 1)
    allowed = [column < doc_lens[query_docs[query, slot]] for slot in slots]
    causal = lax.broadcasted_iota(jnp.int32, (length, length), 0) >= lax.broadcasted_iota(
        jnp.int32, (length, length), 1
    )
    for h in range(heads):
        rows = turned(wide[pl.ds(h, length, stride=heads), :], cosine, sine).astype(jnp.bfloat16)
        scores = lax.dot_general(rows, keys[...], NT, preferred_element_type=jnp.float32)
        scores = scores * head_dim ** (-0.5)
        parts = [
            jnp.where(allowed[j], scores[:, j * doc_max : (j + 1) * doc_max], -jnp.inf)
            for j in range(docs)
        ] + [jnp.where(causal, scores[:, base:], -jnp.inf)]
        scores = jnp.concatenate(parts, axis=1)
        ceiling = jnp.max(scores, axis=1, keepdims=True)
        probs = jnp.exp(scores - ceiling)
        denominator = jnp.sum(probs, axis=1, keepdims=True)
        mixed = dot(probs.astype(jnp.bfloat16), vals[...])
        out[:, h * head_dim : (h + 1) * head_dim] = (mixed / denominator).astype(jnp.bfloat16)


def attention(here, query_docs, doc_lens, q, pieces, tables, pool_dev):
    length, head_dim = tables[0].shape
    heads = q.shape[0] // length - 2
    rows = 5 * length
    return call(
        functools.partial(attention_body, pool_dev),
        jax.ShapeDtypeStruct((length, heads * head_dim), jnp.bfloat16),
        [
            pltpu.VMEM((heads * length, head_dim), jnp.float32),
            pltpu.VMEM((rows, head_dim), jnp.bfloat16),
            pltpu.VMEM((rows, head_dim), jnp.bfloat16),
        ],
        in_specs=[SMEM] * 3 + [VMEM] * 9,
        out_specs=VMEM,
        name="attention",
    )(here, query_docs, doc_lens, q, *pieces, *tables)


def project_rows(here, flip, a, b, rows):
    device, lane = (here[0], here[1])
    high = (device ^ query_of(device, lane ^ flip)) >> 1
    rows[high] = a[...]
    rows[1 - high] = b[...]


def project_early_body(here, a, b, weight, close, far, rows):
    project_rows(here, 0, a, b, rows)
    far[...] = dot(rows[1], weight[...]).astype(jnp.bfloat16)
    close[...] = dot(rows[0], weight[...]).astype(jnp.bfloat16)


def project_late_body(here, a, b, weight, early, own, near, far, rows):
    project_rows(here, 2, a, b, rows)
    far[...] = dot(rows[1], weight[...]).astype(jnp.bfloat16)
    late = dot(rows[0], weight[...]).astype(jnp.bfloat16)
    first = here[1] < 2
    own[...] = jnp.where(first, early[...], late)
    near[...] = jnp.where(first, late, early[...])


def project(body, here, parts, weight, outs, *early):
    length, depth = parts[0].shape
    return call(
        body,
        [jax.ShapeDtypeStruct((length, weight.shape[1]), jnp.bfloat16)] * outs,
        [pltpu.VMEM((2, length, depth), jnp.bfloat16)],
        in_specs=[SMEM] + [VMEM] * (3 + len(early)),
        out_specs=[VMEM] * outs,
        name="project",
    )(here, *parts, weight, *early)


def routing_body(experts, here, c0, c1, c2, c3, pick, spread):
    _, local, capacity, length = pick.shape
    first = here[0] * local
    before = (
        lax.broadcasted_iota(jnp.int32, (length, length), 0)
        < lax.broadcasted_iota(jnp.int32, (length, length), 1)
    ).astype(jnp.bfloat16)
    place = lax.broadcasted_iota(jnp.int32, (capacity, length), 0).astype(jnp.float32)
    row = lax.broadcasted_iota(jnp.int32, (8, length), 0)
    for d, piece in enumerate((c0, c1, c2, c3)):
        ids = piece[piece.shape[0] - 16 :, :].astype(jnp.float32).astype(jnp.int32)
        chosen = jnp.zeros((8, length), jnp.float32)
        for k in range(8):
            named = jnp.logical_and(ids[k : k + 1, :] == first + row, row < local)
            chosen = jnp.where(named, 1.0, chosen)
        rank = dot(chosen.astype(jnp.bfloat16), before)
        wide = []
        for e in range(local):
            here_e = jnp.logical_and(rank[e : e + 1, :] == place, chosen[e : e + 1, :] > 0.0)
            wide.append(jnp.where(here_e, 1.0, 0.0))
            pick[d, e] = wide[-1].astype(jnp.bfloat16)
        spread[d] = jnp.transpose(jnp.concatenate(wide, axis=0)).astype(jnp.bfloat16)


def routing(here, pieces, experts, local, capacity):
    length = pieces[0].shape[1]
    rows = pieces[0].shape[0]
    return call(
        functools.partial(routing_body, experts),
        [
            jax.ShapeDtypeStruct((4, local, capacity, length), jnp.bfloat16),
            jax.ShapeDtypeStruct((4, length, local * capacity), jnp.bfloat16),
        ],
        [],
        in_specs=[SMEM] + [VMEM] * 4,
        out_specs=[VMEM] * 2,
        name="routing",
    )(here, *pieces)


def residual_body(hidden, p0, p1, p2, after, out):
    total = hidden[...].astype(jnp.float32) + p0[...].astype(jnp.float32)
    for part in (p1, p2):
        total = total + part[...].astype(jnp.float32)
    out[...] = total.astype(jnp.bfloat16)


def add_parts(hidden, parts, after):
    return call(
        residual_body,
        jax.ShapeDtypeStruct(hidden.shape, jnp.bfloat16),
        [],
        in_specs=[VMEM] * 4 + [pl.BlockSpec(memory_space=pl.ANY)],
        out_specs=VMEM,
        name="residual",
    )(hidden, *parts, after)


def measure_body(*refs):
    *tokens, gain, router, stats = refs
    rows = stats.shape[0]
    length = tokens[0].shape[0]
    for d, ref in enumerate(tokens):
        wide = ref[...].astype(jnp.float32)
        grown = wide * gain[...]
        high = grown.astype(jnp.bfloat16)
        rest = grown - high.astype(jnp.float32)
        middle = rest.astype(jnp.bfloat16)
        low = (rest - middle.astype(jnp.float32)).astype(jnp.bfloat16)
        logits = dot(high, router[...]) + (dot(middle, router[...]) + dot(low, router[...]))
        squares = jnp.sum(wide * wide, axis=1, keepdims=True)
        column = lax.broadcasted_iota(jnp.int32, logits.shape, 1)
        both = jnp.where(column == rows - 8, squares, logits)
        stats[:, d * length : (d + 1) * length] = jnp.transpose(both)[:rows, :]


def squares_and_logits(tokens, gain, router, experts):
    n, length = (len(tokens), tokens[0].shape[0])
    return call(
        measure_body,
        jax.ShapeDtypeStruct((experts + 8, n * length), jnp.float32),
        [],
        in_specs=[VMEM] * (n + 2),
        out_specs=VMEM,
        name="stats",
    )(*tokens, gain, router)


def gate_up_body(ds, order, *refs):
    tokens = refs[: len(ds)]
    gain, pick, weight, out, rows = refs[len(ds) :]
    hid = weight.shape[3]
    capacity = pick.shape[2]
    expert = order[pl.program_id(0)]
    for k, d in enumerate(ds):
        chosen = dot(pick[d, expert], tokens[k][...]) * gain[...]
        rows[k * capacity : (k + 1) * capacity, :] = chosen.astype(jnp.bfloat16)
    for g in range(2):
        out[0, :, g * hid : (g + 1) * hid] = dot(rows[...], weight[0, g]).astype(jnp.bfloat16)


def gate_up(ds, order, tokens, gain, pick, weight):
    _, _, width, hid = weight.shape
    count = order.shape[0]
    capacity = pick.shape[2]
    rows = len(ds) * capacity
    whole = lambda rank: lambda i, order: (0,) * rank
    return call(
        functools.partial(gate_up_body, ds),
        jax.ShapeDtypeStruct((count, rows, 2 * hid), jnp.bfloat16),
        None,
        grid_spec=pltpu.PrefetchScalarGridSpec(
            num_scalar_prefetch=1,
            grid=(count,),
            in_specs=[pl.BlockSpec(tokens[0].shape, whole(2))] * len(ds)
            + [
                pl.BlockSpec(gain.shape, whole(2)),
                pl.BlockSpec(pick.shape, whole(4)),
                pl.BlockSpec((1, 2, width, hid), lambda i, order: (order[i], 0, 0, 0)),
            ],
            out_specs=pl.BlockSpec((1, rows, 2 * hid), lambda i, order: (i, 0, 0)),
            scratch_shapes=[pltpu.VMEM((rows, width), jnp.bfloat16)],
        ),
        name="gate_up",
    )(order, *tokens, gain, pick, weight)


def activate_body(groups, features, here, pick, stats, *refs):
    out = refs[-1]
    _, local, capacity, length = pick.shape
    hid = out.shape[1]
    experts = stats.shape[0] - 8
    device, lane = (here[0], here[1])
    expert = lax.broadcasted_iota(jnp.int32, (experts, length), 0)
    base, refs = (0, list(refs))
    for ds in groups:
        kept, taken, across = refs[:3]
        pieces = refs[3 : 3 + len(ds)]
        refs = refs[3 + len(ds) :]
        for k, d in enumerate(ds):
            ids = pieces[k][pieces[k].shape[0] - 16 :, :].astype(jnp.float32).astype(jnp.int32)
            chosen = jnp.zeros((experts, length), jnp.float32)
            for c in range(8):
                chosen = jnp.where(ids[c : c + 1, :] == expert, 1.0, chosen)
            block = slice((base // capacity + k) * length, (base // capacity + k + 1) * length)
            inv_rms = lax.rsqrt(stats[experts : experts + 1, block] / features + norm_eps)
            logits = jnp.where(chosen > 0.0, stats[:experts, block] * inv_rms, -jnp.inf)
            grown = jnp.exp(logits - jnp.max(logits, axis=0, keepdims=True))
            mix = grown / jnp.sum(grown, axis=0, keepdims=True)
            mine = jnp.where(expert == device * local + lane, mix, 0.0)
            mix = jnp.sum(mine, axis=0, keepdims=True)
            places = pick[d, lane].astype(jnp.float32)
            inv_row = jnp.sum(places * inv_rms, axis=1, keepdims=True)
            mix_row = jnp.sum(places * mix, axis=1, keepdims=True)
            rows = slice(k * capacity, (k + 1) * capacity)
            summed = kept[0, rows, :].astype(jnp.float32) + taken[0, rows, :].astype(jnp.float32)
            summed = (summed + across[rows, :].astype(jnp.float32)) * inv_row
            gate = summed[:, :hid]
            act = gate / (1.0 + jnp.exp(-gate)) * summed[:, hid:] * mix_row
            out[base + k * capacity : base + (k + 1) * capacity, :] = act.astype(jnp.bfloat16)
        base += len(ds) * capacity


def activate(groups, features, here, sums, pick, stats, pieces, flops=1 << 20):
    operands = []
    for ds, terms in zip(groups, sums):
        operands += list(terms) + [pieces[d] for d in ds]
    rows = sum(terms[2].shape[0] for terms in sums)
    return call(
        functools.partial(activate_body, groups, features),
        jax.ShapeDtypeStruct((rows, sums[0][2].shape[1] // 2), jnp.bfloat16),
        [],
        in_specs=[SMEM] + [VMEM] * (2 + len(operands)),
        out_specs=VMEM,
        flops=flops,
        name="activate",
    )(here, pick, stats, *operands)


def down_body(ds, order, a, b, c, d, spread, weight, *rest):
    outs, results = (rest[:-1], rest[-1])
    i = pl.program_id(0)
    capacity = results.shape[2]
    expert = order[i]
    for j, ref in enumerate((a, b, c, d)):

        @pl.when(i == j)
        def _():
            result = dot(ref[...], weight[0]).astype(jnp.bfloat16)
            for k in range(len(ds)):
                results[k, expert] = result[k * capacity : (k + 1) * capacity, :]

    @pl.when(i == pl.num_programs(0) - 1)
    def _():
        half = spread.shape[1] // 2
        for k, d in enumerate(ds):
            rows = results[k].reshape(-1, results.shape[3])
            block = dot(spread[d], rows).astype(jnp.bfloat16)
            if k < len(ds) - 1:
                outs[k][...] = block
            elif len(outs) == len(ds):
                outs[k][...] = block
            else:
                outs[k][...] = block[:half]
                outs[k + 1][...] = block[half:]


def down(ds, order, acts, spread, weight, halved=False):
    local, hid, width = weight.shape
    capacity = acts[0].shape[0] // len(ds)
    length = spread.shape[1]
    shape = jax.ShapeDtypeStruct((length, width), jnp.bfloat16)
    half = jax.ShapeDtypeStruct((length // 2, width), jnp.bfloat16)
    shapes = [shape] * (len(ds) - 1) + [half] * 2 if halved else [shape] * len(ds)
    whole = lambda rank: lambda i, order: (0,) * rank
    return call(
        functools.partial(down_body, ds),
        shapes,
        None,
        grid_spec=pltpu.PrefetchScalarGridSpec(
            num_scalar_prefetch=1,
            grid=(local,),
            in_specs=[pl.BlockSpec(acts[0].shape, whole(2))] * 4
            + [
                pl.BlockSpec(spread.shape, whole(3)),
                pl.BlockSpec((1, hid, width), lambda i, order: (order[i], 0, 0)),
            ],
            out_specs=[pl.BlockSpec(s.shape, whole(2)) for s in shapes],
            scratch_shapes=[pltpu.VMEM((len(ds), local, capacity, width), jnp.bfloat16)],
        ),
        name="down",
    )(order, *acts, spread, weight)


def per_device_square(
    question_q,
    question_kv,
    doc_kv,
    doc_lens,
    query_docs,
    ctx_pos,
    hidden,
    out_proj,
    norm_gain,
    router_weight,
    w_gate_up,
    w_down,
    expert_ids,
):
    n = 4
    lane = lax.axis_index("tp")
    device = lax.axis_index("ep")
    length, heads_here, head_dim = question_q.shape
    pool_dev = doc_kv.shape[0]
    width_here = hidden.shape[1]
    experts = router_weight.shape[1]
    local = w_gate_up.shape[0]
    capacity = length * expert_ids.shape[1] // experts
    here = jnp.stack([device, lane]).astype(jnp.int32)
    order = (lane ^ jnp.array([0, 2, 1, 3], jnp.int32)).astype(jnp.int32)

    pool = jnp.transpose(doc_kv, (0, 2, 3, 1, 4))
    ids_rows = jnp.pad(expert_ids.T.astype(jnp.bfloat16), ((0, 8), (0, 0)))
    pieces = prepare(here, query_docs, pool, ids_rows)
    q_rows, pieces = turn(
        question_q.reshape(length * heads_here, head_dim), question_kv, device, lane, n, pieces
    )
    pieces = [pieces[0]] + [lax.ppermute(pieces[d], "ep", pairs(n, d)) for d in range(1, n)]
    tables = list(angles(here, query_docs, ctx_pos, pool_dev, length, head_dim))

    one = lax.optimization_barrier(jnp.ones((), jnp.bfloat16))
    tables[0], out_proj = lax.optimization_barrier((tables[0], out_proj * one))
    attended = attention(here, query_docs, doc_lens, q_rows, pieces, tables, pool_dev)
    far = lax.ppermute(attended, "tp", pairs(n, 2))
    near = lax.ppermute(attended, "tp", pairs(n, 1))
    farther = lax.ppermute(far, "tp", pairs(n, 1))
    gain = norm_gain.astype(jnp.float32)[None, :]
    router = jnp.pad(router_weight, ((0, 0), (0, 128 - experts)))
    close, early = project(project_early_body, here, (attended, near), out_proj, 2)
    given = lax.ppermute(early, "ep", pairs(n, 1))
    kept, near, late = project(project_late_body, here, (far, farther), out_proj, 3, close)
    kept, w_gate_up = lax.optimization_barrier((kept, w_gate_up))
    late = (late.astype(jnp.float32) + given.astype(jnp.float32)).astype(jnp.bfloat16)
    moves = [
        (e * n + t, (e ^ (3 if t < 2 else 2)) * n + t) for e in range(n) for t in range(n)
    ]
    sent = [kept, lax.ppermute(late, ("ep", "tp"), moves), lax.ppermute(near, "ep", pairs(n, 1))]
    pick, spread = routing(here, pieces, experts, local, capacity)
    weight = jnp.transpose(w_gate_up, (0, 2, 1, 3))
    sent[0], pick, router, gain = lax.optimization_barrier((sent[0], pick, router, gain))
    residual = add_parts(hidden, sent, weight)

    tokens = [residual] + [None] * (n - 1)
    for d in (2, 1):
        tokens[d] = lax.ppermute(residual, "ep", pairs(n, d))
    tokens[3] = lax.ppermute(tokens[2], "ep", pairs(n, 1))

    features = width_here * n

    def spread_act(act, before=()):
        far = lax.ppermute(act, "tp", pairs(n, 2))
        far, *before = lax.optimization_barrier((far, *before))
        near = lax.ppermute(act, "tp", pairs(n, 1))
        return [act, far, near, lax.ppermute(far, "tp", pairs(n, 1))]

    def chip_sum(kept, taken):
        return (kept[1].astype(jnp.float32) + taken[1].astype(jnp.float32)).astype(jnp.bfloat16)

    def terms_of(ds, order):
        blocks = [tokens[d] for d in ds]
        given = gate_up(ds, order[2:], blocks, gain, pick, weight)
        return (gate_up(ds, order[:2], blocks, gain, pick, weight), given)

    def stats_of(ds):
        return squares_and_logits([tokens[d] for d in ds], gain, router, experts)

    one_chunk, two_chunk = ((1, 2), (0, 3))
    kept, given = terms_of(one_chunk, order)
    taken = lax.ppermute(given, "tp", pairs(n, 1))
    _, stats = lax.optimization_barrier((given, stats_of(one_chunk)))
    stats_far = lax.ppermute(stats, "tp", pairs(n, 2))
    taken, stats_far = lax.optimization_barrier((taken, stats_far))
    stats = stats + stats_far
    stats_near = lax.ppermute(stats, "tp", pairs(n, 1))
    far_sum = chip_sum(kept, taken)
    across = lax.ppermute(far_sum, "tp", pairs(n, 2))

    order, _, stats_near = lax.optimization_barrier((order, far_sum, stats_near))
    stats = stats + stats_near
    kept_2, given = terms_of(two_chunk, order)
    stats_2 = stats_of(two_chunk)
    given, across, stats_2 = lax.optimization_barrier((given, across, stats_2))
    stats_far = lax.ppermute(stats_2, "tp", pairs(n, 2))
    taken_2 = lax.ppermute(given, "tp", pairs(n, 1))
    sums = [(kept, taken, across)]
    acts = spread_act(activate((one_chunk,), features, here, sums, pick, stats, pieces))
    far_sum = chip_sum(kept_2, taken_2)
    far_sum, stats_far, acts[1] = lax.optimization_barrier((far_sum, stats_far, acts[1]))
    stats_2 = stats_2 + stats_far
    stats_near = lax.ppermute(stats_2, "tp", pairs(n, 1))
    acts[3] = lax.ppermute(acts[1], "tp", pairs(n, 1))
    across = lax.ppermute(far_sum, "tp", pairs(n, 2))
    near, *far = down(one_chunk, order, acts, spread, w_down, halved=True)
    far = [lax.ppermute(part, "ep", pairs(n, 2)) for part in far]
    across, far[0] = lax.optimization_barrier((across, far[0]))
    sums = [(kept_2, taken_2, across)]
    stats_2 = stats_2 + stats_near
    acts = spread_act(
        activate((two_chunk,), features, here, sums, pick, stats_2, pieces, 1 << 32), far[1:]
    )
    mine, last = down(two_chunk, order, acts, spread, w_down)
    last, near = lax.optimization_barrier((last, near))
    last = lax.ppermute(last, "ep", pairs(n, 3))
    near = lax.ppermute(near, "ep", pairs(n, 1))
    returned = [mine, near, jnp.concatenate(far, axis=0), last]
    total = residual.astype(jnp.float32)
    for part in returned:
        total = total + part.astype(jnp.float32)
    return total.astype(jnp.bfloat16)


def solution(mesh):
    placed = (
        P(("grp", "ep"), "tp", None),
        P(("grp", "ep"), None, None, None),
        P(("grp", "ep"), None, None, None, None),
        P("grp"),
        P("grp", None),
        P("grp", None),
        P(("grp", "ep"), "tp"),
        P("ep", "tp"),
        P("tp"),
        P("tp", None),
        P("ep", "tp", None, None),
        P("ep", None, "tp"),
        P(("grp", "ep"), None),
    )
    def per_device(*args):
        square = (
            lax.axis_size("tp") == 4
            and lax.axis_size("ep") == 4
            and args[1].shape[1] == 4
            and args[4].shape == (4, 4)
        )
        return (per_device_square if square else per_device_general)(*args)

    return jax.shard_map(
        per_device, mesh=mesh, in_specs=placed, out_specs=P(("grp", "ep"), "tp"), check_vma=False
    )
```

```python
import functools
import math

import jax
import jax.numpy as jnp
from jax import lax
from jax.experimental import pallas as pl
from jax.experimental.pallas import tpu as pltpu
from jax.sharding import PartitionSpec as P

rope_theta = 1000000.0
norm_eps = 1e-06


def tables(positions, head_dim):
    half = head_dim // 2
    freq = jnp.exp(jnp.arange(half, dtype=jnp.float32) * (-2.0 * math.log(rope_theta) / head_dim))
    angle = positions.astype(jnp.float32)[:, None] * freq[None, :]
    return (jnp.cos(angle), jnp.sin(angle))


def rotate(values, positions):
    half = values.shape[-1] // 2
    cosine, sine = tables(positions, values.shape[-1])
    shape = (values.shape[0],) + (1,) * (values.ndim - 2) + (half,)
    cosine, sine = (cosine.reshape(shape), sine.reshape(shape))
    floats = values.astype(jnp.float32)
    first = floats[..., :half]
    second = floats[..., half:]
    return jnp.concatenate(
        [first * cosine - second * sine, second * cosine + first * sine], axis=-1
    )


def attend(q_rows, own_kv, context, starts, lengths, question_start):
    length, heads_here, head_dim = q_rows.shape
    docs_per, doc_max, _ = context.shape
    question_pos = question_start + jnp.arange(length, dtype=jnp.int32)
    queries = rotate(q_rows, question_pos).astype(jnp.bfloat16)
    own_keys = rotate(own_kv[:, :head_dim], question_pos).astype(jnp.bfloat16)
    positions = jnp.repeat(starts, doc_max, total_repeat_length=docs_per * doc_max)
    doc_keys = rotate(context[:, :, :head_dim].reshape(docs_per * doc_max, head_dim), positions)
    keys = jnp.concatenate([doc_keys.astype(jnp.bfloat16), own_keys], axis=0)
    values = jnp.concatenate(
        [context[:, :, head_dim:].reshape(docs_per * doc_max, head_dim), own_kv[:, head_dim:]],
        axis=0,
    )
    valid = (jnp.arange(doc_max, dtype=jnp.int32)[None, :] < lengths[:, None]).reshape(-1)
    causal = jnp.arange(length)[:, None] >= jnp.arange(length)[None, :]
    allowed = jnp.concatenate(
        [jnp.broadcast_to(valid[None, :], (length, valid.shape[0])), causal], axis=1
    )
    scores = jnp.einsum("ihd,jd->hij", queries, keys, preferred_element_type=jnp.float32)
    scores = jnp.where(allowed[None], scores * head_dim ** (-0.5), -jnp.inf)
    ceiling = jnp.max(scores, axis=-1, keepdims=True)
    probs = jnp.exp(scores - ceiling)
    denominator = jnp.sum(probs, axis=-1, keepdims=True)
    mixed = jnp.einsum(
        "hij,jd->hid", probs.astype(jnp.bfloat16), values, preferred_element_type=jnp.float32
    )
    return (
        jnp.transpose(mixed / denominator, (1, 0, 2))
        .reshape(length, heads_here * head_dim)
        .astype(jnp.bfloat16)
    )


def context_by_row(doc_kv, doc_lens, query_docs, ctx_pos, device, kv_pick):
    pool_dev, doc_max, _, pair, head_dim = doc_kv.shape
    docs_per = query_docs.shape[1]
    pool_head = lax.dynamic_index_in_dim(doc_kv, kv_pick, 2, keepdims=False).reshape(
        pool_dev, doc_max, pair * head_dim
    )
    held = device * pool_dev + jnp.arange(pool_dev, dtype=jnp.int32)
    wanted = jnp.sum((query_docs[:, :, None] == held[None, None, :]).astype(jnp.float32), axis=1)
    sending = jnp.einsum(
        "rl,lkc->rkc", wanted.astype(jnp.bfloat16), pool_head, preferred_element_type=jnp.float32
    ).astype(jnp.bfloat16)
    received = lax.all_to_all(sending, "ep", split_axis=0, concat_axis=0, tiled=True)
    my_docs = lax.dynamic_index_in_dim(query_docs, device, 0, keepdims=False)
    starts = lax.dynamic_index_in_dim(ctx_pos, device, 0, keepdims=False)
    return (jnp.take(received, my_docs // pool_dev, axis=0), starts[:docs_per], jnp.take(doc_lens, my_docs))


def per_device_general(
    question_q,
    question_kv,
    doc_kv,
    doc_lens,
    query_docs,
    ctx_pos,
    hidden,
    out_proj,
    norm_gain,
    router_weight,
    w_gate_up,
    w_down,
    expert_ids,
):
    lanes = lax.axis_size("tp")
    groups = lax.axis_size("ep")
    lane = lax.axis_index("tp")
    device = lax.axis_index("ep")
    length, heads_here, head_dim = question_q.shape
    kv_heads = question_kv.shape[1]
    docs_per = query_docs.shape[1]
    width_here = hidden.shape[1]
    ids = lax.all_gather(expert_ids, "ep", axis=0, tiled=False)
    kv_pick = lane * kv_heads // lanes
    kv_head = lax.dynamic_index_in_dim(question_kv, kv_pick, 1, keepdims=False).reshape(
        length, 2 * head_dim
    )
    context, starts, lengths = context_by_row(
        doc_kv, doc_lens, query_docs, ctx_pos, device, kv_pick
    )
    question_start = lax.dynamic_index_in_dim(ctx_pos, device, 0, keepdims=False)[docs_per]
    attended = attend(question_q, kv_head, context, starts, lengths, question_start)
    projected = jnp.dot(
        lax.all_gather(attended, "tp", axis=1, tiled=True),
        lax.all_gather(out_proj, "ep", axis=0, tiled=True),
        preferred_element_type=jnp.float32,
    )
    residual = (hidden.astype(jnp.float32) + projected.astype(jnp.float32)).astype(jnp.bfloat16)

    tokens = lax.all_gather(residual, "ep", axis=0, tiled=False)
    wide = tokens.astype(jnp.float32)
    gain = norm_gain.astype(jnp.float32)
    scaled = wide * gain
    logit_part = jnp.einsum(
        "snd,de->sne", scaled, router_weight.astype(jnp.float32), precision=lax.Precision.HIGHEST
    )
    square_part = jnp.sum(wide * wide, axis=2, keepdims=True)
    stats = jnp.sum(
        lax.all_gather(jnp.concatenate([logit_part, square_part], axis=2), "tp", axis=0), axis=0
    )
    experts = router_weight.shape[1]
    inv_rms = lax.rsqrt(stats[:, :, experts] / (width_here * lanes) + norm_eps)
    logits = stats[:, :, :experts] * inv_rms[:, :, None]

    local_experts = w_gate_up.shape[0]
    capacity = length * expert_ids.shape[1] // experts
    hid = w_gate_up.shape[3]
    chosen_all = jnp.any(
        ids[:, :, :, None] == jnp.arange(experts, dtype=jnp.int32), axis=2
    )
    top = jnp.max(jnp.where(chosen_all, logits, -jnp.inf), axis=2, keepdims=True)
    weight = jnp.where(chosen_all, jnp.exp(logits - top), 0.0)
    mix = weight / jnp.sum(weight, axis=2, keepdims=True)

    shuffled, scaled_rows = (chosen_all, scaled.astype(jnp.bfloat16))
    first = device * local_experts
    chosen = lax.dynamic_slice_in_dim(shuffled, first, local_experts, 2)
    mix_here = lax.dynamic_slice_in_dim(mix, first, local_experts, 2)
    before = (jnp.arange(length)[:, None] > jnp.arange(length)[None, :]).astype(jnp.bfloat16)
    rank = jnp.einsum(
        "mn,sne->sem", before, chosen.astype(jnp.bfloat16), preferred_element_type=jnp.float32
    ).astype(jnp.int32)
    pick = jnp.logical_and(
        jnp.transpose(chosen, (0, 2, 1))[:, :, None, :],
        rank[:, :, None, :] == jnp.arange(capacity, dtype=jnp.int32)[None, None, :, None],
    )
    onehot = pick.astype(jnp.bfloat16)
    inv_row = jnp.sum(jnp.where(pick, inv_rms[:, None, None, :], 0.0), axis=3)
    mix_row = jnp.sum(jnp.where(pick, jnp.transpose(mix_here, (0, 2, 1))[:, :, None, :], 0.0), axis=3)

    rows = jnp.einsum(
        "sern,snd->serd", onehot, scaled_rows, preferred_element_type=jnp.float32
    ).astype(jnp.bfloat16)
    term = jnp.einsum(
        "serd,edgh->sergh", rows, w_gate_up, preferred_element_type=jnp.float32
    ).astype(jnp.bfloat16)
    per_lane = groups * local_experts * capacity // lanes
    term = term.reshape(lanes, per_lane, 2 * hid)
    inv_row = inv_row.reshape(lanes, per_lane, 1)
    summed = lax.psum_scatter(term, "tp", scatter_dimension=0, tiled=True)[0].astype(jnp.float32)
    inv_mine = lax.dynamic_index_in_dim(inv_row, lane, 0, keepdims=False)
    summed = summed * inv_mine
    act = (jax.nn.silu(summed[:, :hid]) * summed[:, hid:]).astype(jnp.bfloat16)
    acts = lax.all_gather(act, "tp", axis=0, tiled=False)
    acts = acts.reshape(groups, local_experts, capacity, hid)
    expert_out = jnp.einsum("serh,ehd->serd", acts, w_down, preferred_element_type=jnp.float32)
    expert_out = (expert_out * mix_row[:, :, :, None]).astype(jnp.bfloat16)
    combined = jnp.einsum(
        "sern,serd->snd", onehot, expert_out, preferred_element_type=jnp.float32
    ).astype(jnp.bfloat16)
    returned = lax.psum_scatter(combined, "ep", scatter_dimension=0, tiled=True)[0]
    return (residual.astype(jnp.float32) + returned.astype(jnp.float32)).astype(jnp.bfloat16)


def pairs(lanes, flip):
    return [(i, i ^ flip) for i in range(lanes)]


def query_of(device, lane):
    return 2 * (lane & 1) + ((lane >> 1) ^ (device & 1))


def turn(question, keys_values, device, lane, n, meanwhile):
    crosses = lambda e, t: ((e ^ t) & 1) != (t >> 1)
    devices = [(e, t) for e in range(n) for t in range(n)]
    swap = [(e * n + t, e * n + (t ^ 3)) for e, t in devices if crosses(e, t)]
    crossed = lax.ppermute(question, ("ep", "tp"), swap)
    crossed, *meanwhile = lax.optimization_barrier((crossed, *meanwhile))
    heads = jnp.where(crosses(device, lane), lane ^ 3, lane)
    picked = lax.dynamic_index_in_dim(keys_values, heads, 1, keepdims=False)
    picked = jnp.transpose(picked, (1, 0, 2)).reshape(-1, question.shape[1])
    held = jnp.where(crosses(device, lane), crossed, question)
    moves = []
    for e, t in devices:
        h = t ^ 3 if crosses(e, t) else t
        moves.append((e * n + t, h * n + 2 * ((e ^ h) & 1) + (e >> 1)))
    return (lax.ppermute(jnp.concatenate([held, picked], axis=0), ("ep", "tp"), moves), meanwhile)


def call(body, outs, scratch, flops=1 << 20, **kwargs):
    return pl.pallas_call(
        body,
        out_shape=outs,
        **({} if scratch is None else {"scratch_shapes": scratch}),
        compiler_params=pltpu.CompilerParams(vmem_limit_bytes=20 * 1024 * 1024),
        cost_estimate=pl.CostEstimate(flops=flops, bytes_accessed=1 << 18, transcendentals=0),
        **kwargs,
    )


VMEM = pl.BlockSpec(memory_space=pltpu.VMEM)
SMEM = pl.BlockSpec(memory_space=pltpu.SMEM)
NT = (((1,), (1,)), ((), ()))


def dot(a, b):
    return jnp.dot(a, b, preferred_element_type=jnp.float32)


def document_slots(here, query_docs, pool_dev):
    device, lane = (here[0], here[1])
    query = query_of(device, lane)
    slots = []
    for d in range(4):
        slot = jnp.int32(0)
        for j in range(query_docs.shape[1]):
            offset = query_docs[query, j] - (device ^ d) * pool_dev
            slot = jnp.where(jnp.logical_and(offset >= 0, offset < pool_dev), j, slot)
        slots.append(slot)
    return (query, slots)


def prepare_body(here, query_docs, pool, ids, *outs):
    pool_dev = pool.shape[0]
    docs_per = query_docs.shape[1]
    rows = pool.shape[2] * pool.shape[3]
    device, lane = (here[0], here[1])
    for d, out in enumerate(outs):
        target = device ^ d
        query = query_of(target, lane)
        local = jnp.int32(0)
        for j in range(docs_per):
            offset = query_docs[query, j] - device * pool_dev
            inside = jnp.logical_and(offset >= 0, offset < pool_dev)
            local = jnp.where(inside, offset, local)
        out[:rows, :] = pool[local, target].reshape(rows, pool.shape[4])
        out[rows:, :] = ids[...]


def prepare(here, query_docs, pool, ids):
    _, _, pair, doc_max, head_dim = pool.shape
    shape = jax.ShapeDtypeStruct((pair * doc_max + ids.shape[0], head_dim), jnp.bfloat16)
    return call(
        prepare_body,
        [shape] * 4,
        [],
        in_specs=[SMEM, SMEM, VMEM, VMEM],
        out_specs=[VMEM] * 4,
        name="prepare",
    )(here, query_docs, pool, ids)


def angles_body(pool_dev, here, query_docs, ctx_pos, cos_q, sin_q, cos_d, sin_d):
    query, slots = document_slots(here, query_docs, pool_dev)
    docs_per = query_docs.shape[1]
    head_dim = cos_q.shape[1]

    def fill(starts, cosine, sine):
        column = lax.broadcasted_iota(jnp.int32, cosine.shape, 1)
        half = jnp.where(column < head_dim // 2, column, column - head_dim // 2)
        freq = jnp.exp(half.astype(jnp.float32) * (-2.0 * math.log(rope_theta) / head_dim))
        angle = starts.astype(jnp.float32) * freq
        cosine[...] = jnp.cos(angle)
        wave = jnp.sin(angle)
        sine[...] = jnp.where(column < head_dim // 2, -wave, wave)

    row = lax.broadcasted_iota(jnp.int32, cos_q.shape, 0)
    fill(ctx_pos[query, docs_per] + row, cos_q, sin_q)
    row = lax.broadcasted_iota(jnp.int32, cos_d.shape, 0)
    starts = jnp.zeros(cos_d.shape, jnp.int32)
    for d, slot in enumerate(slots):
        starts = jnp.where(row == d, ctx_pos[query, slot], starts)
    fill(starts, cos_d, sin_d)


def angles(here, query_docs, ctx_pos, pool_dev, length, head_dim):
    shapes = [jax.ShapeDtypeStruct((rows, head_dim), jnp.float32) for rows in (length, length, 8, 8)]
    return call(
        functools.partial(angles_body, pool_dev),
        shapes,
        [],
        in_specs=[SMEM] * 3,
        out_specs=[VMEM] * 4,
        name="angles",
    )(here, query_docs, ctx_pos)


def attention_body(
    pool_dev, here, query_docs, doc_lens, q, c0, c1, c2, c3, cos_q, sin_q, cos_d, sin_d, out, wide, keys, vals
):
    length, head_dim = cos_q.shape
    heads = out.shape[1] // head_dim
    pieces = (c0, c1, c2, c3)
    docs = len(pieces)
    doc_max = (keys.shape[0] - length) // docs
    half = head_dim // 2
    query, slots = document_slots(here, query_docs, pool_dev)

    def turned(x, cosine, sine):
        return x * cosine + pltpu.roll(x, half, 1) * sine

    cosine, sine = (cos_q[...], sin_q[...])
    for j, piece in enumerate(pieces):
        key = turned(piece[:doc_max, :].astype(jnp.float32), cos_d[j : j + 1, :], sin_d[j : j + 1, :])
        keys[j * doc_max : (j + 1) * doc_max, :] = key.astype(jnp.bfloat16)
        vals[j * doc_max : (j + 1) * doc_max, :] = piece[doc_max : 2 * doc_max, :]
    base = docs * doc_max
    first = heads * length
    keys[base:, :] = turned(q[first : first + length, :].astype(jnp.float32), cosine, sine).astype(
        jnp.bfloat16
    )
    vals[base:, :] = q[first + length :, :]
    wide[...] = q[:first, :].astype(jnp.float32)
    column = lax.broadcasted_iota(jnp.int32, (1, doc_max), 1)
    allowed = [column < doc_lens[query_docs[query, slot]] for slot in slots]
    causal = lax.broadcasted_iota(jnp.int32, (length, length), 0) >= lax.broadcasted_iota(
        jnp.int32, (length, length), 1
    )
    for h in range(heads):
        rows = turned(wide[pl.ds(h, length, stride=heads), :], cosine, sine).astype(jnp.bfloat16)
        scores = lax.dot_general(rows, keys[...], NT, preferred_element_type=jnp.float32)
        scores = scores * head_dim ** (-0.5)
        parts = [
            jnp.where(allowed[j], scores[:, j * doc_max : (j + 1) * doc_max], -jnp.inf)
            for j in range(docs)
        ] + [jnp.where(causal, scores[:, base:], -jnp.inf)]
        scores = jnp.concatenate(parts, axis=1)
        ceiling = jnp.max(scores, axis=1, keepdims=True)
        probs = jnp.exp(scores - ceiling)
        denominator = jnp.sum(probs, axis=1, keepdims=True)
        mixed = dot(probs.astype(jnp.bfloat16), vals[...])
        out[:, h * head_dim : (h + 1) * head_dim] = (mixed / denominator).astype(jnp.bfloat16)


def attention(here, query_docs, doc_lens, q, pieces, tables, pool_dev):
    length, head_dim = tables[0].shape
    heads = q.shape[0] // length - 2
    rows = 5 * length
    return call(
        functools.partial(attention_body, pool_dev),
        jax.ShapeDtypeStruct((length, heads * head_dim), jnp.bfloat16),
        [
            pltpu.VMEM((heads * length, head_dim), jnp.float32),
            pltpu.VMEM((rows, head_dim), jnp.bfloat16),
            pltpu.VMEM((rows, head_dim), jnp.bfloat16),
        ],
        in_specs=[SMEM] * 3 + [VMEM] * 9,
        out_specs=VMEM,
        name="attention",
    )(here, query_docs, doc_lens, q, *pieces, *tables)


def project_rows(here, flip, a, b, rows):
    device, lane = (here[0], here[1])
    high = (device ^ query_of(device, lane ^ flip)) >> 1
    rows[high] = a[...]
    rows[1 - high] = b[...]


def project_early_body(here, a, b, weight, close, far, rows):
    project_rows(here, 0, a, b, rows)
    far[...] = dot(rows[1], weight[...]).astype(jnp.bfloat16)
    close[...] = dot(rows[0], weight[...]).astype(jnp.bfloat16)


def project_late_body(here, a, b, weight, early, own, near, far, rows):
    project_rows(here, 2, a, b, rows)
    far[...] = dot(rows[1], weight[...]).astype(jnp.bfloat16)
    late = dot(rows[0], weight[...]).astype(jnp.bfloat16)
    first = here[1] < 2
    own[...] = jnp.where(first, early[...], late)
    near[...] = jnp.where(first, late, early[...])


def project(body, here, parts, weight, outs, *early):
    length, depth = parts[0].shape
    return call(
        body,
        [jax.ShapeDtypeStruct((length, weight.shape[1]), jnp.bfloat16)] * outs,
        [pltpu.VMEM((2, length, depth), jnp.bfloat16)],
        in_specs=[SMEM] + [VMEM] * (3 + len(early)),
        out_specs=[VMEM] * outs,
        name="project",
    )(here, *parts, weight, *early)


def routing_body(experts, here, c0, c1, c2, c3, pick, spread):
    _, local, capacity, length = pick.shape
    first = here[0] * local
    before = (
        lax.broadcasted_iota(jnp.int32, (length, length), 0)
        < lax.broadcasted_iota(jnp.int32, (length, length), 1)
    ).astype(jnp.bfloat16)
    place = lax.broadcasted_iota(jnp.int32, (capacity, length), 0).astype(jnp.float32)
    row = lax.broadcasted_iota(jnp.int32, (8, length), 0)
    for d, piece in enumerate((c0, c1, c2, c3)):
        ids = piece[piece.shape[0] - 16 :, :].astype(jnp.float32).astype(jnp.int32)
        chosen = jnp.zeros((8, length), jnp.float32)
        for k in range(8):
            named = jnp.logical_and(ids[k : k + 1, :] == first + row, row < local)
            chosen = jnp.where(named, 1.0, chosen)
        rank = dot(chosen.astype(jnp.bfloat16), before)
        wide = []
        for e in range(local):
            here_e = jnp.logical_and(rank[e : e + 1, :] == place, chosen[e : e + 1, :] > 0.0)
            wide.append(jnp.where(here_e, 1.0, 0.0))
            pick[d, e] = wide[-1].astype(jnp.bfloat16)
        spread[d] = jnp.transpose(jnp.concatenate(wide, axis=0)).astype(jnp.bfloat16)


def routing(here, pieces, experts, local, capacity):
    length = pieces[0].shape[1]
    rows = pieces[0].shape[0]
    return call(
        functools.partial(routing_body, experts),
        [
            jax.ShapeDtypeStruct((4, local, capacity, length), jnp.bfloat16),
            jax.ShapeDtypeStruct((4, length, local * capacity), jnp.bfloat16),
        ],
        [],
        in_specs=[SMEM] + [VMEM] * 4,
        out_specs=[VMEM] * 2,
        name="routing",
    )(here, *pieces)


def residual_body(hidden, p0, p1, p2, after, out):
    total = hidden[...].astype(jnp.float32) + p0[...].astype(jnp.float32)
    for part in (p1, p2):
        total = total + part[...].astype(jnp.float32)
    out[...] = total.astype(jnp.bfloat16)


def add_parts(hidden, parts, after):
    return call(
        residual_body,
        jax.ShapeDtypeStruct(hidden.shape, jnp.bfloat16),
        [],
        in_specs=[VMEM] * 4 + [pl.BlockSpec(memory_space=pl.ANY)],
        out_specs=VMEM,
        name="residual",
    )(hidden, *parts, after)


def measure_body(*refs):
    *tokens, gain, router, stats = refs
    rows = stats.shape[0]
    length = tokens[0].shape[0]
    for d, ref in enumerate(tokens):
        wide = ref[...].astype(jnp.float32)
        grown = wide * gain[...]
        high = grown.astype(jnp.bfloat16)
        rest = grown - high.astype(jnp.float32)
        middle = rest.astype(jnp.bfloat16)
        low = (rest - middle.astype(jnp.float32)).astype(jnp.bfloat16)
        logits = dot(high, router[...]) + (dot(middle, router[...]) + dot(low, router[...]))
        squares = jnp.sum(wide * wide, axis=1, keepdims=True)
        column = lax.broadcasted_iota(jnp.int32, logits.shape, 1)
        both = jnp.where(column == rows - 8, squares, logits)
        stats[:, d * length : (d + 1) * length] = jnp.transpose(both)[:rows, :]


def squares_and_logits(tokens, gain, router, experts):
    n, length = (len(tokens), tokens[0].shape[0])
    return call(
        measure_body,
        jax.ShapeDtypeStruct((experts + 8, n * length), jnp.float32),
        [],
        in_specs=[VMEM] * (n + 2),
        out_specs=VMEM,
        name="stats",
    )(*tokens, gain, router)


def gate_up_body(ds, order, *refs):
    tokens = refs[: len(ds)]
    gain, pick, weight, out, rows = refs[len(ds) :]
    hid = weight.shape[3]
    capacity = pick.shape[2]
    expert = order[pl.program_id(0)]
    for k, d in enumerate(ds):
        chosen = dot(pick[d, expert], tokens[k][...]) * gain[...]
        rows[k * capacity : (k + 1) * capacity, :] = chosen.astype(jnp.bfloat16)
    for g in range(2):
        out[0, :, g * hid : (g + 1) * hid] = dot(rows[...], weight[0, g]).astype(jnp.bfloat16)


def gate_up(ds, order, tokens, gain, pick, weight):
    _, _, width, hid = weight.shape
    count = order.shape[0]
    capacity = pick.shape[2]
    rows = len(ds) * capacity
    whole = lambda rank: lambda i, order: (0,) * rank
    return call(
        functools.partial(gate_up_body, ds),
        jax.ShapeDtypeStruct((count, rows, 2 * hid), jnp.bfloat16),
        None,
        grid_spec=pltpu.PrefetchScalarGridSpec(
            num_scalar_prefetch=1,
            grid=(count,),
            in_specs=[pl.BlockSpec(tokens[0].shape, whole(2))] * len(ds)
            + [
                pl.BlockSpec(gain.shape, whole(2)),
                pl.BlockSpec(pick.shape, whole(4)),
                pl.BlockSpec((1, 2, width, hid), lambda i, order: (order[i], 0, 0, 0)),
            ],
            out_specs=pl.BlockSpec((1, rows, 2 * hid), lambda i, order: (i, 0, 0)),
            scratch_shapes=[pltpu.VMEM((rows, width), jnp.bfloat16)],
        ),
        name="gate_up",
    )(order, *tokens, gain, pick, weight)


def activate_body(groups, features, here, pick, stats, *refs):
    out = refs[-1]
    _, local, capacity, length = pick.shape
    hid = out.shape[1]
    experts = stats.shape[0] - 8
    device, lane = (here[0], here[1])
    expert = lax.broadcasted_iota(jnp.int32, (experts, length), 0)
    base, refs = (0, list(refs))
    for ds in groups:
        kept, taken, across = refs[:3]
        pieces = refs[3 : 3 + len(ds)]
        refs = refs[3 + len(ds) :]
        for k, d in enumerate(ds):
            ids = pieces[k][pieces[k].shape[0] - 16 :, :].astype(jnp.float32).astype(jnp.int32)
            chosen = jnp.zeros((experts, length), jnp.float32)
            for c in range(8):
                chosen = jnp.where(ids[c : c + 1, :] == expert, 1.0, chosen)
            block = slice((base // capacity + k) * length, (base // capacity + k + 1) * length)
            inv_rms = lax.rsqrt(stats[experts : experts + 1, block] / features + norm_eps)
            logits = jnp.where(chosen > 0.0, stats[:experts, block] * inv_rms, -jnp.inf)
            grown = jnp.exp(logits - jnp.max(logits, axis=0, keepdims=True))
            mix = grown / jnp.sum(grown, axis=0, keepdims=True)
            mine = jnp.where(expert == device * local + lane, mix, 0.0)
            mix = jnp.sum(mine, axis=0, keepdims=True)
            places = pick[d, lane].astype(jnp.float32)
            inv_row = jnp.sum(places * inv_rms, axis=1, keepdims=True)
            mix_row = jnp.sum(places * mix, axis=1, keepdims=True)
            rows = slice(k * capacity, (k + 1) * capacity)
            summed = kept[0, rows, :].astype(jnp.float32) + taken[0, rows, :].astype(jnp.float32)
            summed = (summed + across[rows, :].astype(jnp.float32)) * inv_row
            gate = summed[:, :hid]
            act = gate / (1.0 + jnp.exp(-gate)) * summed[:, hid:] * mix_row
            out[base + k * capacity : base + (k + 1) * capacity, :] = act.astype(jnp.bfloat16)
        base += len(ds) * capacity


def activate(groups, features, here, sums, pick, stats, pieces, flops=1 << 20):
    operands = []
    for ds, terms in zip(groups, sums):
        operands += list(terms) + [pieces[d] for d in ds]
    rows = sum(terms[2].shape[0] for terms in sums)
    return call(
        functools.partial(activate_body, groups, features),
        jax.ShapeDtypeStruct((rows, sums[0][2].shape[1] // 2), jnp.bfloat16),
        [],
        in_specs=[SMEM] + [VMEM] * (2 + len(operands)),
        out_specs=VMEM,
        flops=flops,
        name="activate",
    )(here, pick, stats, *operands)


def down_body(ds, order, a, b, c, d, spread, weight, *rest):
    outs, results = (rest[:-1], rest[-1])
    i = pl.program_id(0)
    capacity = results.shape[2]
    expert = order[i]
    for j, ref in enumerate((a, b, c, d)):

        @pl.when(i == j)
        def _():
            result = dot(ref[...], weight[0]).astype(jnp.bfloat16)
            for k in range(len(ds)):
                results[k, expert] = result[k * capacity : (k + 1) * capacity, :]

    @pl.when(i == pl.num_programs(0) - 1)
    def _():
        half = spread.shape[1] // 2
        for k, d in enumerate(ds):
            rows = results[k].reshape(-1, results.shape[3])
            block = dot(spread[d], rows).astype(jnp.bfloat16)
            if len(outs) == len(ds):
                outs[k][...] = block
            else:
                outs[2 * k][...] = block[:half]
                outs[2 * k + 1][...] = block[half:]


def down(ds, order, acts, spread, weight, halved=False):
    local, hid, width = weight.shape
    capacity = acts[0].shape[0] // len(ds)
    length = spread.shape[1]
    shape = jax.ShapeDtypeStruct((length, width), jnp.bfloat16)
    half = jax.ShapeDtypeStruct((length // 2, width), jnp.bfloat16)
    shapes = [half] * (2 * len(ds)) if halved else [shape] * len(ds)
    whole = lambda rank: lambda i, order: (0,) * rank
    return call(
        functools.partial(down_body, ds),
        shapes,
        None,
        grid_spec=pltpu.PrefetchScalarGridSpec(
            num_scalar_prefetch=1,
            grid=(local,),
            in_specs=[pl.BlockSpec(acts[0].shape, whole(2))] * 4
            + [
                pl.BlockSpec(spread.shape, whole(3)),
                pl.BlockSpec((1, hid, width), lambda i, order: (order[i], 0, 0)),
            ],
            out_specs=[pl.BlockSpec(s.shape, whole(2)) for s in shapes],
            scratch_shapes=[pltpu.VMEM((len(ds), local, capacity, width), jnp.bfloat16)],
        ),
        name="down",
    )(order, *acts, spread, weight)


def per_device_square(
    question_q,
    question_kv,
    doc_kv,
    doc_lens,
    query_docs,
    ctx_pos,
    hidden,
    out_proj,
    norm_gain,
    router_weight,
    w_gate_up,
    w_down,
    expert_ids,
):
    n = 4
    lane = lax.axis_index("tp")
    device = lax.axis_index("ep")
    length, heads_here, head_dim = question_q.shape
    pool_dev = doc_kv.shape[0]
    width_here = hidden.shape[1]
    experts = router_weight.shape[1]
    local = w_gate_up.shape[0]
    capacity = length * expert_ids.shape[1] // experts
    here = jnp.stack([device, lane]).astype(jnp.int32)
    order = (lane ^ jnp.array([0, 2, 1, 3], jnp.int32)).astype(jnp.int32)

    pool = jnp.transpose(doc_kv, (0, 2, 3, 1, 4))
    ids_rows = jnp.pad(expert_ids.T.astype(jnp.bfloat16), ((0, 8), (0, 0)))
    pieces = prepare(here, query_docs, pool, ids_rows)
    q_rows, pieces = turn(
        question_q.reshape(length * heads_here, head_dim), question_kv, device, lane, n, pieces
    )
    pieces = [pieces[0]] + [lax.ppermute(pieces[d], "ep", pairs(n, d)) for d in range(1, n)]
    tables = list(angles(here, query_docs, ctx_pos, pool_dev, length, head_dim))

    one = lax.optimization_barrier(jnp.ones((), jnp.bfloat16))
    tables[0], out_proj = lax.optimization_barrier((tables[0], out_proj * one))
    attended = attention(here, query_docs, doc_lens, q_rows, pieces, tables, pool_dev)
    far = lax.ppermute(attended, "tp", pairs(n, 2))
    near = lax.ppermute(attended, "tp", pairs(n, 1))
    farther = lax.ppermute(far, "tp", pairs(n, 1))
    gain = norm_gain.astype(jnp.float32)[None, :]
    router = jnp.pad(router_weight, ((0, 0), (0, 128 - experts)))
    close, early = project(project_early_body, here, (attended, near), out_proj, 2)
    given = lax.ppermute(early, "ep", pairs(n, 1))
    kept, near, late = project(project_late_body, here, (far, farther), out_proj, 3, close)
    kept, w_gate_up = lax.optimization_barrier((kept, w_gate_up))
    late = (late.astype(jnp.float32) + given.astype(jnp.float32)).astype(jnp.bfloat16)
    moves = [
        (e * n + t, (e ^ (3 if t < 2 else 2)) * n + t) for e in range(n) for t in range(n)
    ]
    sent = [kept, lax.ppermute(late, ("ep", "tp"), moves), lax.ppermute(near, "ep", pairs(n, 1))]
    pick, spread = routing(here, pieces, experts, local, capacity)
    weight = jnp.transpose(w_gate_up, (0, 2, 1, 3))
    sent[0], pick, router, gain = lax.optimization_barrier((sent[0], pick, router, gain))
    residual = add_parts(hidden, sent, weight)

    tokens = [residual] + [None] * (n - 1)
    for d in (2, 1):
        tokens[d] = lax.ppermute(residual, "ep", pairs(n, d))
    tokens[3] = lax.ppermute(tokens[2], "ep", pairs(n, 1))

    features = width_here * n

    def spread_act(act, before=()):
        far = lax.ppermute(act, "tp", pairs(n, 2))
        far, *before = lax.optimization_barrier((far, *before))
        near = lax.ppermute(act, "tp", pairs(n, 1))
        return [act, far, near, lax.ppermute(far, "tp", pairs(n, 1))]

    def chip_sum(kept, taken):
        return (kept[1].astype(jnp.float32) + taken[1].astype(jnp.float32)).astype(jnp.bfloat16)

    def terms_of(ds, order):
        blocks = [tokens[d] for d in ds]
        given = gate_up(ds, order[2:], blocks, gain, pick, weight)
        return (gate_up(ds, order[:2], blocks, gain, pick, weight), given)

    def stats_of(ds):
        return squares_and_logits([tokens[d] for d in ds], gain, router, experts)

    one_chunk, two_chunk = ((1, 2), (0, 3))
    kept, given = terms_of(one_chunk, order)
    taken = lax.ppermute(given, "tp", pairs(n, 1))
    _, stats = lax.optimization_barrier((given, stats_of(one_chunk)))
    stats_far = lax.ppermute(stats, "tp", pairs(n, 2))
    taken, stats_far = lax.optimization_barrier((taken, stats_far))
    stats = stats + stats_far
    stats_near = lax.ppermute(stats, "tp", pairs(n, 1))
    far_sum = chip_sum(kept, taken)
    across = lax.ppermute(far_sum, "tp", pairs(n, 2))

    order, _, stats_near = lax.optimization_barrier((order, far_sum, stats_near))
    stats = stats + stats_near
    kept_2, given = terms_of(two_chunk, order)
    stats_2 = stats_of(two_chunk)
    given, across, stats_2 = lax.optimization_barrier((given, across, stats_2))
    stats_far = lax.ppermute(stats_2, "tp", pairs(n, 2))
    taken_2 = lax.ppermute(given, "tp", pairs(n, 1))
    sums = [(kept, taken, across)]
    acts = spread_act(activate((one_chunk,), features, here, sums, pick, stats, pieces))
    far_sum = chip_sum(kept_2, taken_2)
    far_sum, stats_far, acts[1] = lax.optimization_barrier((far_sum, stats_far, acts[1]))
    stats_2 = stats_2 + stats_far
    stats_near = lax.ppermute(stats_2, "tp", pairs(n, 1))
    acts[3] = lax.ppermute(acts[1], "tp", pairs(n, 1))
    across = lax.ppermute(far_sum, "tp", pairs(n, 2))
    parts = down(one_chunk, order, acts, spread, w_down, halved=True)
    far = [lax.ppermute(part, "ep", pairs(n, 2)) for part in parts[2:]]
    near = [lax.ppermute(part, "ep", pairs(n, 1)) for part in parts[:2]]
    across, far[0], near[0] = lax.optimization_barrier((across, far[0], near[0]))
    sums = [(kept_2, taken_2, across)]
    stats_2 = stats_2 + stats_near
    acts = spread_act(
        activate((two_chunk,), features, here, sums, pick, stats_2, pieces, 1 << 32),
        (far[1], near[1]),
    )
    mine, last = down(two_chunk, order, acts, spread, w_down)
    last = lax.ppermute(last, "ep", pairs(n, 3))
    returned = [mine, jnp.concatenate(near, axis=0), jnp.concatenate(far, axis=0), last]
    total = residual.astype(jnp.float32)
    for part in returned:
        total = total + part.astype(jnp.float32)
    return total.astype(jnp.bfloat16)


def solution(mesh):
    placed = (
        P(("grp", "ep"), "tp", None),
        P(("grp", "ep"), None, None, None),
        P(("grp", "ep"), None, None, None, None),
        P("grp"),
        P("grp", None),
        P("grp", None),
        P(("grp", "ep"), "tp"),
        P("ep", "tp"),
        P("tp"),
        P("tp", None),
        P("ep", "tp", None, None),
        P("ep", None, "tp"),
        P(("grp", "ep"), None),
    )
    def per_device(*args):
        square = (
            lax.axis_size("tp") == 4
            and lax.axis_size("ep") == 4
            and args[1].shape[1] == 4
            and args[4].shape == (4, 4)
        )
        return (per_device_square if square else per_device_general)(*args)

    return jax.shard_map(
        per_device, mesh=mesh, in_specs=placed, out_specs=P(("grp", "ep"), "tp"), check_vma=False
    )
```

```python
import functools
import math

import jax
import jax.numpy as jnp
from jax import lax
from jax.experimental import pallas as pl
from jax.experimental.pallas import tpu as pltpu
from jax.sharding import PartitionSpec as P

rope_theta = 1000000.0
norm_eps = 1e-06


def tables(positions, head_dim):
    half = head_dim // 2
    freq = jnp.exp(jnp.arange(half, dtype=jnp.float32) * (-2.0 * math.log(rope_theta) / head_dim))
    angle = positions.astype(jnp.float32)[:, None] * freq[None, :]
    return (jnp.cos(angle), jnp.sin(angle))


def rotate(values, positions):
    half = values.shape[-1] // 2
    cosine, sine = tables(positions, values.shape[-1])
    shape = (values.shape[0],) + (1,) * (values.ndim - 2) + (half,)
    cosine, sine = (cosine.reshape(shape), sine.reshape(shape))
    floats = values.astype(jnp.float32)
    first = floats[..., :half]
    second = floats[..., half:]
    return jnp.concatenate(
        [first * cosine - second * sine, second * cosine + first * sine], axis=-1
    )


def attend(q_rows, own_kv, context, starts, lengths, question_start):
    length, heads_here, head_dim = q_rows.shape
    docs_per, doc_max, _ = context.shape
    question_pos = question_start + jnp.arange(length, dtype=jnp.int32)
    queries = rotate(q_rows, question_pos).astype(jnp.bfloat16)
    own_keys = rotate(own_kv[:, :head_dim], question_pos).astype(jnp.bfloat16)
    positions = jnp.repeat(starts, doc_max, total_repeat_length=docs_per * doc_max)
    doc_keys = rotate(context[:, :, :head_dim].reshape(docs_per * doc_max, head_dim), positions)
    keys = jnp.concatenate([doc_keys.astype(jnp.bfloat16), own_keys], axis=0)
    values = jnp.concatenate(
        [context[:, :, head_dim:].reshape(docs_per * doc_max, head_dim), own_kv[:, head_dim:]],
        axis=0,
    )
    valid = (jnp.arange(doc_max, dtype=jnp.int32)[None, :] < lengths[:, None]).reshape(-1)
    causal = jnp.arange(length)[:, None] >= jnp.arange(length)[None, :]
    allowed = jnp.concatenate(
        [jnp.broadcast_to(valid[None, :], (length, valid.shape[0])), causal], axis=1
    )
    scores = jnp.einsum("ihd,jd->hij", queries, keys, preferred_element_type=jnp.float32)
    scores = jnp.where(allowed[None], scores * head_dim ** (-0.5), -jnp.inf)
    ceiling = jnp.max(scores, axis=-1, keepdims=True)
    probs = jnp.exp(scores - ceiling)
    denominator = jnp.sum(probs, axis=-1, keepdims=True)
    mixed = jnp.einsum(
        "hij,jd->hid", probs.astype(jnp.bfloat16), values, preferred_element_type=jnp.float32
    )
    return (
        jnp.transpose(mixed / denominator, (1, 0, 2))
        .reshape(length, heads_here * head_dim)
        .astype(jnp.bfloat16)
    )


def context_by_row(doc_kv, doc_lens, query_docs, ctx_pos, device, kv_pick):
    pool_dev, doc_max, _, pair, head_dim = doc_kv.shape
    docs_per = query_docs.shape[1]
    pool_head = lax.dynamic_index_in_dim(doc_kv, kv_pick, 2, keepdims=False).reshape(
        pool_dev, doc_max, pair * head_dim
    )
    held = device * pool_dev + jnp.arange(pool_dev, dtype=jnp.int32)
    wanted = jnp.sum((query_docs[:, :, None] == held[None, None, :]).astype(jnp.float32), axis=1)
    sending = jnp.einsum(
        "rl,lkc->rkc", wanted.astype(jnp.bfloat16), pool_head, preferred_element_type=jnp.float32
    ).astype(jnp.bfloat16)
    received = lax.all_to_all(sending, "ep", split_axis=0, concat_axis=0, tiled=True)
    my_docs = lax.dynamic_index_in_dim(query_docs, device, 0, keepdims=False)
    starts = lax.dynamic_index_in_dim(ctx_pos, device, 0, keepdims=False)
    return (jnp.take(received, my_docs // pool_dev, axis=0), starts[:docs_per], jnp.take(doc_lens, my_docs))


def per_device_general(
    question_q,
    question_kv,
    doc_kv,
    doc_lens,
    query_docs,
    ctx_pos,
    hidden,
    out_proj,
    norm_gain,
    router_weight,
    w_gate_up,
    w_down,
    expert_ids,
):
    lanes = lax.axis_size("tp")
    groups = lax.axis_size("ep")
    lane = lax.axis_index("tp")
    device = lax.axis_index("ep")
    length, heads_here, head_dim = question_q.shape
    kv_heads = question_kv.shape[1]
    docs_per = query_docs.shape[1]
    width_here = hidden.shape[1]
    ids = lax.all_gather(expert_ids, "ep", axis=0, tiled=False)
    kv_pick = lane * kv_heads // lanes
    kv_head = lax.dynamic_index_in_dim(question_kv, kv_pick, 1, keepdims=False).reshape(
        length, 2 * head_dim
    )
    context, starts, lengths = context_by_row(
        doc_kv, doc_lens, query_docs, ctx_pos, device, kv_pick
    )
    question_start = lax.dynamic_index_in_dim(ctx_pos, device, 0, keepdims=False)[docs_per]
    attended = attend(question_q, kv_head, context, starts, lengths, question_start)
    projected = jnp.dot(
        lax.all_gather(attended, "tp", axis=1, tiled=True),
        lax.all_gather(out_proj, "ep", axis=0, tiled=True),
        preferred_element_type=jnp.float32,
    )
    residual = (hidden.astype(jnp.float32) + projected.astype(jnp.float32)).astype(jnp.bfloat16)

    tokens = lax.all_gather(residual, "ep", axis=0, tiled=False)
    wide = tokens.astype(jnp.float32)
    gain = norm_gain.astype(jnp.float32)
    scaled = wide * gain
    logit_part = jnp.einsum(
        "snd,de->sne", scaled, router_weight.astype(jnp.float32), precision=lax.Precision.HIGHEST
    )
    square_part = jnp.sum(wide * wide, axis=2, keepdims=True)
    stats = jnp.sum(
        lax.all_gather(jnp.concatenate([logit_part, square_part], axis=2), "tp", axis=0), axis=0
    )
    experts = router_weight.shape[1]
    inv_rms = lax.rsqrt(stats[:, :, experts] / (width_here * lanes) + norm_eps)
    logits = stats[:, :, :experts] * inv_rms[:, :, None]

    local_experts = w_gate_up.shape[0]
    capacity = length * expert_ids.shape[1] // experts
    hid = w_gate_up.shape[3]
    chosen_all = jnp.any(
        ids[:, :, :, None] == jnp.arange(experts, dtype=jnp.int32), axis=2
    )
    top = jnp.max(jnp.where(chosen_all, logits, -jnp.inf), axis=2, keepdims=True)
    weight = jnp.where(chosen_all, jnp.exp(logits - top), 0.0)
    mix = weight / jnp.sum(weight, axis=2, keepdims=True)

    shuffled, scaled_rows = (chosen_all, scaled.astype(jnp.bfloat16))
    first = device * local_experts
    chosen = lax.dynamic_slice_in_dim(shuffled, first, local_experts, 2)
    mix_here = lax.dynamic_slice_in_dim(mix, first, local_experts, 2)
    before = (jnp.arange(length)[:, None] > jnp.arange(length)[None, :]).astype(jnp.bfloat16)
    rank = jnp.einsum(
        "mn,sne->sem", before, chosen.astype(jnp.bfloat16), preferred_element_type=jnp.float32
    ).astype(jnp.int32)
    pick = jnp.logical_and(
        jnp.transpose(chosen, (0, 2, 1))[:, :, None, :],
        rank[:, :, None, :] == jnp.arange(capacity, dtype=jnp.int32)[None, None, :, None],
    )
    onehot = pick.astype(jnp.bfloat16)
    inv_row = jnp.sum(jnp.where(pick, inv_rms[:, None, None, :], 0.0), axis=3)
    mix_row = jnp.sum(jnp.where(pick, jnp.transpose(mix_here, (0, 2, 1))[:, :, None, :], 0.0), axis=3)

    rows = jnp.einsum(
        "sern,snd->serd", onehot, scaled_rows, preferred_element_type=jnp.float32
    ).astype(jnp.bfloat16)
    term = jnp.einsum(
        "serd,edgh->sergh", rows, w_gate_up, preferred_element_type=jnp.float32
    ).astype(jnp.bfloat16)
    per_lane = groups * local_experts * capacity // lanes
    term = term.reshape(lanes, per_lane, 2 * hid)
    inv_row = inv_row.reshape(lanes, per_lane, 1)
    summed = lax.psum_scatter(term, "tp", scatter_dimension=0, tiled=True)[0].astype(jnp.float32)
    inv_mine = lax.dynamic_index_in_dim(inv_row, lane, 0, keepdims=False)
    summed = summed * inv_mine
    act = (jax.nn.silu(summed[:, :hid]) * summed[:, hid:]).astype(jnp.bfloat16)
    acts = lax.all_gather(act, "tp", axis=0, tiled=False)
    acts = acts.reshape(groups, local_experts, capacity, hid)
    expert_out = jnp.einsum("serh,ehd->serd", acts, w_down, preferred_element_type=jnp.float32)
    expert_out = (expert_out * mix_row[:, :, :, None]).astype(jnp.bfloat16)
    combined = jnp.einsum(
        "sern,serd->snd", onehot, expert_out, preferred_element_type=jnp.float32
    ).astype(jnp.bfloat16)
    returned = lax.psum_scatter(combined, "ep", scatter_dimension=0, tiled=True)[0]
    return (residual.astype(jnp.float32) + returned.astype(jnp.float32)).astype(jnp.bfloat16)


def pairs(lanes, flip):
    return [(i, i ^ flip) for i in range(lanes)]


def query_of(device, lane):
    return 2 * (lane & 1) + ((lane >> 1) ^ (device & 1))


def turn(question, keys_values, device, lane, n, meanwhile):
    crosses = lambda e, t: ((e ^ t) & 1) != (t >> 1)
    devices = [(e, t) for e in range(n) for t in range(n)]
    swap = [(e * n + t, e * n + (t ^ 3)) for e, t in devices if crosses(e, t)]
    crossed = lax.ppermute(question, ("ep", "tp"), swap)
    crossed, *meanwhile = lax.optimization_barrier((crossed, *meanwhile))
    heads = jnp.where(crosses(device, lane), lane ^ 3, lane)
    picked = lax.dynamic_index_in_dim(keys_values, heads, 1, keepdims=False)
    picked = jnp.transpose(picked, (1, 0, 2)).reshape(-1, question.shape[1])
    held = jnp.where(crosses(device, lane), crossed, question)
    moves = []
    for e, t in devices:
        h = t ^ 3 if crosses(e, t) else t
        moves.append((e * n + t, h * n + 2 * ((e ^ h) & 1) + (e >> 1)))
    return (lax.ppermute(jnp.concatenate([held, picked], axis=0), ("ep", "tp"), moves), meanwhile)


def call(body, outs, scratch, flops=1 << 20, **kwargs):
    return pl.pallas_call(
        body,
        out_shape=outs,
        **({} if scratch is None else {"scratch_shapes": scratch}),
        compiler_params=pltpu.CompilerParams(vmem_limit_bytes=20 * 1024 * 1024),
        cost_estimate=pl.CostEstimate(flops=flops, bytes_accessed=1 << 18, transcendentals=0),
        **kwargs,
    )


VMEM = pl.BlockSpec(memory_space=pltpu.VMEM)
SMEM = pl.BlockSpec(memory_space=pltpu.SMEM)
NT = (((1,), (1,)), ((), ()))


def dot(a, b):
    return jnp.dot(a, b, preferred_element_type=jnp.float32)


def document_slots(here, query_docs, pool_dev):
    device, lane = (here[0], here[1])
    query = query_of(device, lane)
    slots = []
    for d in range(4):
        slot = jnp.int32(0)
        for j in range(query_docs.shape[1]):
            offset = query_docs[query, j] - (device ^ d) * pool_dev
            slot = jnp.where(jnp.logical_and(offset >= 0, offset < pool_dev), j, slot)
        slots.append(slot)
    return (query, slots)


def prepare_body(here, query_docs, pool, ids, *outs):
    pool_dev = pool.shape[0]
    docs_per = query_docs.shape[1]
    rows = pool.shape[2] * pool.shape[3]
    device, lane = (here[0], here[1])
    for d, out in enumerate(outs):
        target = device ^ d
        query = query_of(target, lane)
        local = jnp.int32(0)
        for j in range(docs_per):
            offset = query_docs[query, j] - device * pool_dev
            inside = jnp.logical_and(offset >= 0, offset < pool_dev)
            local = jnp.where(inside, offset, local)
        out[:rows, :] = pool[local, target].reshape(rows, pool.shape[4])
        out[rows:, :] = ids[...]


def prepare(here, query_docs, pool, ids):
    _, _, pair, doc_max, head_dim = pool.shape
    shape = jax.ShapeDtypeStruct((pair * doc_max + ids.shape[0], head_dim), jnp.bfloat16)
    return call(
        prepare_body,
        [shape] * 4,
        [],
        in_specs=[SMEM, SMEM, VMEM, VMEM],
        out_specs=[VMEM] * 4,
        name="prepare",
    )(here, query_docs, pool, ids)


def angles_body(pool_dev, here, query_docs, ctx_pos, cos_q, sin_q, cos_d, sin_d):
    query, slots = document_slots(here, query_docs, pool_dev)
    docs_per = query_docs.shape[1]
    head_dim = cos_q.shape[1]

    def fill(starts, cosine, sine):
        column = lax.broadcasted_iota(jnp.int32, cosine.shape, 1)
        half = jnp.where(column < head_dim // 2, column, column - head_dim // 2)
        freq = jnp.exp(half.astype(jnp.float32) * (-2.0 * math.log(rope_theta) / head_dim))
        angle = starts.astype(jnp.float32) * freq
        cosine[...] = jnp.cos(angle)
        wave = jnp.sin(angle)
        sine[...] = jnp.where(column < head_dim // 2, -wave, wave)

    row = lax.broadcasted_iota(jnp.int32, cos_q.shape, 0)
    fill(ctx_pos[query, docs_per] + row, cos_q, sin_q)
    row = lax.broadcasted_iota(jnp.int32, cos_d.shape, 0)
    starts = jnp.zeros(cos_d.shape, jnp.int32)
    for d, slot in enumerate(slots):
        starts = jnp.where(row == d, ctx_pos[query, slot], starts)
    fill(starts, cos_d, sin_d)


def angles(here, query_docs, ctx_pos, pool_dev, length, head_dim):
    shapes = [jax.ShapeDtypeStruct((rows, head_dim), jnp.float32) for rows in (length, length, 8, 8)]
    return call(
        functools.partial(angles_body, pool_dev),
        shapes,
        [],
        in_specs=[SMEM] * 3,
        out_specs=[VMEM] * 4,
        name="angles",
    )(here, query_docs, ctx_pos)


def attention_body(
    pool_dev, here, query_docs, doc_lens, q, c0, c1, c2, c3, cos_q, sin_q, cos_d, sin_d, out, wide, keys, vals
):
    length, head_dim = cos_q.shape
    heads = out.shape[1] // head_dim
    pieces = (c0, c1, c2, c3)
    docs = len(pieces)
    doc_max = (keys.shape[0] - length) // docs
    half = head_dim // 2
    query, slots = document_slots(here, query_docs, pool_dev)

    def turned(x, cosine, sine):
        return x * cosine + pltpu.roll(x, half, 1) * sine

    cosine, sine = (cos_q[...], sin_q[...])
    for j, piece in enumerate(pieces):
        key = turned(piece[:doc_max, :].astype(jnp.float32), cos_d[j : j + 1, :], sin_d[j : j + 1, :])
        keys[j * doc_max : (j + 1) * doc_max, :] = key.astype(jnp.bfloat16)
        vals[j * doc_max : (j + 1) * doc_max, :] = piece[doc_max : 2 * doc_max, :]
    base = docs * doc_max
    first = heads * length
    keys[base:, :] = turned(q[first : first + length, :].astype(jnp.float32), cosine, sine).astype(
        jnp.bfloat16
    )
    vals[base:, :] = q[first + length :, :]
    wide[...] = q[:first, :].astype(jnp.float32)
    column = lax.broadcasted_iota(jnp.int32, (1, doc_max), 1)
    allowed = [column < doc_lens[query_docs[query, slot]] for slot in slots]
    causal = lax.broadcasted_iota(jnp.int32, (length, length), 0) >= lax.broadcasted_iota(
        jnp.int32, (length, length), 1
    )
    for h in range(heads):
        rows = turned(wide[pl.ds(h, length, stride=heads), :], cosine, sine).astype(jnp.bfloat16)
        scores = lax.dot_general(rows, keys[...], NT, preferred_element_type=jnp.float32)
        scores = scores * head_dim ** (-0.5)
        parts = [
            jnp.where(allowed[j], scores[:, j * doc_max : (j + 1) * doc_max], -jnp.inf)
            for j in range(docs)
        ] + [jnp.where(causal, scores[:, base:], -jnp.inf)]
        scores = jnp.concatenate(parts, axis=1)
        ceiling = jnp.max(scores, axis=1, keepdims=True)
        probs = jnp.exp(scores - ceiling)
        denominator = jnp.sum(probs, axis=1, keepdims=True)
        mixed = dot(probs.astype(jnp.bfloat16), vals[...])
        out[:, h * head_dim : (h + 1) * head_dim] = (mixed / denominator).astype(jnp.bfloat16)


def attention(here, query_docs, doc_lens, q, pieces, tables, pool_dev):
    length, head_dim = tables[0].shape
    heads = q.shape[0] // length - 2
    rows = 5 * length
    return call(
        functools.partial(attention_body, pool_dev),
        jax.ShapeDtypeStruct((length, heads * head_dim), jnp.bfloat16),
        [
            pltpu.VMEM((heads * length, head_dim), jnp.float32),
            pltpu.VMEM((rows, head_dim), jnp.bfloat16),
            pltpu.VMEM((rows, head_dim), jnp.bfloat16),
        ],
        in_specs=[SMEM] * 3 + [VMEM] * 9,
        out_specs=VMEM,
        name="attention",
    )(here, query_docs, doc_lens, q, *pieces, *tables)


def project_rows(here, flip, a, b, rows):
    device, lane = (here[0], here[1])
    high = (device ^ query_of(device, lane ^ flip)) >> 1
    rows[high] = a[...]
    rows[1 - high] = b[...]


def project_early_body(here, a, b, weight, close, far, rows):
    project_rows(here, 0, a, b, rows)
    far[...] = dot(rows[1], weight[...]).astype(jnp.bfloat16)
    close[...] = dot(rows[0], weight[...]).astype(jnp.bfloat16)


def project_late_body(here, a, b, weight, early, own, near, far, rows):
    project_rows(here, 2, a, b, rows)
    far[...] = dot(rows[1], weight[...]).astype(jnp.bfloat16)
    late = dot(rows[0], weight[...]).astype(jnp.bfloat16)
    first = here[1] < 2
    own[...] = jnp.where(first, early[...], late)
    near[...] = jnp.where(first, late, early[...])


def project(body, here, parts, weight, outs, *early):
    length, depth = parts[0].shape
    return call(
        body,
        [jax.ShapeDtypeStruct((length, weight.shape[1]), jnp.bfloat16)] * outs,
        [pltpu.VMEM((2, length, depth), jnp.bfloat16)],
        in_specs=[SMEM] + [VMEM] * (3 + len(early)),
        out_specs=[VMEM] * outs,
        name="project",
    )(here, *parts, weight, *early)


def routing_body(experts, here, c0, c1, c2, c3, pick, spread):
    _, local, capacity, length = pick.shape
    first = here[0] * local
    before = (
        lax.broadcasted_iota(jnp.int32, (length, length), 0)
        < lax.broadcasted_iota(jnp.int32, (length, length), 1)
    ).astype(jnp.bfloat16)
    place = lax.broadcasted_iota(jnp.int32, (capacity, length), 0).astype(jnp.float32)
    row = lax.broadcasted_iota(jnp.int32, (8, length), 0)
    for d, piece in enumerate((c0, c1, c2, c3)):
        ids = piece[piece.shape[0] - 16 :, :].astype(jnp.float32).astype(jnp.int32)
        chosen = jnp.zeros((8, length), jnp.float32)
        for k in range(8):
            named = jnp.logical_and(ids[k : k + 1, :] == first + row, row < local)
            chosen = jnp.where(named, 1.0, chosen)
        rank = dot(chosen.astype(jnp.bfloat16), before)
        wide = []
        for e in range(local):
            here_e = jnp.logical_and(rank[e : e + 1, :] == place, chosen[e : e + 1, :] > 0.0)
            wide.append(jnp.where(here_e, 1.0, 0.0))
            pick[d, e] = wide[-1].astype(jnp.bfloat16)
        spread[d] = jnp.transpose(jnp.concatenate(wide, axis=0)).astype(jnp.bfloat16)


def routing(here, pieces, experts, local, capacity):
    length = pieces[0].shape[1]
    rows = pieces[0].shape[0]
    return call(
        functools.partial(routing_body, experts),
        [
            jax.ShapeDtypeStruct((4, local, capacity, length), jnp.bfloat16),
            jax.ShapeDtypeStruct((4, length, local * capacity), jnp.bfloat16),
        ],
        [],
        in_specs=[SMEM] + [VMEM] * 4,
        out_specs=[VMEM] * 2,
        name="routing",
    )(here, *pieces)


def residual_body(hidden, p0, p1, p2, after, out):
    total = hidden[...].astype(jnp.float32) + p0[...].astype(jnp.float32)
    for part in (p1, p2):
        total = total + part[...].astype(jnp.float32)
    out[...] = total.astype(jnp.bfloat16)


def add_parts(hidden, parts, after):
    return call(
        residual_body,
        jax.ShapeDtypeStruct(hidden.shape, jnp.bfloat16),
        [],
        in_specs=[VMEM] * 4 + [pl.BlockSpec(memory_space=pl.ANY)],
        out_specs=VMEM,
        name="residual",
    )(hidden, *parts, after)


def measure_body(*refs):
    *tokens, gain, router, stats = refs
    rows = stats.shape[0]
    length = tokens[0].shape[0]
    for d, ref in enumerate(tokens):
        wide = ref[...].astype(jnp.float32)
        grown = wide * gain[...]
        high = grown.astype(jnp.bfloat16)
        rest = grown - high.astype(jnp.float32)
        middle = rest.astype(jnp.bfloat16)
        low = (rest - middle.astype(jnp.float32)).astype(jnp.bfloat16)
        logits = dot(high, router[...]) + (dot(middle, router[...]) + dot(low, router[...]))
        squares = jnp.sum(wide * wide, axis=1, keepdims=True)
        column = lax.broadcasted_iota(jnp.int32, logits.shape, 1)
        both = jnp.where(column == rows - 8, squares, logits)
        stats[:, d * length : (d + 1) * length] = jnp.transpose(both)[:rows, :]


def squares_and_logits(tokens, gain, router, experts):
    n, length = (len(tokens), tokens[0].shape[0])
    return call(
        measure_body,
        jax.ShapeDtypeStruct((experts + 8, n * length), jnp.float32),
        [],
        in_specs=[VMEM] * (n + 2),
        out_specs=VMEM,
        name="stats",
    )(*tokens, gain, router)


def gate_up_body(ds, order, *refs):
    tokens = refs[: len(ds)]
    gain, pick, weight, out, rows = refs[len(ds) :]
    hid = weight.shape[3]
    capacity = pick.shape[2]
    expert = order[pl.program_id(0)]
    for k, d in enumerate(ds):
        chosen = dot(pick[d, expert], tokens[k][...]) * gain[...]
        rows[k * capacity : (k + 1) * capacity, :] = chosen.astype(jnp.bfloat16)
    for g in range(2):
        out[0, :, g * hid : (g + 1) * hid] = dot(rows[...], weight[0, g]).astype(jnp.bfloat16)


def gate_up(ds, order, tokens, gain, pick, weight):
    _, _, width, hid = weight.shape
    count = order.shape[0]
    capacity = pick.shape[2]
    rows = len(ds) * capacity
    whole = lambda rank: lambda i, order: (0,) * rank
    return call(
        functools.partial(gate_up_body, ds),
        jax.ShapeDtypeStruct((count, rows, 2 * hid), jnp.bfloat16),
        None,
        grid_spec=pltpu.PrefetchScalarGridSpec(
            num_scalar_prefetch=1,
            grid=(count,),
            in_specs=[pl.BlockSpec(tokens[0].shape, whole(2))] * len(ds)
            + [
                pl.BlockSpec(gain.shape, whole(2)),
                pl.BlockSpec(pick.shape, whole(4)),
                pl.BlockSpec((1, 2, width, hid), lambda i, order: (order[i], 0, 0, 0)),
            ],
            out_specs=pl.BlockSpec((1, rows, 2 * hid), lambda i, order: (i, 0, 0)),
            scratch_shapes=[pltpu.VMEM((rows, width), jnp.bfloat16)],
        ),
        name="gate_up",
    )(order, *tokens, gain, pick, weight)


def activate_body(groups, features, offset, here, pick, stats, *refs):
    out = refs[-1]
    _, local, capacity, length = pick.shape
    hid = out.shape[1]
    experts = stats.shape[0] - 8
    device, lane = (here[0], here[1])
    expert = lax.broadcasted_iota(jnp.int32, (experts, length), 0)
    base, refs = (0, list(refs))
    for ds in groups:
        kept, taken, across = refs[:3]
        pieces = refs[3 : 3 + len(ds)]
        refs = refs[3 + len(ds) :]
        for k, d in enumerate(ds):
            ids = pieces[k][pieces[k].shape[0] - 16 :, :].astype(jnp.float32).astype(jnp.int32)
            chosen = jnp.zeros((experts, length), jnp.float32)
            for c in range(8):
                chosen = jnp.where(ids[c : c + 1, :] == expert, 1.0, chosen)
            block = slice((offset + k) * length, (offset + k + 1) * length)
            inv_rms = lax.rsqrt(stats[experts : experts + 1, block] / features + norm_eps)
            logits = jnp.where(chosen > 0.0, stats[:experts, block] * inv_rms, -jnp.inf)
            grown = jnp.exp(logits - jnp.max(logits, axis=0, keepdims=True))
            mix = grown / jnp.sum(grown, axis=0, keepdims=True)
            mine = jnp.where(expert == device * local + lane, mix, 0.0)
            mix = jnp.sum(mine, axis=0, keepdims=True)
            places = pick[d, lane].astype(jnp.float32)
            inv_row = jnp.sum(places * inv_rms, axis=1, keepdims=True)
            mix_row = jnp.sum(places * mix, axis=1, keepdims=True)
            rows = slice(k * capacity, (k + 1) * capacity)
            summed = kept[0, rows, :].astype(jnp.float32) + taken[0, rows, :].astype(jnp.float32)
            summed = (summed + across[rows, :].astype(jnp.float32)) * inv_row
            gate = summed[:, :hid]
            act = gate / (1.0 + jnp.exp(-gate)) * summed[:, hid:] * mix_row
            out[base + k * capacity : base + (k + 1) * capacity, :] = act.astype(jnp.bfloat16)
        base += len(ds) * capacity
        offset += len(ds)


def activate(groups, features, here, sums, pick, stats, pieces, flops=1 << 20, offset=0):
    operands = []
    for ds, terms in zip(groups, sums):
        operands += list(terms) + [pieces[d] for d in ds]
    rows = sum(terms[2].shape[0] for terms in sums)
    return call(
        functools.partial(activate_body, groups, features, offset),
        jax.ShapeDtypeStruct((rows, sums[0][2].shape[1] // 2), jnp.bfloat16),
        [],
        in_specs=[SMEM] + [VMEM] * (2 + len(operands)),
        out_specs=VMEM,
        flops=flops,
        name="activate",
    )(here, pick, stats, *operands)


def down_body(ds, order, a, b, c, d, spread, weight, *rest):
    outs, results = (rest[:-1], rest[-1])
    i = pl.program_id(0)
    capacity = results.shape[2]
    expert = order[i]
    for j, ref in enumerate((a, b, c, d)):

        @pl.when(i == j)
        def _():
            result = dot(ref[...], weight[0]).astype(jnp.bfloat16)
            for k in range(len(ds)):
                results[k, expert] = result[k * capacity : (k + 1) * capacity, :]

    @pl.when(i == pl.num_programs(0) - 1)
    def _():
        half = spread.shape[1] // 2
        for k, d in enumerate(ds):
            rows = results[k].reshape(-1, results.shape[3])
            block = dot(spread[d], rows).astype(jnp.bfloat16)
            if len(outs) == len(ds):
                outs[k][...] = block
            else:
                outs[2 * k][...] = block[:half]
                outs[2 * k + 1][...] = block[half:]


def down(ds, order, acts, spread, weight, halved=False):
    local, hid, width = weight.shape
    capacity = acts[0].shape[0] // len(ds)
    length = spread.shape[1]
    shape = jax.ShapeDtypeStruct((length, width), jnp.bfloat16)
    half = jax.ShapeDtypeStruct((length // 2, width), jnp.bfloat16)
    shapes = [half] * (2 * len(ds)) if halved else [shape] * len(ds)
    whole = lambda rank: lambda i, order: (0,) * rank
    return call(
        functools.partial(down_body, ds),
        shapes,
        None,
        grid_spec=pltpu.PrefetchScalarGridSpec(
            num_scalar_prefetch=1,
            grid=(local,),
            in_specs=[pl.BlockSpec(acts[0].shape, whole(2))] * 4
            + [
                pl.BlockSpec(spread.shape, whole(3)),
                pl.BlockSpec((1, hid, width), lambda i, order: (order[i], 0, 0)),
            ],
            out_specs=[pl.BlockSpec(s.shape, whole(2)) for s in shapes],
            scratch_shapes=[pltpu.VMEM((len(ds), local, capacity, width), jnp.bfloat16)],
        ),
        name="down",
    )(order, *acts, spread, weight)


def per_device_square(
    question_q,
    question_kv,
    doc_kv,
    doc_lens,
    query_docs,
    ctx_pos,
    hidden,
    out_proj,
    norm_gain,
    router_weight,
    w_gate_up,
    w_down,
    expert_ids,
):
    n = 4
    lane = lax.axis_index("tp")
    device = lax.axis_index("ep")
    length, heads_here, head_dim = question_q.shape
    pool_dev = doc_kv.shape[0]
    width_here = hidden.shape[1]
    experts = router_weight.shape[1]
    local = w_gate_up.shape[0]
    capacity = length * expert_ids.shape[1] // experts
    here = jnp.stack([device, lane]).astype(jnp.int32)
    order = (lane ^ jnp.array([0, 2, 1, 3], jnp.int32)).astype(jnp.int32)

    pool = jnp.transpose(doc_kv, (0, 2, 3, 1, 4))
    ids_rows = jnp.pad(expert_ids.T.astype(jnp.bfloat16), ((0, 8), (0, 0)))
    pieces = prepare(here, query_docs, pool, ids_rows)
    q_rows, pieces = turn(
        question_q.reshape(length * heads_here, head_dim), question_kv, device, lane, n, pieces
    )
    pieces = [pieces[0]] + [lax.ppermute(pieces[d], "ep", pairs(n, d)) for d in range(1, n)]
    tables = list(angles(here, query_docs, ctx_pos, pool_dev, length, head_dim))

    one = lax.optimization_barrier(jnp.ones((), jnp.bfloat16))
    tables[0], out_proj = lax.optimization_barrier((tables[0], out_proj * one))
    attended = attention(here, query_docs, doc_lens, q_rows, pieces, tables, pool_dev)
    far = lax.ppermute(attended, "tp", pairs(n, 2))
    near = lax.ppermute(attended, "tp", pairs(n, 1))
    farther = lax.ppermute(far, "tp", pairs(n, 1))
    gain = norm_gain.astype(jnp.float32)[None, :]
    router = jnp.pad(router_weight, ((0, 0), (0, 128 - experts)))
    close, early = project(project_early_body, here, (attended, near), out_proj, 2)
    given = lax.ppermute(early, "ep", pairs(n, 1))
    kept, near, late = project(project_late_body, here, (far, farther), out_proj, 3, close)
    kept, w_gate_up = lax.optimization_barrier((kept, w_gate_up))
    late = (late.astype(jnp.float32) + given.astype(jnp.float32)).astype(jnp.bfloat16)
    moves = [
        (e * n + t, (e ^ (3 if t < 2 else 2)) * n + t) for e in range(n) for t in range(n)
    ]
    sent = [kept, lax.ppermute(late, ("ep", "tp"), moves), lax.ppermute(near, "ep", pairs(n, 1))]
    pick, spread = routing(here, pieces, experts, local, capacity)
    weight = jnp.transpose(w_gate_up, (0, 2, 1, 3))
    sent[0], pick, router, gain = lax.optimization_barrier((sent[0], pick, router, gain))
    residual = add_parts(hidden, sent, weight)

    tokens = [residual] + [None] * (n - 1)
    for d in (2, 1):
        tokens[d] = lax.ppermute(residual, "ep", pairs(n, d))
    tokens[3] = lax.ppermute(tokens[2], "ep", pairs(n, 1))

    features = width_here * n

    def spread_act(act, before=()):
        far = lax.ppermute(act, "tp", pairs(n, 2))
        far, *before = lax.optimization_barrier((far, *before))
        near = lax.ppermute(act, "tp", pairs(n, 1))
        return [act, far, near, lax.ppermute(far, "tp", pairs(n, 1))]

    def chip_sum(kept, taken):
        return (kept[1].astype(jnp.float32) + taken[1].astype(jnp.float32)).astype(jnp.bfloat16)

    def terms_of(ds, order):
        blocks = [tokens[d] for d in ds]
        given = gate_up(ds, order[2:], blocks, gain, pick, weight)
        return (gate_up(ds, order[:2], blocks, gain, pick, weight), given)

    def stats_of(ds):
        return squares_and_logits([tokens[d] for d in ds], gain, router, experts)

    one_chunk = (1, 2)
    kept_0, given_0 = terms_of((0,), order)
    order, kept_0, given_0 = lax.optimization_barrier((order, kept_0, given_0))
    kept, given = terms_of(one_chunk, order)
    taken = lax.ppermute(given, "tp", pairs(n, 1))
    _, stats = lax.optimization_barrier((given, stats_of(one_chunk)))
    stats_far = lax.ppermute(stats, "tp", pairs(n, 2))
    taken, stats_far = lax.optimization_barrier((taken, stats_far))
    stats = stats + stats_far
    stats_near = lax.ppermute(stats, "tp", pairs(n, 1))
    far_sum = chip_sum(kept, taken)
    across = lax.ppermute(far_sum, "tp", pairs(n, 2))

    order, _, stats_near = lax.optimization_barrier((order, far_sum, stats_near))
    stats = stats + stats_near
    kept_3, given_3 = terms_of((3,), order)
    stats_2 = stats_of((3, 0))
    given_3, given_0, across, stats_2 = lax.optimization_barrier((given_3, given_0, across, stats_2))
    stats_far = lax.ppermute(stats_2, "tp", pairs(n, 2))
    taken_3 = lax.ppermute(given_3, "tp", pairs(n, 1))
    taken_0 = lax.ppermute(given_0, "tp", pairs(n, 1))
    sums = [(kept, taken, across)]
    acts = spread_act(activate((one_chunk,), features, here, sums, pick, stats, pieces))
    sum_3, sum_0 = (chip_sum(kept_3, taken_3), chip_sum(kept_0, taken_0))
    sum_3, sum_0, stats_far, acts[1] = lax.optimization_barrier((sum_3, sum_0, stats_far, acts[1]))
    stats_2 = stats_2 + stats_far
    stats_near = lax.ppermute(stats_2, "tp", pairs(n, 1))
    acts[3] = lax.ppermute(acts[1], "tp", pairs(n, 1))
    across_3 = lax.ppermute(sum_3, "tp", pairs(n, 2))
    across_0 = lax.ppermute(sum_0, "tp", pairs(n, 2))
    parts = down(one_chunk, order, acts, spread, w_down, halved=True)
    across_3, *parts = lax.optimization_barrier((across_3, *parts))
    far = [lax.ppermute(part, "ep", pairs(n, 2)) for part in parts[2:]]
    near = [lax.ppermute(part, "ep", pairs(n, 1)) for part in parts[:2]]
    stats_2 = stats_2 + stats_near
    sums = [(kept_3, taken_3, across_3)]
    act_3 = activate(((3,),), features, here, sums, pick, stats_2, pieces)
    across_0, far[0], near[0] = lax.optimization_barrier((across_0, far[0], near[0]))
    acts = spread_act(act_3)
    sums = [(kept_0, taken_0, across_0)]
    act_0 = activate(((0,),), features, here, sums, pick, stats_2, pieces, 1 << 20, 1)
    acts_0 = spread_act(act_0, (far[1], near[1]))
    (last,) = down((3,), order, acts, spread, w_down)
    last, *acts_0 = lax.optimization_barrier((last, *acts_0))
    last = lax.ppermute(last, "ep", pairs(n, 3))
    (mine,) = down((0,), order, acts_0, spread, w_down)
    returned = [mine, jnp.concatenate(near, axis=0), jnp.concatenate(far, axis=0), last]
    total = residual.astype(jnp.float32)
    for part in returned:
        total = total + part.astype(jnp.float32)
    return total.astype(jnp.bfloat16)


def solution(mesh):
    placed = (
        P(("grp", "ep"), "tp", None),
        P(("grp", "ep"), None, None, None),
        P(("grp", "ep"), None, None, None, None),
        P("grp"),
        P("grp", None),
        P("grp", None),
        P(("grp", "ep"), "tp"),
        P("ep", "tp"),
        P("tp"),
        P("tp", None),
        P("ep", "tp", None, None),
        P("ep", None, "tp"),
        P(("grp", "ep"), None),
    )
    def per_device(*args):
        square = (
            lax.axis_size("tp") == 4
            and lax.axis_size("ep") == 4
            and args[1].shape[1] == 4
            and args[4].shape == (4, 4)
        )
        return (per_device_square if square else per_device_general)(*args)

    return jax.shard_map(
        per_device, mesh=mesh, in_specs=placed, out_specs=P(("grp", "ep"), "tp"), check_vma=False
    )
```

```python
import functools
import math

import jax
import jax.numpy as jnp
from jax import lax
from jax.experimental import pallas as pl
from jax.experimental.pallas import tpu as pltpu
from jax.sharding import PartitionSpec as P

rope_theta = 1000000.0
norm_eps = 1e-06


def tables(positions, head_dim):
    half = head_dim // 2
    freq = jnp.exp(jnp.arange(half, dtype=jnp.float32) * (-2.0 * math.log(rope_theta) / head_dim))
    angle = positions.astype(jnp.float32)[:, None] * freq[None, :]
    return (jnp.cos(angle), jnp.sin(angle))


def rotate(values, positions):
    half = values.shape[-1] // 2
    cosine, sine = tables(positions, values.shape[-1])
    shape = (values.shape[0],) + (1,) * (values.ndim - 2) + (half,)
    cosine, sine = (cosine.reshape(shape), sine.reshape(shape))
    floats = values.astype(jnp.float32)
    first = floats[..., :half]
    second = floats[..., half:]
    return jnp.concatenate(
        [first * cosine - second * sine, second * cosine + first * sine], axis=-1
    )


def attend(q_rows, own_kv, context, starts, lengths, question_start):
    length, heads_here, head_dim = q_rows.shape
    docs_per, doc_max, _ = context.shape
    question_pos = question_start + jnp.arange(length, dtype=jnp.int32)
    queries = rotate(q_rows, question_pos).astype(jnp.bfloat16)
    own_keys = rotate(own_kv[:, :head_dim], question_pos).astype(jnp.bfloat16)
    positions = jnp.repeat(starts, doc_max, total_repeat_length=docs_per * doc_max)
    doc_keys = rotate(context[:, :, :head_dim].reshape(docs_per * doc_max, head_dim), positions)
    keys = jnp.concatenate([doc_keys.astype(jnp.bfloat16), own_keys], axis=0)
    values = jnp.concatenate(
        [context[:, :, head_dim:].reshape(docs_per * doc_max, head_dim), own_kv[:, head_dim:]],
        axis=0,
    )
    valid = (jnp.arange(doc_max, dtype=jnp.int32)[None, :] < lengths[:, None]).reshape(-1)
    causal = jnp.arange(length)[:, None] >= jnp.arange(length)[None, :]
    allowed = jnp.concatenate(
        [jnp.broadcast_to(valid[None, :], (length, valid.shape[0])), causal], axis=1
    )
    scores = jnp.einsum("ihd,jd->hij", queries, keys, preferred_element_type=jnp.float32)
    scores = jnp.where(allowed[None], scores * head_dim ** (-0.5), -jnp.inf)
    ceiling = jnp.max(scores, axis=-1, keepdims=True)
    probs = jnp.exp(scores - ceiling)
    denominator = jnp.sum(probs, axis=-1, keepdims=True)
    mixed = jnp.einsum(
        "hij,jd->hid", probs.astype(jnp.bfloat16), values, preferred_element_type=jnp.float32
    )
    return (
        jnp.transpose(mixed / denominator, (1, 0, 2))
        .reshape(length, heads_here * head_dim)
        .astype(jnp.bfloat16)
    )


def context_by_row(doc_kv, doc_lens, query_docs, ctx_pos, device, kv_pick):
    pool_dev, doc_max, _, pair, head_dim = doc_kv.shape
    docs_per = query_docs.shape[1]
    pool_head = lax.dynamic_index_in_dim(doc_kv, kv_pick, 2, keepdims=False).reshape(
        pool_dev, doc_max, pair * head_dim
    )
    held = device * pool_dev + jnp.arange(pool_dev, dtype=jnp.int32)
    wanted = jnp.sum((query_docs[:, :, None] == held[None, None, :]).astype(jnp.float32), axis=1)
    sending = jnp.einsum(
        "rl,lkc->rkc", wanted.astype(jnp.bfloat16), pool_head, preferred_element_type=jnp.float32
    ).astype(jnp.bfloat16)
    received = lax.all_to_all(sending, "ep", split_axis=0, concat_axis=0, tiled=True)
    my_docs = lax.dynamic_index_in_dim(query_docs, device, 0, keepdims=False)
    starts = lax.dynamic_index_in_dim(ctx_pos, device, 0, keepdims=False)
    return (jnp.take(received, my_docs // pool_dev, axis=0), starts[:docs_per], jnp.take(doc_lens, my_docs))


def per_device_general(
    question_q,
    question_kv,
    doc_kv,
    doc_lens,
    query_docs,
    ctx_pos,
    hidden,
    out_proj,
    norm_gain,
    router_weight,
    w_gate_up,
    w_down,
    expert_ids,
):
    lanes = lax.axis_size("tp")
    groups = lax.axis_size("ep")
    lane = lax.axis_index("tp")
    device = lax.axis_index("ep")
    length, heads_here, head_dim = question_q.shape
    kv_heads = question_kv.shape[1]
    docs_per = query_docs.shape[1]
    width_here = hidden.shape[1]
    ids = lax.all_gather(expert_ids, "ep", axis=0, tiled=False)
    kv_pick = lane * kv_heads // lanes
    kv_head = lax.dynamic_index_in_dim(question_kv, kv_pick, 1, keepdims=False).reshape(
        length, 2 * head_dim
    )
    context, starts, lengths = context_by_row(
        doc_kv, doc_lens, query_docs, ctx_pos, device, kv_pick
    )
    question_start = lax.dynamic_index_in_dim(ctx_pos, device, 0, keepdims=False)[docs_per]
    attended = attend(question_q, kv_head, context, starts, lengths, question_start)
    projected = jnp.dot(
        lax.all_gather(attended, "tp", axis=1, tiled=True),
        lax.all_gather(out_proj, "ep", axis=0, tiled=True),
        preferred_element_type=jnp.float32,
    )
    residual = (hidden.astype(jnp.float32) + projected.astype(jnp.float32)).astype(jnp.bfloat16)

    tokens = lax.all_gather(residual, "ep", axis=0, tiled=False)
    wide = tokens.astype(jnp.float32)
    gain = norm_gain.astype(jnp.float32)
    scaled = wide * gain
    logit_part = jnp.einsum(
        "snd,de->sne", scaled, router_weight.astype(jnp.float32), precision=lax.Precision.HIGHEST
    )
    square_part = jnp.sum(wide * wide, axis=2, keepdims=True)
    stats = jnp.sum(
        lax.all_gather(jnp.concatenate([logit_part, square_part], axis=2), "tp", axis=0), axis=0
    )
    experts = router_weight.shape[1]
    inv_rms = lax.rsqrt(stats[:, :, experts] / (width_here * lanes) + norm_eps)
    logits = stats[:, :, :experts] * inv_rms[:, :, None]

    local_experts = w_gate_up.shape[0]
    capacity = length * expert_ids.shape[1] // experts
    hid = w_gate_up.shape[3]
    chosen_all = jnp.any(
        ids[:, :, :, None] == jnp.arange(experts, dtype=jnp.int32), axis=2
    )
    top = jnp.max(jnp.where(chosen_all, logits, -jnp.inf), axis=2, keepdims=True)
    weight = jnp.where(chosen_all, jnp.exp(logits - top), 0.0)
    mix = weight / jnp.sum(weight, axis=2, keepdims=True)

    shuffled, scaled_rows = (chosen_all, scaled.astype(jnp.bfloat16))
    first = device * local_experts
    chosen = lax.dynamic_slice_in_dim(shuffled, first, local_experts, 2)
    mix_here = lax.dynamic_slice_in_dim(mix, first, local_experts, 2)
    before = (jnp.arange(length)[:, None] > jnp.arange(length)[None, :]).astype(jnp.bfloat16)
    rank = jnp.einsum(
        "mn,sne->sem", before, chosen.astype(jnp.bfloat16), preferred_element_type=jnp.float32
    ).astype(jnp.int32)
    pick = jnp.logical_and(
        jnp.transpose(chosen, (0, 2, 1))[:, :, None, :],
        rank[:, :, None, :] == jnp.arange(capacity, dtype=jnp.int32)[None, None, :, None],
    )
    onehot = pick.astype(jnp.bfloat16)
    inv_row = jnp.sum(jnp.where(pick, inv_rms[:, None, None, :], 0.0), axis=3)
    mix_row = jnp.sum(jnp.where(pick, jnp.transpose(mix_here, (0, 2, 1))[:, :, None, :], 0.0), axis=3)

    rows = jnp.einsum(
        "sern,snd->serd", onehot, scaled_rows, preferred_element_type=jnp.float32
    ).astype(jnp.bfloat16)
    term = jnp.einsum(
        "serd,edgh->sergh", rows, w_gate_up, preferred_element_type=jnp.float32
    ).astype(jnp.bfloat16)
    per_lane = groups * local_experts * capacity // lanes
    term = term.reshape(lanes, per_lane, 2 * hid)
    inv_row = inv_row.reshape(lanes, per_lane, 1)
    summed = lax.psum_scatter(term, "tp", scatter_dimension=0, tiled=True)[0].astype(jnp.float32)
    inv_mine = lax.dynamic_index_in_dim(inv_row, lane, 0, keepdims=False)
    summed = summed * inv_mine
    act = (jax.nn.silu(summed[:, :hid]) * summed[:, hid:]).astype(jnp.bfloat16)
    acts = lax.all_gather(act, "tp", axis=0, tiled=False)
    acts = acts.reshape(groups, local_experts, capacity, hid)
    expert_out = jnp.einsum("serh,ehd->serd", acts, w_down, preferred_element_type=jnp.float32)
    expert_out = (expert_out * mix_row[:, :, :, None]).astype(jnp.bfloat16)
    combined = jnp.einsum(
        "sern,serd->snd", onehot, expert_out, preferred_element_type=jnp.float32
    ).astype(jnp.bfloat16)
    returned = lax.psum_scatter(combined, "ep", scatter_dimension=0, tiled=True)[0]
    return (residual.astype(jnp.float32) + returned.astype(jnp.float32)).astype(jnp.bfloat16)


def pairs(lanes, flip):
    return [(i, i ^ flip) for i in range(lanes)]


def query_of(device, lane):
    return 2 * (lane & 1) + ((lane >> 1) ^ (device & 1))


def turn(question, keys_values, device, lane, n, meanwhile):
    crosses = lambda e, t: ((e ^ t) & 1) != (t >> 1)
    devices = [(e, t) for e in range(n) for t in range(n)]
    swap = [(e * n + t, e * n + (t ^ 3)) for e, t in devices if crosses(e, t)]
    crossed = lax.ppermute(question, ("ep", "tp"), swap)
    crossed, *meanwhile = lax.optimization_barrier((crossed, *meanwhile))
    heads = jnp.where(crosses(device, lane), lane ^ 3, lane)
    picked = lax.dynamic_index_in_dim(keys_values, heads, 1, keepdims=False)
    picked = jnp.transpose(picked, (1, 0, 2)).reshape(-1, question.shape[1])
    held = jnp.where(crosses(device, lane), crossed, question)
    moves = []
    for e, t in devices:
        h = t ^ 3 if crosses(e, t) else t
        moves.append((e * n + t, h * n + 2 * ((e ^ h) & 1) + (e >> 1)))
    return (lax.ppermute(jnp.concatenate([held, picked], axis=0), ("ep", "tp"), moves), meanwhile)


def call(body, outs, scratch, flops=1 << 20, **kwargs):
    return pl.pallas_call(
        body,
        out_shape=outs,
        **({} if scratch is None else {"scratch_shapes": scratch}),
        compiler_params=pltpu.CompilerParams(vmem_limit_bytes=20 * 1024 * 1024),
        cost_estimate=pl.CostEstimate(flops=flops, bytes_accessed=1 << 18, transcendentals=0),
        **kwargs,
    )


VMEM = pl.BlockSpec(memory_space=pltpu.VMEM)
SMEM = pl.BlockSpec(memory_space=pltpu.SMEM)
NT = (((1,), (1,)), ((), ()))


def dot(a, b):
    return jnp.dot(a, b, preferred_element_type=jnp.float32)


def document_slots(here, query_docs, pool_dev):
    device, lane = (here[0], here[1])
    query = query_of(device, lane)
    slots = []
    for d in range(4):
        slot = jnp.int32(0)
        for j in range(query_docs.shape[1]):
            offset = query_docs[query, j] - (device ^ d) * pool_dev
            slot = jnp.where(jnp.logical_and(offset >= 0, offset < pool_dev), j, slot)
        slots.append(slot)
    return (query, slots)


def prepare_body(here, query_docs, pool, ids, *outs):
    pool_dev = pool.shape[0]
    docs_per = query_docs.shape[1]
    rows = pool.shape[2] * pool.shape[3]
    device, lane = (here[0], here[1])
    for d, out in enumerate(outs):
        target = device ^ d
        query = query_of(target, lane)
        local = jnp.int32(0)
        for j in range(docs_per):
            offset = query_docs[query, j] - device * pool_dev
            inside = jnp.logical_and(offset >= 0, offset < pool_dev)
            local = jnp.where(inside, offset, local)
        out[:rows, :] = pool[local, target].reshape(rows, pool.shape[4])
        out[rows:, :] = ids[...]


def prepare(here, query_docs, pool, ids):
    _, _, pair, doc_max, head_dim = pool.shape
    shape = jax.ShapeDtypeStruct((pair * doc_max + ids.shape[0], head_dim), jnp.bfloat16)
    return call(
        prepare_body,
        [shape] * 4,
        [],
        in_specs=[SMEM, SMEM, VMEM, VMEM],
        out_specs=[VMEM] * 4,
        name="prepare",
    )(here, query_docs, pool, ids)


def angles_body(pool_dev, here, query_docs, ctx_pos, cos_q, sin_q, cos_d, sin_d):
    query, slots = document_slots(here, query_docs, pool_dev)
    docs_per = query_docs.shape[1]
    head_dim = cos_q.shape[1]

    def fill(starts, cosine, sine):
        column = lax.broadcasted_iota(jnp.int32, cosine.shape, 1)
        half = jnp.where(column < head_dim // 2, column, column - head_dim // 2)
        freq = jnp.exp(half.astype(jnp.float32) * (-2.0 * math.log(rope_theta) / head_dim))
        angle = starts.astype(jnp.float32) * freq
        cosine[...] = jnp.cos(angle)
        wave = jnp.sin(angle)
        sine[...] = jnp.where(column < head_dim // 2, -wave, wave)

    row = lax.broadcasted_iota(jnp.int32, cos_q.shape, 0)
    fill(ctx_pos[query, docs_per] + row, cos_q, sin_q)
    row = lax.broadcasted_iota(jnp.int32, cos_d.shape, 0)
    starts = jnp.zeros(cos_d.shape, jnp.int32)
    for d, slot in enumerate(slots):
        starts = jnp.where(row == d, ctx_pos[query, slot], starts)
    fill(starts, cos_d, sin_d)


def angles(here, query_docs, ctx_pos, pool_dev, length, head_dim):
    shapes = [jax.ShapeDtypeStruct((rows, head_dim), jnp.float32) for rows in (length, length, 8, 8)]
    return call(
        functools.partial(angles_body, pool_dev),
        shapes,
        [],
        in_specs=[SMEM] * 3,
        out_specs=[VMEM] * 4,
        name="angles",
    )(here, query_docs, ctx_pos)


def attention_body(
    pool_dev, here, query_docs, doc_lens, q, c0, c1, c2, c3, cos_q, sin_q, cos_d, sin_d, out, wide, keys, vals
):
    length, head_dim = cos_q.shape
    heads = out.shape[1] // head_dim
    pieces = (c0, c1, c2, c3)
    docs = len(pieces)
    doc_max = (keys.shape[0] - length) // docs
    half = head_dim // 2
    query, slots = document_slots(here, query_docs, pool_dev)

    def turned(x, cosine, sine):
        return x * cosine + pltpu.roll(x, half, 1) * sine

    cosine, sine = (cos_q[...], sin_q[...])
    for j, piece in enumerate(pieces):
        key = turned(piece[:doc_max, :].astype(jnp.float32), cos_d[j : j + 1, :], sin_d[j : j + 1, :])
        keys[j * doc_max : (j + 1) * doc_max, :] = key.astype(jnp.bfloat16)
        vals[j * doc_max : (j + 1) * doc_max, :] = piece[doc_max : 2 * doc_max, :]
    base = docs * doc_max
    first = heads * length
    keys[base:, :] = turned(q[first : first + length, :].astype(jnp.float32), cosine, sine).astype(
        jnp.bfloat16
    )
    vals[base:, :] = q[first + length :, :]
    wide[...] = q[:first, :].astype(jnp.float32)
    column = lax.broadcasted_iota(jnp.int32, (1, doc_max), 1)
    allowed = [column < doc_lens[query_docs[query, slot]] for slot in slots]
    causal = lax.broadcasted_iota(jnp.int32, (length, length), 0) >= lax.broadcasted_iota(
        jnp.int32, (length, length), 1
    )
    for h in range(heads):
        rows = turned(wide[pl.ds(h, length, stride=heads), :], cosine, sine).astype(jnp.bfloat16)
        scores = lax.dot_general(rows, keys[...], NT, preferred_element_type=jnp.float32)
        scores = scores * head_dim ** (-0.5)
        parts = [
            jnp.where(allowed[j], scores[:, j * doc_max : (j + 1) * doc_max], -jnp.inf)
            for j in range(docs)
        ] + [jnp.where(causal, scores[:, base:], -jnp.inf)]
        scores = jnp.concatenate(parts, axis=1)
        ceiling = jnp.max(scores, axis=1, keepdims=True)
        probs = jnp.exp(scores - ceiling)
        denominator = jnp.sum(probs, axis=1, keepdims=True)
        mixed = dot(probs.astype(jnp.bfloat16), vals[...])
        out[:, h * head_dim : (h + 1) * head_dim] = (mixed / denominator).astype(jnp.bfloat16)


def attention(here, query_docs, doc_lens, q, pieces, tables, pool_dev):
    length, head_dim = tables[0].shape
    heads = q.shape[0] // length - 2
    rows = 5 * length
    return call(
        functools.partial(attention_body, pool_dev),
        jax.ShapeDtypeStruct((length, heads * head_dim), jnp.bfloat16),
        [
            pltpu.VMEM((heads * length, head_dim), jnp.float32),
            pltpu.VMEM((rows, head_dim), jnp.bfloat16),
            pltpu.VMEM((rows, head_dim), jnp.bfloat16),
        ],
        in_specs=[SMEM] * 3 + [VMEM] * 9,
        out_specs=VMEM,
        name="attention",
    )(here, query_docs, doc_lens, q, *pieces, *tables)


def project_rows(here, flip, a, b, rows):
    device, lane = (here[0], here[1])
    high = (device ^ query_of(device, lane ^ flip)) >> 1
    rows[high] = a[...]
    rows[1 - high] = b[...]


def project_early_body(here, a, b, weight, close, far, rows):
    project_rows(here, 0, a, b, rows)
    far[...] = dot(rows[1], weight[...]).astype(jnp.bfloat16)
    close[...] = dot(rows[0], weight[...]).astype(jnp.bfloat16)


def project_late_body(here, a, b, weight, early, own, near, far, rows):
    project_rows(here, 2, a, b, rows)
    far[...] = dot(rows[1], weight[...]).astype(jnp.bfloat16)
    late = dot(rows[0], weight[...]).astype(jnp.bfloat16)
    first = here[1] < 2
    own[...] = jnp.where(first, early[...], late)
    near[...] = jnp.where(first, late, early[...])


def project(body, here, parts, weight, outs, *early):
    length, depth = parts[0].shape
    return call(
        body,
        [jax.ShapeDtypeStruct((length, weight.shape[1]), jnp.bfloat16)] * outs,
        [pltpu.VMEM((2, length, depth), jnp.bfloat16)],
        in_specs=[SMEM] + [VMEM] * (3 + len(early)),
        out_specs=[VMEM] * outs,
        name="project",
    )(here, *parts, weight, *early)


def routing_body(experts, here, c0, c1, c2, c3, pick, spread):
    _, local, capacity, length = pick.shape
    first = here[0] * local
    before = (
        lax.broadcasted_iota(jnp.int32, (length, length), 0)
        < lax.broadcasted_iota(jnp.int32, (length, length), 1)
    ).astype(jnp.bfloat16)
    place = lax.broadcasted_iota(jnp.int32, (capacity, length), 0).astype(jnp.float32)
    row = lax.broadcasted_iota(jnp.int32, (8, length), 0)
    for d, piece in enumerate((c0, c1, c2, c3)):
        ids = piece[piece.shape[0] - 16 :, :].astype(jnp.float32).astype(jnp.int32)
        chosen = jnp.zeros((8, length), jnp.float32)
        for k in range(8):
            named = jnp.logical_and(ids[k : k + 1, :] == first + row, row < local)
            chosen = jnp.where(named, 1.0, chosen)
        rank = dot(chosen.astype(jnp.bfloat16), before)
        wide = []
        for e in range(local):
            here_e = jnp.logical_and(rank[e : e + 1, :] == place, chosen[e : e + 1, :] > 0.0)
            wide.append(jnp.where(here_e, 1.0, 0.0))
            pick[d, e] = wide[-1].astype(jnp.bfloat16)
        spread[d] = jnp.transpose(jnp.concatenate(wide, axis=0)).astype(jnp.bfloat16)


def routing(here, pieces, experts, local, capacity):
    length = pieces[0].shape[1]
    rows = pieces[0].shape[0]
    return call(
        functools.partial(routing_body, experts),
        [
            jax.ShapeDtypeStruct((4, local, capacity, length), jnp.bfloat16),
            jax.ShapeDtypeStruct((4, length, local * capacity), jnp.bfloat16),
        ],
        [],
        in_specs=[SMEM] + [VMEM] * 4,
        out_specs=[VMEM] * 2,
        name="routing",
    )(here, *pieces)


def residual_body(hidden, p0, p1, p2, after, out):
    total = hidden[...].astype(jnp.float32) + p0[...].astype(jnp.float32)
    for part in (p1, p2):
        total = total + part[...].astype(jnp.float32)
    out[...] = total.astype(jnp.bfloat16)


def add_parts(hidden, parts, after):
    return call(
        residual_body,
        jax.ShapeDtypeStruct(hidden.shape, jnp.bfloat16),
        [],
        in_specs=[VMEM] * 4 + [pl.BlockSpec(memory_space=pl.ANY)],
        out_specs=VMEM,
        name="residual",
    )(hidden, *parts, after)


def measure_body(*refs):
    *tokens, gain, router, stats = refs
    rows = stats.shape[0]
    length = tokens[0].shape[0]
    for d, ref in enumerate(tokens):
        wide = ref[...].astype(jnp.float32)
        grown = wide * gain[...]
        high = grown.astype(jnp.bfloat16)
        rest = grown - high.astype(jnp.float32)
        middle = rest.astype(jnp.bfloat16)
        low = (rest - middle.astype(jnp.float32)).astype(jnp.bfloat16)
        logits = dot(high, router[...]) + (dot(middle, router[...]) + dot(low, router[...]))
        squares = jnp.sum(wide * wide, axis=1, keepdims=True)
        column = lax.broadcasted_iota(jnp.int32, logits.shape, 1)
        both = jnp.where(column == rows - 8, squares, logits)
        stats[:, d * length : (d + 1) * length] = jnp.transpose(both)[:rows, :]


def squares_and_logits(tokens, gain, router, experts):
    n, length = (len(tokens), tokens[0].shape[0])
    return call(
        measure_body,
        jax.ShapeDtypeStruct((experts + 8, n * length), jnp.float32),
        [],
        in_specs=[VMEM] * (n + 2),
        out_specs=VMEM,
        name="stats",
    )(*tokens, gain, router)


def gate_up_body(ds, order, *refs):
    tokens = refs[: len(ds)]
    gain, pick, weight, out, rows = refs[len(ds) :]
    hid = weight.shape[3]
    capacity = pick.shape[2]
    expert = order[pl.program_id(0)]
    for k, d in enumerate(ds):
        chosen = dot(pick[d, expert], tokens[k][...]) * gain[...]
        rows[k * capacity : (k + 1) * capacity, :] = chosen.astype(jnp.bfloat16)
    for g in range(2):
        out[0, :, g * hid : (g + 1) * hid] = dot(rows[...], weight[0, g]).astype(jnp.bfloat16)


def gate_up(ds, order, tokens, gain, pick, weight):
    _, _, width, hid = weight.shape
    count = order.shape[0]
    capacity = pick.shape[2]
    rows = len(ds) * capacity
    whole = lambda rank: lambda i, order: (0,) * rank
    return call(
        functools.partial(gate_up_body, ds),
        jax.ShapeDtypeStruct((count, rows, 2 * hid), jnp.bfloat16),
        None,
        grid_spec=pltpu.PrefetchScalarGridSpec(
            num_scalar_prefetch=1,
            grid=(count,),
            in_specs=[pl.BlockSpec(tokens[0].shape, whole(2))] * len(ds)
            + [
                pl.BlockSpec(gain.shape, whole(2)),
                pl.BlockSpec(pick.shape, whole(4)),
                pl.BlockSpec((1, 2, width, hid), lambda i, order: (order[i], 0, 0, 0)),
            ],
            out_specs=pl.BlockSpec((1, rows, 2 * hid), lambda i, order: (i, 0, 0)),
            scratch_shapes=[pltpu.VMEM((rows, width), jnp.bfloat16)],
        ),
        name="gate_up",
    )(order, *tokens, gain, pick, weight)


def activate_body(groups, features, offset, here, pick, stats, *refs):
    out = refs[-1]
    _, local, capacity, length = pick.shape
    hid = out.shape[1]
    experts = stats.shape[0] - 8
    device, lane = (here[0], here[1])
    expert = lax.broadcasted_iota(jnp.int32, (experts, length), 0)
    base, refs = (0, list(refs))
    for ds in groups:
        kept, taken, across = refs[:3]
        pieces = refs[3 : 3 + len(ds)]
        refs = refs[3 + len(ds) :]
        for k, d in enumerate(ds):
            ids = pieces[k][pieces[k].shape[0] - 16 :, :].astype(jnp.float32).astype(jnp.int32)
            chosen = jnp.zeros((experts, length), jnp.float32)
            for c in range(8):
                chosen = jnp.where(ids[c : c + 1, :] == expert, 1.0, chosen)
            block = slice((offset + k) * length, (offset + k + 1) * length)
            inv_rms = lax.rsqrt(stats[experts : experts + 1, block] / features + norm_eps)
            logits = jnp.where(chosen > 0.0, stats[:experts, block] * inv_rms, -jnp.inf)
            grown = jnp.exp(logits - jnp.max(logits, axis=0, keepdims=True))
            mix = grown / jnp.sum(grown, axis=0, keepdims=True)
            mine = jnp.where(expert == device * local + lane, mix, 0.0)
            mix = jnp.sum(mine, axis=0, keepdims=True)
            places = pick[d, lane].astype(jnp.float32)
            inv_row = jnp.sum(places * inv_rms, axis=1, keepdims=True)
            mix_row = jnp.sum(places * mix, axis=1, keepdims=True)
            rows = slice(k * capacity, (k + 1) * capacity)
            summed = kept[0, rows, :].astype(jnp.float32) + taken[0, rows, :].astype(jnp.float32)
            summed = (summed + across[rows, :].astype(jnp.float32)) * inv_row
            gate = summed[:, :hid]
            act = gate / (1.0 + jnp.exp(-gate)) * summed[:, hid:] * mix_row
            out[base + k * capacity : base + (k + 1) * capacity, :] = act.astype(jnp.bfloat16)
        base += len(ds) * capacity
        offset += len(ds)


def activate(groups, features, here, sums, pick, stats, pieces, flops=1 << 20, offset=0):
    operands = []
    for ds, terms in zip(groups, sums):
        operands += list(terms) + [pieces[d] for d in ds]
    rows = sum(terms[2].shape[0] for terms in sums)
    return call(
        functools.partial(activate_body, groups, features, offset),
        jax.ShapeDtypeStruct((rows, sums[0][2].shape[1] // 2), jnp.bfloat16),
        [],
        in_specs=[SMEM] + [VMEM] * (2 + len(operands)),
        out_specs=VMEM,
        flops=flops,
        name="activate",
    )(here, pick, stats, *operands)


def down_body(ds, order, a, b, c, d, spread, weight, *rest):
    outs, results = (rest[:-1], rest[-1])
    i = pl.program_id(0)
    capacity = results.shape[2]
    expert = order[i]
    for j, ref in enumerate((a, b, c, d)):

        @pl.when(i == j)
        def _():
            result = dot(ref[...], weight[0]).astype(jnp.bfloat16)
            for k in range(len(ds)):
                results[k, expert] = result[k * capacity : (k + 1) * capacity, :]

    @pl.when(i == pl.num_programs(0) - 1)
    def _():
        half = spread.shape[1] // 2
        for k, d in enumerate(ds):
            rows = results[k].reshape(-1, results.shape[3])
            block = dot(spread[d], rows).astype(jnp.bfloat16)
            if len(outs) == len(ds):
                outs[k][...] = block
            else:
                outs[2 * k][...] = block[:half]
                outs[2 * k + 1][...] = block[half:]


def down(ds, order, acts, spread, weight, halved=False):
    local, hid, width = weight.shape
    capacity = acts[0].shape[0] // len(ds)
    length = spread.shape[1]
    shape = jax.ShapeDtypeStruct((length, width), jnp.bfloat16)
    half = jax.ShapeDtypeStruct((length // 2, width), jnp.bfloat16)
    shapes = [half] * (2 * len(ds)) if halved else [shape] * len(ds)
    whole = lambda rank: lambda i, order: (0,) * rank
    return call(
        functools.partial(down_body, ds),
        shapes,
        None,
        grid_spec=pltpu.PrefetchScalarGridSpec(
            num_scalar_prefetch=1,
            grid=(local,),
            in_specs=[pl.BlockSpec(acts[0].shape, whole(2))] * 4
            + [
                pl.BlockSpec(spread.shape, whole(3)),
                pl.BlockSpec((1, hid, width), lambda i, order: (order[i], 0, 0)),
            ],
            out_specs=[pl.BlockSpec(s.shape, whole(2)) for s in shapes],
            scratch_shapes=[pltpu.VMEM((len(ds), local, capacity, width), jnp.bfloat16)],
        ),
        name="down",
    )(order, *acts, spread, weight)


def per_device_square(
    question_q,
    question_kv,
    doc_kv,
    doc_lens,
    query_docs,
    ctx_pos,
    hidden,
    out_proj,
    norm_gain,
    router_weight,
    w_gate_up,
    w_down,
    expert_ids,
):
    n = 4
    lane = lax.axis_index("tp")
    device = lax.axis_index("ep")
    length, heads_here, head_dim = question_q.shape
    pool_dev = doc_kv.shape[0]
    width_here = hidden.shape[1]
    experts = router_weight.shape[1]
    local = w_gate_up.shape[0]
    capacity = length * expert_ids.shape[1] // experts
    here = jnp.stack([device, lane]).astype(jnp.int32)
    order = (lane ^ jnp.array([0, 2, 1, 3], jnp.int32)).astype(jnp.int32)

    pool = jnp.transpose(doc_kv, (0, 2, 3, 1, 4))
    ids_rows = jnp.pad(expert_ids.T.astype(jnp.bfloat16), ((0, 8), (0, 0)))
    pieces = prepare(here, query_docs, pool, ids_rows)
    q_rows, pieces = turn(
        question_q.reshape(length * heads_here, head_dim), question_kv, device, lane, n, pieces
    )
    pieces = [pieces[0]] + [lax.ppermute(pieces[d], "ep", pairs(n, d)) for d in range(1, n)]
    tables = list(angles(here, query_docs, ctx_pos, pool_dev, length, head_dim))

    one = lax.optimization_barrier(jnp.ones((), jnp.bfloat16))
    tables[0], out_proj = lax.optimization_barrier((tables[0], out_proj * one))
    attended = attention(here, query_docs, doc_lens, q_rows, pieces, tables, pool_dev)
    far = lax.ppermute(attended, "tp", pairs(n, 2))
    near = lax.ppermute(attended, "tp", pairs(n, 1))
    farther = lax.ppermute(far, "tp", pairs(n, 1))
    gain = norm_gain.astype(jnp.float32)[None, :]
    router = jnp.pad(router_weight, ((0, 0), (0, 128 - experts)))
    close, early = project(project_early_body, here, (attended, near), out_proj, 2)
    given = lax.ppermute(early, "ep", pairs(n, 1))
    kept, near, late = project(project_late_body, here, (far, farther), out_proj, 3, close)
    kept, w_gate_up = lax.optimization_barrier((kept, w_gate_up))
    late = (late.astype(jnp.float32) + given.astype(jnp.float32)).astype(jnp.bfloat16)
    moves = [
        (e * n + t, (e ^ (3 if t < 2 else 2)) * n + t) for e in range(n) for t in range(n)
    ]
    sent = [kept, lax.ppermute(late, ("ep", "tp"), moves), lax.ppermute(near, "ep", pairs(n, 1))]
    pick, spread = routing(here, pieces, experts, local, capacity)
    weight = jnp.transpose(w_gate_up, (0, 2, 1, 3))
    sent[0], pick, router, gain = lax.optimization_barrier((sent[0], pick, router, gain))
    residual = add_parts(hidden, sent, weight)

    tokens = [residual] + [None] * (n - 1)
    for d in (2, 1):
        tokens[d] = lax.ppermute(residual, "ep", pairs(n, d))
    tokens[3] = lax.ppermute(tokens[2], "ep", pairs(n, 1))

    features = width_here * n

    def spread_act(act, before=()):
        far = lax.ppermute(act, "tp", pairs(n, 2))
        far, *before = lax.optimization_barrier((far, *before))
        near = lax.ppermute(act, "tp", pairs(n, 1))
        return [act, far, near, lax.ppermute(far, "tp", pairs(n, 1))]

    def chip_sum(kept, taken):
        return (kept[1].astype(jnp.float32) + taken[1].astype(jnp.float32)).astype(jnp.bfloat16)

    def terms_of(ds, order):
        blocks = [tokens[d] for d in ds]
        given = gate_up(ds, order[2:], blocks, gain, pick, weight)
        return (gate_up(ds, order[:2], blocks, gain, pick, weight), given)

    def stats_of(ds):
        return squares_and_logits([tokens[d] for d in ds], gain, router, experts)

    one_chunk = (1, 2)
    kept_0, given_0 = terms_of((0,), order)
    order, kept_0, given_0 = lax.optimization_barrier((order, kept_0, given_0))
    kept, given = terms_of(one_chunk, order)
    taken = lax.ppermute(given, "tp", pairs(n, 1))
    _, stats = lax.optimization_barrier((given, stats_of(one_chunk)))
    stats_far = lax.ppermute(stats, "tp", pairs(n, 2))
    taken, stats_far = lax.optimization_barrier((taken, stats_far))
    stats = stats + stats_far
    stats_near = lax.ppermute(stats, "tp", pairs(n, 1))
    far_sum = chip_sum(kept, taken)
    across = lax.ppermute(far_sum, "tp", pairs(n, 2))

    order, _, stats_near = lax.optimization_barrier((order, far_sum, stats_near))
    stats = stats + stats_near
    kept_3, given_3 = terms_of((3,), order)
    stats_2 = stats_of((3, 0))
    given_3, given_0, across, stats_2 = lax.optimization_barrier((given_3, given_0, across, stats_2))
    stats_far = lax.ppermute(stats_2, "tp", pairs(n, 2))
    taken_3 = lax.ppermute(given_3, "tp", pairs(n, 1))
    taken_0 = lax.ppermute(given_0, "tp", pairs(n, 1))
    sums = [(kept, taken, across)]
    acts = spread_act(activate((one_chunk,), features, here, sums, pick, stats, pieces))
    sum_3, sum_0 = (chip_sum(kept_3, taken_3), chip_sum(kept_0, taken_0))
    sum_3, sum_0, stats_far, acts[1] = lax.optimization_barrier((sum_3, sum_0, stats_far, acts[1]))
    stats_2 = stats_2 + stats_far
    stats_near = lax.ppermute(stats_2, "tp", pairs(n, 1))
    acts[3] = lax.ppermute(acts[1], "tp", pairs(n, 1))
    acts[3], stats_near = lax.optimization_barrier((acts[3], stats_near))
    across_3 = lax.ppermute(sum_3, "tp", pairs(n, 2))
    across_0 = lax.ppermute(sum_0, "tp", pairs(n, 2))
    parts = down(one_chunk, order, acts, spread, w_down, halved=True)
    across_3, *parts = lax.optimization_barrier((across_3, *parts))
    far = [lax.ppermute(part, "ep", pairs(n, 2)) for part in parts[2:]]
    near = [lax.ppermute(part, "ep", pairs(n, 1)) for part in parts[:2]]
    stats_2 = stats_2 + stats_near
    sums = [(kept_3, taken_3, across_3)]
    act_3 = activate(((3,),), features, here, sums, pick, stats_2, pieces)
    across_0, far[0], near[0] = lax.optimization_barrier((across_0, far[0], near[0]))
    acts = spread_act(act_3)
    sums = [(kept_0, taken_0, across_0)]
    act_0 = activate(((0,),), features, here, sums, pick, stats_2, pieces, 1 << 20, 1)
    acts_0 = spread_act(act_0, (far[1], near[1]))
    (last,) = down((3,), order, acts, spread, w_down)
    last, *acts_0 = lax.optimization_barrier((last, *acts_0))
    last = lax.ppermute(last, "ep", pairs(n, 3))
    (mine,) = down((0,), order, acts_0, spread, w_down)
    returned = [mine, jnp.concatenate(near, axis=0), jnp.concatenate(far, axis=0), last]
    total = residual.astype(jnp.float32)
    for part in returned:
        total = total + part.astype(jnp.float32)
    return total.astype(jnp.bfloat16)


def solution(mesh):
    placed = (
        P(("grp", "ep"), "tp", None),
        P(("grp", "ep"), None, None, None),
        P(("grp", "ep"), None, None, None, None),
        P("grp"),
        P("grp", None),
        P("grp", None),
        P(("grp", "ep"), "tp"),
        P("ep", "tp"),
        P("tp"),
        P("tp", None),
        P("ep", "tp", None, None),
        P("ep", None, "tp"),
        P(("grp", "ep"), None),
    )
    def per_device(*args):
        square = (
            lax.axis_size("tp") == 4
            and lax.axis_size("ep") == 4
            and args[1].shape[1] == 4
            and args[4].shape == (4, 4)
        )
        return (per_device_square if square else per_device_general)(*args)

    return jax.shard_map(
        per_device, mesh=mesh, in_specs=placed, out_specs=P(("grp", "ep"), "tp"), check_vma=False
    )
```
